128 devices in a mesh: ctx: 16 (over y, x_lo, core), fsdp: 8 (over x_hi, z).
Axes of the slice: x: 4 (x_hi: 2, x_lo: 2; x = x_hi * 2 + x_lo), y: 4, z: 4, core: 2. Of those that a mesh axis runs over, the one named last changes fastest.
Arguments:
- tokens: bfloat16 [8, 2048, 1536], P('fsdp', 'ctx'), may hold values from -6 to 6
- cotangent: bfloat16 [8, 2048, 1536], P('fsdp', 'ctx'), may hold values from -6 to 6
- routes: int32 [8, 2048, 6], P('fsdp', 'ctx'), may hold values from 0 to 63, all different within a row; in each aligned block of 128 rows (0 to 127, 128 to 255, ..., all dimensions but the last counted through in order) at most 24 rows name the same one
- gates: float32 [8, 2048, 6], P('fsdp', 'ctx'), may hold values from 0.08 to 0.25
- attn_gain: bfloat16 [1536], P(('ctx', 'fsdp')), may hold values from 0.5 to 1.5
- ffn_gain: bfloat16 [1536], P(('ctx', 'fsdp')), may hold values from 0.5 to 1.5
- w_query: bfloat16 [1536, 1536], P(('ctx', 'fsdp')), may hold values from -0.15625 to 0.15625
- key_weight_matrix: bfloat16 [1536, 512], P(('ctx', 'fsdp')), may hold values from -0.15625 to 0.15625
- value_weight_matrix: bfloat16 [1536, 512], P(('ctx', 'fsdp')), may hold values from -0.15625 to 0.15625
- w_out: bfloat16 [1536, 1536], P(None, ('ctx', 'fsdp')), may hold values from -3.5 to 3.5
- shared_gate: bfloat16 [1536, 1024], P(('ctx', 'fsdp')), may hold values from -0.15625 to 0.15625
- shared_up: bfloat16 [1536, 1024], P(('ctx', 'fsdp')), may hold values from -0.15625 to 0.15625
- shared_down: bfloat16 [1024, 1536], P(None, ('ctx', 'fsdp')), may hold values from -0.375 to 0.375
- expert_gate: bfloat16 [64, 1536, 512], P('ctx', 'fsdp'), may hold values from -0.15625 to 0.15625
- expert_up: bfloat16 [64, 1536, 512], P('ctx', 'fsdp'), may hold values from -0.15625 to 0.15625
- expert_down: bfloat16 [64, 512, 1536], P('ctx', None, 'fsdp'), may hold values from -1 to 1
Outputs:
- layer_out: bfloat16 [8, 2048, 1536], P('fsdp', 'ctx')
- input_grad: float32 [8, 2048, 1536], P('fsdp', 'ctx')
- attn_gain_grad: float32 [1536], P(('ctx', 'fsdp'))
- ffn_gain_grad: float32 [1536], P(('ctx', 'fsdp'))
- w_query_grad: float32 [1536, 1536], P(('ctx', 'fsdp'))
- w_key_grad: float32 [1536, 512], P(('ctx', 'fsdp'))
- w_value_grad: float32 [1536, 512], P(('ctx', 'fsdp'))
- w_out_grad: float32 [1536, 1536], P(None, ('ctx', 'fsdp'))
- shared_gate_grad: float32 [1536, 1024], P(('ctx', 'fsdp'))
- shared_up_grad: float32 [1536, 1024], P(('ctx', 'fsdp'))
- shared_down_grad: float32 [1024, 1536], P(None, ('ctx', 'fsdp'))
- expert_gate_grad: float32 [64, 1536, 512], P('ctx', 'fsdp')
- expert_up_grad: float32 [64, 1536, 512], P('ctx', 'fsdp')
- expert_down_grad: float32 [64, 512, 1536], P('ctx', None, 'fsdp')
The draws below stay inside these ranges and needn't reach their ends.
Inputs may be any that keep to these rules, and one draw needn't show every extreme that they name: `routes`: each row names 6 different experts. Among the rows of one device (an aligned block of 128 positions of a sequence) no expert is named more than 24 times, and in every draw some device's rows name one expert exactly 24 times.
All inputs are finite; a program needn't handle non-finite values.
Results may differ from the reference program's by a relative error of at most 0.04.
Values may be sent and summed in bfloat16 or wider, within the bound.
A program may use at most 256 MiB of HBM per device.

```python
import math
import jax
import jax.numpy as jnp
import numpy as np
from jax import lax

MODEL_DIMENSION = 1536
HQ = 12
KEY_VALUE_HEADS = 4
HEAD_DIMENSION = 128
H_EXP = 512
H_SH = 1024
TOP = 6
TOK_DEV = 128
EXPERTS = 64
LEN = 2048
SEQS = 8
CAP = 24
N_CTX = 16


def block_levels(key, dims, split, least, high):
    level = 1.0
    for position, shards_of in split:
        heights = jax.random.uniform(jax.random.fold_in(jax.random.fold_in(key, 6), position), (shards_of,), jnp.float32, least / len(split), high / len(split))
        level = level * jnp.repeat(jnp.exp(heights), dims[position] // shards_of).reshape((-1,) + (1,) * (len(dims) - 1 - position))
    return level


def shared_out(stream_key, own, number, rows, number_of, top, reach, skew):
    sequence = jax.random.permutation(stream_key, number_of)
    packed, ordinary = portions_of(number_of, rows * top, reach, skew, True), portions_of(number_of, rows * top, reach, skew, False)
    places = jnp.arange(number_of)

    def named(lengths, offset_by):
        used = int((lengths > 0).sum())
        fixed = max(1, used // 4)
        moved = fixed + (places - fixed + offset_by * (used - fixed)) % max(1, number_of - fixed)
        return jnp.zeros((number_of,), jnp.int32).at[sequence[jnp.where(places < fixed, places, moved)]].set(jnp.asarray(lengths, jnp.int32))

    lengths = jnp.where(number % 4 == 0, named(packed, number // 4), named(ordinary, number - number // 4 - 1))
    mixed = jax.random.permutation(jax.random.fold_in(own, 3), number_of)
    donor, taker = mixed[0:number_of // 2 * 2:2], mixed[1:number_of // 2 * 2:2]
    slack = jnp.minimum(lengths[donor] - 1, reach - lengths[taker]) // 2
    slack = jnp.where((donor == sequence[0]) | (taker == sequence[0]) | (lengths[taker] == 0), 0, jnp.maximum(slack, 0))
    moved = jax.random.randint(jax.random.fold_in(own, 4), (number_of // 2,), 0, 1 << 20) % (slack + 1)
    lengths = lengths.at[donor].add(-moved).at[taker].add(moved)
    labels = jnp.searchsorted(jnp.cumsum(lengths), jnp.arange(rows * top), side="right").astype(jnp.int32)
    table = labels.reshape(top, rows).T
    table = table[jax.random.permutation(jax.random.fold_in(own, 1), rows)]
    offset_by = jax.random.randint(jax.random.fold_in(own, 2), (rows, 1), 0, top)
    return jnp.take_along_axis(table, (jnp.arange(top)[None, :] + offset_by) % top, axis=1)


def portions_of(number_of, total, most, lean, full):
    weights = [(1 << 20) // math.isqrt(standing ** lean) + 1 for standing in range(1, number_of + 1)]
    largest = most if full else min(most, max(-(-total // number_of), total * weights[0] // sum(weights)))
    least = 1 if total - largest >= number_of - 1 else 0
    counts, spare = [largest] + [least] * (number_of - 1), total - largest - least * (number_of - 1)
    while spare > 0:
        free = [i for i in range(1, number_of) if counts[i] < largest] or [i for i in range(1, number_of) if counts[i] < most]
        whole, left = sum([weights[i] for i in free]), spare
        for i in free:
            addition = min(most - counts[i], max(1, left * weights[i] // whole), spare)
            counts[i] = counts[i] + addition
            spare = spare - addition
    return np.array(counts)


def scatter_about(own_key, extent, spread, reach, split=(), held_as=jnp.bfloat16):
    result = spread * jax.random.normal(own_key, extent, jnp.float32)
    if split:
        result = result * block_levels(own_key, extent, split, -0.22, 0.18)
    return jnp.clip(result, -reach, reach).astype(held_as)


def setup_inputs(seed: int = 0) -> dict:
    key_of = jax.random.split(jax.random.key(seed), 17)
    tokens = scatter_about(key_of[0], (SEQS, LEN, MODEL_DIMENSION), 1.0, 6.0, ((0, 8), (1, 16)))
    cotangent = scatter_about(key_of[1], (SEQS, LEN, MODEL_DIMENSION), 1.0, 6.0, ((0, 8), (1, 16)))
    routes_keys = jax.random.split(jax.random.fold_in(key_of[2], 1), SEQS * LEN // TOK_DEV)
    routes_turns = jax.random.permutation(jax.random.fold_in(key_of[2], 3), SEQS * LEN // TOK_DEV)
    routes = jax.vmap(lambda own, number: shared_out(jax.random.fold_in(key_of[2], 2), own, number, TOK_DEV, EXPERTS, TOP, CAP, 1))(routes_keys, routes_turns).reshape((SEQS, LEN, TOP))
    gates = jnp.clip(0.08 + 0.17 * jax.random.uniform(key_of[3], (SEQS, LEN, TOP), jnp.float32) ** block_levels(key_of[3], (SEQS, LEN, TOP), ((0, 8), (1, 16)), -0.2, 0.2), 0.08, 0.25)
    attn_gain = jnp.clip(1.0 + 0.1 * jax.random.normal(key_of[4], (MODEL_DIMENSION,), jnp.float32), 0.5, 1.5).astype(jnp.bfloat16)
    ffn_gain = jnp.clip(1.0 + 0.1 * jax.random.normal(key_of[5], (MODEL_DIMENSION,), jnp.float32), 0.5, 1.5).astype(jnp.bfloat16)
    w_query = scatter_about(key_of[6], (MODEL_DIMENSION, HQ * HEAD_DIMENSION), MODEL_DIMENSION ** -0.5, 0.15625, ((0, 128),))
    key_weight_matrix = scatter_about(key_of[7], (MODEL_DIMENSION, KEY_VALUE_HEADS * HEAD_DIMENSION), MODEL_DIMENSION ** -0.5, 0.15625, ((0, 128),))
    value_weight_matrix = scatter_about(key_of[8], (MODEL_DIMENSION, KEY_VALUE_HEADS * HEAD_DIMENSION), MODEL_DIMENSION ** -0.5, 0.15625, ((0, 128),))
    w_out = scatter_about(key_of[9], (HQ * HEAD_DIMENSION, MODEL_DIMENSION), (max(HQ * HEAD_DIMENSION * 4 // LEN, 1)) ** -0.5, 3.5, ((1, 128),))
    shared_gate = scatter_about(key_of[10], (MODEL_DIMENSION, H_SH), MODEL_DIMENSION ** -0.5, 0.15625, ((0, 128),))
    shared_up = scatter_about(key_of[11], (MODEL_DIMENSION, H_SH), MODEL_DIMENSION ** -0.5, 0.15625, ((0, 128),))
    shared_down = scatter_about(key_of[12], (H_SH, MODEL_DIMENSION), (H_SH // 4) ** -0.5, 0.375, ((1, 128),))
    expert_gate = scatter_about(key_of[13], (EXPERTS, MODEL_DIMENSION, H_EXP), MODEL_DIMENSION ** -0.5, 0.15625, ((0, 16), (1, 8)))
    expert_up = scatter_about(key_of[14], (EXPERTS, MODEL_DIMENSION, H_EXP), MODEL_DIMENSION ** -0.5, 0.15625, ((0, 16), (1, 8)))
    expert_down = scatter_about(key_of[15], (EXPERTS, H_EXP, MODEL_DIMENSION), (H_EXP // 16) ** -0.5, 1.0, ((0, 16), (2, 8)))
    return {"tokens": tokens, "cotangent": cotangent, "routes": routes, "gates": gates, "attn_gain": attn_gain, "ffn_gain": ffn_gain, "w_query": w_query, "key_weight_matrix": key_weight_matrix, "value_weight_matrix": value_weight_matrix, "w_out": w_out, "shared_gate": shared_gate, "shared_up": shared_up, "shared_down": shared_down, "expert_gate": expert_gate, "expert_up": expert_up, "expert_down": expert_down}


EPS = 1e-05
PRECISE = lax.Precision.HIGHEST

@jax.custom_vjp
def low(v):
    return lax.optimization_barrier(v.astype(jnp.bfloat16)).astype(jnp.float32)

@jax.custom_vjp
def low_back(v):
    return v

def low_keep(v):
    return (low(v), None)

def low_pass(kept, grad):
    return (grad,)

def back_keep(v):
    return (v, None)

def back_low(kept, grad):
    return (low(grad),)
low.defvjp(low_keep, low_pass)
low_back.defvjp(back_keep, back_low)

def rms_norm(values, gain_vec):
    return values * lax.rsqrt(lax.optimization_barrier(jnp.mean(values * values, -1, keepdims=True)) + EPS) * gain_vec

def matmul(left_mat, right_mat):
    return jnp.dot(left_mat, right_mat, precision=PRECISE)

def attention(queries, keys, values):
    seq_len = queries.shape[0]
    row_block = min(512, seq_len)
    kv_heads = keys.shape[1] // HEAD_DIMENSION
    groups = queries.shape[1] // keys.shape[1]
    key_heads = keys.reshape(seq_len, kv_heads, HEAD_DIMENSION)
    value_heads = values.reshape(seq_len, kv_heads, HEAD_DIMENSION)
    query_blocks = queries.reshape(seq_len // row_block, row_block, kv_heads, groups, HEAD_DIMENSION)
    block_starts = jnp.arange(seq_len // row_block, dtype=jnp.int32) * row_block
    key_pos = jnp.arange(seq_len, dtype=jnp.int32)

    def one_block(block_item):
        query_block, first_row = block_item
        scores = jnp.einsum('tkgd,rkd->kgtr', query_block, key_heads, precision=PRECISE) * HEAD_DIMENSION ** (-0.5)
        scores = low_back(scores)
        query_pos = first_row + jnp.arange(row_block, dtype=jnp.int32)
        allowed = key_pos[None, :] <= query_pos[:, None]
        softmax_w = jax.nn.softmax(jnp.where(allowed, scores, -jnp.inf), axis=-1)
        return jnp.einsum('kgtr,rkd->tkgd', low(softmax_w), value_heads, precision=PRECISE)
    outputs = lax.map(jax.checkpoint(one_block), (query_blocks, block_starts))
    return outputs.reshape(seq_len, queries.shape[1])

def swiglu(hidden, gate_mat, up_mat, down_mat):
    gate_pre = low_back(matmul(hidden, gate_mat))
    up_preactivation = low_back(matmul(hidden, up_mat))
    return matmul(low(jax.nn.silu(gate_pre) * up_preactivation), down_mat)

def experts(hidden, route_ids, gate_vals, expert_gate, expert_up, expert_down):
    model_width = hidden.shape[1]
    flat_ids = route_ids.reshape(N_CTX, TOK_DEV * TOP)
    onehot = (flat_ids[:, :, None] == jnp.arange(EXPERTS, dtype=jnp.int32)[None, None, :]).astype(jnp.int32)
    slot_index = lax.optimization_barrier(jnp.sum(onehot * jnp.cumsum(onehot, 1), 2)) - 1
    source = jnp.arange(N_CTX, dtype=jnp.int32)[:, None]
    target = ((flat_ids * N_CTX + source) * CAP + slot_index).reshape(-1).astype(jnp.int32)
    route_rows = low_back(jnp.repeat(hidden, TOP, 0))
    buffer = jnp.zeros((EXPERTS * N_CTX * CAP, model_width), jnp.float32).at[target].set(route_rows)
    buffer = buffer.reshape(EXPERTS, N_CTX * CAP, model_width)
    gate_pre = low_back(jnp.einsum('erd,edh->erh', buffer, expert_gate, precision=PRECISE))
    up_preactivation = low_back(jnp.einsum('erd,edh->erh', buffer, expert_up, precision=PRECISE))
    inner_rows = low(jax.nn.silu(gate_pre) * up_preactivation)
    out_rows = low(low_back(jnp.einsum('erh,ehd->erd', inner_rows, expert_down, precision=PRECISE)))
    route_out = out_rows.reshape(-1, model_width)[target].reshape(hidden.shape[0], TOP, model_width)
    return lax.optimization_barrier(jnp.sum(route_out * gate_vals[:, :, None], 1))

def block_layer(weights, inputs, route_ids, gate_vals):
    gain_one, gain_two, w_query, key_weight_matrix, value_weight_matrix, w_out, shared_gate, shared_up, shared_down, expert_gate, expert_up, expert_down = weights
    hidden_one = low(rms_norm(inputs, gain_one))
    queries = low(low_back(matmul(hidden_one, w_query)))
    keys = low(low_back(matmul(hidden_one, key_weight_matrix)))
    values = low(low_back(matmul(hidden_one, value_weight_matrix)))
    attended = low(low_back(attention(queries, keys, values)))
    resid = inputs + low_back(matmul(attended, w_out))
    hidden_two = low(rms_norm(resid, gain_two))
    routed = experts(hidden_two, route_ids, gate_vals, expert_gate, expert_up, expert_down)
    return resid + routed + swiglu(hidden_two, shared_gate, shared_up, shared_down)

def reference(tokens, cotangent, routes, gates, attn_gain, ffn_gain, w_query, key_weight_matrix, value_weight_matrix, w_out, shared_gate, shared_up, shared_down, expert_gate, expert_up, expert_down):
    weights = tuple((weight.astype(jnp.float32) for weight in (attn_gain, ffn_gain, w_query, key_weight_matrix, value_weight_matrix, w_out, shared_gate, shared_up, shared_down, expert_gate, expert_up, expert_down)))
    inputs = tokens.astype(jnp.float32)
    seq_step = jax.checkpoint(block_layer)

    def forward(weight_set, input_set):

        def scan_body(carry_sum, seq_item):
            return (carry_sum, seq_step(weight_set, seq_item[0], seq_item[1], seq_item[2]))
        _, seq_outs = lax.scan(scan_body, jnp.zeros((), jnp.float32), (input_set, routes, gates))
        return seq_outs
    layer_vals, pull_back = jax.vjp(forward, weights, inputs)
    weight_grads, input_grad = pull_back(cotangent.astype(jnp.float32))
    return (layer_vals.astype(jnp.bfloat16), input_grad, weight_grads[0], weight_grads[1], weight_grads[2], weight_grads[3], weight_grads[4], weight_grads[5], weight_grads[6], weight_grads[7], weight_grads[8], weight_grads[9], weight_grads[10], weight_grads[11])
```

```python
import functools

import jax
import jax.numpy as jnp
from jax import lax
from jax.experimental import pallas as pl
from jax.experimental.pallas import tpu as pltpu
from jax.sharding import PartitionSpec as P

BF = jnp.bfloat16
F32 = jnp.float32
EPS = 1e-05
MESH = pl.DeviceIdType.MESH
ANY = pl.BlockSpec(memory_space=pl.ANY)
VM = pl.BlockSpec(memory_space=pltpu.VMEM)
SDS = jax.ShapeDtypeStruct
SCALE = 128 ** (-0.5)
VMEM_LIMIT = 56 * 2**20


def nn(a, b):
    return lax.dot_general(a, b, (((1,), (0,)), ((), ())), preferred_element_type=F32)


def nt(a, b):
    return lax.dot_general(a, b, (((1,), (1,)), ((), ())), preferred_element_type=F32)


def tn(a, b):
    return lax.dot_general(a, b, (((0,), (0,)), ((), ())), preferred_element_type=F32)


def silu_parts(pre_act):
    sig = 1.0 / (1.0 + jnp.exp(-pre_act))
    return pre_act * sig, sig * (1.0 + pre_act * (1.0 - sig))


def coords():
    c = lax.axis_index("ctx")
    f = lax.axis_index("fsdp")
    return c // 4, (c // 2) % 2, c % 2, f // 4, f % 4


def dev(y, xl, co, xh, z):
    return (y * 4 + xl * 2 + co, xh * 4 + z)


def barrier(peers):
    sem = pltpu.get_barrier_semaphore()
    for peer in peers:
        pl.semaphore_signal(sem, inc=1, device_id=peer, device_id_type=MESH)
    pl.semaphore_wait(sem, len(peers))


class Copies:
    def __init__(self, send, recv):
        self.send, self.recv, self.n, self.started = send, recv, 0, []

    def start(self, src, dst, peer):
        copy = pltpu.make_async_remote_copy(
            src, dst, self.send.at[self.n], self.recv.at[self.n], device_id=peer, device_id_type=MESH
        )
        copy.start()
        self.n += 1
        self.started.append(copy)
        return copy

    def finish(self, received=()):
        for copy in self.started:
            copy.wait_send()
            if not any(copy is r for r in received):
                copy.wait_recv()


def remote(kernel, outs, ins, copies, local, cid, scratch=()):
    return pl.pallas_call(
        kernel,
        out_shape=outs,
        in_specs=[ANY] * len(ins),
        out_specs=jax.tree.map(lambda _: ANY, outs),
        scratch_shapes=[
            pltpu.SemaphoreType.DMA((copies,)),
            pltpu.SemaphoreType.DMA((copies,)),
            pltpu.SemaphoreType.DMA((local,)),
        ]
        + list(scratch),
        compiler_params=pltpu.CompilerParams(
            collective_id=cid, has_side_effects=True, vmem_limit_bytes=VMEM_LIMIT
        ),
    )(*ins)


Y_STEPS = (1, 2, 3)
F_STEPS = tuple((dx, dz) for dx in (0, 1) for dz in range(4) if (dx, dz) != (0, 0))
C_STEPS = tuple((dy, dx) for dy in range(4) for dx in (0, 1) if (dy, dx) != (0, 0))


def gather_start_kernel(
    a_in, b_in, tok, cot, rg, wf, bfull, tokf, cotf, rgf, a2, b1, send, recv, loc
):
    y, xl, co, xh, z = coords()
    c, f = y * 4 + xl * 2 + co, xh * 4 + z
    sib = dev(y, xl, 1 - co, xh, z)
    xpeer = dev(y, 1 - xl, co, xh, z)
    fpeers = [dev(y, xl, co, (xh + dx) % 2, (z + dz) % 4) for dx, dz in F_STEPS]
    cpeers = [
        ((y + dy) % 4, (xl + dx) % 2, (co + dc) % 2)
        for dy in range(4)
        for dx in (0, 1)
        for dc in (0, 1)
        if (dy, dx, dc) != (0, 0, 0)
    ]
    barrier([dev(*p, xh, z) for p in cpeers] + fpeers)
    cp = Copies(send, recv)
    got = []
    lc = [
        pltpu.make_async_copy(a_in.at[y], a2.at[y, xl], loc.at[0]),
        pltpu.make_async_copy(b_in.at[c], b1.at[c], loc.at[1]),
        pltpu.make_async_copy(tok, tokf.at[y], loc.at[2]),
        pltpu.make_async_copy(cot, cotf.at[c], loc.at[3]),
        pltpu.make_async_copy(rg, rgf.at[c], loc.at[4]),
    ]
    for copy in lc:
        copy.start()
    first = [
        cp.start(a_in.at[(y + d) % 4], a2.at[y, xl], dev((y + d) % 4, xl, co, xh, z))
        for d in Y_STEPS
    ]
    bs = [cp.start(b_in.at[p[0] * 4 + p[1] * 2 + p[2]], b1.at[c], dev(*p, xh, z)) for p in cpeers]
    for d in Y_STEPS:
        cp.start(tok, tokf.at[y], dev((y + d) % 4, xl, co, xh, z))
    for p in cpeers:
        cp.start(rg, rgf.at[c], dev(*p, xh, z))
    lc[0].wait()
    for copy in first:
        copy.wait_recv()
        got.append(copy)
    xc = cp.start(a2.at[:, xl], a2.at[:, xl], xpeer)
    cots = [
        cp.start(cot, cotf.at[c], dev((y + dy) % 4, (xl + dx) % 2, co, xh, z)) for dy, dx in C_STEPS
    ]
    cp.start(cot, cotf.at[c], sib)
    xc.wait_recv()
    got.append(xc)
    lw = pltpu.make_async_copy(a2, wf.at[:, :, co, f], loc.at[5])
    lw.start()
    ws = [cp.start(a2, wf.at[:, :, co, f], p) for p in fpeers]
    lc[1].wait()
    for copy in bs:
        copy.wait_recv()
        got.append(copy)
    lb = pltpu.make_async_copy(b1, bfull.at[:, f], loc.at[6])
    lb.start()
    for p in fpeers:
        cp.start(b1, bfull.at[:, f], p)
    lw.wait()
    cp.start(wf.at[:, :, co, f], wf.at[:, :, co, f], sib)
    for (dx, dz), copy in zip(F_STEPS, ws):
        copy.wait_recv()
        got.append(copy)
        part = wf.at[:, :, co, ((xh + dx) % 2) * 4 + (z + 4 - dz) % 4]
        cp.start(part, part, sib)
    for (dy, dx), copy in zip(C_STEPS, cots):
        copy.wait_recv()
        got.append(copy)
        part = cotf.at[((y + 4 - dy) % 4) * 4 + ((xl + dx) % 2) * 2 + co]
        cp.start(part, part, sib)
    for copy in (lc[2], lc[3], lc[4], lb):
        copy.wait()
    cp.finish(got)


def gather_start(a_in, b_in, tok, cot, rg):
    n = a_in.shape[2]
    outs = (
        SDS((4, 2, 2, 8, 16, n), BF),
        SDS((16, 8, 16, b_in.shape[2]), BF),
        SDS((4,) + tok.shape, BF),
        SDS((16,) + cot.shape, BF),
        SDS((16,) + rg.shape, F32),
        SDS((4, 2, 16, n), BF),
        SDS((16, 16, b_in.shape[2]), BF),
    )
    return remote(gather_start_kernel, outs, (a_in, b_in, tok, cot, rg), 84, 8, 1)[:5]


def kv_gather_kernel(kv, out, send, recv, loc):
    y, xl, co, xh, z = coords()
    sib = dev(y, xl, 1 - co, xh, z)
    xpeer = dev(y, 1 - xl, co, xh, z)
    barrier([sib, xpeer])
    cp = Copies(send, recv)
    lc = pltpu.make_async_copy(kv, out.at[:, xl * 2 + co], loc.at[0])
    lc.start()
    a = cp.start(kv, out.at[:, xl * 2 + co], xpeer)
    cp.start(kv, out.at[:, xl * 2 + co], sib)
    a.wait_recv()
    part = out.at[:, (1 - xl) * 2 + co]
    cp.start(part, part, sib)
    lc.wait()
    cp.finish([a])


def kv_gather(kv):
    return remote(kv_gather_kernel, SDS((4, 4) + kv.shape[1:], BF), (kv,), 3, 1, 2)


def kv_scatter_kernel(dkv, out, send, recv, loc):
    y, xl, co, xh, z = coords()
    i = xl * 2 + co
    peers = [(1 - xl, co), (1 - xl, 1 - co), (xl, 1 - co)]
    barrier([dev(y, *p, xh, z) for p in peers])
    cp = Copies(send, recv)
    for p in peers:
        cp.start(dkv.at[:, p[0] * 2 + p[1]], out.at[i], dev(y, *p, xh, z))
    lc = pltpu.make_async_copy(dkv.at[:, i], out.at[i], loc.at[0])
    lc.start()
    lc.wait()
    cp.finish()


def kv_scatter(dkv):
    return remote(kv_scatter_kernel, SDS(dkv.shape, BF), (dkv,), 3, 1, 3)


def exchange_y_kernel(x, out, send, recv, loc):
    y, xl, co, xh, z = coords()
    peers = [dev((y + d) % 4, xl, co, xh, z) for d in Y_STEPS]
    barrier(peers)
    cp = Copies(send, recv)
    for d, p in zip(Y_STEPS, peers):
        cp.start(x.at[(y + d) % 4], out.at[y], p)
    lc = pltpu.make_async_copy(x.at[y], out.at[y], loc.at[0])
    lc.start()
    lc.wait()
    cp.finish()


def exchange_y(x, cid):
    return remote(exchange_y_kernel, SDS(x.shape, x.dtype), (x,), 3, 1, cid)


def gather_y_kernel(x, out, send, recv, loc):
    y, xl, co, xh, z = coords()
    peers = [dev((y + d) % 4, xl, co, xh, z) for d in Y_STEPS]
    barrier(peers)
    cp = Copies(send, recv)
    for p in peers:
        cp.start(x, out.at[y], p)
    lc = pltpu.make_async_copy(x, out.at[y], loc.at[0])
    lc.start()
    lc.wait()
    cp.finish()


def gather_y(x, cid):
    return remote(gather_y_kernel, SDS((4,) + x.shape, x.dtype), (x,), 3, 1, cid)


def gather_ctx_kernel(x, out, send, recv, loc):
    y, xl, co, xh, z = coords()
    c = y * 4 + xl * 2 + co
    sib = dev(y, xl, 1 - co, xh, z)
    peers = [dev((y + dy) % 4, (xl + dx) % 2, co, xh, z) for dy, dx in C_STEPS]
    barrier(peers + [sib])
    cp = Copies(send, recv)
    first = [cp.start(x, out.at[c], p) for p in peers]
    cp.start(x, out.at[c], sib)
    lc = pltpu.make_async_copy(x, out.at[c], loc.at[0])
    lc.start()
    for (dy, dx), copy in zip(C_STEPS, first):
        copy.wait_recv()
        part = out.at[((y + 4 - dy) % 4) * 4 + ((xl + dx) % 2) * 2 + co]
        cp.start(part, part, sib)
    lc.wait()
    cp.finish(first)


def gather_ctx(x, cid):
    return remote(gather_ctx_kernel, SDS((16,) + x.shape, x.dtype), (x,), 15, 1, cid)


def reduce_ctx_kernel(x, out, send, recv, loc, mine, theirs, got, total):
    y, xl, co, xh, z = coords()
    chip = y * 2 + xl
    sib = dev(y, xl, 1 - co, xh, z)
    peers = [((y + dy) % 4, (xl + dx) % 2) for dy, dx in C_STEPS]
    barrier([dev(*p, co, xh, z) for p in peers] + [sib])
    cp = Copies(send, recv)
    order = [p[0] * 2 + p[1] for p in peers] + [chip]
    loads, sibs = [], []
    for k, other in enumerate(order):
        copy = pltpu.make_async_copy(x.at[other, co], mine.at[k], loc.at[k])
        copy.start()
        loads.append(copy)
        sibs.append(cp.start(x.at[other, 1 - co], theirs.at[k], sib))
    outgoing = []
    for k, p in enumerate(peers):
        loads[k].wait()
        sibs[k].wait_recv()
        mine[k] = (mine[k].astype(F32) + theirs[k].astype(F32)).astype(BF)
        outgoing.append(cp.start(mine.at[k], got.at[k], dev(*p, co, xh, z)))
    loads[7].wait()
    sibs[7].wait_recv()
    total[...] = mine[7].astype(F32) + theirs[7].astype(F32)
    for k, copy in enumerate(outgoing):
        copy.wait_recv()
        total[...] += got[k].astype(F32)
    store = pltpu.make_async_copy(total, out, loc.at[8])
    store.start()
    store.wait()
    cp.finish(sibs + outgoing)


def reduce_ctx(x, cid):
    rows, width = x.shape[1:]
    x = x.reshape(8, 2, rows, width)
    scratch = [pltpu.VMEM((8, rows, width), BF)] * 2 + [
        pltpu.VMEM((7, rows, width), BF),
        pltpu.VMEM((rows, width), F32),
    ]
    return remote(reduce_ctx_kernel, SDS((rows, width), F32), (x,), 15, 9, cid, scratch)


def grads_end_kernel(
    da, db, gh, aout, bout, ghout, send, recv, loc, mine, theirs, fgot, s2, xgot, s3, bgot, bmine, sb
):
    y, xl, co, xh, z = coords()
    c, f = y * 4 + xl * 2 + co, xh * 4 + z
    sib = dev(y, xl, 1 - co, xh, z)
    xpeer = dev(y, 1 - xl, co, xh, z)
    fsteps = [((xh + dx) % 2, (z + dz) % 4) for dx, dz in F_STEPS]
    cpeers = [
        ((y + dy) % 4, (xl + dx) % 2, (co + dc) % 2)
        for dy in range(4)
        for dx in (0, 1)
        for dc in (0, 1)
        if (dy, dx, dc) != (0, 0, 0)
    ]
    barrier([dev(*p, xh, z) for p in cpeers] + [dev(y, xl, co, *p) for p in fsteps])
    cp = Copies(send, recv)
    got = []
    load = pltpu.make_async_copy(da.at[:, :, co], mine, loc.at[0])
    load.start()
    bload = pltpu.make_async_copy(db.at[:, f], bmine, loc.at[1])
    bload.start()
    glocal = pltpu.make_async_copy(gh.at[y], ghout.at[y], loc.at[2])
    glocal.start()
    sc = cp.start(da.at[:, :, 1 - co], theirs, sib)
    for d in Y_STEPS:
        cp.start(gh.at[(y + d) % 4], ghout.at[y], dev((y + d) % 4, xl, co, xh, z))
    bs = [
        cp.start(db.at[:, p[0] * 4 + p[1]], bgot.at[k], dev(y, xl, co, *p))
        for k, p in enumerate(fsteps)
    ]
    load.wait()
    sc.wait_recv()
    got.append(sc)
    for a in range(4):
        for b in range(2):
            mine[a, b] = (mine[a, b].astype(F32) + theirs[a, b].astype(F32)).astype(BF)
    fs = [
        cp.start(mine.at[:, :, p[0] * 4 + p[1]], fgot.at[k], dev(y, xl, co, *p))
        for k, p in enumerate(fsteps)
    ]
    bload.wait()
    for copy in bs:
        copy.wait_recv()
        got.append(copy)
    for a in range(16):
        tot = bmine[a].astype(F32)
        for k in range(7):
            tot = tot + bgot[k, a].astype(F32)
        sb[a] = tot.astype(BF)
    for p in cpeers:
        cp.start(sb.at[p[0] * 4 + p[1] * 2 + p[2]], bout.at[c], dev(*p, xh, z))
    bl = pltpu.make_async_copy(sb.at[c], bout.at[c], loc.at[3])
    bl.start()
    for copy in fs:
        copy.wait_recv()
        got.append(copy)
    for a in range(4):
        for b in range(2):
            tot = mine[a, b, f].astype(F32)
            for k in range(7):
                tot = tot + fgot[k, a, b].astype(F32)
            s2[b, a] = tot.astype(BF)
    xc = cp.start(s2.at[1 - xl], xgot, xpeer)
    xc.wait_recv()
    got.append(xc)
    for a in range(4):
        s3[a] = (s2[xl, a].astype(F32) + xgot[a].astype(F32)).astype(BF)
    for d in Y_STEPS:
        cp.start(s3.at[(y + d) % 4], aout.at[y], dev((y + d) % 4, xl, co, xh, z))
    al = pltpu.make_async_copy(s3.at[y], aout.at[y], loc.at[4])
    al.start()
    for copy in (glocal, bl, al):
        copy.wait()
    cp.finish(got)


def grads_end(da, db, gh):
    n, m = da.shape[-1], db.shape[-1]
    outs = (SDS((4, 16, n), BF), SDS((16, 16, m), BF), SDS(gh.shape, BF))
    scratch = [
        pltpu.VMEM((4, 2, 8, 16, n), BF),
        pltpu.VMEM((4, 2, 8, 16, n), BF),
        pltpu.VMEM((7, 4, 2, 16, n), BF),
        pltpu.VMEM((2, 4, 16, n), BF),
        pltpu.VMEM((4, 16, n), BF),
        pltpu.VMEM((4, 16, n), BF),
        pltpu.VMEM((7, 16, 16, m), BF),
        pltpu.VMEM((16, 16, m), BF),
        pltpu.VMEM((16, 16, m), BF),
    ]
    return remote(grads_end_kernel, outs, (da, db, gh), 40, 5, 4, scratch)


def head_rows(ref, j):
    return jnp.concatenate([ref[j * 128 : (j + 1) * 128, h * 128 : (h + 1) * 128] for h in range(3)], 0)


def causal(scores, j):
    n = scores.shape[1]
    i = lax.axis_index("ctx") % 4
    row = lax.broadcasted_iota(jnp.int32, (384, n), 0) % 128
    col = lax.broadcasted_iota(jnp.int32, (384, n), 1)
    return col <= j * 512 + i * 128 + row


def attention_kernel(q_ref, kv_ref, o_ref, att_ref, lse_ref):
    for j in range(4):
        n = (j + 1) * 512
        s = nt(head_rows(q_ref, j), kv_ref[:n, :128]) * SCALE
        s = jnp.where(causal(s, j), s, -1e30)
        m = jnp.max(s, -1, keepdims=True)
        p = jnp.exp(s - m)
        total = jnp.sum(p, -1, keepdims=True)
        o = nn(p.astype(BF), kv_ref[:n, 128:]) / total
        for h in range(3):
            part = o[h * 128 : (h + 1) * 128]
            o_ref[j * 128 : (j + 1) * 128, h * 128 : (h + 1) * 128] = part
            att_ref[j * 128 : (j + 1) * 128, h * 128 : (h + 1) * 128] = part.astype(BF)
        lse_ref[j] = jnp.broadcast_to(m + jnp.log(total), (384, 128))


def attention(q, kv):
    return pl.pallas_call(
        attention_kernel,
        out_shape=(SDS((512, 384), F32), SDS((512, 384), BF), SDS((4, 384, 128), F32)),
        in_specs=[VM, VM],
        out_specs=(VM, VM, VM),
        compiler_params=pltpu.CompilerParams(vmem_limit_bytes=VMEM_LIMIT),
        cost_estimate=pl.CostEstimate(flops=2 * 10**9, bytes_accessed=4 * 10**6, transcendentals=2 * 10**6),
    )(q, kv)


def attention_back_kernel(q_ref, kv_ref, o_ref, lse_ref, go_ref, dq_ref, dkv_ref, dk, dv):
    dk[...] = jnp.zeros_like(dk)
    dv[...] = jnp.zeros_like(dv)
    for j in range(4):
        n = (j + 1) * 512
        q = head_rows(q_ref, j)
        go = head_rows(go_ref, j)
        delta = jnp.sum(head_rows(o_ref, j) * go.astype(F32), -1, keepdims=True)
        lse = lse_ref[j][:, :1]
        s = nt(q, kv_ref[:n, :128]) * SCALE
        p = jnp.where(causal(s, j), jnp.exp(s - lse), 0.0)
        dp = nt(go, kv_ref[:n, 128:])
        gs = (p * (dp - delta)).astype(BF)
        dv[:n] += tn(p.astype(BF), go)
        dk[:n] += tn(gs, q)
        dq = nn(gs, kv_ref[:n, :128]) * SCALE
        for h in range(3):
            dq_ref[j * 128 : (j + 1) * 128, h * 128 : (h + 1) * 128] = dq[
                h * 128 : (h + 1) * 128
            ].astype(BF)
    dkv_ref[:, :128] = (dk[...] * SCALE).astype(BF)
    dkv_ref[:, 128:] = dv[...].astype(BF)


def attention_back(q, kv, o, lse, go):
    return pl.pallas_call(
        attention_back_kernel,
        out_shape=(SDS((512, 384), BF), SDS((2048, 256), BF)),
        in_specs=[VM] * 5,
        out_specs=(VM, VM),
        scratch_shapes=[pltpu.VMEM((2048, 128), F32), pltpu.VMEM((2048, 128), F32)],
        compiler_params=pltpu.CompilerParams(vmem_limit_bytes=VMEM_LIMIT),
        cost_estimate=pl.CostEstimate(flops=5 * 10**9, bytes_accessed=8 * 10**6, transcendentals=2 * 10**6),
    )(q, kv, o, lse, go)


def dispatch_kernel(h2_ref, cot_ref, rg_ref, x_ref, gy_ref, pick_ref, gated_ref):
    first = lax.axis_index("ctx") * 4
    masks, gates = [], []
    for e in range(4):
        ms, gs = [], []
        for s in range(2):
            hit = jnp.where(rg_ref[s, 0:6] == (first + e).astype(F32), 1.0, 0.0)
            ms.append(jnp.sum(hit, 0, keepdims=True))
            gs.append(jnp.sum(hit * rg_ref[s, 8:14], 0, keepdims=True))
        masks.append(jnp.concatenate(ms, 1))
        gates.append(jnp.concatenate(gs, 1))
    mask = jnp.concatenate(masks + [jnp.zeros((4, 256), F32)], 0)
    before = lax.broadcasted_iota(jnp.int32, (256, 256), 0)
    after = lax.broadcasted_iota(jnp.int32, (256, 256), 1)
    tri = jnp.where((before <= after) & (before // 128 == after // 128), 1.0, 0.0).astype(BF)
    place = nn(mask.astype(BF), tri) - 1.0
    lane = lax.broadcasted_iota(jnp.int32, (1, 256), 1)
    slot = lax.broadcasted_iota(jnp.int32, (48, 256), 0).astype(F32)
    picks, gated = [], []
    for e in range(4):
        at = place[e : e + 1] + jnp.where(lane >= 128, 24.0, 0.0)
        at = jnp.where(masks[e] > 0.0, at, -1.0)
        hit = jnp.where(slot == at, 1.0, 0.0)
        picks.append(hit)
        gated.append(hit * gates[e])
    pick = jnp.concatenate(picks, 0).astype(BF)
    gate = jnp.concatenate(gated, 0).astype(BF)
    x_ref[...] = nn(pick, h2_ref[...].reshape(256, 1536)).astype(BF).reshape(4, 1, 48, 1536)
    gy_ref[...] = nn(gate, cot_ref[...].reshape(256, 1536)).astype(BF).reshape(4, 1, 48, 1536)
    pick_ref[0] = pick
    gated_ref[0] = gate


def dispatch(h2, cot, rg):
    rows = pl.BlockSpec((2, 128, 1536), lambda p: (p, 0, 0))
    slots = pl.BlockSpec((4, 1, 48, 1536), lambda p: (0, p, 0, 0))
    picks = pl.BlockSpec((1, 192, 256), lambda p: (p, 0, 0))
    return pl.pallas_call(
        dispatch_kernel,
        grid=(8,),
        out_shape=(SDS((4, 8, 48, 1536), BF),) * 2 + (SDS((8, 192, 256), BF),) * 2,
        in_specs=[rows, rows, pl.BlockSpec((2, 16, 128), lambda p: (p, 0, 0))],
        out_specs=(slots, slots, picks, picks),
        compiler_params=pltpu.CompilerParams(vmem_limit_bytes=VMEM_LIMIT),
        cost_estimate=pl.CostEstimate(flops=3 * 10**9, bytes_accessed=24 * 10**6, transcendentals=0),
    )(h2, cot, rg)


def piece_places():
    f = lax.axis_index("fsdp")
    xh, z = f // 4, f % 4
    steps = ((0, 0),) + F_STEPS
    source = [((xh + dx) % 2) * 4 + (z + 4 - dz) % 4 for dx, dz in steps]
    target = [((xh + dx) % 2) * 4 + (z + dz) % 4 for dx, dz in steps]
    return source, target


def expert_kernel(*refs):
    x_ref, gy_ref = refs[:2]
    pieces = refs[2:10]
    y_ref, gr_ref = refs[10:12]
    grads = refs[12:20]
    w, dw, u_s, ga_s, gb_s = refs[20:]
    source, target = piece_places()
    for k in range(8):
        w[:, pl.ds(pl.multiple_of(source[k] * 192, 192), 192), :] = pieces[k][:, 0]

    for t in range(2):
        cols = slice(t * 256, (t + 1) * 256)
        a = nn(x_ref[0], w[0, :, cols])
        b = nn(x_ref[0], w[1, :, cols])
        gu = nn(gy_ref[0], w[2, :, cols])
        act, slope = silu_parts(a)
        u_s[:, cols] = (act * b).astype(BF)
        ga_s[:, cols] = (gu * b * slope).astype(BF)
        gb_s[:, cols] = (gu * act).astype(BF)

    def tile(t, carry):
        at = pl.ds(pl.multiple_of(t * 256, 256), 256)
        y_ref[0, :, at] = nt(u_s[...], w[2, at, :]).astype(BF)
        gr_ref[0, :, at] = (nt(ga_s[...], w[0, at, :]) + nt(gb_s[...], w[1, at, :])).astype(BF)
        dw[0, at, :] = tn(x_ref[0, :, at], ga_s[...]).astype(BF)
        dw[1, at, :] = tn(x_ref[0, :, at], gb_s[...]).astype(BF)
        dw[2, at, :] = tn(gy_ref[0, :, at], u_s[...]).astype(BF)
        return carry

    lax.fori_loop(0, 6, tile, 0)
    for k in range(8):
        grads[k][:, 0] = dw[:, pl.ds(pl.multiple_of(target[k] * 192, 192), 192), :]


def expert(x, gy, pieces):
    rows = pl.BlockSpec((1, 384, 1536), lambda e: (e, 0, 0))
    piece = pl.BlockSpec((3, 1, 192, 512), lambda e: (0, e, 0, 0))
    out = pl.pallas_call(
        expert_kernel,
        grid=(4,),
        out_shape=(SDS((4, 384, 1536), BF),) * 2 + (SDS((3, 4, 192, 512), BF),) * 8,
        in_specs=[rows, rows] + [piece] * 8,
        out_specs=(rows, rows) + (piece,) * 8,
        scratch_shapes=[
            pltpu.VMEM((3, 1536, 512), BF),
            pltpu.VMEM((3, 1536, 512), BF),
            pltpu.VMEM((384, 512), BF),
            pltpu.VMEM((384, 512), BF),
            pltpu.VMEM((384, 512), BF),
        ],
        compiler_params=pltpu.CompilerParams(vmem_limit_bytes=VMEM_LIMIT),
        cost_estimate=pl.CostEstimate(flops=22 * 10**9, bytes_accessed=60 * 10**6, transcendentals=10**6),
    )(x, gy, *pieces)
    return out[0], out[1], out[2:]


def combine_kernel(pick_ref, gated_ref, y_ref, gr_ref, h2_ref, cot_ref, sw_ref, out_ref, gh_ref, ds_ref):
    @pl.when(pl.program_id(0) == 0)
    def _():
        ds_ref[...] = jnp.zeros_like(ds_ref)

    h2 = h2_ref[...].reshape(256, 1536)
    cot = cot_ref[...].reshape(256, 1536)
    act, slope = silu_parts(nn(h2, sw_ref[:, 0:128]))
    up = nn(h2, sw_ref[:, 128:256])
    gz = nn(cot, sw_ref[:, 256:384])
    hid = (act * up).astype(BF)
    gc = (gz * up * slope).astype(BF)
    gd = (gz * act).astype(BF)
    out = tn(gated_ref[0], y_ref[...].reshape(192, 1536)) + nt(hid, sw_ref[:, 256:384])
    out_ref[...] = out.astype(BF).reshape(2, 128, 1536)
    gh = tn(pick_ref[0], gr_ref[...].reshape(192, 1536)) + nt(gc, sw_ref[:, 0:128])
    gh = gh + nt(gd, sw_ref[:, 128:256])
    gh_ref[...] = gh.astype(BF).reshape(2, 128, 1536)
    ds_ref[:, 0:128] += tn(h2, gc)
    ds_ref[:, 128:256] += tn(h2, gd)
    ds_ref[:, 256:384] += tn(cot, hid)


def combine(pick, gated, y, gr, h2, cot, sw):
    rows = pl.BlockSpec((2, 128, 1536), lambda p: (p, 0, 0))
    slots = pl.BlockSpec((4, 1, 48, 1536), lambda p: (0, p, 0, 0))
    picks = pl.BlockSpec((1, 192, 256), lambda p: (p, 0, 0))
    whole = pl.BlockSpec((1536, 384), lambda p: (0, 0))
    return pl.pallas_call(
        combine_kernel,
        grid=(8,),
        out_shape=(SDS((16, 128, 1536), BF),) * 2 + (SDS((1536, 384), F32),),
        in_specs=[picks, picks, slots, slots, rows, rows, whole],
        out_specs=(rows, rows, whole),
        compiler_params=pltpu.CompilerParams(vmem_limit_bytes=VMEM_LIMIT),
        cost_estimate=pl.CostEstimate(flops=8 * 10**9, bytes_accessed=36 * 10**6, transcendentals=10**6),
    )(pick, gated, y, gr, h2, cot, sw)


def norm_forward(values, gain_vec):
    inverse = lax.rsqrt(jnp.mean(values * values, -1, keepdims=True) + EPS)
    scaled = values * inverse
    return scaled * gain_vec, scaled, inverse


def norm_row_grad(grad_in, scaled, inverse, gain_vec):
    inner = grad_in * gain_vec
    return inverse * (inner - scaled * jnp.mean(inner * scaled, -1, keepdims=True))


def pack_rows():
    row = jnp.arange(96)[:, None]
    col = jnp.arange(128)[None, :]
    return ((row // 12) * 16 + row % 12 == col).astype(BF)


def local(
    tokens,
    cotangent,
    routes,
    gates,
    attn_gain,
    ffn_gain,
    w_query,
    w_key,
    w_value,
    w_out,
    shared_gate,
    shared_up,
    shared_down,
    expert_gate,
    expert_up,
    expert_down,
):
    tok = tokens.reshape(128, 1536)
    cot = cotangent.reshape(128, 1536)
    rg = jnp.concatenate(
        [
            jnp.pad(routes.reshape(128, 6).T.astype(F32), ((0, 2), (0, 0)), constant_values=-1.0),
            jnp.pad(gates.reshape(128, 6).T, ((0, 2), (0, 0))),
        ],
        0,
    )
    gains = jnp.pad(jnp.stack([attn_gain, ffn_gain], 1), ((0, 0), (0, 126)))
    a_in = jnp.concatenate(
        [
            w_query.reshape(12, 4, 384),
            w_key.reshape(12, 4, 128),
            w_value.reshape(12, 4, 128),
            w_out.T.reshape(12, 4, 384),
            jnp.broadcast_to(gains[:, None], (12, 4, 128)),
        ],
        2,
    )
    a_in = jnp.pad(jnp.transpose(a_in, (1, 0, 2)), ((0, 0), (0, 4), (0, 0)))
    b_in = jnp.concatenate(
        [
            shared_gate.reshape(12, 16, 64),
            shared_up.reshape(12, 16, 64),
            shared_down.T.reshape(12, 16, 64),
            jnp.zeros((12, 16, 64), BF),
        ],
        2,
    )
    b_in = jnp.pad(jnp.transpose(b_in, (1, 0, 2)), ((0, 0), (0, 4), (0, 0)))
    w_raw, b_raw, tok_f, cot_f, rg_f = gather_start(a_in, b_in, tok, cot, rg)

    own = jnp.stack([expert_gate, expert_up, jnp.transpose(expert_down, (0, 2, 1))])
    own, w_raw = lax.optimization_barrier((own, w_raw))
    pieces = [own] + [
        lax.ppermute(
            own, "fsdp", [(f, ((f // 4 + dx) % 2) * 4 + (f % 4 + dz) % 4) for f in range(8)]
        )
        for dx, dz in F_STEPS
    ]

    pack = pack_rows()
    w = jnp.einsum("ap,cpn->can", pack, w_raw.reshape(16, 128, 1152), preferred_element_type=F32)
    w = w.astype(BF).reshape(1536, 1152)
    sw = jnp.einsum("ap,cpn->can", pack, b_raw.reshape(16, 128, 256), preferred_element_type=F32)
    sw = sw.astype(BF).reshape(1536, 256)
    sw = jnp.pad(sw[:, :192].reshape(1536, 3, 64), ((0, 0), (0, 0), (0, 64))).reshape(1536, 384)
    w_qkv, w_o = w[:, :640], w[:, 640:1024]
    gain_one, gain_two = w[:, 1024].astype(F32), w[:, 1025].astype(F32)

    h1, xh1, _ = norm_forward(tok_f.reshape(512, 1536).astype(F32), gain_one)
    h1 = h1.astype(BF)
    qkv = nn(h1, w_qkv).astype(BF)
    q = qkv[:, :384]
    kv = kv_gather(qkv[:, 384:].reshape(4, 128, 256)).reshape(2048, 256)
    o, attended, lse = attention(q, kv)
    partial = nt(attended, w_o).astype(BF).reshape(4, 128, 1536)
    inputs = tok.astype(F32)
    resid = inputs + jnp.sum(exchange_y(partial, 5).astype(F32), 0)
    h2, xh2, inv2 = norm_forward(resid, gain_two)
    h2_f = gather_ctx(h2.astype(BF), 6)

    x, gy, pick, gated = dispatch(h2_f, cot_f, rg_f)
    y, gr, egrads = expert(x.reshape(4, 384, 1536), gy.reshape(4, 384, 1536), pieces)
    out_p, gh2_p, ds = combine(
        pick, gated, y.reshape(4, 8, 48, 1536), gr.reshape(4, 8, 48, 1536), h2_f, cot_f, sw
    )
    sums = egrads[0].astype(F32)
    for (dx, dz), piece in zip(F_STEPS, egrads[1:]):
        sums = sums + lax.ppermute(
            piece, "fsdp", [(f, ((f // 4 + dx) % 2) * 4 + (f % 4 + dz) % 4) for f in range(8)]
        ).astype(F32)

    gh2 = reduce_ctx(gh2_p, 7)
    gain_two_grad = jnp.sum(gh2 * xh2, 0)
    gresid = cot.astype(F32) + norm_row_grad(gh2, xh2, inv2, gain_two)
    gattn = gather_y(gresid.astype(BF), 8).reshape(512, 1536)
    layer_out = (resid + reduce_ctx(out_p, 9)).astype(BF)

    go = nn(gattn, w_o).astype(BF)
    dw_o = tn(gattn, attended)
    dq, dkv = attention_back(q, kv, o, lse, go)
    dkv = jnp.sum(kv_scatter(dkv.reshape(4, 4, 128, 256)).astype(F32), 0).astype(BF)
    gqkv = jnp.concatenate([dq, dkv.reshape(512, 256)], 1)
    gh1_p = nt(gqkv, w_qkv)
    dw_qkv = tn(h1, gqkv)
    gain_one_grad = jnp.sum(gh1_p * xh1, 0)
    gain_grads = jnp.pad(jnp.stack([gain_one_grad, gain_two_grad], 1), ((0, 0), (0, 126)))
    da = jnp.concatenate([dw_qkv, dw_o, gain_grads], 1).astype(BF).reshape(16, 96, 1152)
    da = jnp.einsum("ap,can->cpn", pack, da, preferred_element_type=F32).astype(BF)
    db = jnp.pad(ds.reshape(1536, 3, 128)[:, :, :64].reshape(1536, 192), ((0, 0), (0, 64)))
    db = db.astype(BF).reshape(16, 96, 256)
    db = jnp.einsum("ap,can->cpn", pack, db, preferred_element_type=F32).astype(BF)
    a_out, b_out, gh1 = grads_end(
        da.reshape(4, 2, 2, 8, 16, 1152),
        db.reshape(16, 8, 16, 256),
        gh1_p.astype(BF).reshape(4, 128, 1536),
    )
    gh1 = jnp.sum(gh1.astype(F32), 0)
    _, xh1_own, inv1 = norm_forward(inputs, gain_one)
    input_grad = gresid + norm_row_grad(gh1, xh1_own, inv1, gain_one)

    a_out = jnp.transpose(a_out[:, :12].astype(F32), (1, 0, 2))
    b_out = jnp.transpose(b_out[:, :12].astype(F32), (1, 0, 2))
    gain_out = jnp.sum(a_out[:, :, 1024:1026], 1)
    return (
        layer_out.reshape(1, 128, 1536),
        input_grad.reshape(1, 128, 1536),
        gain_out[:, 0],
        gain_out[:, 1],
        a_out[:, :, 0:384].reshape(12, 1536),
        a_out[:, :, 384:512].reshape(12, 512),
        a_out[:, :, 512:640].reshape(12, 512),
        a_out[:, :, 640:1024].reshape(12, 1536).T,
        b_out[:, :, 0:64].reshape(12, 1024),
        b_out[:, :, 64:128].reshape(12, 1024),
        b_out[:, :, 128:192].reshape(12, 1024).T,
        sums[0],
        sums[1],
        jnp.transpose(sums[2], (0, 2, 1)),
    )


def solution(mesh):
    both = ("ctx", "fsdp")
    rows = P("fsdp", "ctx", None)
    weights = (P(both),) * 2 + (P(both, None),) * 3 + (P(None, both),)
    weights = weights + (P(both, None),) * 2 + (P(None, both),)
    weights = weights + (P("ctx", "fsdp", None),) * 2 + (P("ctx", None, "fsdp"),)
    return jax.shard_map(
        local, mesh=mesh, in_specs=(rows,) * 4 + weights, out_specs=(rows,) * 2 + weights, check_vma=False
    )
```

```python
import jax
import jax.numpy as jnp
from jax import lax
from jax.experimental import pallas as pl
from jax.experimental.pallas import tpu as pltpu
from jax.sharding import PartitionSpec as P

BF = jnp.bfloat16
F32 = jnp.float32
EPS = 1e-05
MESH = pl.DeviceIdType.MESH
ANY = pl.BlockSpec(memory_space=pl.ANY)
VM = pl.BlockSpec(memory_space=pltpu.VMEM)
SDS = jax.ShapeDtypeStruct
SCALE = 128 ** (-0.5)
VMEM_LIMIT = 56 * 2**20


def nn(a, b):
    return lax.dot_general(a, b, (((1,), (0,)), ((), ())), preferred_element_type=F32)


def nt(a, b):
    return lax.dot_general(a, b, (((1,), (1,)), ((), ())), preferred_element_type=F32)


def tn(a, b):
    return lax.dot_general(a, b, (((0,), (0,)), ((), ())), preferred_element_type=F32)


def silu_parts(pre_act):
    sig = 1.0 / (1.0 + jnp.exp(-pre_act))
    return pre_act * sig, sig * (1.0 + pre_act * (1.0 - sig))


def coords():
    c = lax.axis_index("ctx")
    f = lax.axis_index("fsdp")
    return c // 4, (c // 2) % 2, c % 2, f // 4, f % 4


def dev(y, xl, co, xh, z):
    return (y * 4 + xl * 2 + co, xh * 4 + z)


def barrier(peers):
    sem = pltpu.get_barrier_semaphore()
    for peer in peers:
        pl.semaphore_signal(sem, inc=1, device_id=peer, device_id_type=MESH)
    pl.semaphore_wait(sem, len(peers))


class Copies:
    def __init__(self, send, recv):
        self.send, self.recv, self.n, self.started = send, recv, 0, []

    def start(self, src, dst, peer):
        copy = pltpu.make_async_remote_copy(
            src, dst, self.send.at[self.n], self.recv.at[self.n], device_id=peer, device_id_type=MESH
        )
        copy.start()
        self.n += 1
        self.started.append(copy)
        return copy

    def finish(self, received=()):
        for copy in self.started:
            copy.wait_send()
            if not any(copy is r for r in received):
                copy.wait_recv()


Y_STEPS = (1, 2, 3)
F_STEPS = tuple((dx, dz) for dx in (0, 1) for dz in range(4) if (dx, dz) != (0, 0))
C_STEPS = tuple((dy, dx) for dy in range(4) for dx in (0, 1) if (dy, dx) != (0, 0))


def one_hot_rows():
    row = lax.broadcasted_iota(jnp.int32, (96, 128), 0)
    col = lax.broadcasted_iota(jnp.int32, (96, 128), 1)
    return jnp.where((row // 12) * 16 + row % 12 == col, 1.0, 0.0).astype(BF)


def spread_columns():
    row = lax.broadcasted_iota(jnp.int32, (256, 384), 0)
    col = lax.broadcasted_iota(jnp.int32, (256, 384), 1)
    return jnp.where((row < 192) & ((row // 64) * 128 + row % 64 == col), 1.0, 0.0).astype(BF)


def eye_rows():
    row = lax.broadcasted_iota(jnp.int32, (8, 128), 0)
    col = lax.broadcasted_iota(jnp.int32, (8, 128), 1)
    return jnp.where(row == col, 1.0, 0.0).astype(BF)


def inverse_norm(values):
    return lax.rsqrt(jnp.mean(values * values, -1, keepdims=True) + EPS)


def head_rows(ref, j, first=0):
    rows = slice(j * 128, (j + 1) * 128)
    return jnp.concatenate([ref[rows, first + h * 128 : first + (h + 1) * 128] for h in range(3)], 0)


def allowed(n):
    i = lax.axis_index("ctx") % 4
    row = lax.broadcasted_iota(jnp.int32, (384, n), 0) % 128
    col = lax.broadcasted_iota(jnp.int32, (384, n), 1)
    return col <= i * 128 + row


def ctx_places(y, xl, co):
    return [
        ((y + dy) % 4, (xl + dx) % 2, (co + dc) % 2)
        for dy in range(4)
        for dx in (0, 1)
        for dc in (0, 1)
        if (dy, dx, dc) != (0, 0, 0)
    ]


def front_kernel(
    a_in, b_in, tok, cot, rg, own,
    cotf, rgf, h2f, wexp, tokf_o, kvf_o,
    w, sw, h1, qkv, att, lse, resid,
    send, recv, loc, a2, wf, b1, bf, tokf, kvf, s_s, part, got, h2,
):
    y, xl, co, xh, z = coords()
    i, c, f = xl * 2 + co, y * 4 + xl * 2 + co, xh * 4 + z
    sib = dev(y, xl, 1 - co, xh, z)
    xpeer = dev(y, 1 - xl, co, xh, z)
    xfar = dev(y, xl, co, 1 - xh, z)
    ypeers = [dev((y + d) % 4, xl, co, xh, z) for d in Y_STEPS]
    zpeers = [dev(y, xl, co, xh, (z + d) % 4) for d in Y_STEPS]
    fpeers = [dev(y, xl, co, (xh + dx) % 2, (z + dz) % 4) for dx, dz in F_STEPS]
    places = ctx_places(y, xl, co)
    cpeers = [dev(*p, xh, z) for p in places]
    barrier(cpeers + fpeers)
    cp = Copies(send, recv)
    n_local = [0]

    def here(src, dst):
        copy = pltpu.make_async_copy(src, dst, loc.at[n_local[0]])
        n_local[0] += 1
        copy.start()
        return copy

    got_already = []

    def arrive(copy):
        copy.wait_recv()
        got_already.append(copy)

    la = here(a_in.at[y], a2.at[y, xl])
    ya = [cp.start(a_in.at[(y + d) % 4], a2.at[y, xl], p) for d, p in zip(Y_STEPS, ypeers)]
    lb = here(b_in.at[c], b1.at[c])
    lt = here(tok, tokf.at[y])
    later = [here(own, wexp.at[:, :, f]), here(cot, cotf.at[c]), here(rg, rgf.at[c])]
    yt = [cp.start(tok, tokf.at[y], p) for p in ypeers]
    bs = [cp.start(b_in.at[p[0] * 4 + p[1] * 2 + p[2]], b1.at[c], q) for p, q in zip(places, cpeers)]
    la.wait()
    for copy in ya:
        arrive(copy)
    xa = cp.start(a2.at[:, xl], a2.at[:, xl], xpeer)
    for q in cpeers:
        cp.start(rg, rgf.at[c], q)
    arrive(xa)
    ws = [cp.start(a2, wf.at[:, :, co, f], p) for p in fpeers]
    lw = here(a2, wf.at[:, :, co, f])
    ex = cp.start(own.at[2:4], wexp.at[2:4, :, f], xfar)
    ez = [cp.start(own.at[0:2], wexp.at[0:2, :, f], p) for p in zpeers]
    cp.start(own.at[0:2], wexp.at[0:2, :, f], xfar)
    for p in zpeers:
        cp.start(own.at[2:4], wexp.at[2:4, :, f], p)
    lw.wait()
    sw_sib = [cp.start(wf.at[:, :, co, f], wf.at[:, :, co, f], sib)]
    for (dx, dz), copy in zip(F_STEPS, ws):
        arrive(copy)
        piece = wf.at[:, :, co, ((xh + dx) % 2) * 4 + (z + 4 - dz) % 4]
        sw_sib.append(cp.start(piece, piece, sib))
    cots = [
        cp.start(cot, cotf.at[c], dev((y + dy) % 4, (xl + dx) % 2, co, xh, z)) for dy, dx in C_STEPS
    ]
    cp.start(cot, cotf.at[c], sib)
    lb.wait()
    for copy in bs:
        arrive(copy)
    lb = here(b1, bf.at[:, f])
    bsf = [cp.start(b1, bf.at[:, f], p) for p in fpeers]
    for copy in sw_sib:
        arrive(copy)
    rows = one_hot_rows()
    for yy in range(4):
        for k in range(4):
            at = (yy * 4 + k) * 96
            w[at : at + 96] = nn(rows, wf[yy, k // 2, k % 2].reshape(128, -1)).astype(BF)
    gains = nt(eye_rows(), w[:, 1024:1152])
    gain_one, gain_two = gains[0:1], gains[1:2]

    lt.wait()
    for copy in yt:
        arrive(copy)
    for j in range(4):
        v = tokf[j].astype(F32)
        rows_j = slice(j * 128, (j + 1) * 128)
        h1[rows_j] = (v * inverse_norm(v) * gain_one).astype(BF)
        qkv_j = nn(h1[rows_j], w[:, :640]).astype(BF)
        qkv[rows_j] = qkv_j
        kvf[j, i] = qkv_j[:, 384:]
    kx = cp.start(kvf.at[:, i], kvf.at[:, i], xpeer)
    ks = [cp.start(kvf.at[:, i], kvf.at[:, i], sib)]
    saved = [here(tokf, tokf_o)]
    arrive(ex)
    piece = wexp.at[2:4, :, (1 - xh) * 4 + z]
    for p in zpeers:
        cp.start(piece, piece, p)
    arrive(kx)
    piece = kvf.at[:, (1 - xl) * 2 + co]
    ks.append(cp.start(piece, piece, sib))
    for copy in ks:
        arrive(copy)
    saved.append(here(kvf, kvf_o))

    for j in range(4):
        n = (j + 1) * 512
        q = head_rows(qkv, j)
        for t in range(j + 1):
            s = nt(q, kvf[t].reshape(512, 256)[:, :128]) * SCALE
            if t == j:
                s = jnp.where(allowed(512), s, -1e30)
            s_s[:, t * 512 : (t + 1) * 512] = s
        s = s_s[:, :n]
        m = jnp.max(s, -1, keepdims=True)
        p = jnp.exp(s - m)
        total = jnp.sum(p, -1, keepdims=True)
        o = nn(p.astype(BF), kvf[0 : j + 1].reshape(n, 256)[:, 128:]) / total
        rows_j = slice(j * 128, (j + 1) * 128)
        for h in range(3):
            att[rows_j, h * 128 : (h + 1) * 128] = o[h * 128 : (h + 1) * 128].astype(BF)
        lse[j] = jnp.broadcast_to(m + jnp.log(total), (384, 128))
        part[j] = nt(att[rows_j], w[:, 640:1024]).astype(BF)
    ps = [
        cp.start(part.at[(y + d) % 4], got.at[k], p) for k, (d, p) in enumerate(zip(Y_STEPS, ypeers))
    ]
    own_x = []
    for k in (0, 2):
        arrive(ez[k])
        piece = wexp.at[0:2, :, xh * 4 + (z + 4 - Y_STEPS[k]) % 4]
        own_x.append(cp.start(piece, piece, xfar))
    total = tokf[y].astype(F32) + part[y].astype(F32)
    for k, copy in enumerate(ps):
        arrive(copy)
        total = total + got[k].astype(F32)
    resid[...] = total
    h2[...] = (total * inverse_norm(total) * gain_two).astype(BF)
    hs = [cp.start(h2, h2f.at[c], dev((y + dy) % 4, (xl + dx) % 2, co, xh, z)) for dy, dx in C_STEPS]
    cp.start(h2, h2f.at[c], sib)
    later.append(here(h2, h2f.at[c]))

    lb.wait()
    for copy in bsf:
        arrive(copy)
    cols = spread_columns()
    for k in range(16):
        block = nn(rows, bf[k].reshape(128, 256)).astype(BF)
        sw[k * 96 : (k + 1) * 96] = nn(block, cols).astype(BF)
    for (dy, dx), copy in zip(C_STEPS, cots):
        arrive(copy)
        piece = cotf.at[((y + 4 - dy) % 4) * 4 + ((xl + dx) % 2) * 2 + co]
        cp.start(piece, piece, sib)
    arrive(ez[1])
    piece = wexp.at[0:2, :, xh * 4 + (z + 4 - Y_STEPS[1]) % 4]
    cp.start(piece, piece, xfar)
    for (dy, dx), copy in zip(C_STEPS, hs):
        arrive(copy)
        piece = h2f.at[((y + 4 - dy) % 4) * 4 + ((xl + dx) % 2) * 2 + co]
        cp.start(piece, piece, sib)
    for copy in later + saved:
        copy.wait()
    cp.finish(got_already)


def front(a_in, b_in, tok, cot, rg, own):
    outs = (
        SDS((16, 128, 1536), BF),
        SDS((16, 16, 128), F32),
        SDS((16, 128, 1536), BF),
        SDS((4, 3, 8, 192, 512), BF),
        SDS((4, 128, 1536), BF),
        SDS((4, 4, 128, 256), BF),
        SDS((1536, 1152), BF),
        SDS((1536, 384), BF),
        SDS((512, 1536), BF),
        SDS((512, 640), BF),
        SDS((512, 384), BF),
        SDS((4, 384, 128), F32),
        SDS((128, 1536), F32),
    )
    return pl.pallas_call(
        front_kernel,
        out_shape=outs,
        in_specs=[ANY] * 6,
        out_specs=(ANY,) * 6 + (VM,) * 7,
        scratch_shapes=[
            pltpu.SemaphoreType.DMA((112,)),
            pltpu.SemaphoreType.DMA((112,)),
            pltpu.SemaphoreType.DMA((12,)),
            pltpu.VMEM((4, 2, 16, 1152), BF),
            pltpu.VMEM((4, 2, 2, 8, 16, 1152), BF),
            pltpu.VMEM((16, 16, 256), BF),
            pltpu.VMEM((16, 8, 16, 256), BF),
            pltpu.VMEM((4, 128, 1536), BF),
            pltpu.VMEM((4, 4, 128, 256), BF),
            pltpu.VMEM((384, 2048), F32),
            pltpu.VMEM((4, 128, 1536), BF),
            pltpu.VMEM((3, 128, 1536), BF),
            pltpu.VMEM((128, 1536), BF),
        ],
        compiler_params=pltpu.CompilerParams(
            collective_id=1, has_side_effects=True, vmem_limit_bytes=VMEM_LIMIT
        ),
        cost_estimate=pl.CostEstimate(flops=6 * 10**9, bytes_accessed=60 * 10**6, transcendentals=3 * 10**6),
    )(a_in, b_in, tok, cot, rg, own)


def add_blocks(*refs):
    total = refs[0][...].astype(F32)
    for ref in refs[1:-1]:
        total = total + ref[...].astype(F32)
    refs[-1][...] = total.astype(refs[-1].dtype)


def add_arrays(block, ins, out):
    spec = pl.BlockSpec((1, 1) + block, lambda e, m: (e, m) + (0,) * len(block))
    pltpu.emit_pipeline(add_blocks, grid=(2, 3), in_specs=[spec] * len(ins), out_specs=[spec])(*ins, out)


def back_kernel(
    gh2p, outp, eg, resid_i, cot_i, w_i, tokf_i, h1_i, qkv_i, kvf_i, lse_i, att_i, db,
    aout, bout, ego, xa, zb, sa, sb, za, xb, tho, goo,
    lout, igrad,
    send, recv, loc, mine, theirs, got, resid, cot, gres, w, tokf, h1, qkv, kvf, lse, att,
    gattn, go, dk, dv, dkvs, dkvr, gqkv, gh1s, gh1g, da, dath, fgot, s2, xgot, s3, bgot, bmine, bsum,
):
    y, xl, co, xh, z = coords()
    i, c, f = xl * 2 + co, y * 4 + xl * 2 + co, xh * 4 + z
    sib = dev(y, xl, 1 - co, xh, z)
    xpeer = dev(y, 1 - xl, co, xh, z)
    xfar = dev(y, xl, co, 1 - xh, z)
    ypeers = [dev((y + d) % 4, xl, co, xh, z) for d in Y_STEPS]
    zpeers = [dev(y, xl, co, xh, (z + d) % 4) for d in Y_STEPS]
    fsteps = [((xh + dx) % 2, (z + dz) % 4) for dx, dz in F_STEPS]
    fpeers = [dev(y, xl, co, *p) for p in fsteps]
    chips = [((y + dy) % 4, (xl + dx) % 2) for dy, dx in C_STEPS]
    places = ctx_places(y, xl, co)
    cpeers = [dev(*p, xh, z) for p in places]
    barrier(cpeers + fpeers)
    cp = Copies(send, recv)
    n_local = [0]

    def here(src, dst):
        copy = pltpu.make_async_copy(src, dst, loc.at[n_local[0]])
        n_local[0] += 1
        copy.start()
        return copy

    got_already = []

    def arrive(copy):
        copy.wait_recv()
        got_already.append(copy)

    order = chips + [(y, xl)]
    loads, sibs = [], []
    for p in order:
        loads.append(here(gh2p.at[p[0], p[1], co], mine.at[p[0], p[1]]))
        sibs.append(cp.start(gh2p.at[p[0], p[1], 1 - co], theirs.at[p[0], p[1]], sib))
    first = [here(resid_i, resid), here(cot_i, cot), here(w_i, w)]
    second = [here(qkv_i, qkv), here(kvf_i, kvf), here(lse_i, lse), here(att_i, att)]
    third = [here(h1_i, h1), here(tokf_i, tokf)]
    bl = here(db.at[:, f], bmine)
    outgoing = []
    for k, p in enumerate(order):
        loads[k].wait()
        arrive(sibs[k])
        mine[p[0], p[1]] = (mine[p[0], p[1]].astype(F32) + theirs[p[0], p[1]].astype(F32)).astype(BF)
        if k < 7:
            outgoing.append(cp.start(mine.at[p[0], p[1]], got.at[k], dev(*p, co, xh, z)))
    so = cp.start(outp.at[:, :, 1 - co], tho, sib)
    ez = [
        cp.start(eg.at[0:2, :, :, (z + d) % 4], zb.at[k], p)
        for k, (d, p) in enumerate(zip(Y_STEPS, zpeers))
    ]
    bs = [
        cp.start(db.at[:, p[0] * 4 + p[1]], bgot.at[k], q)
        for k, (p, q) in enumerate(zip(fsteps, fpeers))
    ]
    for copy in first:
        copy.wait()
    gains = nt(eye_rows(), w[:, 1024:1152])
    gain_one, gain_two = gains[0:1], gains[1:2]
    inv = inverse_norm(resid[...])
    xh2 = resid[...] * inv
    gh2 = mine[y, xl].astype(F32)
    for k, copy in enumerate(outgoing):
        arrive(copy)
        gh2 = gh2 + got[k].astype(F32)
    gain_two_grad = jnp.sum(gh2 * xh2, 0, keepdims=True)
    inner = gh2 * gain_two
    row = inv * (inner - xh2 * jnp.mean(inner * xh2, -1, keepdims=True))
    gres[...] = cot[...].astype(F32) + row
    gattn[y] = gres[...].astype(BF)
    ga = [cp.start(gattn.at[y], gattn.at[y], p) for p in ypeers]
    ex = cp.start(eg.at[2:4, :, 1 - xh], xa, xfar)

    for copy in outgoing:
        copy.wait_send()
    arrive(so)
    lo = [here(outp.at[:, :, co], mine), here(tho, theirs)]
    for copy in lo:
        copy.wait()
    outs = []
    for k, p in enumerate(order):
        mine[p[0], p[1]] = (mine[p[0], p[1]].astype(F32) + theirs[p[0], p[1]].astype(F32)).astype(BF)
        if k < 7:
            outs.append(cp.start(mine.at[p[0], p[1]], goo.at[k], dev(*p, co, xh, z)))

    for copy in second:
        copy.wait()
    for copy in ga:
        arrive(copy)
    dk[...] = jnp.zeros_like(dk)
    dv[...] = jnp.zeros_like(dv)
    for j in range(4):
        rows_j = slice(j * 128, (j + 1) * 128)
        go[rows_j] = nn(gattn[j], w[:, 640:1024]).astype(BF)
        q, g = head_rows(qkv, j), head_rows(go, j)
        delta = jnp.sum(head_rows(att, j).astype(F32) * g.astype(F32), -1, keepdims=True)
        total = lse[j][:, :1]
        dq = jnp.zeros((384, 128), F32)
        for t in range(j + 1):
            keys = kvf[t].reshape(512, 256)
            s = nt(q, keys[:, :128]) * SCALE
            p = jnp.exp(s - total)
            if t == j:
                p = jnp.where(allowed(512), p, 0.0)
            gs = (p * (nt(g, keys[:, 128:]) - delta)).astype(BF)
            at = slice(t * 512, (t + 1) * 512)
            dv[at] += tn(p.astype(BF), g)
            dk[at] += tn(gs, q)
            dq = dq + nn(gs, keys[:, :128])
        dq = (dq * SCALE).astype(BF)
        for h in range(3):
            gqkv[rows_j, h * 128 : (h + 1) * 128] = dq[h * 128 : (h + 1) * 128]
    for j in range(4):
        for k in range(4):
            at = slice((j * 4 + k) * 128, (j * 4 + k + 1) * 128)
            dkvs[j, k, :, 0:128] = (dk[at] * SCALE).astype(BF)
            dkvs[j, k, :, 128:256] = dv[at].astype(BF)
    kvs = [
        cp.start(dkvs.at[:, p[0] * 2 + p[1]], dkvr.at[k], dev(y, *p, xh, z))
        for k, p in enumerate([(1 - xl, co), (1 - xl, 1 - co), (xl, 1 - co)])
    ]
    rows = one_hot_rows()

    def expand(block, yy, cols):
        for k in range(4):
            part = tn(rows, block[k * 96 : (k + 1) * 96]).astype(BF)
            da[yy, k // 2, k % 2, :, :, cols] = part.reshape(8, 16, -1)

    for yy in range(4):
        tile = slice(yy * 384, (yy + 1) * 384)
        block = tn(gattn[:, :, tile].reshape(512, 384), att[...])
        expand(block.astype(BF), yy, slice(640, 1024))
    for copy in third:
        copy.wait()
    for copy in kvs:
        arrive(copy)
    gain_one_grad = jnp.zeros((1, 1536), F32)
    for j in range(4):
        rows_j = slice(j * 128, (j + 1) * 128)
        kv = dkvs[j, i].astype(F32)
        for k in range(3):
            kv = kv + dkvr[k, j].astype(F32)
        gqkv[rows_j, 384:640] = kv.astype(BF)
        gh1 = nt(gqkv[rows_j], w[:, :640])
        v = tokf[j].astype(F32)
        gain_one_grad = gain_one_grad + jnp.sum(gh1 * (v * inverse_norm(v)), 0, keepdims=True)
        gh1s[j] = gh1.astype(BF)
    hs = [
        cp.start(gh1s.at[(y + d) % 4], gh1g.at[k], p) for k, (d, p) in enumerate(zip(Y_STEPS, ypeers))
    ]
    gain_rows = jnp.concatenate([gain_one_grad, gain_two_grad, jnp.zeros((6, 1536), F32)], 0)
    for yy in range(4):
        tile = slice(yy * 384, (yy + 1) * 384)
        expand(tn(h1[:, tile], gqkv[...]).astype(BF), yy, slice(0, 640))
        expand(tn(gain_rows[:, tile].astype(BF), eye_rows()).astype(BF), yy, slice(1024, 1152))
    sd = cp.start(da.at[:, :, 1 - co], dath, sib)

    bl.wait()
    for copy in bs:
        arrive(copy)
    for a in range(16):
        tot = bmine[a].astype(F32)
        for k in range(7):
            tot = tot + bgot[k, a].astype(F32)
        bsum[a] = tot.astype(BF)
    for p, q in zip(places, cpeers):
        cp.start(bsum.at[p[0] * 4 + p[1] * 2 + p[2]], bout.at[c], q)
    last = [here(bsum.at[c], bout.at[c])]

    arrive(sd)
    for a in range(4):
        for b in range(2):
            da[a, b, co] = (da[a, b, co].astype(F32) + dath[a, b].astype(F32)).astype(BF)
    fs = [
        cp.start(da.at[:, :, co, p[0] * 4 + p[1]], fgot.at[k], q)
        for k, (p, q) in enumerate(zip(fsteps, fpeers))
    ]
    gh1 = gh1s[y].astype(F32)
    for k, copy in enumerate(hs):
        arrive(copy)
        gh1 = gh1 + gh1g[k].astype(F32)
    v = tokf[y].astype(F32)
    inv = inverse_norm(v)
    inner = gh1 * gain_one
    xh1 = v * inv
    igrad[...] = gres[...] + inv * (inner - xh1 * jnp.mean(inner * xh1, -1, keepdims=True))
    pieces = []
    for k, copy in enumerate(outs):
        copy.wait_send()
        arrive(copy)
        pieces.append(here(goo.at[k], got.at[k]))
    total = resid[...] + mine[y, xl].astype(F32)
    for k, copy in enumerate(pieces):
        copy.wait()
        total = total + got[k].astype(F32)
    lout[...] = total.astype(BF)

    for copy in ez:
        arrive(copy)
    add_arrays((2, 192, 512), [eg.at[0:2, :, :, z], zb.at[0], zb.at[1], zb.at[2]], sb)
    exb = cp.start(sb.at[:, :, 1 - xh], xb, xfar)
    arrive(ex)
    add_arrays((4, 192, 512), [eg.at[2:4, :, xh], xa], sa)
    eza = [
        cp.start(sa.at[:, :, (z + d) % 4], za.at[k], p)
        for k, (d, p) in enumerate(zip(Y_STEPS, zpeers))
    ]
    for copy in fs:
        arrive(copy)
    for a in range(4):
        for b in range(2):
            tot = da[a, b, co, f].astype(F32)
            for k in range(7):
                tot = tot + fgot[k, a, b].astype(F32)
            s2[b, a] = tot.astype(BF)
    xc = cp.start(s2.at[1 - xl], xgot, xpeer)
    arrive(xc)
    for a in range(4):
        s3[a] = (s2[xl, a].astype(F32) + xgot[a].astype(F32)).astype(BF)
    for d, p in zip(Y_STEPS, ypeers):
        cp.start(s3.at[(y + d) % 4], aout.at[y], p)
    last.append(here(s3.at[y], aout.at[y]))
    arrive(exb)
    add_arrays((192, 512), [sb.at[:, :, xh], xb], ego.at[0:2])
    for copy in eza:
        arrive(copy)
    add_arrays((192, 512), [sa.at[:, :, z], za.at[0], za.at[1], za.at[2]], ego.at[2:4])
    for copy in last:
        copy.wait()
    for copy in cp.started:
        if not any(copy is r for r in outgoing + outs):
            copy.wait_send()
        if not any(copy is r for r in got_already):
            copy.wait_recv()


def back(*ins):
    outs = (
        SDS((4, 16, 1152), BF),
        SDS((16, 16, 256), BF),
        SDS((4, 3, 192, 512), F32),
        SDS((2, 3, 4, 192, 512), BF),
        SDS((3, 2, 3, 2, 192, 512), BF),
        SDS((2, 3, 4, 192, 512), BF),
        SDS((2, 3, 2, 192, 512), BF),
        SDS((3, 2, 3, 192, 512), BF),
        SDS((2, 3, 192, 512), BF),
        SDS((4, 2, 128, 1536), BF),
        SDS((7, 128, 1536), BF),
        SDS((128, 1536), BF),
        SDS((128, 1536), F32),
    )
    out = pl.pallas_call(
        back_kernel,
        out_shape=outs,
        in_specs=[ANY] * len(ins),
        out_specs=(ANY,) * 11 + (VM,) * 2,
        scratch_shapes=[
            pltpu.SemaphoreType.DMA((96,)),
            pltpu.SemaphoreType.DMA((96,)),
            pltpu.SemaphoreType.DMA((40,)),
            pltpu.VMEM((4, 2, 128, 1536), BF),
            pltpu.VMEM((4, 2, 128, 1536), BF),
            pltpu.VMEM((7, 128, 1536), BF),
            pltpu.VMEM((128, 1536), F32),
            pltpu.VMEM((128, 1536), BF),
            pltpu.VMEM((128, 1536), F32),
            pltpu.VMEM((1536, 1152), BF),
            pltpu.VMEM((4, 128, 1536), BF),
            pltpu.VMEM((512, 1536), BF),
            pltpu.VMEM((512, 640), BF),
            pltpu.VMEM((4, 4, 128, 256), BF),
            pltpu.VMEM((4, 384, 128), F32),
            pltpu.VMEM((512, 384), BF),
            pltpu.VMEM((4, 128, 1536), BF),
            pltpu.VMEM((512, 384), BF),
            pltpu.VMEM((2048, 128), F32),
            pltpu.VMEM((2048, 128), F32),
            pltpu.VMEM((4, 4, 128, 256), BF),
            pltpu.VMEM((3, 4, 128, 256), BF),
            pltpu.VMEM((512, 640), BF),
            pltpu.VMEM((4, 128, 1536), BF),
            pltpu.VMEM((3, 128, 1536), BF),
            pltpu.VMEM((4, 2, 2, 8, 16, 1152), BF),
            pltpu.VMEM((4, 2, 8, 16, 1152), BF),
            pltpu.VMEM((7, 4, 2, 16, 1152), BF),
            pltpu.VMEM((2, 4, 16, 1152), BF),
            pltpu.VMEM((4, 16, 1152), BF),
            pltpu.VMEM((4, 16, 1152), BF),
            pltpu.VMEM((7, 16, 16, 256), BF),
            pltpu.VMEM((16, 16, 256), BF),
            pltpu.VMEM((16, 16, 256), BF),
        ],
        compiler_params=pltpu.CompilerParams(
            collective_id=2, has_side_effects=True, vmem_limit_bytes=VMEM_LIMIT
        ),
        cost_estimate=pl.CostEstimate(flops=12 * 10**9, bytes_accessed=90 * 10**6, transcendentals=3 * 10**6),
    )(*ins)
    return out[0], out[1], out[2], out[11], out[12]


def dispatch_kernel(h2_ref, cot_ref, rg_ref, x_ref, gy_ref, pick_ref, gated_ref):
    first = lax.axis_index("ctx") * 4
    masks, gates = [], []
    for e in range(4):
        ms, gs = [], []
        for s in range(2):
            hit = jnp.where(rg_ref[s, 0:6] == (first + e).astype(F32), 1.0, 0.0)
            ms.append(jnp.sum(hit, 0, keepdims=True))
            gs.append(jnp.sum(hit * rg_ref[s, 8:14], 0, keepdims=True))
        masks.append(jnp.concatenate(ms, 1))
        gates.append(jnp.concatenate(gs, 1))
    mask = jnp.concatenate(masks + [jnp.zeros((4, 256), F32)], 0)
    before = lax.broadcasted_iota(jnp.int32, (256, 256), 0)
    after = lax.broadcasted_iota(jnp.int32, (256, 256), 1)
    tri = jnp.where((before <= after) & (before // 128 == after // 128), 1.0, 0.0).astype(BF)
    place = nn(mask.astype(BF), tri) - 1.0
    lane = lax.broadcasted_iota(jnp.int32, (1, 256), 1)
    slot = lax.broadcasted_iota(jnp.int32, (48, 256), 0).astype(F32)
    picks, gated = [], []
    for e in range(4):
        at = place[e : e + 1] + jnp.where(lane >= 128, 24.0, 0.0)
        at = jnp.where(masks[e] > 0.0, at, -1.0)
        hit = jnp.where(slot == at, 1.0, 0.0)
        picks.append(hit)
        gated.append(hit * gates[e])
    pick = jnp.concatenate(picks, 0).astype(BF)
    gate = jnp.concatenate(gated, 0).astype(BF)
    x_ref[...] = nn(pick, h2_ref[...].reshape(256, 1536)).astype(BF).reshape(4, 1, 48, 1536)
    gy_ref[...] = nn(gate, cot_ref[...].reshape(256, 1536)).astype(BF).reshape(4, 1, 48, 1536)
    pick_ref[0] = pick
    gated_ref[0] = gate


def dispatch(h2, cot, rg):
    rows = pl.BlockSpec((2, 128, 1536), lambda p: (p, 0, 0))
    slots = pl.BlockSpec((4, 1, 48, 1536), lambda p: (0, p, 0, 0))
    picks = pl.BlockSpec((1, 192, 256), lambda p: (p, 0, 0))
    return pl.pallas_call(
        dispatch_kernel,
        grid=(8,),
        out_shape=(SDS((4, 8, 48, 1536), BF),) * 2 + (SDS((8, 192, 256), BF),) * 2,
        in_specs=[rows, rows, pl.BlockSpec((2, 16, 128), lambda p: (p, 0, 0))],
        out_specs=(slots, slots, picks, picks),
        compiler_params=pltpu.CompilerParams(vmem_limit_bytes=VMEM_LIMIT),
        cost_estimate=pl.CostEstimate(flops=3 * 10**9, bytes_accessed=24 * 10**6, transcendentals=0),
    )(h2, cot, rg)


def expert_kernel(x_ref, gy_ref, w, y_ref, gr_ref, dw, u_s, ga_s, gb_s):
    for t in range(2):
        cols = slice(t * 256, (t + 1) * 256)
        a = nn(x_ref[0], w[0, 0, :, cols])
        b = nn(x_ref[0], w[0, 1, :, cols])
        gu = nn(gy_ref[0], w[0, 2, :, cols])
        act, slope = silu_parts(a)
        u_s[:, cols] = (act * b).astype(BF)
        ga_s[:, cols] = (gu * b * slope).astype(BF)
        gb_s[:, cols] = (gu * act).astype(BF)

    def tile(t, carry):
        at = pl.ds(pl.multiple_of(t * 256, 256), 256)
        y_ref[0, :, at] = nt(u_s[...], w[0, 2, at, :]).astype(BF)
        gr_ref[0, :, at] = (nt(ga_s[...], w[0, 0, at, :]) + nt(gb_s[...], w[0, 1, at, :])).astype(BF)
        dw[0, 0, at, :] = tn(x_ref[0, :, at], ga_s[...]).astype(BF)
        dw[0, 1, at, :] = tn(x_ref[0, :, at], gb_s[...]).astype(BF)
        dw[0, 2, at, :] = tn(gy_ref[0, :, at], u_s[...]).astype(BF)
        return carry

    lax.fori_loop(0, 6, tile, 0)


def expert(x, gy, weights):
    rows = pl.BlockSpec((1, 384, 1536), lambda e: (e, 0, 0))
    whole = pl.BlockSpec((1, 3, 1536, 512), lambda e: (e, 0, 0, 0))
    return pl.pallas_call(
        expert_kernel,
        grid=(4,),
        out_shape=(SDS((4, 384, 1536), BF),) * 2 + (SDS((4, 3, 1536, 512), BF),),
        in_specs=[rows, rows, whole],
        out_specs=(rows, rows, whole),
        scratch_shapes=[pltpu.VMEM((384, 512), BF)] * 3,
        compiler_params=pltpu.CompilerParams(vmem_limit_bytes=VMEM_LIMIT),
        cost_estimate=pl.CostEstimate(flops=22 * 10**9, bytes_accessed=60 * 10**6, transcendentals=10**6),
    )(x, gy, weights)


def combine_kernel(pick_ref, gated_ref, y_ref, gr_ref, h2_ref, cot_ref, sw_ref, out_ref, gh_ref, db_ref, ds_ref):
    @pl.when(pl.program_id(0) == 0)
    def _():
        ds_ref[...] = jnp.zeros_like(ds_ref)

    h2 = h2_ref[...].reshape(256, 1536)
    cot = cot_ref[...].reshape(256, 1536)
    act, slope = silu_parts(nn(h2, sw_ref[:, 0:128]))
    up = nn(h2, sw_ref[:, 128:256])
    gz = nn(cot, sw_ref[:, 256:384])
    hid = (act * up).astype(BF)
    gc = (gz * up * slope).astype(BF)
    gd = (gz * act).astype(BF)
    out = tn(gated_ref[0], y_ref[...].reshape(192, 1536)) + nt(hid, sw_ref[:, 256:384])
    out_ref[...] = out.astype(BF).reshape(2, 128, 1536)
    gh = tn(pick_ref[0], gr_ref[...].reshape(192, 1536)) + nt(gc, sw_ref[:, 0:128])
    gh = gh + nt(gd, sw_ref[:, 128:256])
    gh_ref[...] = gh.astype(BF).reshape(2, 128, 1536)
    ds_ref[:, 0:128] += tn(h2, gc)
    ds_ref[:, 128:256] += tn(h2, gd)
    ds_ref[:, 256:384] += tn(cot, hid)

    @pl.when(pl.program_id(0) == 7)
    def _():
        rows, cols = one_hot_rows(), spread_columns()
        for k in range(16):
            block = nt(ds_ref[k * 96 : (k + 1) * 96].astype(BF), cols).astype(BF)
            db_ref[k] = tn(rows, block).astype(BF).reshape(8, 16, 256)


def combine(pick, gated, y, gr, h2, cot, sw):
    rows = pl.BlockSpec((2, 128, 1536), lambda p: (p, 0, 0))
    slots = pl.BlockSpec((4, 1, 48, 1536), lambda p: (0, p, 0, 0))
    picks = pl.BlockSpec((1, 192, 256), lambda p: (p, 0, 0))
    whole = pl.BlockSpec((1536, 384), lambda p: (0, 0))
    return pl.pallas_call(
        combine_kernel,
        grid=(8,),
        out_shape=(SDS((16, 128, 1536), BF),) * 2 + (SDS((16, 8, 16, 256), BF),),
        in_specs=[picks, picks, slots, slots, rows, rows, whole],
        out_specs=(rows, rows, pl.BlockSpec((16, 8, 16, 256), lambda p: (0, 0, 0, 0))),
        scratch_shapes=[pltpu.VMEM((1536, 384), F32)],
        compiler_params=pltpu.CompilerParams(vmem_limit_bytes=VMEM_LIMIT),
        cost_estimate=pl.CostEstimate(flops=8 * 10**9, bytes_accessed=36 * 10**6, transcendentals=10**6),
    )(pick, gated, y, gr, h2, cot, sw)


def local(
    tokens,
    cotangent,
    routes,
    gates,
    attn_gain,
    ffn_gain,
    w_query,
    w_key,
    w_value,
    w_out,
    shared_gate,
    shared_up,
    shared_down,
    expert_gate,
    expert_up,
    expert_down,
):
    tok = tokens.reshape(128, 1536)
    cot = cotangent.reshape(128, 1536)
    rg = jnp.concatenate(
        [
            jnp.pad(routes.reshape(128, 6).T.astype(F32), ((0, 2), (0, 0)), constant_values=-1.0),
            jnp.pad(gates.reshape(128, 6).T, ((0, 2), (0, 0))),
        ],
        0,
    )
    gains = jnp.pad(jnp.stack([attn_gain, ffn_gain], 1), ((0, 0), (0, 126)))
    a_in = jnp.concatenate(
        [
            w_query.reshape(12, 4, 384),
            w_key.reshape(12, 4, 128),
            w_value.reshape(12, 4, 128),
            w_out.T.reshape(12, 4, 384),
            jnp.broadcast_to(gains[:, None], (12, 4, 128)),
        ],
        2,
    )
    a_in = jnp.pad(jnp.transpose(a_in, (1, 0, 2)), ((0, 0), (0, 4), (0, 0)))
    b_in = jnp.concatenate(
        [
            shared_gate.reshape(12, 16, 64),
            shared_up.reshape(12, 16, 64),
            shared_down.T.reshape(12, 16, 64),
            jnp.zeros((12, 16, 64), BF),
        ],
        2,
    )
    b_in = jnp.pad(jnp.transpose(b_in, (1, 0, 2)), ((0, 0), (0, 4), (0, 0)))
    own = jnp.stack([expert_gate, expert_up, jnp.transpose(expert_down, (0, 2, 1))], 1)
    (cot_f, rg_f, h2_f, wexp, tok_f, kv_f, w, sw, h1, qkv, att, lse, resid) = front(
        a_in, b_in, tok, cot, rg, own
    )
    x, gy, pick, gated = dispatch(h2_f, cot_f, rg_f)
    y, gr, eg = expert(
        x.reshape(4, 384, 1536), gy.reshape(4, 384, 1536), wexp.reshape(4, 3, 1536, 512)
    )
    out_p, gh2_p, db = combine(
        pick, gated, y.reshape(4, 8, 48, 1536), gr.reshape(4, 8, 48, 1536), h2_f, cot_f, sw
    )
    a_out, b_out, sums, layer_out, input_grad = back(
        gh2_p.reshape(4, 2, 2, 128, 1536),
        out_p.reshape(4, 2, 2, 128, 1536),
        eg.reshape(4, 3, 2, 4, 192, 512),
        resid,
        cot,
        w,
        tok_f,
        h1,
        qkv,
        kv_f,
        lse,
        att,
        db,
    )
    a_out = jnp.transpose(a_out[:, :12].astype(F32), (1, 0, 2))
    b_out = jnp.transpose(b_out[:, :12].astype(F32), (1, 0, 2))
    gain_out = jnp.sum(a_out[:, :, 1024:1026], 1)
    return (
        layer_out.reshape(1, 128, 1536),
        input_grad.reshape(1, 128, 1536),
        gain_out[:, 0],
        gain_out[:, 1],
        a_out[:, :, 0:384].reshape(12, 1536),
        a_out[:, :, 384:512].reshape(12, 512),
        a_out[:, :, 512:640].reshape(12, 512),
        a_out[:, :, 640:1024].reshape(12, 1536).T,
        b_out[:, :, 0:64].reshape(12, 1024),
        b_out[:, :, 64:128].reshape(12, 1024),
        b_out[:, :, 128:192].reshape(12, 1024).T,
        sums[:, 0],
        sums[:, 1],
        jnp.transpose(sums[:, 2], (0, 2, 1)),
    )


def solution(mesh):
    both = ("ctx", "fsdp")
    rows = P("fsdp", "ctx", None)
    weights = (P(both),) * 2 + (P(both, None),) * 3 + (P(None, both),)
    weights = weights + (P(both, None),) * 2 + (P(None, both),)
    weights = weights + (P("ctx", "fsdp", None),) * 2 + (P("ctx", None, "fsdp"),)
    return jax.shard_map(
        local, mesh=mesh, in_specs=(rows,) * 4 + weights, out_specs=(rows,) * 2 + weights, check_vma=False
    )
```

```python
import jax
import jax.numpy as jnp
from jax import lax
from jax.experimental import pallas as pl
from jax.experimental.pallas import tpu as pltpu
from jax.sharding import PartitionSpec as P

BF = jnp.bfloat16
F32 = jnp.float32
EPS = 1e-05
MESH = pl.DeviceIdType.MESH
ANY = pl.BlockSpec(memory_space=pl.ANY)
VM = pl.BlockSpec(memory_space=pltpu.VMEM)
SDS = jax.ShapeDtypeStruct
SCALE = 128 ** (-0.5)
VMEM_LIMIT = 56 * 2**20


def nn(a, b):
    return lax.dot_general(a, b, (((1,), (0,)), ((), ())), preferred_element_type=F32)


def nt(a, b):
    return lax.dot_general(a, b, (((1,), (1,)), ((), ())), preferred_element_type=F32)


def tn(a, b):
    return lax.dot_general(a, b, (((0,), (0,)), ((), ())), preferred_element_type=F32)


def silu_parts(pre_act):
    sig = 1.0 / (1.0 + jnp.exp(-pre_act))
    return pre_act * sig, sig * (1.0 + pre_act * (1.0 - sig))


def coords():
    c = lax.axis_index("ctx")
    f = lax.axis_index("fsdp")
    return c // 4, (c // 2) % 2, c % 2, f // 4, f % 4


def dev(y, xl, co, xh, z):
    return (y * 4 + xl * 2 + co, xh * 4 + z)


def barrier(peers):
    sem = pltpu.get_barrier_semaphore()
    for peer in peers:
        pl.semaphore_signal(sem, inc=1, device_id=peer, device_id_type=MESH)
    pl.semaphore_wait(sem, len(peers))


class Copies:
    def __init__(self, send, recv):
        self.send, self.recv, self.n, self.started = send, recv, 0, []

    def start(self, src, dst, peer):
        copy = pltpu.make_async_remote_copy(
            src, dst, self.send.at[self.n], self.recv.at[self.n], device_id=peer, device_id_type=MESH
        )
        copy.start()
        self.n += 1
        self.started.append(copy)
        return copy

    def finish(self, received=()):
        for copy in self.started:
            copy.wait_send()
            if not any(copy is r for r in received):
                copy.wait_recv()


Y_STEPS = (1, 2, 3)


def one_hot_rows():
    row = lax.broadcasted_iota(jnp.int32, (96, 128), 0)
    col = lax.broadcasted_iota(jnp.int32, (96, 128), 1)
    return jnp.where((row // 12) * 16 + row % 12 == col, 1.0, 0.0).astype(BF)


def eye_rows():
    row = lax.broadcasted_iota(jnp.int32, (8, 128), 0)
    col = lax.broadcasted_iota(jnp.int32, (8, 128), 1)
    return jnp.where(row == col, 1.0, 0.0).astype(BF)


def inverse_norm(values):
    return lax.rsqrt(jnp.mean(values * values, -1, keepdims=True) + EPS)


def head_rows(ref, j, first=0):
    rows = slice(j * 128, (j + 1) * 128)
    return jnp.concatenate([ref[rows, first + h * 128 : first + (h + 1) * 128] for h in range(3)], 0)


def allowed(n):
    i = lax.axis_index("ctx") % 4
    row = lax.broadcasted_iota(jnp.int32, (384, n), 0) % 128
    col = lax.broadcasted_iota(jnp.int32, (384, n), 1)
    return col <= i * 128 + row


def ctx_places(y, xl, co):
    return [
        ((y + dy) % 4, (xl + dx) % 2, (co + dc) % 2)
        for dy in range(4)
        for dx in (0, 1)
        for dc in (0, 1)
        if (dy, dx, dc) != (0, 0, 0)
    ]


def x_place(xh, xl, d):
    x = (xh * 2 + xl + d) % 4
    return x // 2, x % 2


def plane_gather(cp, arrive, src, out, places, sib, split):
    y, xl, co, xh, z = places
    low, high = pl.ds(0, split), pl.ds(split, 128 - split)
    ypeers = [dev((y + d) % 4, xl, co, xh, z) for d in Y_STEPS]
    xpeers = []
    for d in Y_STEPS:
        h, l = x_place(xh, xl, d)
        xpeers.append(dev(y, l, co, h, z))
    mine = (xh, y, xl, co)

    def first_y():
        return [cp.start(src.at[high], out.at[mine + (high,)], p) for p in ypeers]

    def first_x():
        return [cp.start(src.at[low], out.at[mine + (low,)], p) for p in xpeers]

    def then_y(firsts):
        for copy in firsts:
            arrive(copy)
        piece = out.at[:, y, :, co, low]
        return [cp.start(piece, piece, p) for p in ypeers] + [cp.start(piece, piece, sib)]

    def then_x(firsts):
        for copy in firsts:
            arrive(copy)
        piece = out.at[xh, :, xl, co, high]
        return [cp.start(piece, piece, p) for p in xpeers] + [cp.start(piece, piece, sib)]

    def last_y(seconds):
        sent = []
        for d, copy in zip(Y_STEPS, seconds):
            arrive(copy)
            piece = out.at[:, (y + 4 - d) % 4, :, co, low]
            sent.append(cp.start(piece, piece, sib))
        return sent

    def last_x(seconds):
        sent = []
        for d, copy in zip(Y_STEPS, seconds):
            arrive(copy)
            h, l = x_place(xh, xl, 4 - d)
            piece = out.at[h, :, l, co, high]
            sent.append(cp.start(piece, piece, sib))
        return sent

    return first_y, first_x, then_y, then_x, last_y, last_x


def dispatch_rows(rg, first):
    masks, gates = [], []
    for e in range(2):
        ms, gs = [], []
        for s in range(2):
            hit = jnp.where(rg[s, 0:6] == (first + e).astype(F32), 1.0, 0.0)
            ms.append(jnp.sum(hit, 0, keepdims=True))
            gs.append(jnp.sum(hit * rg[s, 8:14], 0, keepdims=True))
        masks.append(jnp.concatenate(ms, 1))
        gates.append(jnp.concatenate(gs, 1))
    mask = jnp.concatenate(masks + [jnp.zeros((6, 256), F32)], 0)
    before = lax.broadcasted_iota(jnp.int32, (256, 256), 0)
    after = lax.broadcasted_iota(jnp.int32, (256, 256), 1)
    tri = jnp.where((before <= after) & (before // 128 == after // 128), 1.0, 0.0).astype(BF)
    place = nn(mask.astype(BF), tri) - 1.0
    lane = lax.broadcasted_iota(jnp.int32, (1, 256), 1)
    slot = lax.broadcasted_iota(jnp.int32, (48, 256), 0).astype(F32)
    picks, gated = [], []
    for e in range(2):
        at = place[e : e + 1] + jnp.where(lane >= 128, 24.0, 0.0)
        at = jnp.where(masks[e] > 0.0, at, -1.0)
        hit = jnp.where(slot == at, 1.0, 0.0)
        picks.append(hit)
        gated.append(hit * gates[e])
    return jnp.concatenate(picks, 0).astype(BF), jnp.concatenate(gated, 0).astype(BF)


def eye(rows, cols):
    row = lax.broadcasted_iota(jnp.int32, (rows, cols), 0)
    col = lax.broadcasted_iota(jnp.int32, (rows, cols), 1)
    return jnp.where(row == col, 1.0, 0.0).astype(BF)


def half_turn(x):
    return pltpu.roll(x, 64, 1)


def front_kernel(
    tok, cot, routes, gates, gains_in, wq, wk, wv, wo, sg, su, sd, eg, eu, ed,
    cotf, h2f, wexp, tokf_o, kvf_o, gy, pick_o, gated_o, rgf,
    w, sw, qkv, att, lse, resid,
    send, recv, loc, a_s, b_s, own, rg_s, a2, wf, b1, bf, tokf, kvf, s_s, part, got, h2,
):
    y, xl, co, xh, z = coords()
    i, c, f = xl * 2 + co, y * 4 + xl * 2 + co, xh * 4 + z
    f_far = (1 - xh) * 4 + z
    sib = dev(y, xl, 1 - co, xh, z)
    xpeer = dev(y, 1 - xl, co, xh, z)
    xfar = dev(y, xl, co, 1 - xh, z)
    ypeers = [dev((y + d) % 4, xl, co, xh, z) for d in Y_STEPS]
    zpeers = [dev(y, xl, co, xh, (z + d) % 4) for d in Y_STEPS]
    places = ctx_places(y, xl, co)
    cpeers = [dev(*p, xh, z) for p in places]
    plane = cpeers + [dev(*p, 1 - xh, z) for p in places + [(y, xl, co)]]
    peers = plane + zpeers
    sem = pltpu.get_barrier_semaphore()
    for peer in peers:
        pl.semaphore_signal(sem, inc=1, device_id=peer, device_id_type=MESH)

    e16 = eye(16, 12)
    q16, k16, v16 = (nn(e16, ref[...]).astype(BF) for ref in (wq, wk, wv))
    o16 = nt(e16, wo[...]).astype(BF)
    for k in range(4):
        wide, thin = slice(k * 384, (k + 1) * 384), slice(k * 128, (k + 1) * 128)
        a_s[k] = jnp.concatenate([q16[:, wide], k16[:, thin], v16[:, thin], gains_in[...], o16[:, wide]], 1)
    g16, u16, d16 = nn(e16, sg[...]), nn(e16, su[...]), nt(e16, sd[...])
    front_half = lax.broadcasted_iota(jnp.int32, (16, 128), 1) < 64
    for k in range(8):
        at = slice(k * 128, (k + 1) * 128)
        g, u, d = g16[:, at], u16[:, at], d16[:, at]
        for n in range(2):
            if n:
                g, d = half_turn(g), half_turn(d)
            else:
                u = half_turn(u)
            b_s[2 * k + n, :, 0:128] = jnp.where(front_half, g, u).astype(BF)
            b_s[2 * k + n, :, 128:256] = jnp.where(front_half, d, 0.0).astype(BF)
            if not n:
                u = half_turn(u)
    for e in range(4):
        own[e, 0] = eg[e]
        own[e, 1] = eu[e]
        own[e, 2] = nt(eye(192, 192), ed[e]).astype(BF)
    rg_s[0:8] = nt(eye(8, 6), routes[0].astype(F32).astype(BF))
    rg_s[8:16] = nt(eye(8, 6), gates[0].astype(BF))
    pl.semaphore_wait(sem, len(peers))

    cp = Copies(send, recv)
    n_local = [0]

    def here(src, dst):
        copy = pltpu.make_async_copy(src, dst, loc.at[n_local[0]])
        n_local[0] += 1
        copy.start()
        return copy

    got_already = []

    def arrive(copy):
        copy.wait_recv()
        got_already.append(copy)

    me = (y, xl, co, xh, z)
    ya = [cp.start(a_s.at[(y + d) % 4], a2.at[y, xl], p) for d, p in zip(Y_STEPS, ypeers)]
    la = here(a_s.at[y], a2.at[y, xl])
    lb = here(b_s.at[c], b1.at[c])
    lt = here(tok, tokf.at[y])
    lr = here(rg_s, rgf.at[xh, c])
    later = [here(own.at[pl.ds(xh * 2, 2)], wexp.at[:, :, f])]
    own_cot = here(cot, cotf.at[xh, y, xl, co])
    cot_y, cot_x, cot_then_y, cot_then_x, cot_last_y, cot_last_x = plane_gather(
        cp, arrive, cot, cotf, me, sib, 64
    )
    yt = [cp.start(tok, tokf.at[y], p) for p in ypeers]
    cy = cot_y()
    la.wait()
    for copy in ya:
        arrive(copy)
    xa = cp.start(a2.at[:, xl], a2.at[:, xl], xpeer)
    bs = [cp.start(b_s.at[p[0] * 4 + p[1] * 2 + p[2]], b1.at[c], q) for p, q in zip(places, cpeers)]
    rgs = [cp.start(rg_s, rgf.at[xh, c], q) for q in plane]
    arrive(xa)

    head, tail = pl.ds(0, 768), pl.ds(768, 384)

    def slices(cols):
        return a2.at[:, :, :, cols], wf.at[:, :, co, f, :, cols], wf.at[:, :, co, f_far, :, cols]

    src, mine, far = slices(head)
    hx = cp.start(src, mine, xfar)
    hz = [cp.start(src, mine, p) for p in zpeers]
    lw = here(a2, wf.at[:, :, co, f])
    cx = cot_x()
    src_t, mine_t, far_t = slices(tail)
    tx = cp.start(src_t, mine_t, xfar)
    ex = [cp.start(own.at[2 - xh * 2], wexp.at[0, :, f], xfar)]
    lw.wait()
    to_sib = [cp.start(mine, mine, sib)]
    arrive(hx)
    hz2 = [cp.start(far, far, p) for p in zpeers]
    to_sib.append(cp.start(far, far, sib))
    tz = [cp.start(src_t, mine_t, p) for p in zpeers]
    for copies, h in ((hz, xh), (hz2, 1 - xh)):
        for d, copy in zip(Y_STEPS, copies):
            arrive(copy)
            piece = wf.at[:, :, co, h * 4 + (z + 4 - d) % 4, :, head]
            to_sib.append(cp.start(piece, piece, sib))
    own_cot.wait()
    cy2 = cot_then_y(cx)
    arrive(tx)
    tz2 = [cp.start(far_t, far_t, p) for p in zpeers]
    tail_sib = [cp.start(mine_t, mine_t, sib), cp.start(far_t, far_t, sib)]
    for p in zpeers:
        cp.start(own.at[pl.ds(xh * 2, 2)], wexp.at[:, :, f], p)
    for copy in to_sib:
        arrive(copy)
    rows = one_hot_rows()

    def compact(cols):
        for yy in range(4):
            for k in range(4):
                at = (yy * 4 + k) * 96
                block = wf[yy, k // 2, k % 2, :, :, cols].reshape(128, -1)
                w[at : at + 96, cols] = nn(rows, block).astype(BF)

    compact(slice(0, 768))
    gains = nt(eye_rows(), w[:, 640:768])
    gain_one, gain_two = gains[0:1], gains[1:2]

    lt.wait()
    for copy in yt:
        arrive(copy)
    for j in range(4):
        v = tokf[j].astype(F32)
        rows_j = slice(j * 128, (j + 1) * 128)
        h1 = (v * inverse_norm(v) * gain_one).astype(BF)
        qkv_j = nn(h1, w[:, :640]).astype(BF)
        qkv[rows_j] = qkv_j
        kvf[j, i] = qkv_j[:, 384:]
    kx = cp.start(kvf.at[:, i], kvf.at[:, i], xpeer)
    ks = [cp.start(kvf.at[:, i], kvf.at[:, i], sib)]
    saved = [here(tokf, tokf_o)]
    for copies, h in ((tz, xh), (tz2, 1 - xh)):
        for d, copy in zip(Y_STEPS, copies):
            arrive(copy)
            piece = wf.at[:, :, co, h * 4 + (z + 4 - d) % 4, :, tail]
            tail_sib.append(cp.start(piece, piece, sib))
    arrive(kx)
    piece = kvf.at[:, (1 - xl) * 2 + co]
    ks.append(cp.start(piece, piece, sib))
    ex.append(cp.start(own.at[3 - xh * 2], wexp.at[1, :, f], xfar))
    cx2 = cot_then_x(cy)
    for copy in ks:
        arrive(copy)
    saved.append(here(kvf, kvf_o))

    for j in range(4):
        n = (j + 1) * 512
        q = head_rows(qkv, j)
        for t in range(j + 1):
            s = nt(q, kvf[t].reshape(512, 256)[:, :128]) * SCALE
            if t == j:
                s = jnp.where(allowed(512), s, -1e30)
            s_s[:, t * 512 : (t + 1) * 512] = s
        s = s_s[:, :n]
        m = jnp.max(s, -1, keepdims=True)
        p = jnp.exp(s - m)
        total = jnp.sum(p, -1, keepdims=True)
        o = nn(p.astype(BF), kvf[0 : j + 1].reshape(n, 256)[:, 128:]) / total
        rows_j = slice(j * 128, (j + 1) * 128)
        for h in range(3):
            att[rows_j, h * 128 : (h + 1) * 128] = o[h * 128 : (h + 1) * 128].astype(BF)
        lse[j] = jnp.broadcast_to(m + jnp.log(total), (384, 128))
    for copy in tail_sib:
        arrive(copy)
    compact(slice(768, 1152))
    for j in range(4):
        part[j] = nt(att[j * 128 : (j + 1) * 128], w[:, 768:1152]).astype(BF)
    ps = [
        cp.start(part.at[(y + d) % 4], got.at[k], p) for k, (d, p) in enumerate(zip(Y_STEPS, ypeers))
    ]
    far_rows = wexp.at[0, :, f_far]
    arrive(ex[0])
    for p in zpeers:
        cp.start(far_rows, far_rows, p)
    total = tokf[y].astype(F32) + part[y].astype(F32)
    for k, copy in enumerate(ps):
        arrive(copy)
        total = total + got[k].astype(F32)
    resid[...] = total
    h2[...] = (total * inverse_norm(total) * gain_two).astype(BF)
    h2_y, h2_x, h2_then_y, h2_then_x, h2_last_y, h2_last_x = plane_gather(
        cp, arrive, h2, h2f, me, sib, 80
    )
    hx = h2_x()
    hy = h2_y()
    own_h2 = here(h2, h2f.at[xh, y, xl, co])

    cot_sib = [cy2[3], cx2[3]] + cot_last_y(cy2[:3])
    own_h2.wait()
    hy2 = h2_then_y(hx)
    hx2 = h2_then_x(hy)
    far_rows_1 = wexp.at[1, :, f_far]
    arrive(ex[1])
    for p in zpeers:
        cp.start(far_rows_1, far_rows_1, p)
    lb.wait()
    for copy in bs:
        arrive(copy)
    bx = cp.start(b1, bf.at[:, f], xfar)
    bz = [cp.start(b1, bf.at[:, f], p) for p in zpeers]
    lb = here(b1, bf.at[:, f])
    lr.wait()
    for copy in rgs:
        arrive(copy)
    arrive(bx)
    bz += [cp.start(bf.at[:, f_far], bf.at[:, f_far], p) for p in zpeers]
    cot_sib += cot_last_x(cx2[:3])
    for copy in cot_sib:
        arrive(copy)

    first = c * 4 + xh * 2

    def gated_rows(rg_ref, cot_ref, gy_ref, pick_ref, gated_ref):
        pick, gated = dispatch_rows(rg_ref.reshape(2, 16, 128), first)
        gy_ref[...] = nn(gated, cot_ref[...].reshape(256, 1536)).astype(BF).reshape(2, 1, 48, 1536)
        pick_ref[0], gated_ref[0] = pick, gated

    picks = pl.BlockSpec((1, 96, 256), lambda p: (p, 0, 0))
    pltpu.emit_pipeline(
        gated_rows,
        grid=(16,),
        in_specs=[
            pl.BlockSpec((1, 2, 16, 128), lambda p: (p // 8, p % 8, 0, 0)),
            pl.BlockSpec((1, 1, 1, 2, 128, 1536), lambda p: (p // 8, p // 2 % 4, p % 2, 0, 0, 0)),
        ],
        out_specs=[pl.BlockSpec((2, 1, 48, 1536), lambda p: (0, p, 0, 0)), picks, picks],
    )(rgf, cotf, gy, pick_o, gated_o)
    lb.wait()
    for copy in bz:
        arrive(copy)
    for k in range(16):
        sw[k * 96 : (k + 1) * 96] = nn(rows, bf[k].reshape(128, 256)).astype(BF)
    h2_last_y(hy2[:3])
    h2_last_x(hx2[:3])
    for copy in later + saved:
        copy.wait()
    cp.finish(got_already)


def front(*ins):
    outs = (
        SDS((2, 4, 2, 2, 128, 1536), BF),
        SDS((2, 4, 2, 2, 128, 1536), BF),
        SDS((2, 3, 8, 192, 512), BF),
        SDS((4, 128, 1536), BF),
        SDS((4, 4, 128, 256), BF),
        SDS((2, 16, 48, 1536), BF),
        SDS((16, 96, 256), BF),
        SDS((16, 96, 256), BF),
        SDS((2, 16, 16, 128), F32),
        SDS((1536, 1152), BF),
        SDS((1536, 256), BF),
        SDS((512, 640), BF),
        SDS((512, 384), BF),
        SDS((4, 384, 128), F32),
        SDS((128, 1536), F32),
    )
    return pl.pallas_call(
        front_kernel,
        out_shape=outs,
        in_specs=[ANY] * 2 + [VM] * (len(ins) - 2),
        out_specs=(ANY,) * 9 + (VM,) * 6,
        scratch_shapes=[
            pltpu.SemaphoreType.DMA((160,)),
            pltpu.SemaphoreType.DMA((160,)),
            pltpu.SemaphoreType.DMA((16,)),
            pltpu.VMEM((4, 16, 1152), BF),
            pltpu.VMEM((16, 16, 256), BF),
            pltpu.VMEM((4, 3, 192, 512), BF),
            pltpu.VMEM((16, 128), F32),
            pltpu.VMEM((4, 2, 16, 1152), BF),
            pltpu.VMEM((4, 2, 2, 8, 16, 1152), BF),
            pltpu.VMEM((16, 16, 256), BF),
            pltpu.VMEM((16, 8, 16, 256), BF),
            pltpu.VMEM((4, 128, 1536), BF),
            pltpu.VMEM((4, 4, 128, 256), BF),
            pltpu.VMEM((384, 2048), F32),
            pltpu.VMEM((4, 128, 1536), BF),
            pltpu.VMEM((3, 128, 1536), BF),
            pltpu.VMEM((128, 1536), BF),
        ],
        compiler_params=pltpu.CompilerParams(
            collective_id=1, has_side_effects=True, vmem_limit_bytes=VMEM_LIMIT
        ),
        cost_estimate=pl.CostEstimate(flops=6 * 10**9, bytes_accessed=60 * 10**6, transcendentals=3 * 10**6),
    )(*ins)


def add_blocks(*refs):
    total = refs[0][...].astype(F32)
    for ref in refs[1:-1]:
        total = total + ref[...].astype(F32)
    refs[-1][...] = total.astype(refs[-1].dtype)


def add_arrays(block, ins, out):
    spec = pl.BlockSpec((1,) + block, lambda m, r: (m, 0, r, 0))
    pltpu.emit_pipeline(add_blocks, grid=(3, 2), in_specs=[spec] * len(ins), out_specs=[spec])(*ins, out)


def back_kernel(
    gh2p, eg, y_in, gated_in, hid_in, resid_i, cot_i, w_i, sw_i, tokf_i, qkv_i, kvf_i, lse_i, att_i, db,
    outp, zb, sb, xb, thg, tho, goy, gox,
    lout, igrad, gains_o, wq_o, wk_o, wv_o, wo_o, sg_o, su_o, sd_o, eg_o, eu_o, ed_o,
    send, recv, loc, miney, minex, tmpy, tmpx, goty, gotx, gety, getx, resid, cot, gres, w, sdw, tokf, qkv, kvf,
    lse, att, gattn, go, dk, dv, dkvs, dkvr, gqkv, gh1s, gh1g, da, dath, zg, zs, xg, s2, xgot, s3, aout,
    bgot, bmine, bz, bxg, bsum, bout, esum, egot,
):
    y, xl, co, xh, z = coords()
    i, c = xl * 2 + co, y * 4 + xl * 2 + co
    sib = dev(y, xl, 1 - co, xh, z)
    xpeer = dev(y, 1 - xl, co, xh, z)
    xfar = dev(y, xl, co, 1 - xh, z)
    ypeers = [dev((y + d) % 4, xl, co, xh, z) for d in Y_STEPS]
    zpeers = [dev(y, xl, co, xh, (z + d) % 4) for d in Y_STEPS]
    places = ctx_places(y, xl, co)
    cpeers = [dev(*p, xh, z) for p in places]
    xpeers = []
    for d in Y_STEPS:
        hh, ll = x_place(xh, xl, d)
        xpeers.append(dev(y, ll, co, hh, z))
    barrier(cpeers + [dev(y, k, co, 1 - xh, z) for k in range(2)] + zpeers)
    cp = Copies(send, recv)
    n_local = [0]

    def here(src, dst):
        copy = pltpu.make_async_copy(src, dst, loc.at[n_local[0]])
        n_local[0] += 1
        copy.start()
        return copy

    got_already, sent_already = [], []

    def arrive(copy):
        copy.wait_recv()
        got_already.append(copy)

    def gone(copies):
        for copy in copies:
            copy.wait_send()
            sent_already.append(copy)

    low, high = pl.ds(0, 64), pl.ds(64, 64)

    def sum_start(xp, there):
        sibs = {}
        for d in (1, 3, 2, 0):
            yy, (hh, ll) = (y + d) % 4, x_place(xh, xl, d)
            sibs["y", d] = cp.start(xp.at[:, yy, :, 1 - co, low], there.at[:, yy, :, low], sib)
            sibs["x", d] = cp.start(xp.at[hh, :, ll, 1 - co, high], there.at[hh, :, ll, high], sib)
        return sibs

    def sum_push(xp, there, sibs, toy, tox, steps):
        sent, loads = {}, {}

        def load(n):
            axis, d = steps[n]
            arrive(sibs[axis, d])
            if axis == "y":
                yy = (y + d) % 4
                loads[n] = [
                    here(xp.at[:, yy, :, co, low], miney.at[d]),
                    here(there.at[:, yy, :, low], tmpy.at[n % 2]),
                ]
            else:
                hh, ll = x_place(xh, xl, d)
                loads[n] = [
                    here(xp.at[hh, :, ll, co, high], minex.at[d]),
                    here(there.at[hh, :, ll, high], tmpx.at[n % 2]),
                ]

        load(0)
        for n, (axis, d) in enumerate(steps):
            if n + 1 < len(steps):
                load(n + 1)
            for copy in loads[n]:
                copy.wait()
            own, other = (miney, tmpy) if axis == "y" else (minex, tmpx)
            own[d] = (own[d].astype(F32) + other[n % 2].astype(F32)).astype(BF)
            if d and axis == "y":
                sent[axis, d] = cp.start(miney.at[d], toy.at[d - 1], ypeers[d - 1])
            elif d:
                sent[axis, d] = cp.start(minex.at[d], tox.at[d - 1], xpeers[d - 1])
        return sent

    def sum_second():
        for h in range(2):
            for l in range(2):
                tot = miney[0, h, l].astype(F32)
                for k in range(3):
                    tot = tot + goty[k, h, l].astype(F32)
                miney[0, h, l] = tot.astype(BF)
        for a in range(4):
            tot = minex[0, a].astype(F32)
            for k in range(3):
                tot = tot + gotx[k, a].astype(F32)
            minex[0, a] = tot.astype(BF)

    def sum_last(nth):
        sent = []
        for k, d in enumerate(Y_STEPS):
            hh, ll = x_place(xh, xl, d)
            sent.append(cp.start(miney.at[0, hh, ll], gety.at[nth, k], xpeers[k]))
            sent.append(cp.start(minex.at[0, (y + d) % 4], getx.at[nth, k], ypeers[k]))
        return sent

    def sum_end(nth, sent):
        for copy in sent:
            arrive(copy)
        top, bottom = miney[0, xh, xl].astype(F32), minex[0, y].astype(F32)
        for k in range(3):
            top = top + gety[nth, k].astype(F32)
            bottom = bottom + getx[nth, k].astype(F32)
        return jnp.concatenate([top, bottom], 0)

    sibs = sum_start(gh2p, thg)
    first = [here(resid_i, resid), here(cot_i, cot), here(w_i, w), here(sw_i.at[:, pl.ds(128, 128)], sdw)]
    second = [here(qkv_i, qkv), here(kvf_i, kvf), here(lse_i, lse), here(att_i, att)]
    third = [here(tokf_i, tokf)]
    bl = here(db.at[:, :, z], bmine)
    both = [("y", 1), ("x", 1), ("y", 3), ("x", 3), ("y", 2), ("x", 2), ("y", 0), ("x", 0)]
    sent_g = sum_push(gh2p, thg, sibs, goty, gotx, both)
    ez = [
        [
            cp.start(eg.at[e, :, :, (z + d) % 4], zb.at[k, e], p)
            for k, (d, p) in enumerate(zip(Y_STEPS, zpeers))
        ]
        for e in range(2)
    ]
    for copy in first:
        copy.wait()

    def output_rows(shared, gated_ref, y_ref, *refs):
        out = tn(gated_ref[0], y_ref[...].reshape(96, 1536))
        if shared:
            out = out + nt(refs[0][0], sdw[...])
        refs[-1][...] = out.astype(BF).reshape(1, 1, 2, 128, 1536)

    for shared in (True, False):
        h = xh if shared else 1 - xh
        specs = [
            pl.BlockSpec((1, 96, 256), lambda p: (p, 0, 0)),
            pl.BlockSpec((2, 1, 48, 1536), lambda p: (0, p, 0, 0)),
        ]
        args = [gated_in.at[h], y_in.at[:, h]]
        if shared:
            specs.append(pl.BlockSpec((1, 256, 128), lambda p: (p, 0, 0)))
            args.append(hid_in)
        pltpu.emit_pipeline(
            lambda *refs, shared=shared: output_rows(shared, *refs),
            grid=(8,),
            in_specs=specs,
            out_specs=[pl.BlockSpec((1, 1, 2, 128, 1536), lambda p: (p // 2, p % 2, 0, 0, 0))],
        )(*args, outp.at[h])
    sibs = sum_start(outp, tho)

    gains = nt(eye_rows(), w[:, 640:768])
    gain_one, gain_two = gains[0:1], gains[1:2]
    inv = inverse_norm(resid[...])
    xh2 = resid[...] * inv
    for copy in sent_g.values():
        arrive(copy)
    sum_second()
    last_g = sum_last(0)
    gh2 = sum_end(0, last_g)
    gain_two_grad = jnp.sum(gh2 * xh2, 0, keepdims=True)
    inner = gh2 * gain_two
    row = inv * (inner - xh2 * jnp.mean(inner * xh2, -1, keepdims=True))
    gres[...] = cot[...].astype(F32) + row
    gattn[y] = gres[...].astype(BF)
    ga = [cp.start(gattn.at[y], gattn.at[y], p) for p in ypeers]

    gone(list(sent_g.values()) + last_g)
    sent_o = sum_push(outp, tho, sibs, goy, gox, both[:4] + both[4:5] + both[6:])

    for copy in second:
        copy.wait()
    for copy in ga:
        arrive(copy)
    dk[...] = jnp.zeros_like(dk)
    dv[...] = jnp.zeros_like(dv)
    for j in range(4):
        rows_j = slice(j * 128, (j + 1) * 128)
        go[rows_j] = nn(gattn[j], w[:, 768:1152]).astype(BF)
        q, g = head_rows(qkv, j), head_rows(go, j)
        delta = jnp.sum(head_rows(att, j).astype(F32) * g.astype(F32), -1, keepdims=True)
        total = lse[j][:, :1]
        dq = jnp.zeros((384, 128), F32)
        for t in range(j + 1):
            keys = kvf[t].reshape(512, 256)
            s = nt(q, keys[:, :128]) * SCALE
            p = jnp.exp(s - total)
            if t == j:
                p = jnp.where(allowed(512), p, 0.0)
            gs = (p * (nt(g, keys[:, 128:]) - delta)).astype(BF)
            at = slice(t * 512, (t + 1) * 512)
            dv[at] += tn(p.astype(BF), g)
            dk[at] += tn(gs, q)
            dq = dq + nn(gs, keys[:, :128])
        dq = (dq * SCALE).astype(BF)
        for h in range(3):
            gqkv[rows_j, h * 128 : (h + 1) * 128] = dq[h * 128 : (h + 1) * 128]
    for j in range(4):
        for k in range(4):
            at = slice((j * 4 + k) * 128, (j * 4 + k + 1) * 128)
            dkvs[j, k, :, 0:128] = (dk[at] * SCALE).astype(BF)
            dkvs[j, k, :, 128:256] = dv[at].astype(BF)
    kvs = [
        cp.start(dkvs.at[:, p[0] * 2 + p[1]], dkvr.at[k], dev(y, *p, xh, z))
        for k, p in enumerate([(1 - xl, co), (1 - xl, 1 - co), (xl, 1 - co)])
    ]
    sent_o.update(sum_push(outp, tho, sibs, goy, gox, both[5:6]))
    rows = one_hot_rows()

    def expand(block, yy, cols):
        for k in range(4):
            part = tn(rows, block[k * 96 : (k + 1) * 96]).astype(BF)
            da[yy, k // 2, k % 2, :, :, :, cols] = part.reshape(2, 4, 16, -1)

    def dense_core(cols):
        return cp.start(da.at[:, :, 1 - co, :, :, :, cols], dath.at[:, :, :, :, :, cols], sib)

    def dense_z(copy, cols):
        arrive(copy)
        for a in range(4):
            for b in range(2):
                tot = da[a, b, co, :, :, :, cols].astype(F32) + dath[a, b, :, :, :, cols].astype(F32)
                da[a, b, co, :, :, :, cols] = tot.astype(BF)
        return [
            cp.start(da.at[:, :, co, :, (z + d) % 4, :, cols], zg.at[k, :, :, :, :, cols], p)
            for k, (d, p) in enumerate(zip(Y_STEPS, zpeers))
        ]

    def dense_far(copies, cols):
        for copy in copies:
            arrive(copy)
        for a in range(4):
            for b in range(2):
                tot = da[a, b, co, :, z, :, cols].astype(F32)
                for k in range(3):
                    tot = tot + zg[k, a, b, :, :, cols].astype(F32)
                for h in range(2):
                    zs[h, a, b, :, cols] = tot[h].astype(BF)
        return cp.start(zs.at[1 - xh, :, :, :, cols], xg.at[:, :, :, cols], xfar)

    def dense_near(copy, cols):
        arrive(copy)
        for a in range(4):
            for b in range(2):
                tot = zs[xh, a, b, :, cols].astype(F32) + xg[a, b, :, cols].astype(F32)
                s2[b, a, :, cols] = tot.astype(BF)
        return cp.start(s2.at[1 - xl, :, :, cols], xgot.at[:, :, cols], xpeer)

    def dense_y(copy, cols):
        arrive(copy)
        for a in range(4):
            s3[a, :, cols] = (s2[xl, a, :, cols].astype(F32) + xgot[a, :, cols].astype(F32)).astype(BF)
        aout[y, :, cols] = s3[y, :, cols]
        return [
            cp.start(s3.at[(y + d) % 4, :, cols], aout.at[y, :, cols], p) for d, p in zip(Y_STEPS, ypeers)
        ]

    head, tail = pl.ds(0, 768), pl.ds(768, 384)
    for yy in range(4):
        tile = slice(yy * 384, (yy + 1) * 384)
        block = tn(gattn[:, :, tile].reshape(512, 384), att[...])
        expand(block.astype(BF), yy, tail)
    tail_c = dense_core(tail)

    def expert_sums(e):
        for copy in ez[e]:
            arrive(copy)
        add_arrays((2, 96, 512), [eg.at[e, :, :, z], zb.at[0, e], zb.at[1, e], zb.at[2, e]], sb.at[e])
        return cp.start(sb.at[e, :, 1 - xh], xb.at[e], xfar)

    ex0 = expert_sums(0)
    tail_z = dense_z(tail_c, tail)
    bs = [cp.start(db.at[:, :, (z + d) % 4], bgot.at[k], p) for k, (d, p) in enumerate(zip(Y_STEPS, zpeers))]
    for copy in third:
        copy.wait()
    for copy in kvs:
        arrive(copy)
    gone(ga)
    gain_one_grad = jnp.zeros((1, 1536), F32)
    for j in range(4):
        rows_j = slice(j * 128, (j + 1) * 128)
        kv = dkvs[j, i].astype(F32)
        for k in range(3):
            kv = kv + dkvr[k, j].astype(F32)
        gqkv[rows_j, 384:640] = kv.astype(BF)
        gh1 = nt(gqkv[rows_j], w[:, :640])
        v = tokf[j].astype(F32)
        scaled = v * inverse_norm(v)
        gain_one_grad = gain_one_grad + jnp.sum(gh1 * scaled, 0, keepdims=True)
        gattn[j] = (scaled * gain_one).astype(BF)
        gh1s[j] = gh1.astype(BF)
    hs = [
        cp.start(gh1s.at[(y + d) % 4], gh1g.at[k], p) for k, (d, p) in enumerate(zip(Y_STEPS, ypeers))
    ]
    gain_rows = jnp.concatenate([gain_one_grad, gain_two_grad, jnp.zeros((6, 1536), F32)], 0)
    for yy in range(4):
        tile = slice(yy * 384, (yy + 1) * 384)
        block = tn(gattn[:, :, tile].reshape(512, 384), gqkv[...])
        expand(block.astype(BF), yy, pl.ds(0, 640))
        expand(tn(gain_rows[:, tile].astype(BF), eye_rows()).astype(BF), yy, pl.ds(640, 128))
    head_c = dense_core(head)
    head_z = dense_z(head_c, head)

    for copy in sent_o.values():
        arrive(copy)
    back_in = [here(goy, goty), here(gox, gotx)]
    for copy in back_in:
        copy.wait()
    gone(list(sent_o.values()))
    sum_second()
    last_o = sum_last(1)
    gh1 = gh1s[y].astype(F32)
    for k, copy in enumerate(hs):
        arrive(copy)
        gh1 = gh1 + gh1g[k].astype(F32)
    v = tokf[y].astype(F32)
    inv = inverse_norm(v)
    inner = gh1 * gain_one
    xh1 = v * inv
    igrad[...] = gres[...] + inv * (inner - xh1 * jnp.mean(inner * xh1, -1, keepdims=True))

    tail_x = dense_far(tail_z, tail)
    ex1 = expert_sums(1)
    bl.wait()
    for copy in bs:
        arrive(copy)
    for a in range(16):
        tot = bmine[a].astype(F32)
        for k in range(3):
            tot = tot + bgot[k, a].astype(F32)
        bz[0, a], bz[1, a] = tot[0].astype(BF), tot[1].astype(BF)
    bx = cp.start(bz.at[1 - xh], bxg, xfar)
    head_x = dense_far(head_z, head)
    lout[...] = (resid[...] + sum_end(1, last_o)).astype(BF)
    tail_n = dense_near(tail_x, tail)
    arrive(bx)
    for a in range(16):
        bsum[a] = (bz[xh, a].astype(F32) + bxg[a].astype(F32)).astype(BF)
    bo = [cp.start(bsum.at[p[0] * 4 + p[1] * 2 + p[2]], bout.at[c], q) for p, q in zip(places, cpeers)]
    bout[c] = bsum[c]
    head_n = dense_near(head_x, head)
    outs = dense_y(tail_n, tail) + dense_y(head_n, head)

    def expert_end(e, source, pair):
        for k in range(2):
            at = pair * 2 + e
            (eg_o, eu_o)[k][at] = source[k].astype(F32)
        ed_o[pair * 2 + e] = tn(source[2], eye(192, 192))

    for e, copy in enumerate((ex0, ex1)):
        own = here(sb.at[e, :, xh], esum)
        arrive(copy)
        other = here(xb.at[e], egot)
        own.wait()
        expert_end(e, esum, xh)
        other.wait()
        expert_end(e, egot, 1 - xh)

    for copy in outs + bo:
        arrive(copy)
    gain_sum = jnp.zeros((16, 128), F32)
    for k in range(4):
        wide, thin = slice(k * 384, (k + 1) * 384), slice(k * 128, (k + 1) * 128)
        block = aout[k, :, 0:768].astype(F32)
        wq_o[:, wide] = block[:12, 0:384]
        wk_o[:, thin] = block[:12, 384:512]
        wv_o[:, thin] = block[:12, 512:640]
        gain_sum = gain_sum + block[:, 640:768]
        wo_o[wide] = tn(aout[k, :, tail], eye(16, 12))
    gains_o[...] = gain_sum
    front_half = lax.broadcasted_iota(jnp.int32, (16, 128), 1) < 64
    for k in range(8):
        at = slice(k * 128, (k + 1) * 128)
        one, two = bout[2 * k].astype(F32), bout[2 * k + 1].astype(F32)
        sg_o[:, at] = jnp.where(front_half, one[:, :128], half_turn(two[:, :128]))[:12]
        su_o[:, at] = jnp.where(front_half, half_turn(one[:, :128]), two[:, :128])[:12]
        down = jnp.where(front_half, one[:, 128:], half_turn(two[:, 128:]))
        sd_o[at] = tn(down.astype(BF), eye(16, 12))
    for copy in cp.started:
        if not any(copy is r for r in sent_already):
            copy.wait_send()
        if not any(copy is r for r in got_already):
            copy.wait_recv()


def back(*ins):
    outs = (
        SDS((2, 4, 2, 2, 128, 1536), BF),
        SDS((3, 2, 3, 2, 192, 512), BF),
        SDS((2, 3, 2, 192, 512), BF),
        SDS((2, 3, 192, 512), BF),
        SDS((2, 4, 2, 128, 1536), BF),
        SDS((2, 4, 2, 128, 1536), BF),
        SDS((3, 2, 2, 64, 1536), BF),
        SDS((3, 4, 64, 1536), BF),
        SDS((128, 1536), BF),
        SDS((128, 1536), F32),
        SDS((16, 128), F32),
        SDS((12, 1536), F32),
        SDS((12, 512), F32),
        SDS((12, 512), F32),
        SDS((1536, 12), F32),
        SDS((12, 1024), F32),
        SDS((12, 1024), F32),
        SDS((1024, 12), F32),
        SDS((4, 192, 512), F32),
        SDS((4, 192, 512), F32),
        SDS((4, 512, 192), F32),
    )
    out = pl.pallas_call(
        back_kernel,
        out_shape=outs,
        in_specs=[ANY] * len(ins),
        out_specs=(ANY,) * 8 + (VM,) * 13,
        scratch_shapes=[
            pltpu.SemaphoreType.DMA((112,)),
            pltpu.SemaphoreType.DMA((112,)),
            pltpu.SemaphoreType.DMA((64,)),
            pltpu.VMEM((4, 2, 2, 64, 1536), BF),
            pltpu.VMEM((4, 4, 64, 1536), BF),
            pltpu.VMEM((2, 2, 2, 64, 1536), BF),
            pltpu.VMEM((2, 4, 64, 1536), BF),
            pltpu.VMEM((3, 2, 2, 64, 1536), BF),
            pltpu.VMEM((3, 4, 64, 1536), BF),
            pltpu.VMEM((2, 3, 64, 1536), BF),
            pltpu.VMEM((2, 3, 64, 1536), BF),
            pltpu.VMEM((128, 1536), F32),
            pltpu.VMEM((128, 1536), BF),
            pltpu.VMEM((128, 1536), F32),
            pltpu.VMEM((1536, 1152), BF),
            pltpu.VMEM((1536, 128), BF),
            pltpu.VMEM((4, 128, 1536), BF),
            pltpu.VMEM((512, 640), BF),
            pltpu.VMEM((4, 4, 128, 256), BF),
            pltpu.VMEM((4, 384, 128), F32),
            pltpu.VMEM((512, 384), BF),
            pltpu.VMEM((4, 128, 1536), BF),
            pltpu.VMEM((512, 384), BF),
            pltpu.VMEM((2048, 128), F32),
            pltpu.VMEM((2048, 128), F32),
            pltpu.VMEM((4, 4, 128, 256), BF),
            pltpu.VMEM((3, 4, 128, 256), BF),
            pltpu.VMEM((512, 640), BF),
            pltpu.VMEM((4, 128, 1536), BF),
            pltpu.VMEM((3, 128, 1536), BF),
            pltpu.VMEM((4, 2, 2, 2, 4, 16, 1152), BF),
            pltpu.VMEM((4, 2, 2, 4, 16, 1152), BF),
            pltpu.VMEM((3, 4, 2, 2, 16, 1152), BF),
            pltpu.VMEM((2, 4, 2, 16, 1152), BF),
            pltpu.VMEM((4, 2, 16, 1152), BF),
            pltpu.VMEM((2, 4, 16, 1152), BF),
            pltpu.VMEM((4, 16, 1152), BF),
            pltpu.VMEM((4, 16, 1152), BF),
            pltpu.VMEM((4, 16, 1152), BF),
            pltpu.VMEM((3, 16, 2, 16, 256), BF),
            pltpu.VMEM((16, 2, 16, 256), BF),
            pltpu.VMEM((2, 16, 16, 256), BF),
            pltpu.VMEM((16, 16, 256), BF),
            pltpu.VMEM((16, 16, 256), BF),
            pltpu.VMEM((16, 16, 256), BF),
            pltpu.VMEM((3, 192, 512), BF),
            pltpu.VMEM((3, 192, 512), BF),
        ],
        compiler_params=pltpu.CompilerParams(
            collective_id=2, has_side_effects=True, vmem_limit_bytes=62 * 2**20
        ),
        cost_estimate=pl.CostEstimate(flops=12 * 10**9, bytes_accessed=90 * 10**6, transcendentals=3 * 10**6),
    )(*ins)
    return out[8:]


def dispatch_kernel(pick_ref, h2_ref, x_ref):
    x_ref[...] = nn(pick_ref[0], h2_ref[...].reshape(256, 1536)).astype(BF).reshape(2, 1, 48, 1536)


def dispatch(pick, h2):
    return pl.pallas_call(
        dispatch_kernel,
        grid=(16,),
        out_shape=SDS((2, 16, 48, 1536), BF),
        in_specs=[
            pl.BlockSpec((1, 96, 256), lambda p: (p, 0, 0)),
            pl.BlockSpec((2, 128, 1536), lambda p: (p, 0, 0)),
        ],
        out_specs=pl.BlockSpec((2, 1, 48, 1536), lambda p: (0, p, 0, 0)),
        compiler_params=pltpu.CompilerParams(vmem_limit_bytes=VMEM_LIMIT),
        cost_estimate=pl.CostEstimate(flops=2 * 10**9, bytes_accessed=18 * 10**6, transcendentals=0),
    )(pick, h2)


def expert_kernel(x_ref, gy_ref, w, y_ref, gr_ref, dw, u_s, ga_s, gb_s):
    for t in range(2):
        cols = slice(t * 256, (t + 1) * 256)
        a = nn(x_ref[0], w[0, 0, :, cols])
        b = nn(x_ref[0], w[0, 1, :, cols])
        gu = nn(gy_ref[0], w[0, 2, :, cols])
        act, slope = silu_parts(a)
        u_s[:, cols] = (act * b).astype(BF)
        ga_s[:, cols] = (gu * b * slope).astype(BF)
        gb_s[:, cols] = (gu * act).astype(BF)

    def tile(t, carry):
        at = pl.ds(pl.multiple_of(t * 256, 256), 256)
        y_ref[0, :, at] = nt(u_s[...], w[0, 2, at, :]).astype(BF)
        gr_ref[0, :, at] = (nt(ga_s[...], w[0, 0, at, :]) + nt(gb_s[...], w[0, 1, at, :])).astype(BF)
        dw[0, 0, at, :] = tn(x_ref[0, :, at], ga_s[...]).astype(BF)
        dw[0, 1, at, :] = tn(x_ref[0, :, at], gb_s[...]).astype(BF)
        dw[0, 2, at, :] = tn(gy_ref[0, :, at], u_s[...]).astype(BF)
        return carry

    lax.fori_loop(0, 6, tile, 0)


def expert(x, gy, weights):
    rows = pl.BlockSpec((1, 768, 1536), lambda e: (e, 0, 0))
    whole = pl.BlockSpec((1, 3, 1536, 512), lambda e: (e, 0, 0, 0))
    return pl.pallas_call(
        expert_kernel,
        grid=(2,),
        out_shape=(SDS((2, 768, 1536), BF),) * 2 + (SDS((2, 3, 1536, 512), BF),),
        in_specs=[rows, rows, whole],
        out_specs=(rows, rows, whole),
        scratch_shapes=[pltpu.VMEM((768, 512), BF)] * 3,
        compiler_params=pltpu.CompilerParams(vmem_limit_bytes=VMEM_LIMIT),
        cost_estimate=pl.CostEstimate(flops=22 * 10**9, bytes_accessed=60 * 10**6, transcendentals=10**6),
    )(x, gy, weights)


def combine_kernel(xh_ref, pick_ref, gr_ref, h2_ref, cot_ref, sw_ref, gh_ref, hid_ref, db_ref, ds_ref):
    p = pl.program_id(0)

    @pl.when(p == 0)
    def _():
        ds_ref[...] = jnp.zeros_like(ds_ref)

    gh = tn(pick_ref[0], gr_ref[...].reshape(96, 1536))
    own = p // 8 == xh_ref[0]

    @pl.when(jnp.logical_not(own))
    def _():
        gh_ref[...] = gh.astype(BF).reshape(2, 128, 1536)

    @pl.when(own)
    def _():
        h2 = h2_ref[...].reshape(256, 1536)
        cot = cot_ref[...].reshape(256, 1536)
        pre = nn(h2, sw_ref[:, 0:128])
        gz = nn(cot, sw_ref[:, 128:256])
        act, slope = silu_parts(pre)
        up = half_turn(pre)
        lane = lax.broadcasted_iota(jnp.int32, (256, 128), 1)
        hid = jnp.where(lane < 64, act * up, 0.0).astype(BF)
        gcd = jnp.where(lane < 64, gz * up * slope, half_turn(gz * act)).astype(BF)
        gh_ref[...] = (gh + nt(gcd, sw_ref[:, 0:128])).astype(BF).reshape(2, 128, 1536)
        hid_ref[0] = hid
        ds_ref[:, 0:128] += tn(h2, gcd)
        ds_ref[:, 128:256] += tn(cot, hid)

    @pl.when(p == 15)
    def _():
        rows = one_hot_rows()
        for k in range(16):
            block = ds_ref[k * 96 : (k + 1) * 96].astype(BF)
            db_ref[k] = tn(rows, block).astype(BF).reshape(2, 4, 16, 256)


def combine(pick, gr, h2, cot, sw):
    xh = (lax.axis_index("fsdp") // 4).reshape(1).astype(jnp.int32)

    def own(p, xh):
        return jnp.minimum(jnp.maximum(p - xh[0] * 8, 0), 7)

    own_rows = pl.BlockSpec((2, 128, 1536), lambda p, xh: (xh[0] * 8 + own(p, xh), 0, 0))
    return pl.pallas_call(
        combine_kernel,
        grid_spec=pltpu.PrefetchScalarGridSpec(
            num_scalar_prefetch=1,
            grid=(16,),
            in_specs=[
                pl.BlockSpec((1, 96, 256), lambda p, xh: (p, 0, 0)),
                pl.BlockSpec((2, 1, 48, 1536), lambda p, xh: (0, p, 0, 0)),
                own_rows,
                own_rows,
                pl.BlockSpec((1536, 256), lambda p, xh: (0, 0)),
            ],
            out_specs=(
                pl.BlockSpec((2, 128, 1536), lambda p, xh: (p, 0, 0)),
                pl.BlockSpec((1, 256, 128), lambda p, xh: (own(p, xh), 0, 0)),
                pl.BlockSpec((16, 2, 4, 16, 256), lambda p, xh: (0, 0, 0, 0, 0)),
            ),
            scratch_shapes=[pltpu.VMEM((1536, 256), F32)],
        ),
        out_shape=(SDS((32, 128, 1536), BF), SDS((8, 256, 128), BF), SDS((16, 2, 4, 16, 256), BF)),
        compiler_params=pltpu.CompilerParams(vmem_limit_bytes=VMEM_LIMIT),
        cost_estimate=pl.CostEstimate(flops=6 * 10**9, bytes_accessed=40 * 10**6, transcendentals=10**6),
    )(xh, pick, gr, h2, cot, sw)


def local(
    tokens,
    cotangent,
    routes,
    gates,
    attn_gain,
    ffn_gain,
    w_query,
    w_key,
    w_value,
    w_out,
    shared_gate,
    shared_up,
    shared_down,
    expert_gate,
    expert_up,
    expert_down,
):
    tok = tokens.reshape(128, 1536)
    cot = cotangent.reshape(128, 1536)
    gains = jnp.pad(jnp.stack([attn_gain, ffn_gain], 1), ((0, 4), (0, 126)))
    (cot_f, h2_f, wexp, tok_f, kv_f, gy, pick, gated, _, w, sw, qkv, att, lse, resid) = front(
        tok,
        cot,
        routes,
        gates,
        gains,
        w_query,
        w_key,
        w_value,
        w_out,
        shared_gate,
        shared_up,
        shared_down,
        expert_gate,
        expert_up,
        expert_down,
    )
    h2_f, cot_f = h2_f.reshape(32, 128, 1536), cot_f.reshape(32, 128, 1536)
    x = dispatch(pick, h2_f)
    y, gr, eg = expert(
        x.reshape(2, 768, 1536), gy.reshape(2, 768, 1536), wexp.reshape(2, 3, 1536, 512)
    )
    gh2_p, hid, db = combine(pick, gr.reshape(2, 16, 48, 1536), h2_f, cot_f, sw)
    layer_out, input_grad, gain_grads, *weight_grads = back(
        gh2_p.reshape(2, 4, 2, 2, 128, 1536),
        eg.reshape(2, 3, 2, 4, 192, 512),
        y.reshape(2, 2, 8, 48, 1536),
        gated.reshape(2, 8, 96, 256),
        hid,
        resid,
        cot,
        w,
        sw,
        tok_f,
        qkv,
        kv_f,
        lse,
        att,
        db,
    )
    return (
        layer_out.reshape(1, 128, 1536),
        input_grad.reshape(1, 128, 1536),
        gain_grads[:12, 0],
        gain_grads[:12, 1],
        *weight_grads,
    )


def solution(mesh):
    both = ("ctx", "fsdp")
    rows = P("fsdp", "ctx", None)
    weights = (P(both),) * 2 + (P(both, None),) * 3 + (P(None, both),)
    weights = weights + (P(both, None),) * 2 + (P(None, both),)
    weights = weights + (P("ctx", "fsdp", None),) * 2 + (P("ctx", None, "fsdp"),)
    return jax.shard_map(
        local, mesh=mesh, in_specs=(rows,) * 4 + weights, out_specs=(rows,) * 2 + weights, check_vma=False
    )
```

```python
import jax
import jax.numpy as jnp
from jax import lax
from jax.experimental import pallas as pl
from jax.experimental.pallas import tpu as pltpu
from jax.sharding import PartitionSpec as P

BF = jnp.bfloat16
F32 = jnp.float32
EPS = 1e-05
MESH = pl.DeviceIdType.MESH
ANY = pl.BlockSpec(memory_space=pl.ANY)
VM = pl.BlockSpec(memory_space=pltpu.VMEM)
SDS = jax.ShapeDtypeStruct
SCALE = 128 ** (-0.5)
VMEM_LIMIT = 56 * 2**20


def div(x, n):
    return lax.div(x, lax.full_like(x, n))


def rem(x, n):
    return lax.rem(x, lax.full_like(x, n))


def nn(a, b):
    return lax.dot_general(a, b, (((1,), (0,)), ((), ())), preferred_element_type=F32)


def nt(a, b):
    return lax.dot_general(a, b, (((1,), (1,)), ((), ())), preferred_element_type=F32)


def tn(a, b):
    return lax.dot_general(a, b, (((0,), (0,)), ((), ())), preferred_element_type=F32)


def silu_parts(pre_act):
    sig = 1.0 / (1.0 + jnp.exp(-pre_act))
    return pre_act * sig, sig * (1.0 + pre_act * (1.0 - sig))


def coords():
    c = lax.axis_index("ctx")
    f = lax.axis_index("fsdp")
    return c // 4, (c // 2) % 2, c % 2, f // 4, f % 4


def dev(y, xl, co, xh, z):
    return (y * 4 + xl * 2 + co, xh * 4 + z)


def barrier(peers):
    sem = pltpu.get_barrier_semaphore()
    for peer in peers:
        pl.semaphore_signal(sem, inc=1, device_id=peer, device_id_type=MESH)
    pl.semaphore_wait(sem, len(peers))


class Copies:
    def __init__(self, send, recv):
        self.send, self.recv, self.n, self.started = send, recv, 0, []

    def start(self, src, dst, peer):
        copy = pltpu.make_async_remote_copy(
            src, dst, self.send.at[self.n], self.recv.at[self.n], device_id=peer, device_id_type=MESH
        )
        copy.start()
        self.n += 1
        self.started.append(copy)
        return copy

    def finish(self, received=()):
        for copy in self.started:
            copy.wait_send()
            if not any(copy is r for r in received):
                copy.wait_recv()


Y_STEPS = (1, 2, 3)


def one_hot_rows():
    row = lax.broadcasted_iota(jnp.int32, (96, 128), 0)
    col = lax.broadcasted_iota(jnp.int32, (96, 128), 1)
    return jnp.where(div(row, 12) * 16 + rem(row, 12) == col, 1.0, 0.0).astype(BF)


def eye_rows():
    row = lax.broadcasted_iota(jnp.int32, (8, 128), 0)
    col = lax.broadcasted_iota(jnp.int32, (8, 128), 1)
    return jnp.where(row == col, 1.0, 0.0).astype(BF)


def inverse_norm(values):
    return lax.rsqrt(jnp.mean(values * values, -1, keepdims=True) + EPS)


def head_rows(ref, j, first=0):
    rows = slice(j * 128, (j + 1) * 128)
    return jnp.concatenate([ref[rows, first + h * 128 : first + (h + 1) * 128] for h in range(3)], 0)


def allowed(n):
    i = rem(lax.axis_index("ctx"), 4)
    row = rem(lax.broadcasted_iota(jnp.int32, (384, n), 0), 128)
    col = lax.broadcasted_iota(jnp.int32, (384, n), 1)
    return col <= i * 128 + row


def ctx_places(y, xl, co):
    return [
        ((y + dy) % 4, (xl + dx) % 2, (co + dc) % 2)
        for dy in range(4)
        for dx in (0, 1)
        for dc in (0, 1)
        if (dy, dx, dc) != (0, 0, 0)
    ]


def x_place(xh, xl, d):
    x = (xh * 2 + xl + d) % 4
    return x // 2, x % 2


def plane_gather(cp, arrive, src, out, places, sib, split):
    y, xl, co, xh, z = places
    low, high = pl.ds(0, split), pl.ds(split, 128 - split)
    ypeers = [dev((y + d) % 4, xl, co, xh, z) for d in Y_STEPS]
    xpeers = []
    for d in Y_STEPS:
        h, l = x_place(xh, xl, d)
        xpeers.append(dev(y, l, co, h, z))
    mine = (xh, y, xl, co)

    def first_y():
        return [cp.start(src.at[high], out.at[mine + (high,)], p) for p in ypeers]

    def first_x():
        return [cp.start(src.at[low], out.at[mine + (low,)], p) for p in xpeers]

    def then_y(firsts):
        for copy in firsts:
            arrive(copy)
        piece = out.at[:, y, :, co, low]
        return [cp.start(piece, piece, p) for p in ypeers] + [cp.start(piece, piece, sib)]

    def then_x(firsts):
        for copy in firsts:
            arrive(copy)
        piece = out.at[xh, :, xl, co, high]
        return [cp.start(piece, piece, p) for p in xpeers] + [cp.start(piece, piece, sib)]

    def last_y(seconds):
        sent = []
        for d, copy in zip(Y_STEPS, seconds):
            arrive(copy)
            piece = out.at[:, (y + 4 - d) % 4, :, co, low]
            sent.append(cp.start(piece, piece, sib))
        return sent

    def last_x(seconds):
        sent = []
        for d, copy in zip(Y_STEPS, seconds):
            arrive(copy)
            h, l = x_place(xh, xl, 4 - d)
            piece = out.at[h, :, l, co, high]
            sent.append(cp.start(piece, piece, sib))
        return sent

    return first_y, first_x, then_y, then_x, last_y, last_x


def dispatch_rows(rg, first):
    masks, gates = [], []
    for e in range(2):
        ms, gs = [], []
        for s in range(2):
            hit = jnp.where(rg[s, 0:6] == (first + e).astype(F32), 1.0, 0.0)
            ms.append(jnp.sum(hit, 0, keepdims=True))
            gs.append(jnp.sum(hit * rg[s, 8:14], 0, keepdims=True))
        masks.append(jnp.concatenate(ms, 1))
        gates.append(jnp.concatenate(gs, 1))
    mask = jnp.concatenate(masks + [jnp.zeros((6, 256), F32)], 0)
    before = lax.broadcasted_iota(jnp.int32, (256, 256), 0)
    after = lax.broadcasted_iota(jnp.int32, (256, 256), 1)
    tri = jnp.where((before <= after) & (before // 128 == after // 128), 1.0, 0.0).astype(BF)
    place = nn(mask.astype(BF), tri) - 1.0
    lane = lax.broadcasted_iota(jnp.int32, (1, 256), 1)
    slot = lax.broadcasted_iota(jnp.int32, (48, 256), 0).astype(F32)
    picks, gated = [], []
    for e in range(2):
        at = place[e : e + 1] + jnp.where(lane >= 128, 24.0, 0.0)
        at = jnp.where(masks[e] > 0.0, at, -1.0)
        hit = jnp.where(slot == at, 1.0, 0.0)
        picks.append(hit)
        gated.append(hit * gates[e])
    return jnp.concatenate(picks, 0).astype(BF), jnp.concatenate(gated, 0).astype(BF)


def eye(rows, cols):
    row = lax.broadcasted_iota(jnp.int32, (rows, cols), 0)
    col = lax.broadcasted_iota(jnp.int32, (rows, cols), 1)
    return jnp.where(row == col, 1.0, 0.0).astype(BF)


def half_turn(x):
    return pltpu.roll(x, 64, 1)


def front_kernel(
    tok, cot, routes, gates, gains_in, wq, wk, wv, wo, sg, su, sd, eg, eu, ed,
    cotf, h2f, wexp, tokf_o, kvf_o, gy, pick_o, gated_o, rgf,
    w, sw, qkv, att, lse, resid,
    send, recv, loc, a_s, b_s, own, rg_s, a2, wf, b1, bf, tokf, kvf, s_s, part, got, h2,
):
    y, xl, co, xh, z = coords()
    i, c, f = xl * 2 + co, y * 4 + xl * 2 + co, xh * 4 + z
    f_far = (1 - xh) * 4 + z
    sib = dev(y, xl, 1 - co, xh, z)
    xpeer = dev(y, 1 - xl, co, xh, z)
    xfar = dev(y, xl, co, 1 - xh, z)
    ypeers = [dev((y + d) % 4, xl, co, xh, z) for d in Y_STEPS]
    zpeers = [dev(y, xl, co, xh, (z + d) % 4) for d in Y_STEPS]
    places = ctx_places(y, xl, co)
    cpeers = [dev(*p, xh, z) for p in places]
    plane = cpeers + [dev(*p, 1 - xh, z) for p in places + [(y, xl, co)]]
    peers = plane + zpeers
    sem = pltpu.get_barrier_semaphore()
    for peer in peers:
        pl.semaphore_signal(sem, inc=1, device_id=peer, device_id_type=MESH)

    e16 = eye(16, 12)
    q16, k16, v16 = (nn(e16, ref[...]).astype(BF) for ref in (wq, wk, wv))
    o16 = nn(e16, wo[...]).astype(BF)
    gain_rows = nn(eye(128, 2), gains_in[...]).astype(BF)
    gain16 = nt(e16, gain_rows).astype(BF)
    for k in range(4):
        wide, thin = slice(k * 384, (k + 1) * 384), slice(k * 128, (k + 1) * 128)
        a_s[k] = jnp.concatenate([q16[:, wide], k16[:, thin], v16[:, thin], gain16, o16[:, wide]], 1)
    g16, u16, d16 = nn(e16, sg[...]), nn(e16, su[...]), nn(e16, sd[...])
    front_half = lax.broadcasted_iota(jnp.int32, (16, 128), 1) < 64
    for k in range(8):
        at = slice(k * 128, (k + 1) * 128)
        g, u, d = g16[:, at], u16[:, at], d16[:, at]
        for n in range(2):
            if n:
                g, d = half_turn(g), half_turn(d)
            else:
                u = half_turn(u)
            b_s[2 * k + n, :, 0:128] = jnp.where(front_half, g, u).astype(BF)
            b_s[2 * k + n, :, 128:256] = jnp.where(front_half, d, 0.0).astype(BF)
            if not n:
                u = half_turn(u)
    for e in range(4):
        own[e, 0] = eg[e]
        own[e, 1] = eu[e]
        own[e, 2] = ed[e]
    rg_s[...] = jnp.zeros_like(rg_s)
    for k in range(6):
        rg_s[k : k + 1] = routes[k].astype(F32)
        rg_s[8 + k : 9 + k] = gates[k]
    pl.semaphore_wait(sem, len(peers))

    cp = Copies(send, recv)
    n_local = [0]

    def here(src, dst):
        copy = pltpu.make_async_copy(src, dst, loc.at[n_local[0]])
        n_local[0] += 1
        copy.start()
        return copy

    got_already = []

    def arrive(copy):
        copy.wait_recv()
        got_already.append(copy)

    me = (y, xl, co, xh, z)
    ya = [cp.start(a_s.at[(y + d) % 4], a2.at[y, xl], p) for d, p in zip(Y_STEPS, ypeers)]
    la = here(a_s.at[y], a2.at[y, xl])
    lb = here(b_s.at[c], b1.at[c])
    lt = here(tok, tokf.at[y])
    lr = here(rg_s, rgf.at[xh, c])
    later = [here(own.at[pl.ds(xh * 2, 2)], wexp.at[:, :, f])]
    own_cot = here(cot, cotf.at[xh, y, xl, co])
    cot_y, cot_x, cot_then_y, cot_then_x, cot_last_y, cot_last_x = plane_gather(
        cp, arrive, cot, cotf, me, sib, 64
    )
    yt = [cp.start(tok, tokf.at[y], p) for p in ypeers]
    cy = cot_y()
    la.wait()
    for copy in ya:
        arrive(copy)
    xa = cp.start(a2.at[:, xl], a2.at[:, xl], xpeer)
    bs = [cp.start(b_s.at[p[0] * 4 + p[1] * 2 + p[2]], b1.at[c], q) for p, q in zip(places, cpeers)]
    rgs = [cp.start(rg_s, rgf.at[xh, c], q) for q in plane]
    arrive(xa)

    head, tail = pl.ds(0, 768), pl.ds(768, 384)

    def slices(cols):
        return a2.at[:, :, :, cols], wf.at[:, :, co, f, :, cols], wf.at[:, :, co, f_far, :, cols]

    src, mine, far = slices(head)
    hx = cp.start(src, mine, xfar)
    hz = [cp.start(src, mine, p) for p in zpeers]
    lw = here(a2, wf.at[:, :, co, f])
    cx = cot_x()
    src_t, mine_t, far_t = slices(tail)
    tx = cp.start(src_t, mine_t, xfar)
    ex = [cp.start(own.at[2 - xh * 2], wexp.at[0, :, f], xfar)]
    lw.wait()
    to_sib = [cp.start(mine, mine, sib)]
    arrive(hx)
    hz2 = [cp.start(far, far, p) for p in zpeers]
    to_sib.append(cp.start(far, far, sib))
    tz = [cp.start(src_t, mine_t, p) for p in zpeers]
    for copies, h in ((hz, xh), (hz2, 1 - xh)):
        for d, copy in zip(Y_STEPS, copies):
            arrive(copy)
            piece = wf.at[:, :, co, h * 4 + (z + 4 - d) % 4, :, head]
            to_sib.append(cp.start(piece, piece, sib))
    own_cot.wait()
    cy2 = cot_then_y(cx)
    arrive(tx)
    tz2 = [cp.start(far_t, far_t, p) for p in zpeers]
    tail_sib = [cp.start(mine_t, mine_t, sib), cp.start(far_t, far_t, sib)]
    for p in zpeers:
        cp.start(own.at[pl.ds(xh * 2, 2)], wexp.at[:, :, f], p)
    for copy in to_sib:
        arrive(copy)
    rows = one_hot_rows()

    def compact(cols):
        for yy in range(4):
            for k in range(4):
                at = (yy * 4 + k) * 96
                block = wf[yy, k // 2, k % 2, :, :, cols].reshape(128, -1)
                w[at : at + 96, cols] = nn(rows, block).astype(BF)

    compact(slice(0, 768))
    gains = nt(eye_rows(), w[:, 640:768])
    gain_one, gain_two = gains[0:1], gains[1:2]

    lt.wait()
    for copy in yt:
        arrive(copy)
    for j in range(4):
        v = tokf[j].astype(F32)
        rows_j = slice(j * 128, (j + 1) * 128)
        h1 = (v * inverse_norm(v) * gain_one).astype(BF)
        qkv_j = nn(h1, w[:, :640]).astype(BF)
        qkv[rows_j] = qkv_j
        kvf[j, i] = qkv_j[:, 384:]
    kx = cp.start(kvf.at[:, i], kvf.at[:, i], xpeer)
    ks = [cp.start(kvf.at[:, i], kvf.at[:, i], sib)]
    saved = [here(tokf, tokf_o)]
    for copies, h in ((tz, xh), (tz2, 1 - xh)):
        for d, copy in zip(Y_STEPS, copies):
            arrive(copy)
            piece = wf.at[:, :, co, h * 4 + (z + 4 - d) % 4, :, tail]
            tail_sib.append(cp.start(piece, piece, sib))
    arrive(kx)
    piece = kvf.at[:, (1 - xl) * 2 + co]
    ks.append(cp.start(piece, piece, sib))
    ex.append(cp.start(own.at[3 - xh * 2], wexp.at[1, :, f], xfar))
    cx2 = cot_then_x(cy)
    for copy in ks:
        arrive(copy)
    saved.append(here(kvf, kvf_o))

    for j in range(4):
        n = (j + 1) * 512
        q = head_rows(qkv, j)
        for t in range(j + 1):
            s = nt(q, kvf[t].reshape(512, 256)[:, :128]) * SCALE
            if t == j:
                s = jnp.where(allowed(512), s, -1e30)
            s_s[:, t * 512 : (t + 1) * 512] = s
        s = s_s[:, :n]
        m = jnp.max(s, -1, keepdims=True)
        p = jnp.exp(s - m)
        total = jnp.sum(p, -1, keepdims=True)
        o = nn(p.astype(BF), kvf[0 : j + 1].reshape(n, 256)[:, 128:]) / total
        rows_j = slice(j * 128, (j + 1) * 128)
        for h in range(3):
            att[rows_j, h * 128 : (h + 1) * 128] = o[h * 128 : (h + 1) * 128].astype(BF)
        lse[j] = jnp.broadcast_to(m + jnp.log(total), (384, 128))
    for copy in tail_sib:
        arrive(copy)
    compact(slice(768, 1152))
    for j in range(4):
        part[j] = nt(att[j * 128 : (j + 1) * 128], w[:, 768:1152]).astype(BF)
    ps = [
        cp.start(part.at[(y + d) % 4], got.at[k], p) for k, (d, p) in enumerate(zip(Y_STEPS, ypeers))
    ]
    far_rows = wexp.at[0, :, f_far]
    arrive(ex[0])
    for p in zpeers:
        cp.start(far_rows, far_rows, p)
    total = tokf[y].astype(F32) + part[y].astype(F32)
    for k, copy in enumerate(ps):
        arrive(copy)
        total = total + got[k].astype(F32)
    resid[...] = total
    h2[...] = (total * inverse_norm(total) * gain_two).astype(BF)
    h2_y, h2_x, h2_then_y, h2_then_x, h2_last_y, h2_last_x = plane_gather(
        cp, arrive, h2, h2f, me, sib, 80
    )
    hx = h2_x()
    hy = h2_y()
    own_h2 = here(h2, h2f.at[xh, y, xl, co])

    cot_sib = [cy2[3], cx2[3]] + cot_last_y(cy2[:3])
    own_h2.wait()
    hy2 = h2_then_y(hx)
    hx2 = h2_then_x(hy)
    far_rows_1 = wexp.at[1, :, f_far]
    arrive(ex[1])
    for p in zpeers:
        cp.start(far_rows_1, far_rows_1, p)
    lb.wait()
    for copy in bs:
        arrive(copy)
    bx = cp.start(b1, bf.at[:, f], xfar)
    bz = [cp.start(b1, bf.at[:, f], p) for p in zpeers]
    lb = here(b1, bf.at[:, f])
    lr.wait()
    for copy in rgs:
        arrive(copy)
    arrive(bx)
    bz += [cp.start(bf.at[:, f_far], bf.at[:, f_far], p) for p in zpeers]
    cot_sib += cot_last_x(cx2[:3])
    for copy in cot_sib:
        arrive(copy)

    first = c * 4 + xh * 2

    def gated_rows(rg_ref, cot_ref, gy_ref, pick_ref, gated_ref):
        pick, gated = dispatch_rows(rg_ref.reshape(2, 16, 128), first)
        gy_ref[...] = nn(gated, cot_ref[...].reshape(256, 1536)).astype(BF).reshape(2, 1, 48, 1536)
        pick_ref[0], gated_ref[0] = pick, gated

    picks = pl.BlockSpec((1, 96, 256), lambda p: (p, 0, 0))
    pltpu.emit_pipeline(
        gated_rows,
        grid=(16,),
        in_specs=[
            pl.BlockSpec((1, 2, 16, 128), lambda p: (p // 8, p % 8, 0, 0)),
            pl.BlockSpec((1, 1, 1, 2, 128, 1536), lambda p: (p // 8, p // 2 % 4, p % 2, 0, 0, 0)),
        ],
        out_specs=[pl.BlockSpec((2, 1, 48, 1536), lambda p: (0, p, 0, 0)), picks, picks],
    )(rgf, cotf, gy, pick_o, gated_o)
    lb.wait()
    for copy in bz:
        arrive(copy)
    for k in range(16):
        sw[k * 96 : (k + 1) * 96] = nn(rows, bf[k].reshape(128, 256)).astype(BF)
    h2_last_y(hy2[:3])
    h2_last_x(hx2[:3])
    for copy in later + saved:
        copy.wait()
    cp.finish(got_already)


def front(*ins):
    outs = (
        SDS((2, 4, 2, 2, 128, 1536), BF),
        SDS((2, 4, 2, 2, 128, 1536), BF),
        SDS((2, 3, 8, 192, 512), BF),
        SDS((4, 128, 1536), BF),
        SDS((4, 4, 128, 256), BF),
        SDS((2, 16, 48, 1536), BF),
        SDS((16, 96, 256), BF),
        SDS((16, 96, 256), BF),
        SDS((2, 16, 16, 128), F32),
        SDS((1536, 1152), BF),
        SDS((1536, 256), BF),
        SDS((512, 640), BF),
        SDS((512, 384), BF),
        SDS((4, 384, 128), F32),
        SDS((128, 1536), F32),
    )
    return pl.pallas_call(
        front_kernel,
        out_shape=outs,
        in_specs=[ANY] * 2 + [VM] * (len(ins) - 2),
        out_specs=(ANY,) * 9 + (VM,) * 6,
        scratch_shapes=[
            pltpu.SemaphoreType.DMA((160,)),
            pltpu.SemaphoreType.DMA((160,)),
            pltpu.SemaphoreType.DMA((16,)),
            pltpu.VMEM((4, 16, 1152), BF),
            pltpu.VMEM((16, 16, 256), BF),
            pltpu.VMEM((4, 3, 192, 512), BF),
            pltpu.VMEM((16, 128), F32),
            pltpu.VMEM((4, 2, 16, 1152), BF),
            pltpu.VMEM((4, 2, 2, 8, 16, 1152), BF),
            pltpu.VMEM((16, 16, 256), BF),
            pltpu.VMEM((16, 8, 16, 256), BF),
            pltpu.VMEM((4, 128, 1536), BF),
            pltpu.VMEM((4, 4, 128, 256), BF),
            pltpu.VMEM((384, 2048), F32),
            pltpu.VMEM((4, 128, 1536), BF),
            pltpu.VMEM((3, 128, 1536), BF),
            pltpu.VMEM((128, 1536), BF),
        ],
        compiler_params=pltpu.CompilerParams(
            collective_id=1, has_side_effects=True, vmem_limit_bytes=VMEM_LIMIT
        ),
        cost_estimate=pl.CostEstimate(flops=6 * 10**9, bytes_accessed=60 * 10**6, transcendentals=3 * 10**6),
    )(*ins)


def add_blocks(*refs):
    total = refs[0][...].astype(F32)
    for ref in refs[1:-1]:
        total = total + ref[...].astype(F32)
    refs[-1][...] = total.astype(refs[-1].dtype)


def add_arrays(block, ins, out):
    spec = pl.BlockSpec((1,) + block, lambda m, r: (m, 0, r, 0))
    pltpu.emit_pipeline(add_blocks, grid=(3, 2), in_specs=[spec] * len(ins), out_specs=[spec])(*ins, out)


def back_kernel(
    pick_in, gated_in, gy_in, wexp, h2f, cotf, resid_i, cot_i, w_i, sw_i, tokf_i, qkv_i, kvf_i, lse_i, att_i,
    eg, y_b, hid_b, gh2p, outp, zb, sb, xb, thg, tho, goy, gox, aout, bout,
    lout, igrad,
    send, recv, loc, goty, gotx, gety, getx, resid, cot, gres, gattn, dkvr, gh1g, dath, zg, xg, xgot, bgot, bxg,
    sw, db,
):
    y, xl, co, xh, z = coords()
    i, c = xl * 2 + co, y * 4 + xl * 2 + co
    sib = dev(y, xl, 1 - co, xh, z)
    xpeer = dev(y, 1 - xl, co, xh, z)
    xfar = dev(y, xl, co, 1 - xh, z)
    ypeers = [dev((y + d) % 4, xl, co, xh, z) for d in Y_STEPS]
    zpeers = [dev(y, xl, co, xh, (z + d) % 4) for d in Y_STEPS]
    places = ctx_places(y, xl, co)
    cpeers = [dev(*p, xh, z) for p in places]
    xpeers = []
    for d in Y_STEPS:
        hh, ll = x_place(xh, xl, d)
        xpeers.append(dev(y, ll, co, hh, z))
    barrier(cpeers + [dev(y, k, co, 1 - xh, z) for k in range(2)] + zpeers)
    cp = Copies(send, recv)
    n_local = [0]

    def here(src, dst):
        copy = pltpu.make_async_copy(src, dst, loc.at[n_local[0]])
        n_local[0] += 1
        copy.start()
        return copy

    got_already, sent_already = [], []

    def arrive(copy):
        copy.wait_recv()
        got_already.append(copy)

    def gone(copies):
        for copy in copies:
            copy.wait_send()
            sent_already.append(copy)

    low, high = pl.ds(0, 64), pl.ds(64, 64)
    ynext, znext = [(y + d) % 4 for d in range(4)], [(z + d) % 4 for d in range(4)]
    xnext = [x_place(xh, xl, d) for d in range(4)]
    oco, oxl, oxh = 1 - co, 1 - xl, 1 - xh
    xh8, oxh8 = xh * 8, 8 - xh * 8
    place_index = [p[0] * 4 + p[1] * 2 + p[2] for p in places]
    kv_peers = [(a * 2 + b, dev(y, a, b, xh, z)) for a, b in ((oxl, co), (oxl, oco), (xl, oco))]
    first = [here(sw_i, sw), here(resid_i, resid), here(cot_i, cot)]
    pairs = pl.BlockSpec((1, 1, 2, 128, 1536), lambda p: (div(p, 2), rem(p, 2), 0, 0, 0))
    picks = pl.BlockSpec((1, 96, 256), lambda p: (p, 0, 0))

    def expert_copies(e):
        return [
            pltpu.make_async_remote_copy(
                eg.at[e, :, :, znext[d]],
                zb.at[k, e],
                send.at[e * 3 + k],
                recv.at[e * 3 + k],
                device_id=zpeers[k],
                device_id_type=MESH,
            )
            for k, d in enumerate(Y_STEPS)
        ]

    def expert_push(e):
        for copy in expert_copies(e):
            copy.start()

    cp.n = 6

    def experts(xy, gg):
        lg = here(gy_in, gg)

        def work(w, dw, u_s, ga_s, gb_s):
            lw = [here(wexp.at[e], w.at[e]) for e in range(2)]

            def rows_in(pick_ref, h2_ref):
                p = pl.program_id(0)
                x = nn(pick_ref[0], h2_ref[...].reshape(256, 1536)).astype(BF)
                xy[:, p] = x.reshape(2, 48, 1536)

            pltpu.emit_pipeline(
                rows_in,
                grid=(16,),
                in_specs=[
                    picks,
                    pl.BlockSpec((1, 1, 1, 2, 128, 1536), lambda p: (div(p, 8), rem(div(p, 2), 4), rem(p, 2), 0, 0, 0)),
                ],
            )(pick_in, h2f)
            lg.wait()
            copies = []
            for e in range(2):
                lw[e].wait()
                for t in range(2):
                    cols = slice(t * 256, (t + 1) * 256)
                    x, g = xy[e].reshape(768, 1536), gg[e].reshape(768, 1536)
                    a = nn(x, w[e, 0, :, :, cols].reshape(1536, 256))
                    b = nn(x, w[e, 1, :, :, cols].reshape(1536, 256))
                    gu = nn(g, w[e, 2, :, :, cols].reshape(1536, 256))
                    act, slope = silu_parts(a)
                    u_s[:, cols] = (act * b).astype(BF)
                    ga_s[:, cols] = (gu * b * slope).astype(BF)
                    gb_s[:, cols] = (gu * act).astype(BF)
                for copy in copies:
                    copy.wait()

                def tile(t, carry):
                    at = pl.ds(pl.multiple_of(t * 384, 384), 384)
                    two = pl.ds(t * 2, 2)
                    x, g = xy[e, :, :, at].reshape(768, 384), gg[e, :, :, at].reshape(768, 384)
                    h, odd = div(t, 2), rem(t, 2)
                    half = pl.ds(odd * 2, 2)
                    dw[0, h, half] = tn(x, ga_s[...]).astype(BF).reshape(2, 192, 512)
                    dw[1, h, half] = tn(x, gb_s[...]).astype(BF).reshape(2, 192, 512)
                    dw[2, h, half] = tn(g, u_s[...]).astype(BF).reshape(2, 192, 512)
                    out = nt(u_s[...], w[e, 2, two].reshape(384, 512))
                    xy[e, :, :, at] = out.astype(BF).reshape(16, 48, 384)
                    back = nt(ga_s[...], w[e, 0, two].reshape(384, 512))
                    back = back + nt(gb_s[...], w[e, 1, two].reshape(384, 512))
                    gg[e, :, :, at] = back.astype(BF).reshape(16, 48, 384)
                    return carry

                lax.fori_loop(0, 4, tile, 0)
                copies = [here(dw, eg.at[e])]
                if e == 0:
                    copies[0].wait()
                    copies = []
                    expert_push(0)
            for copy in copies:
                copy.wait()
            expert_push(1)

        pl.run_scoped(
            work,
            pltpu.VMEM((2, 3, 8, 192, 512), BF),
            pltpu.VMEM((3, 2, 4, 192, 512), BF),
            pltpu.VMEM((768, 512), BF),
            pltpu.VMEM((768, 512), BF),
            pltpu.VMEM((768, 512), BF),
        )
        ly = here(xy, y_b)
        first[0].wait()

        def combine(ds):
            ds[...] = jnp.zeros_like(ds)

            def other_rows(pick_ref, gh_ref):
                p = oxh8 + pl.program_id(0)
                gh = tn(pick_ref[0], gg[:, p].reshape(96, 1536))
                gh_ref[...] = gh.astype(BF).reshape(1, 1, 2, 128, 1536)

            def own_rows(pick_ref, h2_ref, cot_ref, gh_ref, hid_ref):
                p = xh8 + pl.program_id(0)
                gh = tn(pick_ref[0], gg[:, p].reshape(96, 1536))
                h2, g = h2_ref[...].reshape(256, 1536), cot_ref[...].reshape(256, 1536)
                pre = nn(h2, sw[:, 0:128])
                gz = nn(g, sw[:, 128:256])
                act, slope = silu_parts(pre)
                up = half_turn(pre)
                lane = lax.broadcasted_iota(jnp.int32, (256, 128), 1)
                hid = jnp.where(lane < 64, act * up, 0.0).astype(BF)
                gcd = jnp.where(lane < 64, gz * up * slope, half_turn(gz * act)).astype(BF)
                gh_ref[...] = (gh + nt(gcd, sw[:, 0:128])).astype(BF).reshape(1, 1, 2, 128, 1536)
                hid_ref[0] = hid
                ds[:, 0:128] += tn(h2, gcd)
                ds[:, 128:256] += tn(g, hid)

            pltpu.emit_pipeline(
                own_rows,
                grid=(8,),
                in_specs=[picks, pairs, pairs],
                out_specs=[pairs, pl.BlockSpec((1, 256, 128), lambda p: (p, 0, 0))],
            )(pick_in.at[pl.ds(xh8, 8)], h2f.at[xh], cotf.at[xh], gh2p.at[xh], hid_b)
            pltpu.emit_pipeline(other_rows, grid=(8,), in_specs=[picks], out_specs=[pairs])(
                pick_in.at[pl.ds(oxh8, 8)], gh2p.at[oxh]
            )
            rows = one_hot_rows()
            for k in range(16):
                block = ds[k * 96 : (k + 1) * 96].astype(BF)
                db[k] = tn(rows, block).astype(BF).reshape(2, 4, 16, 256)

        pl.run_scoped(combine, pltpu.VMEM((1536, 256), F32))
        ly.wait()

    pl.run_scoped(experts, pltpu.VMEM((2, 16, 48, 1536), BF), pltpu.VMEM((2, 16, 48, 1536), BF))

    def dense(
        miney, minex, tmpy, tmpx, w, tokf, qkv, kvf, lse, att, go, dk, dv, dkvs, gqkv, gh1s, da, zs, s2, s3, bz, bsum
    ):
        def sum_start(xp, there):
            sibs = {}
            for d in (1, 3, 2, 0):
                yy, (hh, ll) = ynext[d], xnext[d]
                sibs["y", d] = cp.start(xp.at[:, yy, :, oco, low], there.at[:, yy, :, low], sib)
                sibs["x", d] = cp.start(xp.at[hh, :, ll, oco, high], there.at[hh, :, ll, high], sib)
            return sibs

        def sum_push(xp, there, sibs, toy, tox, steps):
            sent, loads = {}, {}

            def load(n):
                axis, d = steps[n]
                arrive(sibs[axis, d])
                if axis == "y":
                    yy = ynext[d]
                    loads[n] = [
                        here(xp.at[:, yy, :, co, low], miney.at[d]),
                        here(there.at[:, yy, :, low], tmpy.at[n % 2]),
                    ]
                else:
                    hh, ll = xnext[d]
                    loads[n] = [
                        here(xp.at[hh, :, ll, co, high], minex.at[d]),
                        here(there.at[hh, :, ll, high], tmpx.at[n % 2]),
                    ]

            load(0)
            for n, (axis, d) in enumerate(steps):
                if n + 1 < len(steps):
                    load(n + 1)
                for copy in loads[n]:
                    copy.wait()
                own, other = (miney, tmpy) if axis == "y" else (minex, tmpx)
                own[d] = (own[d].astype(F32) + other[n % 2].astype(F32)).astype(BF)
                if d and axis == "y":
                    sent[axis, d] = cp.start(miney.at[d], toy.at[d - 1], ypeers[d - 1])
                elif d:
                    sent[axis, d] = cp.start(minex.at[d], tox.at[d - 1], xpeers[d - 1])
            return sent

        def sum_second():
            for h in range(2):
                for l in range(2):
                    tot = miney[0, h, l].astype(F32)
                    for k in range(3):
                        tot = tot + goty[k, h, l].astype(F32)
                    miney[0, h, l] = tot.astype(BF)
            for a in range(4):
                tot = minex[0, a].astype(F32)
                for k in range(3):
                    tot = tot + gotx[k, a].astype(F32)
                minex[0, a] = tot.astype(BF)

        def sum_last(nth):
            sent = []
            for k, d in enumerate(Y_STEPS):
                hh, ll = xnext[d]
                sent.append(cp.start(miney.at[0, hh, ll], gety.at[nth, k], xpeers[k]))
                sent.append(cp.start(minex.at[0, ynext[d]], getx.at[nth, k], ypeers[k]))
            return sent

        def sum_end(nth, sent):
            for copy in sent:
                arrive(copy)
            top, bottom = miney[0, xh, xl].astype(F32), minex[0, y].astype(F32)
            for k in range(3):
                top = top + gety[nth, k].astype(F32)
                bottom = bottom + getx[nth, k].astype(F32)
            return jnp.concatenate([top, bottom], 0)

        sibs = sum_start(gh2p, thg)
        first.append(here(w_i, w))
        second = [here(qkv_i, qkv), here(kvf_i, kvf), here(lse_i, lse), here(att_i, att)]
        third = [here(tokf_i, tokf)]
        both = [("y", 1), ("x", 1), ("y", 3), ("x", 3), ("y", 2), ("x", 2), ("y", 0), ("x", 0)]
        sent_g = sum_push(gh2p, thg, sibs, goty, gotx, both)
        for copy in first[1:]:
            copy.wait()

        def output_rows(shared, gated_ref, y_ref, *refs):
            out = tn(gated_ref[0], y_ref[...].reshape(96, 1536))
            if shared:
                out = out + nt(refs[0][0], sw[:, 128:256])
            refs[-1][...] = out.astype(BF).reshape(1, 1, 2, 128, 1536)

        for shared in (True, False):
            h, h8 = (xh, xh8) if shared else (oxh, oxh8)
            specs = [
                pl.BlockSpec((1, 96, 256), lambda p: (p, 0, 0)),
                pl.BlockSpec((2, 1, 48, 1536), lambda p: (0, p, 0, 0)),
            ]
            args = [gated_in.at[pl.ds(h8, 8)], y_b.at[:, pl.ds(h8, 8)]]
            if shared:
                specs.append(pl.BlockSpec((1, 256, 128), lambda p: (p, 0, 0)))
                args.append(hid_b)
            pltpu.emit_pipeline(
                lambda *refs, shared=shared: output_rows(shared, *refs),
                grid=(8,),
                in_specs=specs,
                out_specs=[pl.BlockSpec((1, 1, 2, 128, 1536), lambda p: (div(p, 2), rem(p, 2), 0, 0, 0))],
            )(*args, outp.at[h])
        sibs = sum_start(outp, tho)

        gains = nt(eye_rows(), w[:, 640:768])
        gain_one, gain_two = gains[0:1], gains[1:2]
        inv = inverse_norm(resid[...])
        xh2 = resid[...] * inv
        for copy in sent_g.values():
            arrive(copy)
        sum_second()
        last_g = sum_last(0)
        gh2 = sum_end(0, last_g)
        gain_two_grad = jnp.sum(gh2 * xh2, 0, keepdims=True)
        inner = gh2 * gain_two
        row = inv * (inner - xh2 * jnp.mean(inner * xh2, -1, keepdims=True))
        gres[...] = cot[...].astype(F32) + row
        gattn[y] = gres[...].astype(BF)
        ga = [cp.start(gattn.at[y], gattn.at[y], p) for p in ypeers]

        gone(list(sent_g.values()) + last_g)
        sent_o = sum_push(outp, tho, sibs, goy, gox, both[:4] + both[4:5] + both[6:])

        for copy in second:
            copy.wait()
        for copy in ga:
            arrive(copy)
        dk[...] = jnp.zeros_like(dk)
        dv[...] = jnp.zeros_like(dv)
        for j in range(4):
            rows_j = slice(j * 128, (j + 1) * 128)
            go[rows_j] = nn(gattn[j], w[:, 768:1152]).astype(BF)
            q, g = head_rows(qkv, j), head_rows(go, j)
            delta = jnp.sum(head_rows(att, j).astype(F32) * g.astype(F32), -1, keepdims=True)
            total = lse[j][:, :1]
            dq = jnp.zeros((384, 128), F32)
            for t in range(j + 1):
                keys = kvf[t].reshape(512, 256)
                s = nt(q, keys[:, :128]) * SCALE
                p = jnp.exp(s - total)
                if t == j:
                    p = jnp.where(allowed(512), p, 0.0)
                gs = (p * (nt(g, keys[:, 128:]) - delta)).astype(BF)
                at = slice(t * 512, (t + 1) * 512)
                dv[at] += tn(p.astype(BF), g)
                dk[at] += tn(gs, q)
                dq = dq + nn(gs, keys[:, :128])
            dq = (dq * SCALE).astype(BF)
            for h in range(3):
                gqkv[rows_j, h * 128 : (h + 1) * 128] = dq[h * 128 : (h + 1) * 128]
        for j in range(4):
            for k in range(4):
                at = slice((j * 4 + k) * 128, (j * 4 + k + 1) * 128)
                dkvs[j, k, :, 0:128] = (dk[at] * SCALE).astype(BF)
                dkvs[j, k, :, 128:256] = dv[at].astype(BF)
        kvs = [
            cp.start(dkvs.at[:, p], dkvr.at[k], q)
            for k, (p, q) in enumerate(kv_peers)
        ]
        sent_o.update(sum_push(outp, tho, sibs, goy, gox, both[5:6]))
        rows = one_hot_rows()

        def expand(block, yy, cols):
            for k in range(4):
                part = tn(rows, block[k * 96 : (k + 1) * 96]).astype(BF)
                da[yy, k // 2, k % 2, :, :, :, cols] = part.reshape(2, 4, 16, -1)

        def dense_core(cols):
            return cp.start(da.at[:, :, oco, :, :, :, cols], dath.at[:, :, :, :, :, cols], sib)

        def dense_z(copy, cols):
            arrive(copy)
            for a in range(4):
                for b in range(2):
                    tot = da[a, b, co, :, :, :, cols].astype(F32) + dath[a, b, :, :, :, cols].astype(F32)
                    da[a, b, co, :, :, :, cols] = tot.astype(BF)
            return [
                cp.start(da.at[:, :, co, :, znext[d], :, cols], zg.at[k, :, :, :, :, cols], p)
                for k, (d, p) in enumerate(zip(Y_STEPS, zpeers))
            ]

        def dense_far(copies, cols):
            for copy in copies:
                arrive(copy)
            for a in range(4):
                for b in range(2):
                    tot = da[a, b, co, :, z, :, cols].astype(F32)
                    for k in range(3):
                        tot = tot + zg[k, a, b, :, :, cols].astype(F32)
                    for h in range(2):
                        zs[h, a, b, :, cols] = tot[h].astype(BF)
            return cp.start(zs.at[oxh, :, :, :, cols], xg.at[:, :, :, cols], xfar)

        def dense_near(copy, cols):
            arrive(copy)
            for a in range(4):
                for b in range(2):
                    tot = zs[xh, a, b, :, cols].astype(F32) + xg[a, b, :, cols].astype(F32)
                    s2[b, a, :, cols] = tot.astype(BF)
            return cp.start(s2.at[oxl, :, :, cols], xgot.at[:, :, cols], xpeer)

        def dense_y(copy, cols):
            arrive(copy)
            for a in range(4):
                s3[a, :, cols] = (s2[xl, a, :, cols].astype(F32) + xgot[a, :, cols].astype(F32)).astype(BF)
            last.append(here(s3.at[y, :, cols], aout.at[y, :, cols]))
            return [
                cp.start(s3.at[ynext[d], :, cols], aout.at[y, :, cols], p) for d, p in zip(Y_STEPS, ypeers)
            ]

        head, tail = pl.ds(0, 768), pl.ds(768, 384)
        last = []
        for yy in range(4):
            tile = slice(yy * 384, (yy + 1) * 384)
            block = tn(gattn[:, :, tile].reshape(512, 384), att[...])
            expand(block.astype(BF), yy, tail)
        tail_c = dense_core(tail)

        def expert_sums(e):
            for copy in expert_copies(e):
                copy.wait()
            add_arrays((2, 96, 512), [eg.at[e, :, :, z], zb.at[0, e], zb.at[1, e], zb.at[2, e]], sb.at[e])
            return cp.start(sb.at[e, :, oxh], xb.at[e], xfar)

        ex0 = expert_sums(0)
        tail_z = dense_z(tail_c, tail)
        bs = [cp.start(db.at[:, :, znext[d]], bgot.at[k], p) for k, (d, p) in enumerate(zip(Y_STEPS, zpeers))]
        for copy in third:
            copy.wait()
        for copy in kvs:
            arrive(copy)
        gone(ga)
        gain_one_grad = jnp.zeros((1, 1536), F32)
        for j in range(4):
            rows_j = slice(j * 128, (j + 1) * 128)
            kv = dkvs[j, i].astype(F32)
            for k in range(3):
                kv = kv + dkvr[k, j].astype(F32)
            gqkv[rows_j, 384:640] = kv.astype(BF)
            gh1 = nt(gqkv[rows_j], w[:, :640])
            v = tokf[j].astype(F32)
            scaled = v * inverse_norm(v)
            gain_one_grad = gain_one_grad + jnp.sum(gh1 * scaled, 0, keepdims=True)
            gattn[j] = (scaled * gain_one).astype(BF)
            gh1s[j] = gh1.astype(BF)
        hs = [
            cp.start(gh1s.at[ynext[d]], gh1g.at[k], p) for k, (d, p) in enumerate(zip(Y_STEPS, ypeers))
        ]
        gain_rows = jnp.concatenate([gain_one_grad, gain_two_grad, jnp.zeros((6, 1536), F32)], 0)
        for yy in range(4):
            tile = slice(yy * 384, (yy + 1) * 384)
            block = tn(gattn[:, :, tile].reshape(512, 384), gqkv[...])
            expand(block.astype(BF), yy, pl.ds(0, 640))
            expand(tn(gain_rows[:, tile].astype(BF), eye_rows()).astype(BF), yy, pl.ds(640, 128))
        head_c = dense_core(head)
        head_z = dense_z(head_c, head)

        for copy in sent_o.values():
            arrive(copy)
        back_in = [here(goy, goty), here(gox, gotx)]
        for copy in back_in:
            copy.wait()
        gone(list(sent_o.values()))
        sum_second()
        last_o = sum_last(1)
        gh1 = gh1s[y].astype(F32)
        for k, copy in enumerate(hs):
            arrive(copy)
            gh1 = gh1 + gh1g[k].astype(F32)
        v = tokf[y].astype(F32)
        inv = inverse_norm(v)
        inner = gh1 * gain_one
        xh1 = v * inv
        igrad[...] = gres[...] + inv * (inner - xh1 * jnp.mean(inner * xh1, -1, keepdims=True))

        tail_x = dense_far(tail_z, tail)
        ex1 = expert_sums(1)
        for copy in bs:
            arrive(copy)
        for a in range(16):
            tot = db[a, :, z].astype(F32)
            for k in range(3):
                tot = tot + bgot[k, a].astype(F32)
            bz[0, a], bz[1, a] = tot[0].astype(BF), tot[1].astype(BF)
        bx = cp.start(bz.at[oxh], bxg, xfar)
        head_x = dense_far(head_z, head)
        lout[...] = (resid[...] + sum_end(1, last_o)).astype(BF)
        tail_n = dense_near(tail_x, tail)
        arrive(bx)
        for a in range(16):
            bsum[a] = (bz[xh, a].astype(F32) + bxg[a].astype(F32)).astype(BF)
        bo = [cp.start(bsum.at[p], bout.at[c], q) for p, q in zip(place_index, cpeers)]
        last.append(here(bsum.at[c], bout.at[c]))
        head_n = dense_near(head_x, head)
        outs = dense_y(tail_n, tail) + dense_y(head_n, head)

        for copy in last:
            copy.wait()
        for copy in cp.started:
            if not any(copy is r for r in sent_already):
                copy.wait_send()
            if not any(copy is r for r in got_already):
                copy.wait_recv()

    pl.run_scoped(
        dense,
        pltpu.VMEM((4, 2, 2, 64, 1536), BF),
        pltpu.VMEM((4, 4, 64, 1536), BF),
        pltpu.VMEM((2, 2, 2, 64, 1536), BF),
        pltpu.VMEM((2, 4, 64, 1536), BF),
        pltpu.VMEM((1536, 1152), BF),
        pltpu.VMEM((4, 128, 1536), BF),
        pltpu.VMEM((512, 640), BF),
        pltpu.VMEM((4, 4, 128, 256), BF),
        pltpu.VMEM((4, 384, 128), F32),
        pltpu.VMEM((512, 384), BF),
        pltpu.VMEM((512, 384), BF),
        pltpu.VMEM((2048, 128), F32),
        pltpu.VMEM((2048, 128), F32),
        pltpu.VMEM((4, 4, 128, 256), BF),
        pltpu.VMEM((512, 640), BF),
        pltpu.VMEM((4, 128, 1536), BF),
        pltpu.VMEM((4, 2, 2, 2, 4, 16, 1152), BF),
        pltpu.VMEM((2, 4, 2, 16, 1152), BF),
        pltpu.VMEM((2, 4, 16, 1152), BF),
        pltpu.VMEM((4, 16, 1152), BF),
        pltpu.VMEM((2, 16, 16, 256), BF),
        pltpu.VMEM((16, 16, 256), BF),
    )


def back(*ins):
    outs = (
        SDS((2, 3, 2, 4, 192, 512), BF),
        SDS((2, 16, 48, 1536), BF),
        SDS((8, 256, 128), BF),
        SDS((2, 4, 2, 2, 128, 1536), BF),
        SDS((2, 4, 2, 2, 128, 1536), BF),
        SDS((3, 2, 3, 2, 192, 512), BF),
        SDS((2, 3, 2, 192, 512), BF),
        SDS((2, 3, 192, 512), BF),
        SDS((2, 4, 2, 128, 1536), BF),
        SDS((2, 4, 2, 128, 1536), BF),
        SDS((3, 2, 2, 64, 1536), BF),
        SDS((3, 4, 64, 1536), BF),
        SDS((4, 16, 1152), BF),
        SDS((16, 16, 256), BF),
        SDS((128, 1536), BF),
        SDS((128, 1536), F32),
    )
    out = pl.pallas_call(
        back_kernel,
        out_shape=outs,
        in_specs=[ANY] * len(ins),
        out_specs=(ANY,) * 14 + (VM,) * 2,
        scratch_shapes=[
            pltpu.SemaphoreType.DMA((112,)),
            pltpu.SemaphoreType.DMA((112,)),
            pltpu.SemaphoreType.DMA((80,)),
            pltpu.VMEM((3, 2, 2, 64, 1536), BF),
            pltpu.VMEM((3, 4, 64, 1536), BF),
            pltpu.VMEM((2, 3, 64, 1536), BF),
            pltpu.VMEM((2, 3, 64, 1536), BF),
            pltpu.VMEM((128, 1536), F32),
            pltpu.VMEM((128, 1536), BF),
            pltpu.VMEM((128, 1536), F32),
            pltpu.VMEM((4, 128, 1536), BF),
            pltpu.VMEM((3, 4, 128, 256), BF),
            pltpu.VMEM((3, 128, 1536), BF),
            pltpu.VMEM((4, 2, 2, 4, 16, 1152), BF),
            pltpu.VMEM((3, 4, 2, 2, 16, 1152), BF),
            pltpu.VMEM((4, 2, 16, 1152), BF),
            pltpu.VMEM((4, 16, 1152), BF),
            pltpu.VMEM((3, 16, 2, 16, 256), BF),
            pltpu.VMEM((16, 16, 256), BF),
            pltpu.VMEM((1536, 256), BF),
            pltpu.VMEM((16, 2, 4, 16, 256), BF),
        ],
        compiler_params=pltpu.CompilerParams(
            collective_id=2, has_side_effects=True, vmem_limit_bytes=62 * 2**20
        ),
        cost_estimate=pl.CostEstimate(flops=36 * 10**9, bytes_accessed=150 * 10**6, transcendentals=5 * 10**6),
    )(*ins)
    return out[14], out[15], out[12], out[13], out[6], out[7]


def unpack_kernel(
    lout, igrad, aout, bout, sb, xb,
    lout_o, igrad_o, gains_o, wq_o, wk_o, wv_o, wo_o, sg_o, su_o, sd_o, eg_o, eu_o, ed_o,
):
    xh = lax.axis_index("fsdp") // 4
    lout_o[...] = lout[...]
    igrad_o[...] = igrad[...]
    for e in range(2):
        for m, ref in enumerate((eg_o, eu_o, ed_o)):
            ref[xh * 2 + e] = sb[e, m, xh].astype(F32)
            ref[2 - xh * 2 + e] = xb[e, m].astype(F32)
    gain_sum = jnp.zeros((16, 128), F32)
    for k in range(4):
        wide, thin = slice(k * 384, (k + 1) * 384), slice(k * 128, (k + 1) * 128)
        block = aout[k].astype(F32)
        wq_o[:, wide] = block[:12, 0:384]
        wk_o[:, thin] = block[:12, 384:512]
        wv_o[:, thin] = block[:12, 512:640]
        gain_sum = gain_sum + block[:, 640:768]
        wo_o[:, wide] = block[:12, 768:1152]
    gains_o[...] = gain_sum
    front_half = lax.broadcasted_iota(jnp.int32, (16, 128), 1) < 64
    for k in range(8):
        at = slice(k * 128, (k + 1) * 128)
        one, two = bout[2 * k].astype(F32), bout[2 * k + 1].astype(F32)
        sg_o[:, at] = jnp.where(front_half, one[:, :128], half_turn(two[:, :128]))[:12]
        su_o[:, at] = jnp.where(front_half, half_turn(one[:, :128]), two[:, :128])[:12]
        sd_o[:, at] = jnp.where(front_half, one[:, 128:], half_turn(two[:, 128:]))[:12]


def unpack(*ins):
    outs = (
        SDS((128, 1536), BF),
        SDS((128, 1536), F32),
        SDS((16, 128), F32),
        SDS((12, 1536), F32),
        SDS((12, 512), F32),
        SDS((12, 512), F32),
        SDS((12, 1536), F32),
        SDS((12, 1024), F32),
        SDS((12, 1024), F32),
        SDS((12, 1024), F32),
        SDS((4, 192, 512), F32),
        SDS((4, 192, 512), F32),
        SDS((4, 192, 512), F32),
    )
    return pl.pallas_call(
        unpack_kernel,
        out_shape=outs,
        in_specs=[VM] * len(ins),
        out_specs=(VM,) * len(outs),
        compiler_params=pltpu.CompilerParams(vmem_limit_bytes=VMEM_LIMIT),
    )(*ins)


def local(
    tokens,
    cotangent,
    routes,
    gates,
    attn_gain,
    ffn_gain,
    w_query,
    w_key,
    w_value,
    w_out,
    shared_gate,
    shared_up,
    shared_down,
    expert_gate,
    expert_up,
    expert_down,
):
    tok = tokens.reshape(128, 1536)
    cot = cotangent.reshape(128, 1536)
    gains = jnp.stack([attn_gain, ffn_gain])
    (cot_f, h2_f, wexp, tok_f, kv_f, gy, pick, gated, _, w, sw, qkv, att, lse, resid) = front(
        tok,
        cot,
        jnp.transpose(routes, (2, 0, 1)),
        jnp.transpose(gates, (2, 0, 1)),
        gains,
        w_query,
        w_key,
        w_value,
        w_out.T,
        shared_gate,
        shared_up,
        shared_down.T,
        expert_gate,
        expert_up,
        jnp.transpose(expert_down, (0, 2, 1)),
    )
    parts = back(
        pick, gated, gy, wexp, h2_f, cot_f, resid, cot, w, sw, tok_f, qkv, kv_f, lse, att
    )
    (layer_out, input_grad, gain_grads, wq, wk, wv, wo, sg, su, sd, eg, eu, ed) = unpack(*parts)
    return (
        layer_out.reshape(1, 128, 1536),
        input_grad.reshape(1, 128, 1536),
        gain_grads[:12, 0],
        gain_grads[:12, 1],
        wq,
        wk,
        wv,
        wo.T,
        sg,
        su,
        sd.T,
        eg,
        eu,
        jnp.transpose(ed, (0, 2, 1)),
    )


def solution(mesh):
    both = ("ctx", "fsdp")
    rows = P("fsdp", "ctx", None)
    weights = (P(both),) * 2 + (P(both, None),) * 3 + (P(None, both),)
    weights = weights + (P(both, None),) * 2 + (P(None, both),)
    weights = weights + (P("ctx", "fsdp", None),) * 2 + (P("ctx", None, "fsdp"),)
    return jax.shard_map(
        local, mesh=mesh, in_specs=(rows,) * 4 + weights, out_specs=(rows,) * 2 + weights, check_vma=False
    )
```

```python
import jax
import jax.numpy as jnp
from jax import lax
from jax.experimental import pallas as pl
from jax.experimental.pallas import tpu as pltpu
from jax.sharding import PartitionSpec as P

BF = jnp.bfloat16
F32 = jnp.float32
EPS = 1e-05
MESH = pl.DeviceIdType.MESH
ANY = pl.BlockSpec(memory_space=pl.ANY)
VM = pl.BlockSpec(memory_space=pltpu.VMEM)
SDS = jax.ShapeDtypeStruct
SCALE = 128 ** (-0.5)
VMEM_LIMIT = 56 * 2**20


def div(x, n):
    return lax.div(x, lax.full_like(x, n))


def rem(x, n):
    return lax.rem(x, lax.full_like(x, n))


def nn(a, b):
    return lax.dot_general(a, b, (((1,), (0,)), ((), ())), preferred_element_type=F32)


def nt(a, b):
    return lax.dot_general(a, b, (((1,), (1,)), ((), ())), preferred_element_type=F32)


def tn(a, b):
    return lax.dot_general(a, b, (((0,), (0,)), ((), ())), preferred_element_type=F32)


def silu_parts(pre_act):
    sig = 1.0 / (1.0 + jnp.exp(-pre_act))
    return pre_act * sig, sig * (1.0 + pre_act * (1.0 - sig))


def coords():
    c = lax.axis_index("ctx")
    f = lax.axis_index("fsdp")
    return c // 4, (c // 2) % 2, c % 2, f // 4, f % 4


def dev(y, xl, co, xh, z):
    return (y * 4 + xl * 2 + co, xh * 4 + z)


def barrier(peers):
    sem = pltpu.get_barrier_semaphore()
    for peer in peers:
        pl.semaphore_signal(sem, inc=1, device_id=peer, device_id_type=MESH)
    pl.semaphore_wait(sem, len(peers))


class Copies:
    def __init__(self, send, recv):
        self.send, self.recv, self.n, self.started = send, recv, 0, []

    def start(self, src, dst, peer):
        copy = pltpu.make_async_remote_copy(
            src, dst, self.send.at[self.n], self.recv.at[self.n], device_id=peer, device_id_type=MESH
        )
        copy.start()
        self.n += 1
        self.started.append(copy)
        return copy

    def finish(self, received=()):
        for copy in self.started:
            copy.wait_send()
            if not any(copy is r for r in received):
                copy.wait_recv()


Y_STEPS = (1, 2, 3)


def one_hot_rows():
    row = lax.broadcasted_iota(jnp.int32, (96, 128), 0)
    col = lax.broadcasted_iota(jnp.int32, (96, 128), 1)
    return jnp.where(div(row, 12) * 16 + rem(row, 12) == col, 1.0, 0.0).astype(BF)


def eye_rows():
    row = lax.broadcasted_iota(jnp.int32, (8, 128), 0)
    col = lax.broadcasted_iota(jnp.int32, (8, 128), 1)
    return jnp.where(row == col, 1.0, 0.0).astype(BF)


def inverse_norm(values):
    return lax.rsqrt(jnp.mean(values * values, -1, keepdims=True) + EPS)


def head_rows(ref, j, first=0):
    rows = slice(j * 128, (j + 1) * 128)
    return jnp.concatenate([ref[rows, first + h * 128 : first + (h + 1) * 128] for h in range(3)], 0)


def allowed(n):
    i = rem(lax.axis_index("ctx"), 4)
    row = rem(lax.broadcasted_iota(jnp.int32, (384, n), 0), 128)
    col = lax.broadcasted_iota(jnp.int32, (384, n), 1)
    return col <= i * 128 + row


def ctx_places(y, xl, co):
    return [
        ((y + dy) % 4, (xl + dx) % 2, (co + dc) % 2)
        for dy in range(4)
        for dx in (0, 1)
        for dc in (0, 1)
        if (dy, dx, dc) != (0, 0, 0)
    ]


def x_place(xh, xl, d):
    x = (xh * 2 + xl + d) % 4
    return x // 2, x % 2


def plane_gather(cp, arrive, src, out, places, sib, split):
    y, xl, co, xh, z = places
    low, high = pl.ds(0, split), pl.ds(split, 128 - split)
    ypeers = [dev((y + d) % 4, xl, co, xh, z) for d in Y_STEPS]
    xpeers = []
    for d in Y_STEPS:
        h, l = x_place(xh, xl, d)
        xpeers.append(dev(y, l, co, h, z))
    mine = (xh, y, xl, co)

    def first_y():
        return [cp.start(src.at[high], out.at[mine + (high,)], p) for p in ypeers]

    def first_x():
        return [cp.start(src.at[low], out.at[mine + (low,)], p) for p in xpeers]

    def piece_y(d):
        return out.at[:, (y + d) % 4, :, co, low]

    def piece_x(d):
        h, l = x_place(xh, xl, d)
        return out.at[h, :, l, co, high]

    def half_y(d, n):
        return out.at[n, (y + d) % 4, :, co, low]

    def half_x(d, n):
        h, l = x_place(xh, xl, d)
        return out.at[h, pl.ds(2 * n, 2), l, co, high]

    def then(firsts, piece, peers):
        for copy in firsts:
            arrive(copy)
        return [
            cp.start(piece(0), piece(0), peers[0]),
            cp.start(piece(0), piece(0), peers[2]),
            cp.start(piece(0), piece(0), sib),
        ]

    def middle(seconds, piece, half, peers):
        arrive(seconds[0])
        one = cp.start(half(3, 0), half(3, 0), peers[0])
        arrive(seconds[1])
        two = cp.start(half(1, 1), half(1, 1), peers[2])
        sibs = [cp.start(piece(d), piece(d), sib) for d in (3, 1)]
        return [one, two] + sibs

    def last(middles, piece):
        for copy in middles[:2]:
            arrive(copy)
        return middles[2:] + [cp.start(piece(2), piece(2), sib)]

    def then_y(firsts):
        return then(firsts, piece_y, ypeers)

    def then_x(firsts):
        return then(firsts, piece_x, xpeers)

    def middle_y(seconds):
        return middle(seconds, piece_y, half_y, ypeers)

    def middle_x(seconds):
        return middle(seconds, piece_x, half_x, xpeers)

    def last_y(middles):
        return last(middles, piece_y)

    def last_x(middles):
        return last(middles, piece_x)

    return (first_y, then_y, middle_y, last_y), (first_x, then_x, middle_x, last_x)


def dispatch_rows(rg, first):
    masks, gates = [], []
    for e in range(2):
        ms, gs = [], []
        for s in range(2):
            hit = jnp.where(rg[s, 0:6] == (first + e).astype(F32), 1.0, 0.0)
            ms.append(jnp.sum(hit, 0, keepdims=True))
            gs.append(jnp.sum(hit * rg[s, 8:14], 0, keepdims=True))
        masks.append(jnp.concatenate(ms, 1))
        gates.append(jnp.concatenate(gs, 1))
    mask = jnp.concatenate(masks + [jnp.zeros((6, 256), F32)], 0)
    before = lax.broadcasted_iota(jnp.int32, (256, 256), 0)
    after = lax.broadcasted_iota(jnp.int32, (256, 256), 1)
    tri = jnp.where((before <= after) & (before // 128 == after // 128), 1.0, 0.0).astype(BF)
    place = nn(mask.astype(BF), tri) - 1.0
    lane = lax.broadcasted_iota(jnp.int32, (1, 256), 1)
    slot = lax.broadcasted_iota(jnp.int32, (48, 256), 0).astype(F32)
    picks, gated = [], []
    for e in range(2):
        at = place[e : e + 1] + jnp.where(lane >= 128, 24.0, 0.0)
        at = jnp.where(masks[e] > 0.0, at, -1.0)
        hit = jnp.where(slot == at, 1.0, 0.0)
        picks.append(hit)
        gated.append(hit * gates[e])
    return jnp.concatenate(picks, 0).astype(BF), jnp.concatenate(gated, 0).astype(BF)


def eye(rows, cols):
    row = lax.broadcasted_iota(jnp.int32, (rows, cols), 0)
    col = lax.broadcasted_iota(jnp.int32, (rows, cols), 1)
    return jnp.where(row == col, 1.0, 0.0).astype(BF)


def half_turn(x):
    return pltpu.roll(x, 64, 1)


def front_kernel(
    tok, cot, routes, gates, gains_in, wq, wk, wv, wo, sg, su, sd, eg, eu, ed,
    cotf, h2f, wexp, tokf_o, kvf_o, gy, pick_o, gated_o, gz_o, rgf,
    w, sw, qkv, att, lse, resid,
    send, recv, loc, a_s, b_s, own, rg_s, a2, wf, b1, bf, tokf, kvf, s_s, part, got, h2,
):
    y, xl, co, xh, z = coords()
    i, c, f = xl * 2 + co, y * 4 + xl * 2 + co, xh * 4 + z
    f_far = (1 - xh) * 4 + z
    sib = dev(y, xl, 1 - co, xh, z)
    xpeer = dev(y, 1 - xl, co, xh, z)
    xfar = dev(y, xl, co, 1 - xh, z)
    ypeers = [dev((y + d) % 4, xl, co, xh, z) for d in Y_STEPS]
    zpeers = [dev(y, xl, co, xh, (z + d) % 4) for d in Y_STEPS]
    places = ctx_places(y, xl, co)
    cpeers = [dev(*p, xh, z) for p in places]
    plane = cpeers + [dev(*p, 1 - xh, z) for p in places + [(y, xl, co)]]
    peers = plane + zpeers
    sem = pltpu.get_barrier_semaphore()
    for peer in peers:
        pl.semaphore_signal(sem, inc=1, device_id=peer, device_id_type=MESH)

    e16 = eye(16, 12)
    q16, k16, v16 = (nn(e16, ref[...]).astype(BF) for ref in (wq, wk, wv))
    o16 = nn(e16, wo[...]).astype(BF)
    gain_rows = nn(eye(128, 2), gains_in[...]).astype(BF)
    gain16 = nt(e16, gain_rows).astype(BF)
    for k in range(4):
        wide, thin = slice(k * 384, (k + 1) * 384), slice(k * 128, (k + 1) * 128)
        a_s[k] = jnp.concatenate([q16[:, wide], k16[:, thin], v16[:, thin], gain16, o16[:, wide]], 1)
    g16, u16, d16 = nn(e16, sg[...]), nn(e16, su[...]), nn(e16, sd[...])
    front_half = lax.broadcasted_iota(jnp.int32, (16, 128), 1) < 64
    for k in range(8):
        at = slice(k * 128, (k + 1) * 128)
        g, u, d = g16[:, at], u16[:, at], d16[:, at]
        for n in range(2):
            if n:
                g, d = half_turn(g), half_turn(d)
            else:
                u = half_turn(u)
            b_s[2 * k + n, :, 0:128] = jnp.where(front_half, g, u).astype(BF)
            b_s[2 * k + n, :, 128:256] = jnp.where(front_half, d, 0.0).astype(BF)
            if not n:
                u = half_turn(u)
    for e in range(4):
        own[e, 0] = eg[e]
        own[e, 1] = eu[e]
        own[e, 2] = ed[e]
    rg_s[...] = jnp.zeros_like(rg_s)
    for k in range(6):
        rg_s[k : k + 1] = routes[k].astype(F32)
        rg_s[8 + k : 9 + k] = gates[k]
    pl.semaphore_wait(sem, len(peers))

    cp = Copies(send, recv)
    n_local = [0]

    def here(src, dst):
        copy = pltpu.make_async_copy(src, dst, loc.at[n_local[0]])
        n_local[0] += 1
        copy.start()
        return copy

    got_already = []

    def arrive(copy):
        copy.wait_recv()
        got_already.append(copy)

    me = (y, xl, co, xh, z)
    ya = [cp.start(a_s.at[(y + d) % 4], a2.at[y, xl], p) for d, p in zip(Y_STEPS, ypeers)]
    la = here(a_s.at[y], a2.at[y, xl])
    lb = here(b_s.at[c], b1.at[c])
    lt = here(tok, tokf.at[y])
    lr = here(rg_s, rgf.at[xh, c])
    later = [here(own.at[pl.ds(xh * 2, 2)], wexp.at[:, :, f])]
    own_cot = here(cot, cotf.at[xh, y, xl, co])
    over_y, over_x = plane_gather(cp, arrive, cot, cotf, me, sib, 80)
    cot_y, cot_then_y, cot_middle_y, cot_last_y = over_y
    cot_x, cot_then_x, cot_middle_x, cot_last_x = over_x
    yt = [cp.start(tok, tokf.at[y], p) for p in ypeers]
    cy = cot_y()
    la.wait()
    for copy in ya:
        arrive(copy)
    xa = cp.start(a2.at[:, xl], a2.at[:, xl], xpeer)
    bs = [cp.start(b_s.at[p[0] * 4 + p[1] * 2 + p[2]], b1.at[c], q) for p, q in zip(places, cpeers)]
    rgs = [cp.start(rg_s, rgf.at[xh, c], q) for q in plane]
    arrive(xa)

    head, tail = pl.ds(0, 768), pl.ds(768, 384)

    def slices(cols):
        return a2.at[:, :, :, cols], wf.at[:, :, co, f, :, cols], wf.at[:, :, co, f_far, :, cols]

    src, mine, far = slices(head)
    hx = cp.start(src, mine, xfar)
    hz = [cp.start(src, mine, p) for p in zpeers]
    lw = here(a2, wf.at[:, :, co, f])
    cx = cot_x()
    src_t, mine_t, far_t = slices(tail)
    tx = cp.start(src_t, mine_t, xfar)
    ex = [cp.start(own.at[2 - xh * 2], wexp.at[0, :, f], xfar)]
    lw.wait()
    to_sib = [cp.start(mine, mine, sib)]
    arrive(hx)
    hz2 = [cp.start(far, far, p) for p in zpeers]
    to_sib.append(cp.start(far, far, sib))
    tz = [cp.start(src_t, mine_t, p) for p in zpeers]
    for copies, h in ((hz, xh), (hz2, 1 - xh)):
        for d, copy in zip(Y_STEPS, copies):
            arrive(copy)
            piece = wf.at[:, :, co, h * 4 + (z + 4 - d) % 4, :, head]
            to_sib.append(cp.start(piece, piece, sib))
    own_cot.wait()
    cy2 = cot_then_y(cx)
    arrive(tx)
    tz2 = [cp.start(far_t, far_t, p) for p in zpeers]
    tail_sib = [cp.start(mine_t, mine_t, sib), cp.start(far_t, far_t, sib)]
    own_z = [cp.start(own.at[pl.ds(xh * 2, 2)], wexp.at[:, :, f], zpeers[k]) for k in (0, 2)]
    lb.wait()
    for copy in bs:
        arrive(copy)
    bx = cp.start(b1, bf.at[:, f], xfar)
    bz = [cp.start(b1, bf.at[:, f], p) for p in zpeers]
    lb = here(b1, bf.at[:, f])
    for copy in to_sib:
        arrive(copy)
    rows = one_hot_rows()

    def compact(cols):
        for yy in range(4):
            for k in range(4):
                at = (yy * 4 + k) * 96
                block = wf[yy, k // 2, k % 2, :, :, cols].reshape(128, -1)
                w[at : at + 96, cols] = nn(rows, block).astype(BF)

    compact(slice(0, 768))
    gains = nt(eye_rows(), w[:, 640:768])
    gain_one, gain_two = gains[0:1], gains[1:2]

    lt.wait()
    for copy in yt:
        arrive(copy)
    for j in range(4):
        v = tokf[j].astype(F32)
        rows_j = slice(j * 128, (j + 1) * 128)
        h1 = (v * inverse_norm(v) * gain_one).astype(BF)
        qkv_j = nn(h1, w[:, :640]).astype(BF)
        qkv[rows_j] = qkv_j
        kvf[j, i] = qkv_j[:, 384:]
    kx = cp.start(kvf.at[:, i], kvf.at[:, i], xpeer)
    ks = [cp.start(kvf.at[:, i], kvf.at[:, i], sib)]
    saved = [here(tokf, tokf_o)]
    for copies, h in ((tz, xh), (tz2, 1 - xh)):
        for d, copy in zip(Y_STEPS, copies):
            arrive(copy)
            piece = wf.at[:, :, co, h * 4 + (z + 4 - d) % 4, :, tail]
            tail_sib.append(cp.start(piece, piece, sib))
    arrive(kx)
    piece = kvf.at[:, (1 - xl) * 2 + co]
    ks.append(cp.start(piece, piece, sib))
    ex.append(cp.start(own.at[3 - xh * 2], wexp.at[1, :, f], xfar))
    cy3 = cot_middle_y(cy2)
    cx2 = cot_then_x(cy)
    for copy in ks:
        arrive(copy)
    saved.append(here(kvf, kvf_o))

    for j in range(4):
        n = (j + 1) * 512
        q = head_rows(qkv, j)
        for t in range(j + 1):
            s = nt(q, kvf[t].reshape(512, 256)[:, :128]) * SCALE
            if t == j:
                s = jnp.where(allowed(512), s, -1e30)
            s_s[:, t * 512 : (t + 1) * 512] = s
        s = s_s[:, :n]
        m = jnp.max(s, -1, keepdims=True)
        p = jnp.exp(s - m)
        total = jnp.sum(p, -1, keepdims=True)
        o = nn(p.astype(BF), kvf[0 : j + 1].reshape(n, 256)[:, 128:]) / total
        rows_j = slice(j * 128, (j + 1) * 128)
        for h in range(3):
            att[rows_j, h * 128 : (h + 1) * 128] = o[h * 128 : (h + 1) * 128].astype(BF)
        lse[j] = jnp.broadcast_to(m + jnp.log(total), (384, 128))
    for copy in tail_sib:
        arrive(copy)
    compact(slice(768, 1152))
    for j in range(4):
        part[j] = nt(att[j * 128 : (j + 1) * 128], w[:, 768:1152]).astype(BF)
    ps = [
        cp.start(part.at[(y + d) % 4], got.at[k], p) for k, (d, p) in enumerate(zip(Y_STEPS, ypeers))
    ]
    def pass_on(copies, h):
        sent = []
        for e, (copy, d) in enumerate(zip(copies, (3, 1))):
            arrive(copy)
            piece = wexp.at[e, :, h * 4 + (z + d) % 4]
            sent.append(cp.start(piece, piece, zpeers[2 * e]))
        return sent

    arrive(bx)
    bz += [cp.start(bf.at[:, f_far], bf.at[:, f_far], p) for p in zpeers]
    pass_on(own_z, xh)
    total = tokf[y].astype(F32) + part[y].astype(F32)
    for k, copy in enumerate(ps):
        arrive(copy)
        total = total + got[k].astype(F32)
    resid[...] = total
    h2[...] = (total * inverse_norm(total) * gain_two).astype(BF)
    over_y, over_x = plane_gather(cp, arrive, h2, h2f, me, sib, 64)
    h2_y, h2_then_y, h2_middle_y, h2_last_y = over_y
    h2_x, h2_then_x, h2_middle_x, h2_last_x = over_x
    hx = h2_x()
    hy = h2_y()
    own_h2 = here(h2, h2f.at[xh, y, xl, co])

    cx3 = cot_middle_x(cx2)
    for copy in ex:
        arrive(copy)
    far_rows = wexp.at[:, :, f_far]
    far_z = [cp.start(far_rows, far_rows, zpeers[k]) for k in (0, 2)]
    own_h2.wait()
    hy2 = h2_then_y(hx)
    hx2 = h2_then_x(hy)
    cot_sib = [cy2[2], cx2[2]] + cot_last_y(cy3) + cot_last_x(cx3)
    lb.wait()
    for copy in bz:
        arrive(copy)
    for k in range(16):
        sw[k * 96 : (k + 1) * 96] = nn(rows, bf[k].reshape(128, 256)).astype(BF)
    lr.wait()
    for copy in rgs + cot_sib:
        arrive(copy)

    first = c * 4 + xh * 2

    def gated_rows(rg_ref, cot_ref, gy_ref, pick_ref, gated_ref, gz_ref):
        pick, gated = dispatch_rows(rg_ref.reshape(2, 16, 128), first)
        g = cot_ref[...].reshape(256, 1536)
        gy_ref[...] = nn(gated, g).astype(BF).reshape(2, 1, 48, 1536)
        gz_ref[0] = nn(g, sw[:, 128:256])
        pick_ref[0], gated_ref[0] = pick, gated

    picks = pl.BlockSpec((1, 96, 256), lambda p: (p, 0, 0))
    whole = pl.BlockSpec((1, 256, 128), lambda p: (p, 0, 0))
    pltpu.emit_pipeline(
        gated_rows,
        grid=(16,),
        in_specs=[
            pl.BlockSpec((1, 2, 16, 128), lambda p: (p // 8, p % 8, 0, 0)),
            pl.BlockSpec(
                (1, 1, 1, 2, 128, 1536),
                lambda p: (p // 8, p // 2 % 4, p % 2, 0, 0, 0),
                pipeline_mode=pl.Buffered(4),
            ),
        ],
        out_specs=[pl.BlockSpec((2, 1, 48, 1536), lambda p: (0, p, 0, 0)), picks, picks, whole],
    )(rgf, cotf, gy, pick_o, gated_o, gz_o)
    hy3 = h2_middle_y(hy2)
    hx3 = h2_middle_x(hx2)
    pass_on(far_z, 1 - xh)
    h2_last_y(hy3)
    h2_last_x(hx3)
    for copy in later + saved:
        copy.wait()
    cp.finish(got_already)


def front(*ins):
    outs = (
        SDS((2, 4, 2, 2, 128, 1536), BF),
        SDS((2, 4, 2, 2, 128, 1536), BF),
        SDS((2, 3, 8, 192, 512), BF),
        SDS((4, 128, 1536), BF),
        SDS((4, 4, 128, 256), BF),
        SDS((2, 16, 48, 1536), BF),
        SDS((16, 96, 256), BF),
        SDS((16, 96, 256), BF),
        SDS((16, 256, 128), F32),
        SDS((2, 16, 16, 128), F32),
        SDS((1536, 1152), BF),
        SDS((1536, 256), BF),
        SDS((512, 640), BF),
        SDS((512, 384), BF),
        SDS((4, 384, 128), F32),
        SDS((128, 1536), F32),
    )
    return pl.pallas_call(
        front_kernel,
        out_shape=outs,
        in_specs=[ANY] * 2 + [VM] * (len(ins) - 2),
        out_specs=(ANY,) * 10 + (VM,) * 6,
        scratch_shapes=[
            pltpu.SemaphoreType.DMA((160,)),
            pltpu.SemaphoreType.DMA((160,)),
            pltpu.SemaphoreType.DMA((16,)),
            pltpu.VMEM((4, 16, 1152), BF),
            pltpu.VMEM((16, 16, 256), BF),
            pltpu.VMEM((4, 3, 192, 512), BF),
            pltpu.VMEM((16, 128), F32),
            pltpu.VMEM((4, 2, 16, 1152), BF),
            pltpu.VMEM((4, 2, 2, 8, 16, 1152), BF),
            pltpu.VMEM((16, 16, 256), BF),
            pltpu.VMEM((16, 8, 16, 256), BF),
            pltpu.VMEM((4, 128, 1536), BF),
            pltpu.VMEM((4, 4, 128, 256), BF),
            pltpu.VMEM((384, 2048), F32),
            pltpu.VMEM((4, 128, 1536), BF),
            pltpu.VMEM((3, 128, 1536), BF),
            pltpu.VMEM((128, 1536), BF),
        ],
        compiler_params=pltpu.CompilerParams(
            collective_id=1, has_side_effects=True, vmem_limit_bytes=VMEM_LIMIT
        ),
        cost_estimate=pl.CostEstimate(flops=6 * 10**9, bytes_accessed=60 * 10**6, transcendentals=3 * 10**6),
    )(*ins)


def add_blocks(*refs):
    total = refs[0][...].astype(F32)
    for ref in refs[1:-1]:
        total = total + ref[...].astype(F32)
    refs[-1][...] = total.astype(refs[-1].dtype)


def add_arrays(block, ins, out):
    spec = pl.BlockSpec((1,) + block, lambda m, r: (m, 0, r, 0))
    pltpu.emit_pipeline(add_blocks, grid=(3, 2), in_specs=[spec] * len(ins), out_specs=[spec])(*ins, out)


def back_kernel(
    pick_in, gated_in, gy_in, gz_in, wexp, h2f, cotf, resid_i, cot_i, w_i, sw_i, tokf_i, qkv_i, kvf_i, lse_i, att_i,
    eg, y_b, y_s, g_s, pick_s, gated_s, hid_b, hid_s, gcd_b, gcd_s, gh2p, outp, zb, sb, xb, goy, gox, aout, bout,
    lout, igrad,
    send, recv, loc, goty, gotx, gety, getx, resid, cot, gres, gattn, dkvr, gh1g, dath, zg, xg, xgot, bgot, bxg,
    sw, sdw, db, ds,
):
    y, xl, co, xh, z = coords()
    i, c = xl * 2 + co, y * 4 + xl * 2 + co
    sib = dev(y, xl, 1 - co, xh, z)
    xpeer = dev(y, 1 - xl, co, xh, z)
    xfar = dev(y, xl, co, 1 - xh, z)
    ypeers = [dev((y + d) % 4, xl, co, xh, z) for d in Y_STEPS]
    zpeers = [dev(y, xl, co, xh, (z + d) % 4) for d in Y_STEPS]
    places = ctx_places(y, xl, co)
    cpeers = [dev(*p, xh, z) for p in places]
    xpeers = []
    for d in Y_STEPS:
        hh, ll = x_place(xh, xl, d)
        xpeers.append(dev(y, ll, co, hh, z))
    barrier(cpeers + [dev(y, k, co, 1 - xh, z) for k in range(2)] + zpeers)
    cp = Copies(send, recv)
    n_local = [0]

    def here(src, dst):
        copy = pltpu.make_async_copy(src, dst, loc.at[n_local[0]])
        n_local[0] += 1
        copy.start()
        return copy

    got_already, sent_already = [], []

    def arrive(copy):
        copy.wait_recv()
        got_already.append(copy)

    def gone(copies):
        for copy in copies:
            copy.wait_send()
            sent_already.append(copy)

    low, high = pl.ds(0, 64), pl.ds(64, 64)
    ynext, znext = [(y + d) % 4 for d in range(4)], [(z + d) % 4 for d in range(4)]
    xnext = [x_place(xh, xl, d) for d in range(4)]
    oco, oxl, oxh = 1 - co, 1 - xl, 1 - xh
    xh8, oxh8 = xh * 8, 8 - xh * 8
    place_index = [p[0] * 4 + p[1] * 2 + p[2] for p in places]
    kv_peers = [(a * 2 + b, dev(y, a, b, xh, z)) for a, b in ((oxl, co), (oxl, oco), (xl, oco))]
    front_cols, back_cols = pl.ds(0, 128), pl.ds(128, 128)
    mine_cols = pl.ds(pl.multiple_of(co * 128, 128), 128)
    first = [
        here(sw_i.at[:, front_cols], sw.at[:, front_cols]),
        here(sw_i.at[:, back_cols], sdw.at[:, front_cols]),
        here(resid_i, resid),
        here(cot_i, cot),
    ]
    pairs = pl.BlockSpec((1, 1, 2, 128, 1536), lambda p: (div(p, 2), rem(p, 2), 0, 0, 0))
    picks = pl.BlockSpec((1, 96, 256), lambda p: (p, 0, 0))

    def expert_copies(e):
        return [
            pltpu.make_async_remote_copy(
                eg.at[e, :, :, znext[d]],
                zb.at[k, e],
                send.at[e * 3 + k],
                recv.at[e * 3 + k],
                device_id=zpeers[k],
                device_id_type=MESH,
            )
            for k, d in enumerate(Y_STEPS)
        ]

    def expert_push(e):
        for copy in expert_copies(e):
            copy.start()

    def expert_rows(e, gg):
        return pltpu.make_async_remote_copy(
            gg.at[e], g_s.at[e], send.at[6 + e], recv.at[6 + e], device_id=sib, device_id_type=MESH
        )

    def expert_out(e, xy):
        return pltpu.make_async_remote_copy(
            xy.at[e], y_s.at[e], send.at[8 + e], recv.at[8 + e], device_id=sib, device_id_type=MESH
        )

    cp.n = 12
    early = [
        cp.start(sw_i.at[:, front_cols], sw.at[:, back_cols], sib),
        cp.start(sw_i.at[:, back_cols], sdw.at[:, back_cols], sib),
        cp.start(pick_in, pick_s, sib),
        cp.start(gated_in, gated_s, sib),
    ]
    for copy in first[:2]:
        copy.wait()

    ds[...] = jnp.zeros_like(ds)

    def hidden_rows(k):
        src, dst = ((gcd_b, gcd_s), (hid_b, hid_s))[k]
        return pltpu.make_async_remote_copy(
            src.at[:, oco], dst, send.at[10 + k], recv.at[10 + k], device_id=sib, device_id_type=MESH
        )

    def at8(own):
        return pl.ds(xh8 if own else oxh8, 8)

    blocks = pl.BlockSpec((1, 1, 128, 1536), lambda p: (div(p, 2), rem(p, 2), 0, 0))
    thin = pl.BlockSpec((1, 2, 128, 128), lambda p: (p, 0, 0, 0))

    def experts(xy, gg, dw):
        lg = here(gy_in, gg)

        def grads_copy(e):
            return pltpu.make_async_copy(dw, eg.at[e], loc.at[78 + e])

        def work(w, u_s, ga_s, gb_s):
            lw = [here(wexp.at[e], w.at[e]) for e in range(2)]

            def own_rows(pick_ref, h2_ref, gz_ref, hid_ref, gcd_ref):
                h2 = h2_ref[...].reshape(256, 1536)
                xy[:, xh8 + pl.program_id(0)] = nn(pick_ref[0], h2).astype(BF).reshape(2, 48, 1536)
                pre, gz = nn(h2, sw[:, 0:128]), gz_ref[0]
                act, slope = silu_parts(pre)
                up = half_turn(pre)
                lane = lax.broadcasted_iota(jnp.int32, (256, 128), 1)
                hid = jnp.where(lane < 64, act * up, 0.0).astype(BF)
                gcd = jnp.where(lane < 64, gz * up * slope, half_turn(gz * act)).astype(BF)
                hid_ref[0] = hid.reshape(2, 128, 128)
                gcd_ref[0] = gcd.reshape(2, 128, 128)
                ds[0:128] += tn(gcd, h2)

            def other_rows(pick_ref, h2_ref):
                x = nn(pick_ref[0], h2_ref[...].reshape(256, 1536)).astype(BF)
                xy[:, oxh8 + pl.program_id(0)] = x.reshape(2, 48, 1536)

            deep = pl.BlockSpec(
                (1, 1, 2, 128, 1536), lambda p: (div(p, 2), rem(p, 2), 0, 0, 0), pipeline_mode=pl.Buffered(4)
            )
            pltpu.emit_pipeline(
                own_rows,
                grid=(8,),
                in_specs=[picks, deep, pl.BlockSpec((1, 256, 128), lambda p: (p, 0, 0))],
                out_specs=[thin, thin],
            )(pick_in.at[at8(True)], h2f.at[xh], gz_in.at[at8(True)], hid_b, gcd_b)
            for e in range(2):
                hidden_rows(e).start()
            pltpu.emit_pipeline(other_rows, grid=(8,), in_specs=[picks, deep])(
                pick_in.at[at8(False)], h2f.at[oxh]
            )
            lg.wait()
            for e in range(2):
                lw[e].wait()
                for t in range(2):
                    cols = slice(t * 256, (t + 1) * 256)
                    x, g = xy[e].reshape(768, 1536), gg[e].reshape(768, 1536)
                    a = nn(x, w[e, 0, :, :, cols].reshape(1536, 256))
                    b = nn(x, w[e, 1, :, :, cols].reshape(1536, 256))
                    gu = nn(g, w[e, 2, :, :, cols].reshape(1536, 256))
                    act, slope = silu_parts(a)
                    u_s[:, cols] = (act * b).astype(BF)
                    ga_s[:, cols] = (gu * b * slope).astype(BF)
                    gb_s[:, cols] = (gu * act).astype(BF)
                if e:
                    grads_copy(0).wait()
                    expert_push(0)

                def row_tile(t, carry):
                    at = pl.ds(pl.multiple_of(t * 384, 384), 384)
                    two, h, half = pl.ds(t * 2, 2), div(t, 2), pl.ds(rem(t, 2) * 2, 2)
                    g = gg[e, :, :, at].reshape(768, 384)
                    dw[2, h, half] = tn(g, u_s[...]).astype(BF).reshape(2, 192, 512)
                    back = nt(ga_s[...], w[e, 0, two].reshape(384, 512))
                    back = back + nt(gb_s[...], w[e, 1, two].reshape(384, 512))
                    gg[e, :, :, at] = back.astype(BF).reshape(16, 48, 384)
                    return carry

                def tile(t, carry):
                    at = pl.ds(pl.multiple_of(t * 384, 384), 384)
                    two, h, half = pl.ds(t * 2, 2), div(t, 2), pl.ds(rem(t, 2) * 2, 2)
                    x = xy[e, :, :, at].reshape(768, 384)
                    dw[0, h, half] = tn(x, ga_s[...]).astype(BF).reshape(2, 192, 512)
                    dw[1, h, half] = tn(x, gb_s[...]).astype(BF).reshape(2, 192, 512)
                    out = nt(u_s[...], w[e, 2, two].reshape(384, 512))
                    xy[e, :, :, at] = out.astype(BF).reshape(16, 48, 384)
                    return carry

                lax.fori_loop(0, 4, row_tile, 0)
                expert_rows(e, gg).start()
                lax.fori_loop(0, 4, tile, 0)
                expert_out(e, xy).start()
                grads_copy(e).start()

        pl.run_scoped(
            work,
            pltpu.VMEM((2, 3, 8, 192, 512), BF),
            pltpu.VMEM((768, 512), BF),
            pltpu.VMEM((768, 512), BF),
            pltpu.VMEM((768, 512), BF),
        )
        ly = here(xy, y_b)
        for e in range(2):
            expert_rows(e, gg).wait()
            hidden_rows(e).wait()

        def row_sums(own):
            first_pair = xh8 if own else oxh8

            def body(pick_ref, other_ref, rows_ref, *refs):
                picks = jnp.concatenate([pick_ref[0, :, mine_cols], other_ref[0, :, mine_cols]], 0)
                here_rows = gg[:, first_pair + pl.program_id(0)].reshape(96, 1536)
                gh = tn(picks, jnp.concatenate([here_rows, rows_ref[...].reshape(96, 1536)], 0))
                if own:
                    gh = gh + nt(jnp.concatenate([refs[0][0, 0], refs[1][0]], 1), sw[...])
                refs[-1][...] = gh.astype(BF).reshape(1, 1, 128, 1536)

            rows = pl.BlockSpec((2, 1, 48, 1536), lambda p: (0, p, 0, 0))
            specs, args = [picks, picks, rows], [pick_in.at[at8(own)], pick_s.at[at8(own)], g_s.at[:, at8(own)]]
            if own:
                specs += [
                    pl.BlockSpec((1, 1, 128, 128), lambda p: (p, 0, 0, 0)),
                    pl.BlockSpec((1, 128, 128), lambda p: (p, 0, 0)),
                ]
                args += [gcd_b.at[:, pl.ds(co, 1)], gcd_s]
            pltpu.emit_pipeline(body, grid=(8,), in_specs=specs, out_specs=[blocks])(
                *args, gh2p.at[xh if own else oxh]
            )

        for copy in early:
            arrive(copy)
        row_sums(True)
        grads_copy(1).wait()
        expert_push(1)
        row_sums(False)
        ly.wait()
        for e in range(2):
            expert_out(e, xy).wait()

    pl.run_scoped(
        experts,
        pltpu.VMEM((2, 16, 48, 1536), BF),
        pltpu.VMEM((2, 16, 48, 1536), BF),
        pltpu.VMEM((3, 2, 4, 192, 512), BF),
    )

    def dense(
        miney, minex, w, tokf, qkv, kvf, lse, att, go, dk, dv, dkvs, gqkv, gh1s, da, zs, s2, s3, bz, bsum
    ):
        def sum_piece(xp, axis, d):
            if axis == "y":
                return xp.at[:, ynext[d], :, low]
            return xp.at[xnext[d][0], :, xnext[d][1], high]

        def sum_push(xp, toy, tox, steps):
            sent = {}
            for axis, d in steps:
                to, peers = (toy, ypeers) if axis == "y" else (tox, xpeers)
                sent[axis, d] = cp.start(sum_piece(xp, axis, d), to.at[d - 1], peers[d - 1])
            return sent

        def sum_own(xp):
            return [here(sum_piece(xp, "y", 0), miney.at[0]), here(sum_piece(xp, "x", 0), minex.at[0])]

        def sum_second():
            for h in range(2):
                for l in range(2):
                    tot = miney[0, h, l].astype(F32)
                    for k in range(3):
                        tot = tot + goty[k, h, l].astype(F32)
                    miney[0, h, l] = tot.astype(BF)
            for a in range(4):
                tot = minex[0, a].astype(F32)
                for k in range(3):
                    tot = tot + gotx[k, a].astype(F32)
                minex[0, a] = tot.astype(BF)

        def sum_last(nth):
            sent = []
            for k, d in enumerate(Y_STEPS):
                hh, ll = xnext[d]
                sent.append(cp.start(miney.at[0, hh, ll], gety.at[nth, k], xpeers[k]))
                sent.append(cp.start(minex.at[0, ynext[d]], getx.at[nth, k], ypeers[k]))
            return sent

        def sum_end(nth, sent):
            for copy in sent:
                arrive(copy)
            top, bottom = miney[0, xh, xl].astype(F32), minex[0, y].astype(F32)
            for k in range(3):
                top = top + gety[nth, k].astype(F32)
                bottom = bottom + getx[nth, k].astype(F32)
            return jnp.concatenate([top, bottom], 0)

        both = [("y", 1), ("x", 1), ("y", 3), ("x", 3), ("y", 2), ("x", 2)]
        sent_g = sum_push(gh2p, goty, gotx, both)
        own_g = sum_own(gh2p)
        first.append(here(w_i, w))
        second = [here(qkv_i, qkv), here(kvf_i, kvf), here(lse_i, lse), here(att_i, att)]
        third = [here(tokf_i, tokf)]
        for copy in first[2:]:
            copy.wait()


        def output_rows(own):
            def body(pick_ref, other_ref, rows_ref, more_ref, *refs):
                picks = jnp.concatenate([pick_ref[0, :, mine_cols], other_ref[0, :, mine_cols]], 0)
                rows = [rows_ref[...].reshape(96, 1536), more_ref[...].reshape(96, 1536)]
                out = tn(picks, jnp.concatenate(rows, 0))
                if own:
                    out = out + nt(jnp.concatenate([refs[0][0, 0], refs[1][0]], 1), sdw[...])
                refs[-1][...] = out.astype(BF).reshape(1, 1, 128, 1536)

            at = at8(own)
            rows = pl.BlockSpec((2, 1, 48, 1536), lambda p: (0, p, 0, 0))
            specs = [picks, picks, rows, rows]
            args = [gated_in.at[at], gated_s.at[at], y_b.at[:, at], y_s.at[:, at]]
            if own:
                specs += [
                    pl.BlockSpec((1, 1, 128, 128), lambda p: (p, 0, 0, 0)),
                    pl.BlockSpec((1, 128, 128), lambda p: (p, 0, 0)),
                ]
                args += [hid_b.at[:, pl.ds(co, 1)], hid_s]
            pltpu.emit_pipeline(body, grid=(8,), in_specs=specs, out_specs=[blocks])(
                *args, outp.at[xh if own else oxh]
            )

        output_rows(True)
        output_rows(False)

        def down_rows(cot_ref, hid_ref):
            ds[128:256] += tn(hid_ref[0].reshape(256, 128), cot_ref[...].reshape(256, 1536))

        pltpu.emit_pipeline(down_rows, grid=(8,), in_specs=[pairs, thin])(cotf.at[xh], hid_b)
        rows = one_hot_rows()
        shared_grads = tn(ds[...].astype(BF), eye(256, 256)).astype(BF)
        for k in range(16):
            block = shared_grads[k * 96 : (k + 1) * 96]
            db[k] = tn(rows, block).astype(BF).reshape(2, 4, 16, 256)
        bs = [cp.start(db.at[:, :, znext[d]], bgot.at[k], p) for k, (d, p) in enumerate(zip(Y_STEPS, zpeers))]

        gains = nt(eye_rows(), w[:, 640:768])
        gain_one, gain_two = gains[0:1], gains[1:2]
        inv = inverse_norm(resid[...])
        xh2 = resid[...] * inv
        for copy in list(sent_g.values()):
            arrive(copy)
        for copy in own_g:
            copy.wait()
        sum_second()
        last_g = sum_last(0)
        gh2 = sum_end(0, last_g)
        gain_two_grad = jnp.sum(gh2 * xh2, 0, keepdims=True)
        inner = gh2 * gain_two
        row = inv * (inner - xh2 * jnp.mean(inner * xh2, -1, keepdims=True))
        gres[...] = cot[...].astype(F32) + row
        gattn[y] = gres[...].astype(BF)
        ga = [cp.start(gattn.at[y], gattn.at[y], p) for p in ypeers]

        gone(list(sent_g.values()) + last_g)
        sent_o = sum_push(outp, goy, gox, both[:5])
        own_o = sum_own(outp)

        def expert_sums(e):
            for copy in expert_copies(e):
                copy.wait()
            ins = [eg.at[e, :, :, z], zb.at[0, e], zb.at[1, e], zb.at[2, e]]
            add_arrays((2, 96, 512), ins, sb.at[e])

        def expert_far(e):
            return cp.start(sb.at[e, :, oxh], xb.at[e], xfar)

        expert_sums(0)
        ex0 = expert_far(0)

        for copy in second:
            copy.wait()
        for copy in ga:
            arrive(copy)
        dk[...] = jnp.zeros_like(dk)
        dv[...] = jnp.zeros_like(dv)
        for j in range(4):
            rows_j = slice(j * 128, (j + 1) * 128)
            go[rows_j] = nn(gattn[j], w[:, 768:1152]).astype(BF)
            q, g = head_rows(qkv, j), head_rows(go, j)
            delta = jnp.sum(head_rows(att, j).astype(F32) * g.astype(F32), -1, keepdims=True)
            total = lse[j][:, :1]
            dq = jnp.zeros((384, 128), F32)
            for t in range(j + 1):
                keys = kvf[t].reshape(512, 256)
                s = nt(q, keys[:, :128]) * SCALE
                p = jnp.exp(s - total)
                if t == j:
                    p = jnp.where(allowed(512), p, 0.0)
                gs = (p * (nt(g, keys[:, 128:]) - delta)).astype(BF)
                at = slice(t * 512, (t + 1) * 512)
                dv[at] += tn(p.astype(BF), g)
                dk[at] += tn(gs, q)
                dq = dq + nn(gs, keys[:, :128])
            dq = (dq * SCALE).astype(BF)
            for h in range(3):
                gqkv[rows_j, h * 128 : (h + 1) * 128] = dq[h * 128 : (h + 1) * 128]
        for j in range(4):
            for k in range(4):
                at = slice((j * 4 + k) * 128, (j * 4 + k + 1) * 128)
                dkvs[j, k, :, 0:128] = (dk[at] * SCALE).astype(BF)
                dkvs[j, k, :, 128:256] = dv[at].astype(BF)
        kvs = [
            cp.start(dkvs.at[:, p], dkvr.at[k], q)
            for k, (p, q) in enumerate(kv_peers)
        ]
        sent_o.update(sum_push(outp, goy, gox, both[5:]))
        def expand(block, yy, cols):
            for k in range(4):
                part = tn(rows, block[k * 96 : (k + 1) * 96]).astype(BF)
                da[yy, k // 2, k % 2, :, :, :, cols] = part.reshape(2, 4, 16, -1)

        def dense_core(cols):
            return cp.start(da.at[:, :, oco, :, :, :, cols], dath.at[:, :, :, :, :, cols], sib)

        def dense_z(copy, cols):
            arrive(copy)
            for a in range(4):
                for b in range(2):
                    tot = da[a, b, co, :, :, :, cols].astype(F32) + dath[a, b, :, :, :, cols].astype(F32)
                    da[a, b, co, :, :, :, cols] = tot.astype(BF)
            return [
                cp.start(da.at[:, :, co, :, znext[d], :, cols], zg.at[k, :, :, :, :, cols], p)
                for k, (d, p) in enumerate(zip(Y_STEPS, zpeers))
            ]

        def dense_far(copies, cols):
            for copy in copies:
                arrive(copy)
            for a in range(4):
                for b in range(2):
                    tot = da[a, b, co, :, z, :, cols].astype(F32)
                    for k in range(3):
                        tot = tot + zg[k, a, b, :, :, cols].astype(F32)
                    for h in range(2):
                        zs[h, a, b, :, cols] = tot[h].astype(BF)
            return cp.start(zs.at[oxh, :, :, :, cols], xg.at[:, :, :, cols], xfar)

        def dense_near(copy, cols):
            arrive(copy)
            for a in range(4):
                for b in range(2):
                    tot = zs[xh, a, b, :, cols].astype(F32) + xg[a, b, :, cols].astype(F32)
                    s2[b, a, :, cols] = tot.astype(BF)
            return cp.start(s2.at[oxl, :, :, cols], xgot.at[:, :, cols], xpeer)

        def dense_y(copy, cols):
            arrive(copy)
            for a in range(4):
                s3[a, :, cols] = (s2[xl, a, :, cols].astype(F32) + xgot[a, :, cols].astype(F32)).astype(BF)
            last.append(here(s3.at[y, :, cols], aout.at[y, :, cols]))
            return [
                cp.start(s3.at[ynext[d], :, cols], aout.at[y, :, cols], p) for d, p in zip(Y_STEPS, ypeers)
            ]

        head, tail = pl.ds(0, 768), pl.ds(768, 384)
        last = []
        for yy in range(4):
            tile = slice(yy * 384, (yy + 1) * 384)
            block = tn(gattn[:, :, tile].reshape(512, 384), att[...])
            expand(block.astype(BF), yy, tail)
        tail_c = dense_core(tail)
        expert_sums(1)
        ex1 = expert_far(1)

        tail_z = dense_z(tail_c, tail)
        for copy in third:
            copy.wait()
        for copy in kvs:
            arrive(copy)
        gone(ga)
        gain_one_grad = jnp.zeros((1, 1536), F32)
        for j in range(4):
            rows_j = slice(j * 128, (j + 1) * 128)
            kv = dkvs[j, i].astype(F32)
            for k in range(3):
                kv = kv + dkvr[k, j].astype(F32)
            gqkv[rows_j, 384:640] = kv.astype(BF)
            gh1 = nt(gqkv[rows_j], w[:, :640])
            v = tokf[j].astype(F32)
            scaled = v * inverse_norm(v)
            gain_one_grad = gain_one_grad + jnp.sum(gh1 * scaled, 0, keepdims=True)
            gattn[j] = (scaled * gain_one).astype(BF)
            gh1s[j] = gh1.astype(BF)
        hs = [
            cp.start(gh1s.at[ynext[d]], gh1g.at[k], p) for k, (d, p) in enumerate(zip(Y_STEPS, ypeers))
        ]
        gain_rows = jnp.concatenate([gain_one_grad, gain_two_grad, jnp.zeros((6, 1536), F32)], 0)
        for yy in range(4):
            tile = slice(yy * 384, (yy + 1) * 384)
            block = tn(gattn[:, :, tile].reshape(512, 384), gqkv[...])
            expand(block.astype(BF), yy, pl.ds(0, 640))
            expand(tn(gain_rows[:, tile].astype(BF), eye_rows()).astype(BF), yy, pl.ds(640, 128))
        head_c = dense_core(head)
        head_z = dense_z(head_c, head)

        tail_x = dense_far(tail_z, tail)
        for copy in bs:
            arrive(copy)
        for a in range(16):
            tot = db[a, :, z].astype(F32)
            for k in range(3):
                tot = tot + bgot[k, a].astype(F32)
            bz[0, a], bz[1, a] = tot[0].astype(BF), tot[1].astype(BF)
        bx = cp.start(bz.at[oxh], bxg, xfar)

        for copy in sent_o.values():
            arrive(copy)
        back_in = [here(goy, goty), here(gox, gotx)]
        for copy in back_in + own_o:
            copy.wait()
        gone(list(sent_o.values()))
        sum_second()
        last_o = sum_last(1)
        head_x = dense_far(head_z, head)
        gh1 = gh1s[y].astype(F32)
        for k, copy in enumerate(hs):
            arrive(copy)
            gh1 = gh1 + gh1g[k].astype(F32)
        v = tokf[y].astype(F32)
        inv = inverse_norm(v)
        inner = gh1 * gain_one
        xh1 = v * inv
        igrad[...] = gres[...] + inv * (inner - xh1 * jnp.mean(inner * xh1, -1, keepdims=True))
        lout[...] = (resid[...] + sum_end(1, last_o)).astype(BF)

        tail_n = dense_near(tail_x, tail)
        arrive(bx)
        for a in range(16):
            bsum[a] = (bz[xh, a].astype(F32) + bxg[a].astype(F32)).astype(BF)
        bo = [cp.start(bsum.at[p], bout.at[c], q) for p, q in zip(place_index, cpeers)]
        last.append(here(bsum.at[c], bout.at[c]))
        head_n = dense_near(head_x, head)
        outs = dense_y(tail_n, tail) + dense_y(head_n, head)

        for copy in last:
            copy.wait()
        for copy in cp.started:
            if not any(copy is r for r in sent_already):
                copy.wait_send()
            if not any(copy is r for r in got_already):
                copy.wait_recv()

    pl.run_scoped(
        dense,
        pltpu.VMEM((1, 2, 2, 64, 1536), BF),
        pltpu.VMEM((1, 4, 64, 1536), BF),
        pltpu.VMEM((1536, 1152), BF),
        pltpu.VMEM((4, 128, 1536), BF),
        pltpu.VMEM((512, 640), BF),
        pltpu.VMEM((4, 4, 128, 256), BF),
        pltpu.VMEM((4, 384, 128), F32),
        pltpu.VMEM((512, 384), BF),
        pltpu.VMEM((512, 384), BF),
        pltpu.VMEM((2048, 128), F32),
        pltpu.VMEM((2048, 128), F32),
        pltpu.VMEM((4, 4, 128, 256), BF),
        pltpu.VMEM((512, 640), BF),
        pltpu.VMEM((4, 128, 1536), BF),
        pltpu.VMEM((4, 2, 2, 2, 4, 16, 1152), BF),
        pltpu.VMEM((2, 4, 2, 16, 1152), BF),
        pltpu.VMEM((2, 4, 16, 1152), BF),
        pltpu.VMEM((4, 16, 1152), BF),
        pltpu.VMEM((2, 16, 16, 256), BF),
        pltpu.VMEM((16, 16, 256), BF),
    )


def back(*ins):
    outs = (
        SDS((2, 3, 2, 4, 192, 512), BF),
        SDS((2, 16, 48, 1536), BF),
        SDS((2, 16, 48, 1536), BF),
        SDS((2, 16, 48, 1536), BF),
        SDS((16, 96, 256), BF),
        SDS((16, 96, 256), BF),
        SDS((8, 2, 128, 128), BF),
        SDS((8, 128, 128), BF),
        SDS((8, 2, 128, 128), BF),
        SDS((8, 128, 128), BF),
        SDS((2, 4, 2, 128, 1536), BF),
        SDS((2, 4, 2, 128, 1536), BF),
        SDS((3, 2, 3, 2, 192, 512), BF),
        SDS((2, 3, 2, 192, 512), BF),
        SDS((2, 3, 192, 512), BF),
        SDS((3, 2, 2, 64, 1536), BF),
        SDS((3, 4, 64, 1536), BF),
        SDS((4, 16, 1152), BF),
        SDS((16, 16, 256), BF),
        SDS((128, 1536), BF),
        SDS((128, 1536), F32),
    )
    out = pl.pallas_call(
        back_kernel,
        out_shape=outs,
        in_specs=[ANY] * len(ins),
        out_specs=(ANY,) * 19 + (VM,) * 2,
        scratch_shapes=[
            pltpu.SemaphoreType.DMA((112,)),
            pltpu.SemaphoreType.DMA((112,)),
            pltpu.SemaphoreType.DMA((80,)),
            pltpu.VMEM((3, 2, 2, 64, 1536), BF),
            pltpu.VMEM((3, 4, 64, 1536), BF),
            pltpu.VMEM((2, 3, 64, 1536), BF),
            pltpu.VMEM((2, 3, 64, 1536), BF),
            pltpu.VMEM((128, 1536), F32),
            pltpu.VMEM((128, 1536), BF),
            pltpu.VMEM((128, 1536), F32),
            pltpu.VMEM((4, 128, 1536), BF),
            pltpu.VMEM((3, 4, 128, 256), BF),
            pltpu.VMEM((3, 128, 1536), BF),
            pltpu.VMEM((4, 2, 2, 4, 16, 1152), BF),
            pltpu.VMEM((3, 4, 2, 2, 16, 1152), BF),
            pltpu.VMEM((4, 2, 16, 1152), BF),
            pltpu.VMEM((4, 16, 1152), BF),
            pltpu.VMEM((3, 16, 2, 16, 256), BF),
            pltpu.VMEM((16, 16, 256), BF),
            pltpu.VMEM((1536, 256), BF),
            pltpu.VMEM((1536, 256), BF),
            pltpu.VMEM((16, 2, 4, 16, 256), BF),
            pltpu.VMEM((256, 1536), F32),
        ],
        compiler_params=pltpu.CompilerParams(
            collective_id=2, has_side_effects=True, vmem_limit_bytes=62 * 2**20
        ),
        cost_estimate=pl.CostEstimate(flops=36 * 10**9, bytes_accessed=150 * 10**6, transcendentals=5 * 10**6),
    )(*ins)
    return out[19], out[20], out[17], out[18], out[13], out[14]


def unpack_kernel(
    lout, igrad, aout, bout, sb, xb,
    lout_o, igrad_o, gains_o, wq_o, wk_o, wv_o, wo_o, sg_o, su_o, sd_o, eg_o, eu_o, ed_o,
):
    xh = lax.axis_index("fsdp") // 4
    lout_o[...] = lout[...]
    igrad_o[...] = igrad[...]
    for e in range(2):
        for m, ref in enumerate((eg_o, eu_o, ed_o)):
            ref[xh * 2 + e] = sb[e, m, xh].astype(F32)
            ref[2 - xh * 2 + e] = xb[e, m].astype(F32)
    gain_sum = jnp.zeros((16, 128), F32)
    for k in range(4):
        wide, thin = slice(k * 384, (k + 1) * 384), slice(k * 128, (k + 1) * 128)
        block = aout[k].astype(F32)
        wq_o[:, wide] = block[:12, 0:384]
        wk_o[:, thin] = block[:12, 384:512]
        wv_o[:, thin] = block[:12, 512:640]
        gain_sum = gain_sum + block[:, 640:768]
        wo_o[:, wide] = block[:12, 768:1152]
    gains_o[...] = gain_sum
    front_half = lax.broadcasted_iota(jnp.int32, (16, 128), 1) < 64
    for k in range(8):
        at = slice(k * 128, (k + 1) * 128)
        one, two = bout[2 * k].astype(F32), bout[2 * k + 1].astype(F32)
        sg_o[:, at] = jnp.where(front_half, one[:, :128], half_turn(two[:, :128]))[:12]
        su_o[:, at] = jnp.where(front_half, half_turn(one[:, :128]), two[:, :128])[:12]
        sd_o[:, at] = jnp.where(front_half, one[:, 128:], half_turn(two[:, 128:]))[:12]


def unpack(*ins):
    outs = (
        SDS((128, 1536), BF),
        SDS((128, 1536), F32),
        SDS((16, 128), F32),
        SDS((12, 1536), F32),
        SDS((12, 512), F32),
        SDS((12, 512), F32),
        SDS((12, 1536), F32),
        SDS((12, 1024), F32),
        SDS((12, 1024), F32),
        SDS((12, 1024), F32),
        SDS((4, 192, 512), F32),
        SDS((4, 192, 512), F32),
        SDS((4, 192, 512), F32),
    )
    return pl.pallas_call(
        unpack_kernel,
        out_shape=outs,
        in_specs=[VM] * len(ins),
        out_specs=(VM,) * len(outs),
        compiler_params=pltpu.CompilerParams(vmem_limit_bytes=VMEM_LIMIT),
    )(*ins)


def local(
    tokens,
    cotangent,
    routes,
    gates,
    attn_gain,
    ffn_gain,
    w_query,
    w_key,
    w_value,
    w_out,
    shared_gate,
    shared_up,
    shared_down,
    expert_gate,
    expert_up,
    expert_down,
):
    tok = tokens.reshape(128, 1536)
    cot = cotangent.reshape(128, 1536)
    gains = jnp.stack([attn_gain, ffn_gain])
    (cot_f, h2_f, wexp, tok_f, kv_f, gy, pick, gated, gz, _, w, sw, qkv, att, lse, resid) = front(
        tok,
        cot,
        jnp.transpose(routes, (2, 0, 1)),
        jnp.transpose(gates, (2, 0, 1)),
        gains,
        w_query,
        w_key,
        w_value,
        w_out.T,
        shared_gate,
        shared_up,
        shared_down.T,
        expert_gate,
        expert_up,
        jnp.transpose(expert_down, (0, 2, 1)),
    )
    parts = back(
        pick, gated, gy, gz, wexp, h2_f, cot_f, resid, cot, w, sw, tok_f, qkv, kv_f, lse, att
    )
    (layer_out, input_grad, gain_grads, wq, wk, wv, wo, sg, su, sd, eg, eu, ed) = unpack(*parts)
    return (
        layer_out.reshape(1, 128, 1536),
        input_grad.reshape(1, 128, 1536),
        gain_grads[:12, 0],
        gain_grads[:12, 1],
        wq,
        wk,
        wv,
        wo.T,
        sg,
        su,
        sd.T,
        eg,
        eu,
        jnp.transpose(ed, (0, 2, 1)),
    )


def solution(mesh):
    both = ("ctx", "fsdp")
    rows = P("fsdp", "ctx", None)
    weights = (P(both),) * 2 + (P(both, None),) * 3 + (P(None, both),)
    weights = weights + (P(both, None),) * 2 + (P(None, both),)
    weights = weights + (P("ctx", "fsdp", None),) * 2 + (P("ctx", None, "fsdp"),)
    return jax.shard_map(
        local, mesh=mesh, in_specs=(rows,) * 4 + weights, out_specs=(rows,) * 2 + weights, check_vma=False
    )
```

```python
import jax
import jax.numpy as jnp
from jax import lax
from jax.experimental import pallas as pl
from jax.experimental.pallas import tpu as pltpu
from jax.sharding import PartitionSpec as P

BF = jnp.bfloat16
F32 = jnp.float32
EPS = 1e-05
MESH = pl.DeviceIdType.MESH
ANY = pl.BlockSpec(memory_space=pl.ANY)
VM = pl.BlockSpec(memory_space=pltpu.VMEM)
SDS = jax.ShapeDtypeStruct
SCALE = 128 ** (-0.5)
VMEM_LIMIT = 56 * 2**20


def div(x, n):
    return lax.div(x, lax.full_like(x, n))


def rem(x, n):
    return lax.rem(x, lax.full_like(x, n))


def nn(a, b):
    return lax.dot_general(a, b, (((1,), (0,)), ((), ())), preferred_element_type=F32)


def nt(a, b):
    return lax.dot_general(a, b, (((1,), (1,)), ((), ())), preferred_element_type=F32)


def tn(a, b):
    return lax.dot_general(a, b, (((0,), (0,)), ((), ())), preferred_element_type=F32)


def silu_parts(pre_act):
    sig = 1.0 / (1.0 + jnp.exp(-pre_act))
    return pre_act * sig, sig * (1.0 + pre_act * (1.0 - sig))


def coords():
    c = lax.axis_index("ctx")
    f = lax.axis_index("fsdp")
    return c // 4, (c // 2) % 2, c % 2, f // 4, f % 4


def dev(y, xl, co, xh, z):
    return (y * 4 + xl * 2 + co, xh * 4 + z)


def barrier(peers):
    sem = pltpu.get_barrier_semaphore()
    for peer in peers:
        pl.semaphore_signal(sem, inc=1, device_id=peer, device_id_type=MESH)
    pl.semaphore_wait(sem, len(peers))


class Copies:
    def __init__(self, send, recv):
        self.send, self.recv, self.n, self.started = send, recv, 0, []

    def start(self, src, dst, peer):
        copy = pltpu.make_async_remote_copy(
            src, dst, self.send.at[self.n], self.recv.at[self.n], device_id=peer, device_id_type=MESH
        )
        copy.start()
        self.n += 1
        self.started.append(copy)
        return copy

    def finish(self, received=()):
        for copy in self.started:
            copy.wait_send()
            if not any(copy is r for r in received):
                copy.wait_recv()


Y_STEPS = (1, 2, 3)


def one_hot_rows():
    row = lax.broadcasted_iota(jnp.int32, (96, 128), 0)
    col = lax.broadcasted_iota(jnp.int32, (96, 128), 1)
    return jnp.where(div(row, 12) * 16 + rem(row, 12) == col, 1.0, 0.0).astype(BF)


def eye_rows():
    row = lax.broadcasted_iota(jnp.int32, (8, 128), 0)
    col = lax.broadcasted_iota(jnp.int32, (8, 128), 1)
    return jnp.where(row == col, 1.0, 0.0).astype(BF)


def inverse_norm(values):
    return lax.rsqrt(jnp.mean(values * values, -1, keepdims=True) + EPS)


def head_rows(ref, j, first=0):
    rows = slice(j * 128, (j + 1) * 128)
    return jnp.concatenate([ref[rows, first + h * 128 : first + (h + 1) * 128] for h in range(3)], 0)


def allowed(n):
    i = rem(lax.axis_index("ctx"), 4)
    row = rem(lax.broadcasted_iota(jnp.int32, (384, n), 0), 128)
    col = lax.broadcasted_iota(jnp.int32, (384, n), 1)
    return col <= i * 128 + row


def ctx_places(y, xl, co):
    return [
        ((y + dy) % 4, (xl + dx) % 2, (co + dc) % 2)
        for dy in range(4)
        for dx in (0, 1)
        for dc in (0, 1)
        if (dy, dx, dc) != (0, 0, 0)
    ]


def x_place(xh, xl, d):
    x = (xh * 2 + xl + d) % 4
    return x // 2, x % 2


def plane_gather(cp, arrive, src, out, places, sib, split):
    y, xl, co, xh, z = places
    low, high = pl.ds(0, split), pl.ds(split, 128 - split)
    ypeers = [dev((y + d) % 4, xl, co, xh, z) for d in Y_STEPS]
    xpeers = []
    for d in Y_STEPS:
        h, l = x_place(xh, xl, d)
        xpeers.append(dev(y, l, co, h, z))
    mine = (xh, y, xl, co)

    def first_y():
        return [cp.start(src.at[high], out.at[mine + (high,)], p) for p in ypeers]

    def first_x():
        return [cp.start(src.at[low], out.at[mine + (low,)], p) for p in xpeers]

    def piece_y(d):
        return out.at[:, (y + d) % 4, :, co, low]

    def piece_x(d):
        h, l = x_place(xh, xl, d)
        return out.at[h, :, l, co, high]

    def half_y(d, n):
        return out.at[n, (y + d) % 4, :, co, low]

    def half_x(d, n):
        h, l = x_place(xh, xl, d)
        return out.at[h, pl.ds(2 * n, 2), l, co, high]

    def then(firsts, piece, peers):
        for copy in firsts:
            arrive(copy)
        return [
            cp.start(piece(0), piece(0), peers[0]),
            cp.start(piece(0), piece(0), peers[2]),
            cp.start(piece(0), piece(0), sib),
        ]

    def middle(seconds, piece, half, peers):
        arrive(seconds[0])
        one = cp.start(half(3, 0), half(3, 0), peers[0])
        arrive(seconds[1])
        two = cp.start(half(1, 1), half(1, 1), peers[2])
        sibs = [cp.start(piece(d), piece(d), sib) for d in (3, 1)]
        return [one, two] + sibs

    def last(middles, piece):
        for copy in middles[:2]:
            arrive(copy)
        return middles[2:] + [cp.start(piece(2), piece(2), sib)]

    def then_y(firsts):
        return then(firsts, piece_y, ypeers)

    def then_x(firsts):
        return then(firsts, piece_x, xpeers)

    def middle_y(seconds):
        return middle(seconds, piece_y, half_y, ypeers)

    def middle_x(seconds):
        return middle(seconds, piece_x, half_x, xpeers)

    def last_y(middles):
        return last(middles, piece_y)

    def last_x(middles):
        return last(middles, piece_x)

    return (first_y, then_y, middle_y, last_y), (first_x, then_x, middle_x, last_x)


def dispatch_rows(rg, first):
    masks, gates = [], []
    for e in range(2):
        ms, gs = [], []
        for s in range(2):
            hit = jnp.where(rg[s, 0:6] == (first + e).astype(F32), 1.0, 0.0)
            ms.append(jnp.sum(hit, 0, keepdims=True))
            gs.append(jnp.sum(hit * rg[s, 8:14], 0, keepdims=True))
        masks.append(jnp.concatenate(ms, 1))
        gates.append(jnp.concatenate(gs, 1))
    mask = jnp.concatenate(masks + [jnp.zeros((6, 256), F32)], 0)
    before = lax.broadcasted_iota(jnp.int32, (256, 256), 0)
    after = lax.broadcasted_iota(jnp.int32, (256, 256), 1)
    tri = jnp.where((before <= after) & (before // 128 == after // 128), 1.0, 0.0).astype(BF)
    place = nn(mask.astype(BF), tri) - 1.0
    lane = lax.broadcasted_iota(jnp.int32, (1, 256), 1)
    slot = lax.broadcasted_iota(jnp.int32, (48, 256), 0).astype(F32)
    picks, gated = [], []
    for e in range(2):
        at = place[e : e + 1] + jnp.where(lane >= 128, 24.0, 0.0)
        at = jnp.where(masks[e] > 0.0, at, -1.0)
        hit = jnp.where(slot == at, 1.0, 0.0)
        picks.append(hit)
        gated.append(hit * gates[e])
    return jnp.concatenate(picks, 0).astype(BF), jnp.concatenate(gated, 0).astype(BF)


def eye(rows, cols):
    row = lax.broadcasted_iota(jnp.int32, (rows, cols), 0)
    col = lax.broadcasted_iota(jnp.int32, (rows, cols), 1)
    return jnp.where(row == col, 1.0, 0.0).astype(BF)


def half_turn(x):
    return pltpu.roll(x, 64, 1)


def front_kernel(
    tok, cot, routes, gates, gains_in, wq, wk, wv, wo, sg, su, sd, eg, eu, ed,
    cotf, h2f, wexp, tokf_o, kvf_o, gy, pick_o, gated_o, gz_o, rgf,
    w_o, sw_o, qkv_o, att_o, lse_o, resid_o,
    send, recv, loc, w, sw, qkv, att, lse, resid, a_s, b_s, own, rg_s, a2, wf, b1, bf, tokf, kvf, s_s, part, got, h2,
):
    y, xl, co, xh, z = coords()
    i, c, f = xl * 2 + co, y * 4 + xl * 2 + co, xh * 4 + z
    f_far = (1 - xh) * 4 + z
    sib = dev(y, xl, 1 - co, xh, z)
    xpeer = dev(y, 1 - xl, co, xh, z)
    xfar = dev(y, xl, co, 1 - xh, z)
    ypeers = [dev((y + d) % 4, xl, co, xh, z) for d in Y_STEPS]
    zpeers = [dev(y, xl, co, xh, (z + d) % 4) for d in Y_STEPS]
    places = ctx_places(y, xl, co)
    cpeers = [dev(*p, xh, z) for p in places]
    plane = cpeers + [dev(*p, 1 - xh, z) for p in places + [(y, xl, co)]]
    peers = plane + zpeers
    sem = pltpu.get_barrier_semaphore()
    for peer in peers:
        pl.semaphore_signal(sem, inc=1, device_id=peer, device_id_type=MESH)

    e16 = eye(16, 12)
    q16, k16, v16 = (nn(e16, ref[...]).astype(BF) for ref in (wq, wk, wv))
    o16 = nn(e16, wo[...]).astype(BF)
    gain_rows = nn(eye(128, 2), gains_in[...]).astype(BF)
    gain16 = nt(e16, gain_rows).astype(BF)
    for k in range(4):
        wide, thin = slice(k * 384, (k + 1) * 384), slice(k * 128, (k + 1) * 128)
        a_s[k] = jnp.concatenate([q16[:, wide], k16[:, thin], v16[:, thin], gain16, o16[:, wide]], 1)
    pl.semaphore_wait(sem, len(peers))

    cp = Copies(send, recv)
    n_local = [0]

    def here(src, dst):
        copy = pltpu.make_async_copy(src, dst, loc.at[n_local[0]])
        n_local[0] += 1
        copy.start()
        return copy

    got_already = []

    def arrive(copy):
        copy.wait_recv()
        got_already.append(copy)

    me = (y, xl, co, xh, z)
    ya = [cp.start(a_s.at[(y + d) % 4], a2.at[y, xl], p) for d, p in zip(Y_STEPS, ypeers)]
    la = here(a_s.at[y], a2.at[y, xl])
    lt = here(tok, tokf.at[y])
    owns = [here(ref, own.at[:, k]) for k, ref in enumerate((eg, eu, ed))]
    own_cot = here(cot, cotf.at[xh, y, xl, co])
    over_y, over_x = plane_gather(cp, arrive, cot, cotf, me, sib, 80)
    cot_y, cot_then_y, cot_middle_y, cot_last_y = over_y
    cot_x, cot_then_x, cot_middle_x, cot_last_x = over_x
    yt = [cp.start(tok, tokf.at[y], p) for p in ypeers]
    cy = cot_y()
    g16, u16, d16 = nn(e16, sg[...]), nn(e16, su[...]), nn(e16, sd[...])
    front_half = lax.broadcasted_iota(jnp.int32, (16, 128), 1) < 64
    for k in range(8):
        at = slice(k * 128, (k + 1) * 128)
        g, u, d = g16[:, at], u16[:, at], d16[:, at]
        for n in range(2):
            if n:
                g, d = half_turn(g), half_turn(d)
            else:
                u = half_turn(u)
            b_s[2 * k + n, :, 0:128] = jnp.where(front_half, g, u).astype(BF)
            b_s[2 * k + n, :, 128:256] = jnp.where(front_half, d, 0.0).astype(BF)
            if not n:
                u = half_turn(u)
    rg_s[...] = jnp.zeros_like(rg_s)
    for k in range(6):
        rg_s[k : k + 1] = routes[k].astype(F32)
        rg_s[8 + k : 9 + k] = gates[k]
    lb = here(b_s.at[c], b1.at[c])
    lr = here(rg_s, rgf.at[xh, c])
    for copy in owns:
        copy.wait()
    later = [here(own.at[pl.ds(xh * 2, 2)], wexp.at[:, :, f])]
    la.wait()
    for copy in ya:
        arrive(copy)
    xa = cp.start(a2.at[:, xl], a2.at[:, xl], xpeer)
    bs = [cp.start(b_s.at[p[0] * 4 + p[1] * 2 + p[2]], b1.at[c], q) for p, q in zip(places, cpeers)]
    rgs = [cp.start(rg_s, rgf.at[xh, c], q) for q in plane]
    arrive(xa)

    head, tail = pl.ds(0, 768), pl.ds(768, 384)

    def slices(cols):
        return a2.at[:, :, :, cols], wf.at[:, :, co, f, :, cols], wf.at[:, :, co, f_far, :, cols]

    src, mine, far = slices(head)
    hx = cp.start(src, mine, xfar)
    hz = [cp.start(src, mine, p) for p in zpeers]
    lw = here(a2, wf.at[:, :, co, f])
    cx = cot_x()
    src_t, mine_t, far_t = slices(tail)
    tx = cp.start(src_t, mine_t, xfar)
    lw.wait()
    to_sib = [cp.start(mine, mine, sib)]
    arrive(hx)
    hz2 = [cp.start(far, far, p) for p in zpeers]
    to_sib.append(cp.start(far, far, sib))
    tz = [cp.start(src_t, mine_t, p) for p in zpeers]
    for copies, h in ((hz, xh), (hz2, 1 - xh)):
        for d, copy in zip(Y_STEPS, copies):
            arrive(copy)
            piece = wf.at[:, :, co, h * 4 + (z + 4 - d) % 4, :, head]
            to_sib.append(cp.start(piece, piece, sib))
    own_cot.wait()
    cy2 = cot_then_y(cx)
    arrive(tx)
    tz2 = [cp.start(far_t, far_t, p) for p in zpeers]
    tail_sib = [cp.start(mine_t, mine_t, sib), cp.start(far_t, far_t, sib)]
    own_z = [cp.start(own.at[pl.ds(xh * 2, 2)], wexp.at[:, :, f], zpeers[k]) for k in (0, 2)]
    lb.wait()
    for copy in bs:
        arrive(copy)
    bx = cp.start(b1, bf.at[:, f], xfar)
    bz = [cp.start(b1, bf.at[:, f], p) for p in zpeers]
    lb = here(b1, bf.at[:, f])
    for copy in to_sib:
        arrive(copy)
    rows = one_hot_rows()

    def compact(cols):
        for yy in range(4):
            for k in range(4):
                at = (yy * 4 + k) * 96
                block = wf[yy, k // 2, k % 2, :, :, cols].reshape(128, -1)
                w[at : at + 96, cols] = nn(rows, block).astype(BF)

    compact(slice(0, 768))
    gains = nt(eye_rows(), w[:, 640:768])
    gain_one, gain_two = gains[0:1], gains[1:2]

    lt.wait()
    for copy in yt:
        arrive(copy)
    for j in range(4):
        v = tokf[j].astype(F32)
        rows_j = slice(j * 128, (j + 1) * 128)
        h1 = (v * inverse_norm(v) * gain_one).astype(BF)
        qkv_j = nn(h1, w[:, :640]).astype(BF)
        qkv[rows_j] = qkv_j
        kvf[j, i] = qkv_j[:, 384:]
    kx = cp.start(kvf.at[:, i], kvf.at[:, i], xpeer)
    ks = [cp.start(kvf.at[:, i], kvf.at[:, i], sib)]
    saved = [here(tokf, tokf_o), here(qkv, qkv_o)]
    for copies, h in ((tz, xh), (tz2, 1 - xh)):
        for d, copy in zip(Y_STEPS, copies):
            arrive(copy)
            piece = wf.at[:, :, co, h * 4 + (z + 4 - d) % 4, :, tail]
            tail_sib.append(cp.start(piece, piece, sib))
    arrive(kx)
    piece = kvf.at[:, (1 - xl) * 2 + co]
    ks.append(cp.start(piece, piece, sib))
    ex = [cp.start(own.at[pl.ds(2 - xh * 2, 2)], wexp.at[:, :, f], xfar)]
    cx2 = cot_then_x(cy)
    for copy in ks:
        arrive(copy)
    saved.append(here(kvf, kvf_o))

    for j in range(4):
        n = (j + 1) * 512
        q = head_rows(qkv, j)
        for t in range(j + 1):
            s = nt(q, kvf[t].reshape(512, 256)[:, :128]) * SCALE
            if t == j:
                s = jnp.where(allowed(512), s, -1e30)
            s_s[:, t * 512 : (t + 1) * 512] = s
        s = s_s[:, :n]
        m = jnp.max(s, -1, keepdims=True)
        p = jnp.exp(s - m)
        total = jnp.sum(p, -1, keepdims=True)
        o = nn(p.astype(BF), kvf[0 : j + 1].reshape(n, 256)[:, 128:]) / total
        rows_j = slice(j * 128, (j + 1) * 128)
        for h in range(3):
            att[rows_j, h * 128 : (h + 1) * 128] = o[h * 128 : (h + 1) * 128].astype(BF)
        lse[j] = jnp.broadcast_to(m + jnp.log(total), (384, 128))
    for copy in tail_sib:
        arrive(copy)
    compact(slice(768, 1152))
    saved += [here(w, w_o), here(att, att_o), here(lse, lse_o)]
    for j in range(4):
        part[j] = nt(att[j * 128 : (j + 1) * 128], w[:, 768:1152]).astype(BF)
    ps = [
        cp.start(part.at[(y + d) % 4], got.at[k], p) for k, (d, p) in enumerate(zip(Y_STEPS, ypeers))
    ]
    def pass_on(copies, h):
        sent = []
        for e, (copy, d) in enumerate(zip(copies, (3, 1))):
            arrive(copy)
            piece = wexp.at[e, :, h * 4 + (z + d) % 4]
            sent.append(cp.start(piece, piece, zpeers[2 * e]))
        return sent

    cy3 = cot_middle_y(cy2)
    arrive(bx)
    bz += [cp.start(bf.at[:, f_far], bf.at[:, f_far], p) for p in zpeers]
    pass_on(own_z, xh)
    total = tokf[y].astype(F32) + part[y].astype(F32)
    for k, copy in enumerate(ps):
        arrive(copy)
        total = total + got[k].astype(F32)
    resid[...] = total
    saved.append(here(resid, resid_o))
    h2[...] = (total * inverse_norm(total) * gain_two).astype(BF)
    over_y, over_x = plane_gather(cp, arrive, h2, h2f, me, sib, 64)
    h2_y, h2_then_y, h2_middle_y, h2_last_y = over_y
    h2_x, h2_then_x, h2_middle_x, h2_last_x = over_x
    hx = h2_x()
    hy = h2_y()
    own_h2 = here(h2, h2f.at[xh, y, xl, co])

    cx3 = cot_middle_x(cx2)
    for copy in ex:
        arrive(copy)
    far_rows = wexp.at[:, :, f_far]
    far_z = [cp.start(far_rows, far_rows, zpeers[k]) for k in (0, 2)]
    own_h2.wait()
    hy2 = h2_then_y(hx)
    hx2 = h2_then_x(hy)
    cot_sib = [cy2[2], cx2[2]] + cot_last_y(cy3) + cot_last_x(cx3)
    lb.wait()
    for copy in bz:
        arrive(copy)
    for k in range(16):
        sw[k * 96 : (k + 1) * 96] = nn(rows, bf[k].reshape(128, 256)).astype(BF)
    saved.append(here(sw, sw_o))
    lr.wait()
    for copy in rgs + cot_sib:
        arrive(copy)

    first = c * 4 + xh * 2

    def gated_rows(rg_ref, cot_ref, gy_ref, pick_ref, gated_ref, gz_ref):
        pick, gated = dispatch_rows(rg_ref, first)
        g = cot_ref[...].reshape(256, 1536)
        gy_ref[...] = nn(gated, g).astype(BF).reshape(2, 1, 48, 1536)
        gz_ref[0] = nn(g, sw[:, 128:256])
        pick_ref[0], gated_ref[0] = pick, gated

    picks = pl.BlockSpec((1, 96, 256), lambda p: (p, 0, 0))
    whole = pl.BlockSpec((1, 256, 128), lambda p: (p, 0, 0))
    def gated_half(h):
        at = pl.ds(h * 8, 8)
        pltpu.emit_pipeline(
            gated_rows,
            grid=(8,),
            in_specs=[
                pl.BlockSpec((2, 16, 128), lambda p: (p, 0, 0)),
                pl.BlockSpec(
                    (1, 1, 2, 128, 1536), lambda p: (p // 2, p % 2, 0, 0, 0), pipeline_mode=pl.Buffered(4)
                ),
            ],
            out_specs=[pl.BlockSpec((2, 1, 48, 1536), lambda p: (0, p, 0, 0)), picks, picks, whole],
        )(rgf.at[h], cotf.at[h], gy.at[:, at], pick_o.at[at], gated_o.at[at], gz_o.at[at])

    gated_half(0)
    pass_on(far_z, 1 - xh)
    hy3 = h2_middle_y(hy2)
    hx3 = h2_middle_x(hx2)
    gated_half(1)
    h2_last_y(hy3)
    h2_last_x(hx3)
    for copy in later + saved:
        copy.wait()
    cp.finish(got_already)


def front(*ins):
    outs = (
        SDS((2, 4, 2, 2, 128, 1536), BF),
        SDS((2, 4, 2, 2, 128, 1536), BF),
        SDS((2, 3, 8, 192, 512), BF),
        SDS((4, 128, 1536), BF),
        SDS((4, 4, 128, 256), BF),
        SDS((2, 16, 48, 1536), BF),
        SDS((16, 96, 256), BF),
        SDS((16, 96, 256), BF),
        SDS((16, 256, 128), F32),
        SDS((2, 16, 16, 128), F32),
        SDS((1536, 1152), BF),
        SDS((1536, 256), BF),
        SDS((512, 640), BF),
        SDS((512, 384), BF),
        SDS((4, 384, 128), F32),
        SDS((128, 1536), F32),
    )
    return pl.pallas_call(
        front_kernel,
        out_shape=outs,
        in_specs=[ANY] * 2 + [VM] * (len(ins) - 5) + [ANY] * 3,
        out_specs=(ANY,) * 16,
        scratch_shapes=[
            pltpu.SemaphoreType.DMA((160,)),
            pltpu.SemaphoreType.DMA((160,)),
            pltpu.SemaphoreType.DMA((24,)),
            pltpu.VMEM((1536, 1152), BF),
            pltpu.VMEM((1536, 256), BF),
            pltpu.VMEM((512, 640), BF),
            pltpu.VMEM((512, 384), BF),
            pltpu.VMEM((4, 384, 128), F32),
            pltpu.VMEM((128, 1536), F32),
            pltpu.VMEM((4, 16, 1152), BF),
            pltpu.VMEM((16, 16, 256), BF),
            pltpu.VMEM((4, 3, 192, 512), BF),
            pltpu.VMEM((16, 128), F32),
            pltpu.VMEM((4, 2, 16, 1152), BF),
            pltpu.VMEM((4, 2, 2, 8, 16, 1152), BF),
            pltpu.VMEM((16, 16, 256), BF),
            pltpu.VMEM((16, 8, 16, 256), BF),
            pltpu.VMEM((4, 128, 1536), BF),
            pltpu.VMEM((4, 4, 128, 256), BF),
            pltpu.VMEM((384, 2048), F32),
            pltpu.VMEM((4, 128, 1536), BF),
            pltpu.VMEM((3, 128, 1536), BF),
            pltpu.VMEM((128, 1536), BF),
        ],
        compiler_params=pltpu.CompilerParams(
            collective_id=1, has_side_effects=True, vmem_limit_bytes=VMEM_LIMIT
        ),
        cost_estimate=pl.CostEstimate(flops=6 * 10**9, bytes_accessed=60 * 10**6, transcendentals=3 * 10**6),
    )(*ins)


def add_blocks(*refs):
    total = refs[0][...].astype(F32)
    for ref in refs[1:-1]:
        total = total + ref[...].astype(F32)
    refs[-1][...] = total.astype(refs[-1].dtype)


def add_arrays(block, ins, out):
    spec = pl.BlockSpec((1,) + block, lambda m, r: (m, 0, r, 0))
    pltpu.emit_pipeline(add_blocks, grid=(3, 2), in_specs=[spec] * len(ins), out_specs=[spec])(*ins, out)


def back_kernel(
    pick_in, gated_in, gy_in, gz_in, wexp, h2f, cotf, resid_i, cot_i, w_i, sw_i, tokf_i, qkv_i, kvf_i, lse_i, att_i,
    eg, y_b, y_s, g_s, pick_s, gated_s, hid_b, hid_s, gcd_b, gcd_s, gh2p, outp, zb, sb, xb, goy, gox, aout, bout,
    lout_o, igrad_o,
    send, recv, loc, lout, igrad, goty, gotx, gety, getx, resid, cot, gres, gattn, dkvr, gh1g, dath, zg, xg, xgot, bgot, bxg,
    sw, sdw, db, ds,
):
    y, xl, co, xh, z = coords()
    i, c = xl * 2 + co, y * 4 + xl * 2 + co
    sib = dev(y, xl, 1 - co, xh, z)
    xpeer = dev(y, 1 - xl, co, xh, z)
    xfar = dev(y, xl, co, 1 - xh, z)
    ypeers = [dev((y + d) % 4, xl, co, xh, z) for d in Y_STEPS]
    zpeers = [dev(y, xl, co, xh, (z + d) % 4) for d in Y_STEPS]
    places = ctx_places(y, xl, co)
    cpeers = [dev(*p, xh, z) for p in places]
    xpeers = []
    for d in Y_STEPS:
        hh, ll = x_place(xh, xl, d)
        xpeers.append(dev(y, ll, co, hh, z))
    barrier(cpeers + [dev(y, k, co, 1 - xh, z) for k in range(2)] + zpeers)
    cp = Copies(send, recv)
    n_local = [0]

    def here(src, dst):
        copy = pltpu.make_async_copy(src, dst, loc.at[n_local[0]])
        n_local[0] += 1
        copy.start()
        return copy

    got_already, sent_already = [], []

    def arrive(copy):
        copy.wait_recv()
        got_already.append(copy)

    def gone(copies):
        for copy in copies:
            copy.wait_send()
            sent_already.append(copy)

    low, high = pl.ds(0, 64), pl.ds(64, 64)
    ynext, znext = [(y + d) % 4 for d in range(4)], [(z + d) % 4 for d in range(4)]
    xnext = [x_place(xh, xl, d) for d in range(4)]
    oco, oxl, oxh = 1 - co, 1 - xl, 1 - xh
    xh8, oxh8 = xh * 8, 8 - xh * 8
    place_index = [p[0] * 4 + p[1] * 2 + p[2] for p in places]
    kv_peers = [(a * 2 + b, dev(y, a, b, xh, z)) for a, b in ((oxl, co), (oxl, oco), (xl, oco))]
    front_cols, back_cols = pl.ds(0, 128), pl.ds(128, 128)
    mine_cols = pl.ds(pl.multiple_of(co * 128, 128), 128)
    first = [
        here(sw_i.at[:, front_cols], sw.at[:, front_cols]),
        here(sw_i.at[:, back_cols], sdw.at[:, front_cols]),
        here(resid_i, resid),
        here(cot_i, cot),
    ]
    pairs = pl.BlockSpec((1, 1, 2, 128, 1536), lambda p: (div(p, 2), rem(p, 2), 0, 0, 0))
    picks = pl.BlockSpec((1, 96, 256), lambda p: (p, 0, 0))

    def expert_copies(e):
        return [
            pltpu.make_async_remote_copy(
                eg.at[e, :, :, znext[d]],
                zb.at[k, e],
                send.at[e * 3 + k],
                recv.at[e * 3 + k],
                device_id=zpeers[k],
                device_id_type=MESH,
            )
            for k, d in enumerate(Y_STEPS)
        ]

    def expert_push(e):
        for copy in expert_copies(e):
            copy.start()

    def expert_rows(e, gg):
        return pltpu.make_async_remote_copy(
            gg.at[e], g_s.at[e], send.at[6 + e], recv.at[6 + e], device_id=sib, device_id_type=MESH
        )

    def expert_out(e, xy):
        return pltpu.make_async_remote_copy(
            xy.at[e], y_s.at[e], send.at[8 + e], recv.at[8 + e], device_id=sib, device_id_type=MESH
        )

    cp.n = 12
    early = [
        cp.start(sw_i.at[:, front_cols], sw.at[:, back_cols], sib),
        cp.start(sw_i.at[:, back_cols], sdw.at[:, back_cols], sib),
        cp.start(pick_in, pick_s, sib),
        cp.start(gated_in, gated_s, sib),
    ]
    for copy in first[:2]:
        copy.wait()

    ds[...] = jnp.zeros_like(ds)

    def hidden_rows(k):
        src, dst = ((gcd_b, gcd_s), (hid_b, hid_s))[k]
        return pltpu.make_async_remote_copy(
            src.at[:, oco], dst, send.at[10 + k], recv.at[10 + k], device_id=sib, device_id_type=MESH
        )

    def at8(own):
        return pl.ds(xh8 if own else oxh8, 8)

    blocks = pl.BlockSpec((1, 1, 128, 1536), lambda p: (div(p, 2), rem(p, 2), 0, 0))
    thin = pl.BlockSpec((1, 2, 128, 128), lambda p: (p, 0, 0, 0))

    def experts(xy, gg, dw):
        lg = here(gy_in, gg)

        def grads_copy(e):
            return pltpu.make_async_copy(dw, eg.at[e], loc.at[78 + e])

        def work(w, u_s, ga_s, gb_s):
            lw = [here(wexp.at[0], w.at[0])]

            def own_rows(pick_ref, h2_ref, gz_ref, hid_ref, gcd_ref):
                h2 = h2_ref[...].reshape(256, 1536)
                xy[:, xh8 + pl.program_id(0)] = nn(pick_ref[0], h2).astype(BF).reshape(2, 48, 1536)
                pre, gz = nn(h2, sw[:, 0:128]), gz_ref[0]
                act, slope = silu_parts(pre)
                up = half_turn(pre)
                lane = lax.broadcasted_iota(jnp.int32, (256, 128), 1)
                hid = jnp.where(lane < 64, act * up, 0.0).astype(BF)
                gcd = jnp.where(lane < 64, gz * up * slope, half_turn(gz * act)).astype(BF)
                hid_ref[0] = hid.reshape(2, 128, 128)
                gcd_ref[0] = gcd.reshape(2, 128, 128)
                ds[0:128] += tn(gcd, h2)

            def other_rows(pick_ref, h2_ref):
                x = nn(pick_ref[0], h2_ref[...].reshape(256, 1536)).astype(BF)
                xy[:, oxh8 + pl.program_id(0)] = x.reshape(2, 48, 1536)

            deep = pl.BlockSpec(
                (1, 1, 2, 128, 1536), lambda p: (div(p, 2), rem(p, 2), 0, 0, 0), pipeline_mode=pl.Buffered(4)
            )
            pltpu.emit_pipeline(
                own_rows,
                grid=(8,),
                in_specs=[picks, deep, pl.BlockSpec((1, 256, 128), lambda p: (p, 0, 0))],
                out_specs=[thin, thin],
            )(pick_in.at[at8(True)], h2f.at[xh], gz_in.at[at8(True)], hid_b, gcd_b)
            for e in range(2):
                hidden_rows(e).start()
            pltpu.emit_pipeline(other_rows, grid=(8,), in_specs=[picks, deep])(
                pick_in.at[at8(False)], h2f.at[oxh]
            )
            lw.append(here(wexp.at[1], w.at[1]))
            lg.wait()
            for e in range(2):
                lw[e].wait()
                for t in range(2):
                    cols = slice(t * 256, (t + 1) * 256)
                    x, g = xy[e].reshape(768, 1536), gg[e].reshape(768, 1536)
                    a = nn(x, w[e, 0, :, :, cols].reshape(1536, 256))
                    b = nn(x, w[e, 1, :, :, cols].reshape(1536, 256))
                    gu = nn(g, w[e, 2, :, :, cols].reshape(1536, 256))
                    act, slope = silu_parts(a)
                    u_s[:, cols] = (act * b).astype(BF)
                    ga_s[:, cols] = (gu * b * slope).astype(BF)
                    gb_s[:, cols] = (gu * act).astype(BF)
                if e:
                    grads_copy(0).wait()
                    expert_push(0)

                def row_tile(t, carry):
                    at = pl.ds(pl.multiple_of(t * 384, 384), 384)
                    two, h, half = pl.ds(t * 2, 2), div(t, 2), pl.ds(rem(t, 2) * 2, 2)
                    g = gg[e, :, :, at].reshape(768, 384)
                    dw[2, h, half] = tn(g, u_s[...]).astype(BF).reshape(2, 192, 512)
                    back = nt(ga_s[...], w[e, 0, two].reshape(384, 512))
                    back = back + nt(gb_s[...], w[e, 1, two].reshape(384, 512))
                    gg[e, :, :, at] = back.astype(BF).reshape(16, 48, 384)
                    return carry

                def tile(t, carry):
                    at = pl.ds(pl.multiple_of(t * 384, 384), 384)
                    two, h, half = pl.ds(t * 2, 2), div(t, 2), pl.ds(rem(t, 2) * 2, 2)
                    x = xy[e, :, :, at].reshape(768, 384)
                    dw[0, h, half] = tn(x, ga_s[...]).astype(BF).reshape(2, 192, 512)
                    dw[1, h, half] = tn(x, gb_s[...]).astype(BF).reshape(2, 192, 512)
                    out = nt(u_s[...], w[e, 2, two].reshape(384, 512))
                    xy[e, :, :, at] = out.astype(BF).reshape(16, 48, 384)
                    return carry

                lax.fori_loop(0, 4, row_tile, 0)
                expert_rows(e, gg).start()
                lax.fori_loop(0, 4, tile, 0)
                expert_out(e, xy).start()
                grads_copy(e).start()

        pl.run_scoped(
            work,
            pltpu.VMEM((2, 3, 8, 192, 512), BF),
            pltpu.VMEM((768, 512), BF),
            pltpu.VMEM((768, 512), BF),
            pltpu.VMEM((768, 512), BF),
        )
        ly = here(xy, y_b)
        for e in range(2):
            expert_rows(e, gg).wait()
            hidden_rows(e).wait()

        def row_sums(pick_ref, other_ref, rows_ref, hid_ref, more_ref, gh_ref):
            p = pl.program_id(0)
            picks = jnp.concatenate([pick_ref[0, :, mine_cols], other_ref[0, :, mine_cols]], 0)
            rows = jnp.concatenate([gg[:, p].reshape(96, 1536), rows_ref[...].reshape(96, 1536)], 0)
            gh = tn(picks, rows)
            own = div(p, 8) == xh

            @pl.when(own)
            def _():
                hidden = jnp.concatenate([hid_ref[0, 0], more_ref[0]], 1)
                gh_ref[...] = (gh + nt(hidden, sw[...])).astype(BF).reshape(1, 1, 1, 128, 1536)

            @pl.when(jnp.logical_not(own))
            def _():
                gh_ref[...] = gh.astype(BF).reshape(1, 1, 1, 128, 1536)

        def own_pair(p):
            return jnp.minimum(jnp.maximum(p - xh8, 0), 7)

        deep_rows = pl.BlockSpec((2, 1, 48, 1536), lambda p: (0, p, 0, 0), pipeline_mode=pl.Buffered(3))
        for copy in early:
            arrive(copy)
        pltpu.emit_pipeline(
            row_sums,
            grid=(16,),
            in_specs=[
                picks,
                picks,
                deep_rows,
                pl.BlockSpec((1, 1, 128, 128), lambda p: (own_pair(p), 0, 0, 0)),
                pl.BlockSpec((1, 128, 128), lambda p: (own_pair(p), 0, 0)),
            ],
            out_specs=[pl.BlockSpec((1, 1, 1, 128, 1536), lambda p: (div(p, 8), rem(div(p, 2), 4), rem(p, 2), 0, 0))],
        )(pick_in, pick_s, g_s, gcd_b.at[:, pl.ds(co, 1)], gcd_s, gh2p)
        grads_copy(1).wait()
        expert_push(1)
        ly.wait()
        for e in range(2):
            expert_out(e, xy).wait()

    pl.run_scoped(
        experts,
        pltpu.VMEM((2, 16, 48, 1536), BF),
        pltpu.VMEM((2, 16, 48, 1536), BF),
        pltpu.VMEM((3, 2, 4, 192, 512), BF),
    )

    def dense(
        miney, minex, w, tokf, qkv, kvf, lse, att, go, dk, dv, dkvs, gqkv, gh1s, da, zs, s2, s3, bz, bsum
    ):
        def sum_piece(xp, axis, d):
            if axis == "y":
                return xp.at[:, ynext[d], :, low]
            return xp.at[xnext[d][0], :, xnext[d][1], high]

        def sum_push(xp, toy, tox, steps):
            sent = {}
            for axis, d in steps:
                to, peers = (toy, ypeers) if axis == "y" else (tox, xpeers)
                sent[axis, d] = cp.start(sum_piece(xp, axis, d), to.at[d - 1], peers[d - 1])
            return sent

        def sum_own(xp):
            return [here(sum_piece(xp, "y", 0), miney.at[0]), here(sum_piece(xp, "x", 0), minex.at[0])]

        def sum_second():
            for h in range(2):
                for l in range(2):
                    tot = miney[0, h, l].astype(F32)
                    for k in range(3):
                        tot = tot + goty[k, h, l].astype(F32)
                    miney[0, h, l] = tot.astype(BF)
            for a in range(4):
                tot = minex[0, a].astype(F32)
                for k in range(3):
                    tot = tot + gotx[k, a].astype(F32)
                minex[0, a] = tot.astype(BF)

        def sum_last(nth):
            sent = []
            for k, d in enumerate(Y_STEPS):
                hh, ll = xnext[d]
                sent.append(cp.start(miney.at[0, hh, ll], gety.at[nth, k], xpeers[k]))
                sent.append(cp.start(minex.at[0, ynext[d]], getx.at[nth, k], ypeers[k]))
            return sent

        def sum_end(nth, sent):
            for copy in sent:
                arrive(copy)
            top, bottom = miney[0, xh, xl].astype(F32), minex[0, y].astype(F32)
            for k in range(3):
                top = top + gety[nth, k].astype(F32)
                bottom = bottom + getx[nth, k].astype(F32)
            return jnp.concatenate([top, bottom], 0)

        both = [("y", 1), ("x", 1), ("y", 3), ("x", 3), ("y", 2), ("x", 2)]
        sent_g = sum_push(gh2p, goty, gotx, both)
        own_g = sum_own(gh2p)
        first.append(here(w_i, w))
        second = [here(qkv_i, qkv), here(kvf_i, kvf), here(lse_i, lse), here(att_i, att)]
        third = [here(tokf_i, tokf)]

        def expert_sums(e):
            for copy in expert_copies(e):
                copy.wait()
            ins = [eg.at[e, :, :, z], zb.at[0, e], zb.at[1, e], zb.at[2, e]]
            add_arrays((2, 96, 512), ins, sb.at[e])

        def expert_far(e):
            return cp.start(sb.at[e, :, oxh], xb.at[e], xfar)


        def output_rows(own):
            def body(pick_ref, other_ref, rows_ref, more_ref, *refs):
                picks = jnp.concatenate([pick_ref[0, :, mine_cols], other_ref[0, :, mine_cols]], 0)
                rows = [rows_ref[...].reshape(96, 1536), more_ref[...].reshape(96, 1536)]
                out = tn(picks, jnp.concatenate(rows, 0))
                if own:
                    out = out + nt(jnp.concatenate([refs[0][0, 0], refs[1][0]], 1), sdw[...])
                refs[-1][...] = out.astype(BF).reshape(1, 1, 128, 1536)

            at = at8(own)
            rows = pl.BlockSpec((2, 1, 48, 1536), lambda p: (0, p, 0, 0))
            specs = [picks, picks, rows, rows]
            args = [gated_in.at[at], gated_s.at[at], y_b.at[:, at], y_s.at[:, at]]
            if own:
                specs += [
                    pl.BlockSpec((1, 1, 128, 128), lambda p: (p, 0, 0, 0)),
                    pl.BlockSpec((1, 128, 128), lambda p: (p, 0, 0)),
                ]
                args += [hid_b.at[:, pl.ds(co, 1)], hid_s]
            pltpu.emit_pipeline(body, grid=(8,), in_specs=specs, out_specs=[blocks])(
                *args, outp.at[xh if own else oxh]
            )

        output_rows(True)
        output_rows(False)

        def down_rows(cot_ref, hid_ref):
            ds[128:256] += tn(hid_ref[0].reshape(256, 128), cot_ref[...].reshape(256, 1536))

        pltpu.emit_pipeline(down_rows, grid=(8,), in_specs=[pairs, thin])(cotf.at[xh], hid_b)
        rows = one_hot_rows()
        shared_grads = tn(ds[...].astype(BF), eye(256, 256)).astype(BF)
        for k in range(16):
            block = shared_grads[k * 96 : (k + 1) * 96]
            db[k] = tn(rows, block).astype(BF).reshape(2, 4, 16, 256)
        bs = [cp.start(db.at[:, :, znext[d]], bgot.at[k], p) for k, (d, p) in enumerate(zip(Y_STEPS, zpeers))]

        expert_sums(0)
        for copy in first[2:]:
            copy.wait()
        gains = nt(eye_rows(), w[:, 640:768])
        gain_one, gain_two = gains[0:1], gains[1:2]
        inv = inverse_norm(resid[...])
        xh2 = resid[...] * inv
        for copy in list(sent_g.values()):
            arrive(copy)
        for copy in own_g:
            copy.wait()
        sum_second()
        last_g = sum_last(0)
        gh2 = sum_end(0, last_g)
        gain_two_grad = jnp.sum(gh2 * xh2, 0, keepdims=True)
        inner = gh2 * gain_two
        row = inv * (inner - xh2 * jnp.mean(inner * xh2, -1, keepdims=True))
        gres[...] = cot[...].astype(F32) + row
        gattn[y] = gres[...].astype(BF)
        ga = [cp.start(gattn.at[y], gattn.at[y], p) for p in ypeers]

        gone(list(sent_g.values()) + last_g)
        sent_o = sum_push(outp, goy, gox, both[:5])
        own_o = sum_own(outp)
        ex0 = expert_far(0)

        for copy in second:
            copy.wait()
        for copy in ga:
            arrive(copy)
        dk[...] = jnp.zeros_like(dk)
        dv[...] = jnp.zeros_like(dv)
        for j in range(4):
            rows_j = slice(j * 128, (j + 1) * 128)
            go[rows_j] = nn(gattn[j], w[:, 768:1152]).astype(BF)
            q, g = head_rows(qkv, j), head_rows(go, j)
            delta = jnp.sum(head_rows(att, j).astype(F32) * g.astype(F32), -1, keepdims=True)
            total = lse[j][:, :1]
            dq = jnp.zeros((384, 128), F32)
            for t in range(j + 1):
                keys = kvf[t].reshape(512, 256)
                s = nt(q, keys[:, :128]) * SCALE
                p = jnp.exp(s - total)
                if t == j:
                    p = jnp.where(allowed(512), p, 0.0)
                gs = (p * (nt(g, keys[:, 128:]) - delta)).astype(BF)
                at = slice(t * 512, (t + 1) * 512)
                dv[at] += tn(p.astype(BF), g)
                dk[at] += tn(gs, q)
                dq = dq + nn(gs, keys[:, :128])
            dq = (dq * SCALE).astype(BF)
            for h in range(3):
                gqkv[rows_j, h * 128 : (h + 1) * 128] = dq[h * 128 : (h + 1) * 128]
        for j in range(4):
            for k in range(4):
                at = slice((j * 4 + k) * 128, (j * 4 + k + 1) * 128)
                dkvs[j, k, :, 0:128] = (dk[at] * SCALE).astype(BF)
                dkvs[j, k, :, 128:256] = dv[at].astype(BF)
        kvs = [
            cp.start(dkvs.at[:, p], dkvr.at[k], q)
            for k, (p, q) in enumerate(kv_peers)
        ]
        sent_o.update(sum_push(outp, goy, gox, both[5:]))
        def expand(block, yy, cols):
            for k in range(4):
                part = tn(rows, block[k * 96 : (k + 1) * 96]).astype(BF)
                da[yy, k // 2, k % 2, :, :, :, cols] = part.reshape(2, 4, 16, -1)

        def dense_core(cols):
            return cp.start(da.at[:, :, oco, :, :, :, cols], dath.at[:, :, :, :, :, cols], sib)

        def dense_z(copy, cols):
            arrive(copy)
            for a in range(4):
                for b in range(2):
                    tot = da[a, b, co, :, :, :, cols].astype(F32) + dath[a, b, :, :, :, cols].astype(F32)
                    da[a, b, co, :, :, :, cols] = tot.astype(BF)
            return [
                cp.start(da.at[:, :, co, :, znext[d], :, cols], zg.at[k, :, :, :, :, cols], p)
                for k, (d, p) in enumerate(zip(Y_STEPS, zpeers))
            ]

        def dense_far(copies, cols):
            for copy in copies:
                arrive(copy)
            for a in range(4):
                for b in range(2):
                    tot = da[a, b, co, :, z, :, cols].astype(F32)
                    for k in range(3):
                        tot = tot + zg[k, a, b, :, :, cols].astype(F32)
                    for h in range(2):
                        zs[h, a, b, :, cols] = tot[h].astype(BF)
            return cp.start(zs.at[oxh, :, :, :, cols], xg.at[:, :, :, cols], xfar)

        def dense_near(copy, cols):
            arrive(copy)
            for a in range(4):
                for b in range(2):
                    tot = zs[xh, a, b, :, cols].astype(F32) + xg[a, b, :, cols].astype(F32)
                    s2[b, a, :, cols] = tot.astype(BF)
            return cp.start(s2.at[oxl, :, :, cols], xgot.at[:, :, cols], xpeer)

        def dense_y(copy, cols):
            arrive(copy)
            for a in range(4):
                s3[a, :, cols] = (s2[xl, a, :, cols].astype(F32) + xgot[a, :, cols].astype(F32)).astype(BF)
            last.append(here(s3.at[y, :, cols], aout.at[y, :, cols]))
            return [
                cp.start(s3.at[ynext[d], :, cols], aout.at[y, :, cols], p) for d, p in zip(Y_STEPS, ypeers)
            ]

        head, tail = pl.ds(0, 768), pl.ds(768, 384)
        last = []
        for yy in range(4):
            tile = slice(yy * 384, (yy + 1) * 384)
            block = tn(gattn[:, :, tile].reshape(512, 384), att[...])
            expand(block.astype(BF), yy, tail)
        tail_c = dense_core(tail)
        expert_sums(1)
        ex1 = expert_far(1)

        tail_z = dense_z(tail_c, tail)
        for copy in third:
            copy.wait()
        for copy in kvs:
            arrive(copy)
        gone(ga)
        gain_one_grad = jnp.zeros((1, 1536), F32)
        for j in range(4):
            rows_j = slice(j * 128, (j + 1) * 128)
            kv = dkvs[j, i].astype(F32)
            for k in range(3):
                kv = kv + dkvr[k, j].astype(F32)
            gqkv[rows_j, 384:640] = kv.astype(BF)
            gh1 = nt(gqkv[rows_j], w[:, :640])
            v = tokf[j].astype(F32)
            scaled = v * inverse_norm(v)
            gain_one_grad = gain_one_grad + jnp.sum(gh1 * scaled, 0, keepdims=True)
            gattn[j] = (scaled * gain_one).astype(BF)
            gh1s[j] = gh1.astype(BF)
        hs = [
            cp.start(gh1s.at[ynext[d]], gh1g.at[k], p) for k, (d, p) in enumerate(zip(Y_STEPS, ypeers))
        ]
        gain_rows = jnp.concatenate([gain_one_grad, gain_two_grad, jnp.zeros((6, 1536), F32)], 0)
        for yy in range(4):
            tile = slice(yy * 384, (yy + 1) * 384)
            block = tn(gattn[:, :, tile].reshape(512, 384), gqkv[...])
            expand(block.astype(BF), yy, pl.ds(0, 640))
            expand(tn(gain_rows[:, tile].astype(BF), eye_rows()).astype(BF), yy, pl.ds(640, 128))
        head_c = dense_core(head)
        head_z = dense_z(head_c, head)

        tail_x = dense_far(tail_z, tail)
        for copy in bs:
            arrive(copy)
        for a in range(16):
            tot = db[a, :, z].astype(F32)
            for k in range(3):
                tot = tot + bgot[k, a].astype(F32)
            bz[0, a], bz[1, a] = tot[0].astype(BF), tot[1].astype(BF)
        bx = cp.start(bz.at[oxh], bxg, xfar)

        for copy in sent_o.values():
            arrive(copy)
        back_in = [here(goy, goty), here(gox, gotx)]
        for copy in back_in + own_o:
            copy.wait()
        gone(list(sent_o.values()))
        sum_second()
        last_o = sum_last(1)
        head_x = dense_far(head_z, head)
        gh1 = gh1s[y].astype(F32)
        for k, copy in enumerate(hs):
            arrive(copy)
            gh1 = gh1 + gh1g[k].astype(F32)
        v = tokf[y].astype(F32)
        inv = inverse_norm(v)
        inner = gh1 * gain_one
        xh1 = v * inv
        igrad[...] = gres[...] + inv * (inner - xh1 * jnp.mean(inner * xh1, -1, keepdims=True))
        igrad_c = here(igrad, igrad_o)

        tail_n = dense_near(tail_x, tail)
        arrive(bx)
        for a in range(16):
            bsum[a] = (bz[xh, a].astype(F32) + bxg[a].astype(F32)).astype(BF)
        bo = [cp.start(bsum.at[p], bout.at[c], q) for p, q in zip(place_index, cpeers)]
        last.append(here(bsum.at[c], bout.at[c]))
        head_n = dense_near(head_x, head)
        outs = dense_y(tail_n, tail) + dense_y(head_n, head)

        lout[...] = (resid[...] + sum_end(1, last_o)).astype(BF)
        last += [igrad_c, here(lout, lout_o)]
        for copy in last:
            copy.wait()
        for copy in cp.started:
            if not any(copy is r for r in sent_already):
                copy.wait_send()
            if not any(copy is r for r in got_already):
                copy.wait_recv()

    pl.run_scoped(
        dense,
        pltpu.VMEM((1, 2, 2, 64, 1536), BF),
        pltpu.VMEM((1, 4, 64, 1536), BF),
        pltpu.VMEM((1536, 1152), BF),
        pltpu.VMEM((4, 128, 1536), BF),
        pltpu.VMEM((512, 640), BF),
        pltpu.VMEM((4, 4, 128, 256), BF),
        pltpu.VMEM((4, 384, 128), F32),
        pltpu.VMEM((512, 384), BF),
        pltpu.VMEM((512, 384), BF),
        pltpu.VMEM((2048, 128), F32),
        pltpu.VMEM((2048, 128), F32),
        pltpu.VMEM((4, 4, 128, 256), BF),
        pltpu.VMEM((512, 640), BF),
        pltpu.VMEM((4, 128, 1536), BF),
        pltpu.VMEM((4, 2, 2, 2, 4, 16, 1152), BF),
        pltpu.VMEM((2, 4, 2, 16, 1152), BF),
        pltpu.VMEM((2, 4, 16, 1152), BF),
        pltpu.VMEM((4, 16, 1152), BF),
        pltpu.VMEM((2, 16, 16, 256), BF),
        pltpu.VMEM((16, 16, 256), BF),
    )


def back(*ins):
    outs = (
        SDS((2, 3, 2, 4, 192, 512), BF),
        SDS((2, 16, 48, 1536), BF),
        SDS((2, 16, 48, 1536), BF),
        SDS((2, 16, 48, 1536), BF),
        SDS((16, 96, 256), BF),
        SDS((16, 96, 256), BF),
        SDS((8, 2, 128, 128), BF),
        SDS((8, 128, 128), BF),
        SDS((8, 2, 128, 128), BF),
        SDS((8, 128, 128), BF),
        SDS((2, 4, 2, 128, 1536), BF),
        SDS((2, 4, 2, 128, 1536), BF),
        SDS((3, 2, 3, 2, 192, 512), BF),
        SDS((2, 3, 2, 192, 512), BF),
        SDS((2, 3, 192, 512), BF),
        SDS((3, 2, 2, 64, 1536), BF),
        SDS((3, 4, 64, 1536), BF),
        SDS((4, 16, 1152), BF),
        SDS((16, 16, 256), BF),
        SDS((128, 1536), BF),
        SDS((128, 1536), F32),
    )
    out = pl.pallas_call(
        back_kernel,
        out_shape=outs,
        in_specs=[ANY] * len(ins),
        out_specs=(ANY,) * 21,
        scratch_shapes=[
            pltpu.SemaphoreType.DMA((112,)),
            pltpu.SemaphoreType.DMA((112,)),
            pltpu.SemaphoreType.DMA((80,)),
            pltpu.VMEM((128, 1536), BF),
            pltpu.VMEM((128, 1536), F32),
            pltpu.VMEM((3, 2, 2, 64, 1536), BF),
            pltpu.VMEM((3, 4, 64, 1536), BF),
            pltpu.VMEM((2, 3, 64, 1536), BF),
            pltpu.VMEM((2, 3, 64, 1536), BF),
            pltpu.VMEM((128, 1536), F32),
            pltpu.VMEM((128, 1536), BF),
            pltpu.VMEM((128, 1536), F32),
            pltpu.VMEM((4, 128, 1536), BF),
            pltpu.VMEM((3, 4, 128, 256), BF),
            pltpu.VMEM((3, 128, 1536), BF),
            pltpu.VMEM((4, 2, 2, 4, 16, 1152), BF),
            pltpu.VMEM((3, 4, 2, 2, 16, 1152), BF),
            pltpu.VMEM((4, 2, 16, 1152), BF),
            pltpu.VMEM((4, 16, 1152), BF),
            pltpu.VMEM((3, 16, 2, 16, 256), BF),
            pltpu.VMEM((16, 16, 256), BF),
            pltpu.VMEM((1536, 256), BF),
            pltpu.VMEM((1536, 256), BF),
            pltpu.VMEM((16, 2, 4, 16, 256), BF),
            pltpu.VMEM((256, 1536), F32),
        ],
        compiler_params=pltpu.CompilerParams(
            collective_id=2, has_side_effects=True, vmem_limit_bytes=62 * 2**20
        ),
        cost_estimate=pl.CostEstimate(flops=36 * 10**9, bytes_accessed=150 * 10**6, transcendentals=5 * 10**6),
    )(*ins)
    return out[19], out[20], out[17], out[18], out[13], out[14]


def unpack_kernel(
    lout, igrad, aout, bout, sb, xb,
    lout_o, igrad_o, gains_o, wq_o, wk_o, wv_o, wo_o, sg_o, su_o, sd_o, eg_o, eu_o, ed_o,
):
    xh = lax.axis_index("fsdp") // 4
    lout_o[...] = lout[...]
    igrad_o[...] = igrad[...]
    for e in range(2):
        for m, ref in enumerate((eg_o, eu_o, ed_o)):
            ref[xh * 2 + e] = sb[e, m, xh].astype(F32)
            ref[2 - xh * 2 + e] = xb[e, m].astype(F32)
    gain_sum = jnp.zeros((16, 128), F32)
    for k in range(4):
        wide, thin = slice(k * 384, (k + 1) * 384), slice(k * 128, (k + 1) * 128)
        block = aout[k].astype(F32)
        wq_o[:, wide] = block[:12, 0:384]
        wk_o[:, thin] = block[:12, 384:512]
        wv_o[:, thin] = block[:12, 512:640]
        gain_sum = gain_sum + block[:, 640:768]
        wo_o[:, wide] = block[:12, 768:1152]
    gains_o[...] = gain_sum
    front_half = lax.broadcasted_iota(jnp.int32, (16, 128), 1) < 64
    for k in range(8):
        at = slice(k * 128, (k + 1) * 128)
        one, two = bout[2 * k].astype(F32), bout[2 * k + 1].astype(F32)
        sg_o[:, at] = jnp.where(front_half, one[:, :128], half_turn(two[:, :128]))[:12]
        su_o[:, at] = jnp.where(front_half, half_turn(one[:, :128]), two[:, :128])[:12]
        sd_o[:, at] = jnp.where(front_half, one[:, 128:], half_turn(two[:, 128:]))[:12]


def unpack(*ins):
    outs = (
        SDS((128, 1536), BF),
        SDS((128, 1536), F32),
        SDS((16, 128), F32),
        SDS((12, 1536), F32),
        SDS((12, 512), F32),
        SDS((12, 512), F32),
        SDS((12, 1536), F32),
        SDS((12, 1024), F32),
        SDS((12, 1024), F32),
        SDS((12, 1024), F32),
        SDS((4, 192, 512), F32),
        SDS((4, 192, 512), F32),
        SDS((4, 192, 512), F32),
    )
    return pl.pallas_call(
        unpack_kernel,
        out_shape=outs,
        in_specs=[VM] * len(ins),
        out_specs=(VM,) * len(outs),
        compiler_params=pltpu.CompilerParams(vmem_limit_bytes=VMEM_LIMIT),
    )(*ins)


def local(
    tokens,
    cotangent,
    routes,
    gates,
    attn_gain,
    ffn_gain,
    w_query,
    w_key,
    w_value,
    w_out,
    shared_gate,
    shared_up,
    shared_down,
    expert_gate,
    expert_up,
    expert_down,
):
    tok = tokens.reshape(128, 1536)
    cot = cotangent.reshape(128, 1536)
    gains = jnp.stack([attn_gain, ffn_gain])
    (cot_f, h2_f, wexp, tok_f, kv_f, gy, pick, gated, gz, _, w, sw, qkv, att, lse, resid) = front(
        tok,
        cot,
        jnp.transpose(routes, (2, 0, 1)),
        jnp.transpose(gates, (2, 0, 1)),
        gains,
        w_query,
        w_key,
        w_value,
        w_out.T,
        shared_gate,
        shared_up,
        shared_down.T,
        expert_gate,
        expert_up,
        jnp.transpose(expert_down, (0, 2, 1)),
    )
    parts = back(
        pick, gated, gy, gz, wexp, h2_f, cot_f, resid, cot, w, sw, tok_f, qkv, kv_f, lse, att
    )
    (layer_out, input_grad, gain_grads, wq, wk, wv, wo, sg, su, sd, eg, eu, ed) = unpack(*parts)
    return (
        layer_out.reshape(1, 128, 1536),
        input_grad.reshape(1, 128, 1536),
        gain_grads[:12, 0],
        gain_grads[:12, 1],
        wq,
        wk,
        wv,
        wo.T,
        sg,
        su,
        sd.T,
        eg,
        eu,
        jnp.transpose(ed, (0, 2, 1)),
    )


def solution(mesh):
    both = ("ctx", "fsdp")
    rows = P("fsdp", "ctx", None)
    weights = (P(both),) * 2 + (P(both, None),) * 3 + (P(None, both),)
    weights = weights + (P(both, None),) * 2 + (P(None, both),)
    weights = weights + (P("ctx", "fsdp", None),) * 2 + (P("ctx", None, "fsdp"),)
    return jax.shard_map(
        local, mesh=mesh, in_specs=(rows,) * 4 + weights, out_specs=(rows,) * 2 + weights, check_vma=False
    )
```

```python
import jax
import jax.numpy as jnp
from jax import lax
from jax.experimental import pallas as pl
from jax.experimental.pallas import tpu as pltpu
from jax.sharding import PartitionSpec as P

BF = jnp.bfloat16
F32 = jnp.float32
EPS = 1e-05
MESH = pl.DeviceIdType.MESH
ANY = pl.BlockSpec(memory_space=pl.ANY)
VM = pl.BlockSpec(memory_space=pltpu.VMEM)
SDS = jax.ShapeDtypeStruct
SCALE = 128 ** (-0.5)
VMEM_LIMIT = 56 * 2**20


def div(x, n):
    return lax.div(x, lax.full_like(x, n))


def rem(x, n):
    return lax.rem(x, lax.full_like(x, n))


def nn(a, b):
    return lax.dot_general(a, b, (((1,), (0,)), ((), ())), preferred_element_type=F32)


def nt(a, b):
    return lax.dot_general(a, b, (((1,), (1,)), ((), ())), preferred_element_type=F32)


def tn(a, b):
    return lax.dot_general(a, b, (((0,), (0,)), ((), ())), preferred_element_type=F32)


def silu_parts(pre_act):
    sig = 1.0 / (1.0 + jnp.exp(-pre_act))
    return pre_act * sig, sig * (1.0 + pre_act * (1.0 - sig))


def coords():
    c = lax.axis_index("ctx")
    f = lax.axis_index("fsdp")
    return c // 4, (c // 2) % 2, c % 2, f // 4, f % 4


def dev(y, xl, co, xh, z):
    return (y * 4 + xl * 2 + co, xh * 4 + z)


def barrier(peers):
    sem = pltpu.get_barrier_semaphore()
    for peer in peers:
        pl.semaphore_signal(sem, inc=1, device_id=peer, device_id_type=MESH)
    pl.semaphore_wait(sem, len(peers))


class Copies:
    def __init__(self, send, recv):
        self.send, self.recv, self.n, self.started = send, recv, 0, []

    def start(self, src, dst, peer):
        copy = pltpu.make_async_remote_copy(
            src, dst, self.send.at[self.n], self.recv.at[self.n], device_id=peer, device_id_type=MESH
        )
        copy.start()
        self.n += 1
        self.started.append(copy)
        return copy

    def finish(self, received=()):
        for copy in self.started:
            copy.wait_send()
            if not any(copy is r for r in received):
                copy.wait_recv()


Y_STEPS = (1, 2, 3)


def one_hot_rows():
    row = lax.broadcasted_iota(jnp.int32, (96, 128), 0)
    col = lax.broadcasted_iota(jnp.int32, (96, 128), 1)
    return jnp.where(div(row, 12) * 16 + rem(row, 12) == col, 1.0, 0.0).astype(BF)


def eye_rows():
    row = lax.broadcasted_iota(jnp.int32, (8, 128), 0)
    col = lax.broadcasted_iota(jnp.int32, (8, 128), 1)
    return jnp.where(row == col, 1.0, 0.0).astype(BF)


def inverse_norm(values):
    return lax.rsqrt(jnp.mean(values * values, -1, keepdims=True) + EPS)


def head_rows(ref, j, first=0):
    rows = slice(j * 128, (j + 1) * 128)
    return jnp.concatenate([ref[rows, first + h * 128 : first + (h + 1) * 128] for h in range(3)], 0)


def allowed(n):
    i = rem(lax.axis_index("ctx"), 4)
    row = rem(lax.broadcasted_iota(jnp.int32, (384, n), 0), 128)
    col = lax.broadcasted_iota(jnp.int32, (384, n), 1)
    return col <= i * 128 + row


def ctx_places(y, xl, co):
    return [
        ((y + dy) % 4, (xl + dx) % 2, (co + dc) % 2)
        for dy in range(4)
        for dx in (0, 1)
        for dc in (0, 1)
        if (dy, dx, dc) != (0, 0, 0)
    ]


def x_place(xh, xl, d):
    x = (xh * 2 + xl + d) % 4
    return x // 2, x % 2


def plane_gather(cp, arrive, src, out, places, sib, split):
    y, xl, co, xh, z = places
    low, high = pl.ds(0, split), pl.ds(split, 128 - split)
    ypeers = [dev((y + d) % 4, xl, co, xh, z) for d in Y_STEPS]
    xpeers = []
    for d in Y_STEPS:
        h, l = x_place(xh, xl, d)
        xpeers.append(dev(y, l, co, h, z))
    mine = (xh, y, xl, co)

    def first_y():
        return [cp.start(src.at[high], out.at[mine + (high,)], p) for p in ypeers]

    def first_x():
        return [cp.start(src.at[low], out.at[mine + (low,)], p) for p in xpeers]

    def piece_y(d):
        return out.at[:, (y + d) % 4, :, co, low]

    def piece_x(d):
        h, l = x_place(xh, xl, d)
        return out.at[h, :, l, co, high]

    def half_y(d, n):
        return out.at[n, (y + d) % 4, :, co, low]

    def half_x(d, n):
        h, l = x_place(xh, xl, d)
        return out.at[h, pl.ds(2 * n, 2), l, co, high]

    def then(firsts, piece, peers):
        for copy in firsts:
            arrive(copy)
        return [
            cp.start(piece(0), piece(0), peers[0]),
            cp.start(piece(0), piece(0), peers[2]),
            cp.start(piece(0), piece(0), sib),
        ]

    def middle(seconds, piece, half, peers):
        arrive(seconds[0])
        one = cp.start(half(3, 0), half(3, 0), peers[0])
        arrive(seconds[1])
        two = cp.start(half(1, 1), half(1, 1), peers[2])
        sibs = [cp.start(piece(d), piece(d), sib) for d in (3, 1)]
        return [one, two] + sibs

    def last(middles, piece):
        for copy in middles[:2]:
            arrive(copy)
        return middles[2:] + [cp.start(piece(2), piece(2), sib)]

    def then_y(firsts):
        return then(firsts, piece_y, ypeers)

    def then_x(firsts):
        return then(firsts, piece_x, xpeers)

    def middle_y(seconds):
        return middle(seconds, piece_y, half_y, ypeers)

    def middle_x(seconds):
        return middle(seconds, piece_x, half_x, xpeers)

    def last_y(middles):
        return last(middles, piece_y)

    def last_x(middles):
        return last(middles, piece_x)

    return (first_y, then_y, middle_y, last_y), (first_x, then_x, middle_x, last_x)


def dispatch_rows(rg, first):
    masks, gates = [], []
    for e in range(2):
        ms, gs = [], []
        for s in range(2):
            hit = jnp.where(rg[s, 0:6] == (first + e).astype(F32), 1.0, 0.0)
            ms.append(jnp.sum(hit, 0, keepdims=True))
            gs.append(jnp.sum(hit * rg[s, 8:14], 0, keepdims=True))
        masks.append(jnp.concatenate(ms, 1))
        gates.append(jnp.concatenate(gs, 1))
    mask = jnp.concatenate(masks + [jnp.zeros((6, 256), F32)], 0)
    before = lax.broadcasted_iota(jnp.int32, (256, 256), 0)
    after = lax.broadcasted_iota(jnp.int32, (256, 256), 1)
    tri = jnp.where((before <= after) & (before // 128 == after // 128), 1.0, 0.0).astype(BF)
    place = nn(mask.astype(BF), tri) - 1.0
    lane = lax.broadcasted_iota(jnp.int32, (1, 256), 1)
    slot = lax.broadcasted_iota(jnp.int32, (48, 256), 0).astype(F32)
    picks, gated = [], []
    for e in range(2):
        at = place[e : e + 1] + jnp.where(lane >= 128, 24.0, 0.0)
        at = jnp.where(masks[e] > 0.0, at, -1.0)
        hit = jnp.where(slot == at, 1.0, 0.0)
        picks.append(hit)
        gated.append(hit * gates[e])
    return jnp.concatenate(picks, 0).astype(BF), jnp.concatenate(gated, 0).astype(BF)


def eye(rows, cols):
    row = lax.broadcasted_iota(jnp.int32, (rows, cols), 0)
    col = lax.broadcasted_iota(jnp.int32, (rows, cols), 1)
    return jnp.where(row == col, 1.0, 0.0).astype(BF)


def half_turn(x):
    return pltpu.roll(x, 64, 1)


def front_kernel(
    tok, cot, routes, gates, gains_in, wq, wk, wv, wo, sg, su, sd, eg, eu, ed,
    cotf, h2f, wexp, tokf_o, kvf_o, gy, pick_o, gated_o, gz_o, rgf,
    w_o, sw_o, qkv_o, att_o, lse_o, resid_o,
    send, recv, loc, w, sw, qkv, att, lse, resid, a_s, b_s, own, rg_s, a2, wf, b1, bf, tokf, kvf, s_s, part, got, h2,
):
    y, xl, co, xh, z = coords()
    i, c, f = xl * 2 + co, y * 4 + xl * 2 + co, xh * 4 + z
    f_far = (1 - xh) * 4 + z
    sib = dev(y, xl, 1 - co, xh, z)
    xpeer = dev(y, 1 - xl, co, xh, z)
    xfar = dev(y, xl, co, 1 - xh, z)
    ypeers = [dev((y + d) % 4, xl, co, xh, z) for d in Y_STEPS]
    zpeers = [dev(y, xl, co, xh, (z + d) % 4) for d in Y_STEPS]
    places = ctx_places(y, xl, co)
    cpeers = [dev(*p, xh, z) for p in places]
    plane = cpeers + [dev(*p, 1 - xh, z) for p in places + [(y, xl, co)]]
    peers = plane + zpeers
    sem = pltpu.get_barrier_semaphore()
    for peer in peers:
        pl.semaphore_signal(sem, inc=1, device_id=peer, device_id_type=MESH)

    e16 = eye(16, 12)
    q16, k16, v16 = (nn(e16, ref[...]).astype(BF) for ref in (wq, wk, wv))
    o16 = nn(e16, wo[...]).astype(BF)
    gain_rows = nn(eye(128, 2), gains_in[...]).astype(BF)
    gain16 = nt(e16, gain_rows).astype(BF)
    for k in range(4):
        wide, thin = slice(k * 384, (k + 1) * 384), slice(k * 128, (k + 1) * 128)
        a_s[k] = jnp.concatenate([q16[:, wide], k16[:, thin], v16[:, thin], gain16, o16[:, wide]], 1)
    pl.semaphore_wait(sem, len(peers))

    cp = Copies(send, recv)
    n_local = [0]

    def here(src, dst):
        copy = pltpu.make_async_copy(src, dst, loc.at[n_local[0]])
        n_local[0] += 1
        copy.start()
        return copy

    got_already = []

    def arrive(copy):
        copy.wait_recv()
        got_already.append(copy)

    me = (y, xl, co, xh, z)
    ya = [cp.start(a_s.at[(y + d) % 4], a2.at[y, xl], p) for d, p in zip(Y_STEPS, ypeers)]
    la = here(a_s.at[y], a2.at[y, xl])
    lt = here(tok, tokf.at[y])
    owns = [here(ref, own.at[:, k]) for k, ref in enumerate((eg, eu, ed))]
    own_cot = here(cot, cotf.at[xh, y, xl, co])
    over_y, over_x = plane_gather(cp, arrive, cot, cotf, me, sib, 80)
    cot_y, cot_then_y, cot_middle_y, cot_last_y = over_y
    cot_x, cot_then_x, cot_middle_x, cot_last_x = over_x
    yt = [cp.start(tok, tokf.at[y], p) for p in ypeers]
    cy = cot_y()
    g16, u16, d16 = nn(e16, sg[...]), nn(e16, su[...]), nn(e16, sd[...])
    front_half = lax.broadcasted_iota(jnp.int32, (16, 128), 1) < 64
    for k in range(8):
        at = slice(k * 128, (k + 1) * 128)
        g, u, d = g16[:, at], u16[:, at], d16[:, at]
        for n in range(2):
            if n:
                g, d = half_turn(g), half_turn(d)
            else:
                u = half_turn(u)
            b_s[2 * k + n, :, 0:128] = jnp.where(front_half, g, u).astype(BF)
            b_s[2 * k + n, :, 128:256] = jnp.where(front_half, d, 0.0).astype(BF)
            if not n:
                u = half_turn(u)
    rg_s[...] = jnp.zeros_like(rg_s)
    for k in range(6):
        rg_s[k : k + 1] = routes[k].astype(F32)
        rg_s[8 + k : 9 + k] = gates[k]
    lb = here(b_s.at[c], b1.at[c])
    lr = here(rg_s, rgf.at[xh, c])
    for copy in owns:
        copy.wait()
    later = [here(own.at[pl.ds(xh * 2, 2)], wexp.at[:, :, f])]
    la.wait()
    for copy in ya:
        arrive(copy)
    xa = cp.start(a2.at[:, xl], a2.at[:, xl], xpeer)
    bs = [cp.start(b_s.at[p[0] * 4 + p[1] * 2 + p[2]], b1.at[c], q) for p, q in zip(places, cpeers)]
    rgs = [cp.start(rg_s, rgf.at[xh, c], q) for q in plane]
    arrive(xa)

    head, tail = pl.ds(0, 768), pl.ds(768, 384)

    def slices(cols):
        return a2.at[:, :, :, cols], wf.at[:, :, co, f, :, cols], wf.at[:, :, co, f_far, :, cols]

    src, mine, far = slices(head)
    hx = cp.start(src, mine, xfar)
    hz = [cp.start(src, mine, p) for p in zpeers]
    lw = here(a2, wf.at[:, :, co, f])
    cx = cot_x()
    src_t, mine_t, far_t = slices(tail)
    tx = cp.start(src_t, mine_t, xfar)
    lw.wait()
    to_sib = [cp.start(mine, mine, sib)]
    arrive(hx)
    hz2 = [cp.start(far, far, p) for p in zpeers]
    to_sib.append(cp.start(far, far, sib))
    tz = [cp.start(src_t, mine_t, p) for p in zpeers]
    for copies, h in ((hz, xh), (hz2, 1 - xh)):
        for d, copy in zip(Y_STEPS, copies):
            arrive(copy)
            piece = wf.at[:, :, co, h * 4 + (z + 4 - d) % 4, :, head]
            to_sib.append(cp.start(piece, piece, sib))
    own_cot.wait()
    cy2 = cot_then_y(cx)
    arrive(tx)
    tz2 = [cp.start(far_t, far_t, p) for p in zpeers]
    tail_sib = [cp.start(mine_t, mine_t, sib), cp.start(far_t, far_t, sib)]
    own_z = [cp.start(own.at[pl.ds(xh * 2, 2)], wexp.at[:, :, f], zpeers[k]) for k in (0, 2)]
    lb.wait()
    for copy in bs:
        arrive(copy)
    bx = cp.start(b1, bf.at[:, f], xfar)
    bz = [cp.start(b1, bf.at[:, f], p) for p in zpeers]
    lb = here(b1, bf.at[:, f])
    for copy in to_sib:
        arrive(copy)
    rows = one_hot_rows()

    def compact(cols):
        for yy in range(4):
            for k in range(4):
                at = (yy * 4 + k) * 96
                block = wf[yy, k // 2, k % 2, :, :, cols].reshape(128, -1)
                w[at : at + 96, cols] = nn(rows, block).astype(BF)

    compact(slice(0, 768))
    gains = nt(eye_rows(), w[:, 640:768])
    gain_one, gain_two = gains[0:1], gains[1:2]

    lt.wait()
    for copy in yt:
        arrive(copy)
    for j in range(4):
        v = tokf[j].astype(F32)
        rows_j = slice(j * 128, (j + 1) * 128)
        h1 = (v * inverse_norm(v) * gain_one).astype(BF)
        qkv_j = nn(h1, w[:, :640]).astype(BF)
        qkv[rows_j] = qkv_j
        kvf[j, i] = qkv_j[:, 384:]
    kx = cp.start(kvf.at[:, i], kvf.at[:, i], xpeer)
    ks = [cp.start(kvf.at[:, i], kvf.at[:, i], sib)]
    saved = [here(tokf, tokf_o), here(qkv, qkv_o)]
    for copies, h in ((tz, xh), (tz2, 1 - xh)):
        for d, copy in zip(Y_STEPS, copies):
            arrive(copy)
            piece = wf.at[:, :, co, h * 4 + (z + 4 - d) % 4, :, tail]
            tail_sib.append(cp.start(piece, piece, sib))
    arrive(kx)
    piece = kvf.at[:, (1 - xl) * 2 + co]
    ks.append(cp.start(piece, piece, sib))
    ex = [cp.start(own.at[pl.ds(2 - xh * 2, 2)], wexp.at[:, :, f], xfar)]
    cx2 = cot_then_x(cy)
    for copy in ks:
        arrive(copy)
    saved.append(here(kvf, kvf_o))

    for j in range(4):
        n = (j + 1) * 512
        q = head_rows(qkv, j)
        for t in range(j + 1):
            s = nt(q, kvf[t].reshape(512, 256)[:, :128]) * SCALE
            if t == j:
                s = jnp.where(allowed(512), s, -1e30)
            s_s[:, t * 512 : (t + 1) * 512] = s
        s = s_s[:, :n]
        m = jnp.max(s, -1, keepdims=True)
        p = jnp.exp(s - m)
        total = jnp.sum(p, -1, keepdims=True)
        o = nn(p.astype(BF), kvf[0 : j + 1].reshape(n, 256)[:, 128:]) / total
        rows_j = slice(j * 128, (j + 1) * 128)
        for h in range(3):
            att[rows_j, h * 128 : (h + 1) * 128] = o[h * 128 : (h + 1) * 128].astype(BF)
        lse[j] = jnp.broadcast_to(m + jnp.log(total), (384, 128))
    for copy in tail_sib:
        arrive(copy)
    compact(slice(768, 1152))
    saved += [here(w, w_o), here(att, att_o), here(lse, lse_o)]
    for j in range(4):
        part[j] = nt(att[j * 128 : (j + 1) * 128], w[:, 768:1152]).astype(BF)
    ps = [
        cp.start(part.at[(y + d) % 4], got.at[k], p) for k, (d, p) in enumerate(zip(Y_STEPS, ypeers))
    ]
    def pass_on(copies, h):
        sent = []
        for e, (copy, d) in enumerate(zip(copies, (3, 1))):
            arrive(copy)
            piece = wexp.at[e, :, h * 4 + (z + d) % 4]
            sent.append(cp.start(piece, piece, zpeers[2 * e]))
        return sent

    cy3 = cot_middle_y(cy2)
    arrive(bx)
    bz += [cp.start(bf.at[:, f_far], bf.at[:, f_far], p) for p in zpeers]
    pass_on(own_z, xh)
    total = tokf[y].astype(F32) + part[y].astype(F32)
    for k, copy in enumerate(ps):
        arrive(copy)
        total = total + got[k].astype(F32)
    resid[...] = total
    saved.append(here(resid, resid_o))
    h2[...] = (total * inverse_norm(total) * gain_two).astype(BF)
    over_y, over_x = plane_gather(cp, arrive, h2, h2f, me, sib, 64)
    h2_y, h2_then_y, h2_middle_y, h2_last_y = over_y
    h2_x, h2_then_x, h2_middle_x, h2_last_x = over_x
    hx = h2_x()
    hy = h2_y()
    own_h2 = here(h2, h2f.at[xh, y, xl, co])

    cx3 = cot_middle_x(cx2)
    for copy in ex:
        arrive(copy)
    far_rows = wexp.at[:, :, f_far]
    far_z = [cp.start(far_rows, far_rows, zpeers[k]) for k in (0, 2)]
    own_h2.wait()
    hy2 = h2_then_y(hx)
    hx2 = h2_then_x(hy)
    cot_sib = [cy2[2], cx2[2]] + cot_last_y(cy3) + cot_last_x(cx3)
    lb.wait()
    for copy in bz:
        arrive(copy)
    for k in range(16):
        sw[k * 96 : (k + 1) * 96] = nn(rows, bf[k].reshape(128, 256)).astype(BF)
    saved.append(here(sw, sw_o))
    lr.wait()
    for copy in rgs + cot_sib:
        arrive(copy)

    first = c * 4 + xh * 2

    def gated_rows(rg_ref, cot_ref, gy_ref, pick_ref, gated_ref, gz_ref):
        pick, gated = dispatch_rows(rg_ref, first)
        g = cot_ref[...].reshape(256, 1536)
        gy_ref[...] = nn(gated, g).astype(BF).reshape(2, 1, 48, 1536)
        gz_ref[0] = nn(g, sw[:, 128:256])
        pick_ref[0], gated_ref[0] = pick, gated

    picks = pl.BlockSpec((1, 96, 256), lambda p: (p, 0, 0))
    whole = pl.BlockSpec((1, 256, 128), lambda p: (p, 0, 0))
    def gated_half(h):
        at = pl.ds(h * 8, 8)
        pltpu.emit_pipeline(
            gated_rows,
            grid=(8,),
            in_specs=[
                pl.BlockSpec((2, 16, 128), lambda p: (p, 0, 0)),
                pl.BlockSpec(
                    (1, 1, 2, 128, 1536), lambda p: (p // 2, p % 2, 0, 0, 0), pipeline_mode=pl.Buffered(4)
                ),
            ],
            out_specs=[pl.BlockSpec((2, 1, 48, 1536), lambda p: (0, p, 0, 0)), picks, picks, whole],
        )(rgf.at[h], cotf.at[h], gy.at[:, at], pick_o.at[at], gated_o.at[at], gz_o.at[at])

    gated_half(0)
    pass_on(far_z, 1 - xh)
    hy3 = h2_middle_y(hy2)
    hx3 = h2_middle_x(hx2)
    gated_half(1)
    h2_last_y(hy3)
    h2_last_x(hx3)
    for copy in later + saved:
        copy.wait()
    cp.finish(got_already)


def front(*ins):
    outs = (
        SDS((2, 4, 2, 2, 128, 1536), BF),
        SDS((2, 4, 2, 2, 128, 1536), BF),
        SDS((2, 3, 8, 192, 512), BF),
        SDS((4, 128, 1536), BF),
        SDS((4, 4, 128, 256), BF),
        SDS((2, 16, 48, 1536), BF),
        SDS((16, 96, 256), BF),
        SDS((16, 96, 256), BF),
        SDS((16, 256, 128), F32),
        SDS((2, 16, 16, 128), F32),
        SDS((1536, 1152), BF),
        SDS((1536, 256), BF),
        SDS((512, 640), BF),
        SDS((512, 384), BF),
        SDS((4, 384, 128), F32),
        SDS((128, 1536), F32),
    )
    return pl.pallas_call(
        front_kernel,
        out_shape=outs,
        in_specs=[ANY] * 2 + [VM] * (len(ins) - 5) + [ANY] * 3,
        out_specs=(ANY,) * 16,
        scratch_shapes=[
            pltpu.SemaphoreType.DMA((160,)),
            pltpu.SemaphoreType.DMA((160,)),
            pltpu.SemaphoreType.DMA((24,)),
            pltpu.VMEM((1536, 1152), BF),
            pltpu.VMEM((1536, 256), BF),
            pltpu.VMEM((512, 640), BF),
            pltpu.VMEM((512, 384), BF),
            pltpu.VMEM((4, 384, 128), F32),
            pltpu.VMEM((128, 1536), F32),
            pltpu.VMEM((4, 16, 1152), BF),
            pltpu.VMEM((16, 16, 256), BF),
            pltpu.VMEM((4, 3, 192, 512), BF),
            pltpu.VMEM((16, 128), F32),
            pltpu.VMEM((4, 2, 16, 1152), BF),
            pltpu.VMEM((4, 2, 2, 8, 16, 1152), BF),
            pltpu.VMEM((16, 16, 256), BF),
            pltpu.VMEM((16, 8, 16, 256), BF),
            pltpu.VMEM((4, 128, 1536), BF),
            pltpu.VMEM((4, 4, 128, 256), BF),
            pltpu.VMEM((384, 2048), F32),
            pltpu.VMEM((4, 128, 1536), BF),
            pltpu.VMEM((3, 128, 1536), BF),
            pltpu.VMEM((128, 1536), BF),
        ],
        compiler_params=pltpu.CompilerParams(
            collective_id=1, has_side_effects=True, vmem_limit_bytes=VMEM_LIMIT
        ),
        cost_estimate=pl.CostEstimate(flops=6 * 10**9, bytes_accessed=60 * 10**6, transcendentals=3 * 10**6),
    )(*ins)


def add_blocks(*refs):
    total = refs[0][...].astype(F32)
    for ref in refs[1:-1]:
        total = total + ref[...].astype(F32)
    refs[-1][...] = total.astype(refs[-1].dtype)


def add_arrays(block, ins, out):
    spec = pl.BlockSpec((1,) + block, lambda m, r: (m, 0, r, 0))
    pltpu.emit_pipeline(add_blocks, grid=(3, 2), in_specs=[spec] * len(ins), out_specs=[spec])(*ins, out)


def back_kernel(
    pick_in, gated_in, gy_in, gz_in, wexp, h2f, cotf, resid_i, cot_i, w_i, sw_i, tokf_i, qkv_i, kvf_i, lse_i, att_i,
    eg, y_b, y_s, g_s, pick_s, gated_s, hid_b, hid_s, gcd_b, gcd_s, gh2p, outp, zb, sb, xb, goy, gox, aout, bout,
    lout_o, igrad_o,
    send, recv, loc, lout, igrad, goty, gotx, midy, midx, moy, mox, gety, getx, resid, cot, gres, gattn, dkvr, gh1g, dath, zg, xg, xgot, bgot, bxg,
    sw, sdw, db, ds,
):
    y, xl, co, xh, z = coords()
    i, c = xl * 2 + co, y * 4 + xl * 2 + co
    sib = dev(y, xl, 1 - co, xh, z)
    xpeer = dev(y, 1 - xl, co, xh, z)
    xfar = dev(y, xl, co, 1 - xh, z)
    ypeers = [dev((y + d) % 4, xl, co, xh, z) for d in Y_STEPS]
    zpeers = [dev(y, xl, co, xh, (z + d) % 4) for d in Y_STEPS]
    places = ctx_places(y, xl, co)
    cpeers = [dev(*p, xh, z) for p in places]
    xpeers = []
    for d in Y_STEPS:
        hh, ll = x_place(xh, xl, d)
        xpeers.append(dev(y, ll, co, hh, z))
    barrier(cpeers + [dev(y, k, co, 1 - xh, z) for k in range(2)] + zpeers)
    cp = Copies(send, recv)
    n_local = [0]

    def here(src, dst):
        copy = pltpu.make_async_copy(src, dst, loc.at[n_local[0]])
        n_local[0] += 1
        copy.start()
        return copy

    got_already, sent_already = [], []

    def arrive(copy):
        copy.wait_recv()
        got_already.append(copy)

    def gone(copies):
        for copy in copies:
            copy.wait_send()
            sent_already.append(copy)

    low, high = pl.ds(0, 64), pl.ds(64, 64)
    ynext, znext = [(y + d) % 4 for d in range(4)], [(z + d) % 4 for d in range(4)]
    xnext = [x_place(xh, xl, d) for d in range(4)]
    oco, oxl, oxh = 1 - co, 1 - xl, 1 - xh
    xh8, oxh8 = xh * 8, 8 - xh * 8
    place_index = [p[0] * 4 + p[1] * 2 + p[2] for p in places]
    kv_peers = [(a * 2 + b, dev(y, a, b, xh, z)) for a, b in ((oxl, co), (oxl, oco), (xl, oco))]
    front_cols, back_cols = pl.ds(0, 128), pl.ds(128, 128)
    mine_cols = pl.ds(pl.multiple_of(co * 128, 128), 128)
    first = [
        here(sw_i.at[:, front_cols], sw.at[:, front_cols]),
        here(sw_i.at[:, back_cols], sdw.at[:, front_cols]),
        here(resid_i, resid),
        here(cot_i, cot),
    ]
    pairs = pl.BlockSpec((1, 1, 2, 128, 1536), lambda p: (div(p, 2), rem(p, 2), 0, 0, 0))
    picks = pl.BlockSpec((1, 96, 256), lambda p: (p, 0, 0))

    def expert_copies(e):
        return [
            pltpu.make_async_remote_copy(
                eg.at[e, :, :, znext[d]],
                zb.at[k, e],
                send.at[e * 3 + k],
                recv.at[e * 3 + k],
                device_id=zpeers[k],
                device_id_type=MESH,
            )
            for k, d in enumerate(Y_STEPS)
        ]

    def expert_push(e):
        for copy in expert_copies(e):
            copy.start()

    def expert_rows(e, gg):
        return pltpu.make_async_remote_copy(
            gg.at[e], g_s.at[e], send.at[6 + e], recv.at[6 + e], device_id=sib, device_id_type=MESH
        )

    def expert_out(e, xy):
        return pltpu.make_async_remote_copy(
            xy.at[e], y_s.at[e], send.at[8 + e], recv.at[8 + e], device_id=sib, device_id_type=MESH
        )

    cp.n = 12
    early = [
        cp.start(sw_i.at[:, front_cols], sw.at[:, back_cols], sib),
        cp.start(sw_i.at[:, back_cols], sdw.at[:, back_cols], sib),
        cp.start(pick_in, pick_s, sib),
        cp.start(gated_in, gated_s, sib),
    ]
    for copy in first[:2]:
        copy.wait()

    ds[...] = jnp.zeros_like(ds)

    def hidden_rows(k):
        src, dst = ((gcd_b, gcd_s), (hid_b, hid_s))[k]
        return pltpu.make_async_remote_copy(
            src.at[:, oco], dst, send.at[10 + k], recv.at[10 + k], device_id=sib, device_id_type=MESH
        )

    def at8(own):
        return pl.ds(xh8 if own else oxh8, 8)

    blocks = pl.BlockSpec((1, 1, 128, 1536), lambda p: (div(p, 2), rem(p, 2), 0, 0))
    thin = pl.BlockSpec((1, 2, 128, 128), lambda p: (p, 0, 0, 0))

    def experts(xy, gg, dw):
        lg = here(gy_in, gg)

        def grads_copy(e):
            return pltpu.make_async_copy(dw, eg.at[e], loc.at[78 + e])

        def work(w, u_s, ga_s, gb_s):
            lw = [here(wexp.at[0], w.at[0])]

            def own_rows(pick_ref, h2_ref, gz_ref, hid_ref, gcd_ref):
                h2 = h2_ref[...].reshape(256, 1536)
                xy[:, xh8 + pl.program_id(0)] = nn(pick_ref[0], h2).astype(BF).reshape(2, 48, 1536)
                pre, gz = nn(h2, sw[:, 0:128]), gz_ref[0]
                act, slope = silu_parts(pre)
                up = half_turn(pre)
                lane = lax.broadcasted_iota(jnp.int32, (256, 128), 1)
                hid = jnp.where(lane < 64, act * up, 0.0).astype(BF)
                gcd = jnp.where(lane < 64, gz * up * slope, half_turn(gz * act)).astype(BF)
                hid_ref[0] = hid.reshape(2, 128, 128)
                gcd_ref[0] = gcd.reshape(2, 128, 128)
                ds[0:128] += tn(gcd, h2)

            def other_rows(pick_ref, h2_ref):
                x = nn(pick_ref[0], h2_ref[...].reshape(256, 1536)).astype(BF)
                xy[:, oxh8 + pl.program_id(0)] = x.reshape(2, 48, 1536)

            deep = pl.BlockSpec(
                (1, 1, 2, 128, 1536), lambda p: (div(p, 2), rem(p, 2), 0, 0, 0), pipeline_mode=pl.Buffered(4)
            )
            pltpu.emit_pipeline(
                own_rows,
                grid=(8,),
                in_specs=[picks, deep, pl.BlockSpec((1, 256, 128), lambda p: (p, 0, 0))],
                out_specs=[thin, thin],
            )(pick_in.at[at8(True)], h2f.at[xh], gz_in.at[at8(True)], hid_b, gcd_b)
            for e in range(2):
                hidden_rows(e).start()
            pltpu.emit_pipeline(other_rows, grid=(8,), in_specs=[picks, deep])(
                pick_in.at[at8(False)], h2f.at[oxh]
            )
            lw.append(here(wexp.at[1], w.at[1]))
            lg.wait()
            for e in range(2):
                lw[e].wait()
                for t in range(2):
                    cols = slice(t * 256, (t + 1) * 256)
                    x, g = xy[e].reshape(768, 1536), gg[e].reshape(768, 1536)
                    a = nn(x, w[e, 0, :, :, cols].reshape(1536, 256))
                    b = nn(x, w[e, 1, :, :, cols].reshape(1536, 256))
                    gu = nn(g, w[e, 2, :, :, cols].reshape(1536, 256))
                    act, slope = silu_parts(a)
                    u_s[:, cols] = (act * b).astype(BF)
                    ga_s[:, cols] = (gu * b * slope).astype(BF)
                    gb_s[:, cols] = (gu * act).astype(BF)
                if e:
                    grads_copy(0).wait()
                    expert_push(0)

                def row_tile(t, carry):
                    at = pl.ds(pl.multiple_of(t * 384, 384), 384)
                    two, h, half = pl.ds(t * 2, 2), div(t, 2), pl.ds(rem(t, 2) * 2, 2)
                    g = gg[e, :, :, at].reshape(768, 384)
                    dw[2, h, half] = tn(g, u_s[...]).astype(BF).reshape(2, 192, 512)
                    back = nt(ga_s[...], w[e, 0, two].reshape(384, 512))
                    back = back + nt(gb_s[...], w[e, 1, two].reshape(384, 512))
                    gg[e, :, :, at] = back.astype(BF).reshape(16, 48, 384)
                    return carry

                def tile(t, carry):
                    at = pl.ds(pl.multiple_of(t * 384, 384), 384)
                    two, h, half = pl.ds(t * 2, 2), div(t, 2), pl.ds(rem(t, 2) * 2, 2)
                    x = xy[e, :, :, at].reshape(768, 384)
                    dw[0, h, half] = tn(x, ga_s[...]).astype(BF).reshape(2, 192, 512)
                    dw[1, h, half] = tn(x, gb_s[...]).astype(BF).reshape(2, 192, 512)
                    out = nt(u_s[...], w[e, 2, two].reshape(384, 512))
                    xy[e, :, :, at] = out.astype(BF).reshape(16, 48, 384)
                    return carry

                lax.fori_loop(0, 4, row_tile, 0)
                expert_rows(e, gg).start()
                lax.fori_loop(0, 4, tile, 0)
                expert_out(e, xy).start()
                grads_copy(e).start()

        pl.run_scoped(
            work,
            pltpu.VMEM((2, 3, 8, 192, 512), BF),
            pltpu.VMEM((768, 512), BF),
            pltpu.VMEM((768, 512), BF),
            pltpu.VMEM((768, 512), BF),
        )
        ly = here(xy, y_b)
        for e in range(2):
            expert_rows(e, gg).wait()
            hidden_rows(e).wait()

        def row_sums(pick_ref, other_ref, rows_ref, hid_ref, more_ref, gh_ref):
            p = pl.program_id(0)
            picks = jnp.concatenate([pick_ref[0, :, mine_cols], other_ref[0, :, mine_cols]], 0)
            rows = jnp.concatenate([gg[:, p].reshape(96, 1536), rows_ref[...].reshape(96, 1536)], 0)
            gh = tn(picks, rows)
            own = div(p, 8) == xh

            @pl.when(own)
            def _():
                hidden = jnp.concatenate([hid_ref[0, 0], more_ref[0]], 1)
                gh_ref[...] = (gh + nt(hidden, sw[...])).astype(BF).reshape(1, 1, 1, 128, 1536)

            @pl.when(jnp.logical_not(own))
            def _():
                gh_ref[...] = gh.astype(BF).reshape(1, 1, 1, 128, 1536)

        def own_pair(p):
            return jnp.minimum(jnp.maximum(p - xh8, 0), 7)

        deep_rows = pl.BlockSpec((2, 1, 48, 1536), lambda p: (0, p, 0, 0), pipeline_mode=pl.Buffered(3))
        for copy in early:
            arrive(copy)
        pltpu.emit_pipeline(
            row_sums,
            grid=(16,),
            in_specs=[
                picks,
                picks,
                deep_rows,
                pl.BlockSpec((1, 1, 128, 128), lambda p: (own_pair(p), 0, 0, 0)),
                pl.BlockSpec((1, 128, 128), lambda p: (own_pair(p), 0, 0)),
            ],
            out_specs=[pl.BlockSpec((1, 1, 1, 128, 1536), lambda p: (div(p, 8), rem(div(p, 2), 4), rem(p, 2), 0, 0))],
        )(pick_in, pick_s, g_s, gcd_b.at[:, pl.ds(co, 1)], gcd_s, gh2p)
        grads_copy(1).wait()
        expert_push(1)
        ly.wait()
        for e in range(2):
            expert_out(e, xy).wait()

    pl.run_scoped(
        experts,
        pltpu.VMEM((2, 16, 48, 1536), BF),
        pltpu.VMEM((2, 16, 48, 1536), BF),
        pltpu.VMEM((3, 2, 4, 192, 512), BF),
    )

    def dense(
        augy, augx, miney, minex, w, tokf, qkv, kvf, lse, att, go, dk, dv, dkvs, gqkv, gh1s, da, zs, s2, s3, bz, bsum
    ):
        def sum_piece(xp, axis, d):
            if axis == "y":
                return xp.at[:, ynext[d], :, low]
            return xp.at[xnext[d][0], :, xnext[d][1], high]

        def sum_half(xp, axis, d, n):
            if axis == "y":
                return xp.at[n, ynext[d], :, low]
            return xp.at[xnext[d][0], pl.ds(2 * n, 2), xnext[d][1], high]

        def landing(to, axis, k, n):
            return to.at[k, n] if axis == "y" else to.at[k, pl.ds(2 * n, 2)]

        def sum_push(xp, mids, to):
            halves, sent, loads = {}, [], {}
            for axis, peers in (("y", ypeers), ("x", xpeers)):
                for n in range(2):
                    halves[axis, n] = cp.start(sum_half(xp, axis, 2, n), mids[axis].at[n], peers[2 * n])
            for axis, peers in (("y", ypeers), ("x", xpeers)):
                for n in range(2):
                    src = sum_half(xp, axis, (1, 3)[n], 1 - n)
                    sent.append(cp.start(src, landing(to[axis], axis, n, 1 - n), peers[2 * n]))
                    loads[axis, n] = here(sum_half(xp, axis, (1, 3)[n], n), aug[axis].at[n])
            return halves, sent, loads

        def sum_middle(axis, mids, to, started):
            halves, sent, loads = started
            peers = ypeers if axis == "y" else xpeers
            for n in range(2):
                loads[axis, n].wait()
                arrive(halves[axis, n])
                for k in range(2):
                    tot = aug[axis][n, k].astype(F32) + mids[axis][n, k].astype(F32)
                    aug[axis][n, k] = tot.astype(BF)
                sent.append(cp.start(aug[axis].at[n], landing(to[axis], axis, n, n), peers[2 * n]))

        aug = {"y": augy, "x": augx}
        mids_g, mids_o = {"y": midy, "x": midx}, {"y": moy, "x": mox}
        to_g, to_o = {"y": goty, "x": gotx}, {"y": goy, "x": gox}

        def sum_own(xp):
            return [here(sum_piece(xp, "y", 0), miney.at[0]), here(sum_piece(xp, "x", 0), minex.at[0])]

        def sum_second():
            for h in range(2):
                for l in range(2):
                    tot = miney[0, h, l].astype(F32)
                    for k in range(2):
                        tot = tot + goty[k, h, l].astype(F32)
                    miney[0, h, l] = tot.astype(BF)
            for a in range(4):
                tot = minex[0, a].astype(F32)
                for k in range(2):
                    tot = tot + gotx[k, a].astype(F32)
                minex[0, a] = tot.astype(BF)

        def sum_last(nth):
            sent = []
            for k, d in enumerate(Y_STEPS):
                hh, ll = xnext[d]
                sent.append(cp.start(miney.at[0, hh, ll], gety.at[nth, k], xpeers[k]))
                sent.append(cp.start(minex.at[0, ynext[d]], getx.at[nth, k], ypeers[k]))
            return sent

        def sum_end(nth, sent):
            for copy in sent:
                arrive(copy)
            top, bottom = miney[0, xh, xl].astype(F32), minex[0, y].astype(F32)
            for k in range(3):
                top = top + gety[nth, k].astype(F32)
                bottom = bottom + getx[nth, k].astype(F32)
            return jnp.concatenate([top, bottom], 0)

        sums_g = sum_push(gh2p, mids_g, to_g)
        own_g = sum_own(gh2p)
        first.append(here(w_i, w))
        second = [here(qkv_i, qkv), here(kvf_i, kvf), here(lse_i, lse), here(att_i, att)]
        third = [here(tokf_i, tokf)]

        def expert_sums(e):
            for copy in expert_copies(e):
                copy.wait()
            ins = [eg.at[e, :, :, z], zb.at[0, e], zb.at[1, e], zb.at[2, e]]
            add_arrays((2, 96, 512), ins, sb.at[e])

        def expert_far(e):
            return cp.start(sb.at[e, :, oxh], xb.at[e], xfar)


        def output_rows(own):
            def body(pick_ref, other_ref, rows_ref, more_ref, *refs):
                picks = jnp.concatenate([pick_ref[0, :, mine_cols], other_ref[0, :, mine_cols]], 0)
                rows = [rows_ref[...].reshape(96, 1536), more_ref[...].reshape(96, 1536)]
                out = tn(picks, jnp.concatenate(rows, 0))
                if own:
                    out = out + nt(jnp.concatenate([refs[0][0, 0], refs[1][0]], 1), sdw[...])
                refs[-1][...] = out.astype(BF).reshape(1, 1, 128, 1536)

            at = at8(own)
            rows = pl.BlockSpec((2, 1, 48, 1536), lambda p: (0, p, 0, 0))
            specs = [picks, picks, rows, rows]
            args = [gated_in.at[at], gated_s.at[at], y_b.at[:, at], y_s.at[:, at]]
            if own:
                specs += [
                    pl.BlockSpec((1, 1, 128, 128), lambda p: (p, 0, 0, 0)),
                    pl.BlockSpec((1, 128, 128), lambda p: (p, 0, 0)),
                ]
                args += [hid_b.at[:, pl.ds(co, 1)], hid_s]
            pltpu.emit_pipeline(body, grid=(8,), in_specs=specs, out_specs=[blocks])(
                *args, outp.at[xh if own else oxh]
            )

        output_rows(True)
        sum_middle("y", mids_g, to_g, sums_g)
        sum_middle("x", mids_g, to_g, sums_g)
        output_rows(False)

        def down_rows(cot_ref, hid_ref):
            ds[128:256] += tn(hid_ref[0].reshape(256, 128), cot_ref[...].reshape(256, 1536))

        pltpu.emit_pipeline(down_rows, grid=(8,), in_specs=[pairs, thin])(cotf.at[xh], hid_b)
        rows = one_hot_rows()
        shared_grads = tn(ds[...].astype(BF), eye(256, 256)).astype(BF)
        for k in range(16):
            block = shared_grads[k * 96 : (k + 1) * 96]
            db[k] = tn(rows, block).astype(BF).reshape(2, 4, 16, 256)
        bs = [cp.start(db.at[:, :, znext[d]], bgot.at[k], p) for k, (d, p) in enumerate(zip(Y_STEPS, zpeers))]

        expert_sums(0)
        for copy in first[2:]:
            copy.wait()
        gains = nt(eye_rows(), w[:, 640:768])
        gain_one, gain_two = gains[0:1], gains[1:2]
        inv = inverse_norm(resid[...])
        xh2 = resid[...] * inv
        for copy in sums_g[1]:
            arrive(copy)
        for copy in own_g:
            copy.wait()
        sum_second()
        last_g = sum_last(0)
        gh2 = sum_end(0, last_g)
        gain_two_grad = jnp.sum(gh2 * xh2, 0, keepdims=True)
        inner = gh2 * gain_two
        row = inv * (inner - xh2 * jnp.mean(inner * xh2, -1, keepdims=True))
        gres[...] = cot[...].astype(F32) + row
        gattn[y] = gres[...].astype(BF)
        ga = [cp.start(gattn.at[y], gattn.at[y], p) for p in ypeers]

        gone(list(sums_g[0].values()) + sums_g[1] + last_g)
        sums_o = sum_push(outp, mids_o, to_o)
        own_o = sum_own(outp)

        for copy in second:
            copy.wait()
        sum_middle("x", mids_o, to_o, sums_o)
        for copy in ga:
            arrive(copy)
        dk[...] = jnp.zeros_like(dk)
        dv[...] = jnp.zeros_like(dv)
        for j in range(4):
            rows_j = slice(j * 128, (j + 1) * 128)
            go[rows_j] = nn(gattn[j], w[:, 768:1152]).astype(BF)
            q, g = head_rows(qkv, j), head_rows(go, j)
            delta = jnp.sum(head_rows(att, j).astype(F32) * g.astype(F32), -1, keepdims=True)
            total = lse[j][:, :1]
            dq = jnp.zeros((384, 128), F32)
            for t in range(j + 1):
                keys = kvf[t].reshape(512, 256)
                s = nt(q, keys[:, :128]) * SCALE
                p = jnp.exp(s - total)
                if t == j:
                    p = jnp.where(allowed(512), p, 0.0)
                gs = (p * (nt(g, keys[:, 128:]) - delta)).astype(BF)
                at = slice(t * 512, (t + 1) * 512)
                dv[at] += tn(p.astype(BF), g)
                dk[at] += tn(gs, q)
                dq = dq + nn(gs, keys[:, :128])
            dq = (dq * SCALE).astype(BF)
            for h in range(3):
                gqkv[rows_j, h * 128 : (h + 1) * 128] = dq[h * 128 : (h + 1) * 128]
        for j in range(4):
            for k in range(4):
                at = slice((j * 4 + k) * 128, (j * 4 + k + 1) * 128)
                dkvs[j, k, :, 0:128] = (dk[at] * SCALE).astype(BF)
                dkvs[j, k, :, 128:256] = dv[at].astype(BF)
        kvs = [
            cp.start(dkvs.at[:, p], dkvr.at[k], q)
            for k, (p, q) in enumerate(kv_peers)
        ]
        ex0 = expert_far(0)
        sum_middle("y", mids_o, to_o, sums_o)
        def expand(block, yy, cols):
            for k in range(4):
                part = tn(rows, block[k * 96 : (k + 1) * 96]).astype(BF)
                da[yy, k // 2, k % 2, :, :, :, cols] = part.reshape(2, 4, 16, -1)

        def dense_core(cols):
            return cp.start(da.at[:, :, oco, :, :, :, cols], dath.at[:, :, :, :, :, cols], sib)

        def dense_z(copy, cols):
            arrive(copy)
            for a in range(4):
                for b in range(2):
                    tot = da[a, b, co, :, :, :, cols].astype(F32) + dath[a, b, :, :, :, cols].astype(F32)
                    da[a, b, co, :, :, :, cols] = tot.astype(BF)
            return [
                cp.start(da.at[:, :, co, :, znext[d], :, cols], zg.at[k, :, :, :, :, cols], p)
                for k, (d, p) in enumerate(zip(Y_STEPS, zpeers))
            ]

        def dense_far(copies, cols):
            for copy in copies:
                arrive(copy)
            for a in range(4):
                for b in range(2):
                    tot = da[a, b, co, :, z, :, cols].astype(F32)
                    for k in range(3):
                        tot = tot + zg[k, a, b, :, :, cols].astype(F32)
                    for h in range(2):
                        zs[h, a, b, :, cols] = tot[h].astype(BF)
            return cp.start(zs.at[oxh, :, :, :, cols], xg.at[:, :, :, cols], xfar)

        def dense_near(copy, cols):
            arrive(copy)
            for a in range(4):
                for b in range(2):
                    tot = zs[xh, a, b, :, cols].astype(F32) + xg[a, b, :, cols].astype(F32)
                    s2[b, a, :, cols] = tot.astype(BF)
            return cp.start(s2.at[oxl, :, :, cols], xgot.at[:, :, cols], xpeer)

        def dense_y(copy, cols):
            arrive(copy)
            for a in range(4):
                s3[a, :, cols] = (s2[xl, a, :, cols].astype(F32) + xgot[a, :, cols].astype(F32)).astype(BF)
            last.append(here(s3.at[y, :, cols], aout.at[y, :, cols]))
            return [
                cp.start(s3.at[ynext[d], :, cols], aout.at[y, :, cols], p) for d, p in zip(Y_STEPS, ypeers)
            ]

        head, tail = pl.ds(0, 768), pl.ds(768, 384)
        last = []
        for yy in range(4):
            tile = slice(yy * 384, (yy + 1) * 384)
            block = tn(gattn[:, :, tile].reshape(512, 384), att[...])
            expand(block.astype(BF), yy, tail)
        tail_c = dense_core(tail)
        expert_sums(1)
        ex1 = expert_far(1)

        tail_z = dense_z(tail_c, tail)
        for copy in third:
            copy.wait()
        for copy in kvs:
            arrive(copy)
        gone(ga)
        gain_one_grad = jnp.zeros((1, 1536), F32)
        for j in range(4):
            rows_j = slice(j * 128, (j + 1) * 128)
            kv = dkvs[j, i].astype(F32)
            for k in range(3):
                kv = kv + dkvr[k, j].astype(F32)
            gqkv[rows_j, 384:640] = kv.astype(BF)
            gh1 = nt(gqkv[rows_j], w[:, :640])
            v = tokf[j].astype(F32)
            scaled = v * inverse_norm(v)
            gain_one_grad = gain_one_grad + jnp.sum(gh1 * scaled, 0, keepdims=True)
            gattn[j] = (scaled * gain_one).astype(BF)
            gh1s[j] = gh1.astype(BF)
        hs = [
            cp.start(gh1s.at[ynext[d]], gh1g.at[k], p) for k, (d, p) in enumerate(zip(Y_STEPS, ypeers))
        ]
        gain_rows = jnp.concatenate([gain_one_grad, gain_two_grad, jnp.zeros((6, 1536), F32)], 0)
        for yy in range(4):
            tile = slice(yy * 384, (yy + 1) * 384)
            block = tn(gattn[:, :, tile].reshape(512, 384), gqkv[...])
            expand(block.astype(BF), yy, pl.ds(0, 640))
            expand(tn(gain_rows[:, tile].astype(BF), eye_rows()).astype(BF), yy, pl.ds(640, 128))
        head_c = dense_core(head)
        head_z = dense_z(head_c, head)

        tail_x = dense_far(tail_z, tail)
        for copy in bs:
            arrive(copy)
        for a in range(16):
            tot = db[a, :, z].astype(F32)
            for k in range(3):
                tot = tot + bgot[k, a].astype(F32)
            bz[0, a], bz[1, a] = tot[0].astype(BF), tot[1].astype(BF)
        bx = cp.start(bz.at[oxh], bxg, xfar)

        for copy in sums_o[1]:
            arrive(copy)
        back_in = [here(goy, goty), here(gox, gotx)]
        for copy in back_in + own_o:
            copy.wait()
        sum_second()
        last_o = sum_last(1)
        head_x = dense_far(head_z, head)
        gh1 = gh1s[y].astype(F32)
        for k, copy in enumerate(hs):
            arrive(copy)
            gh1 = gh1 + gh1g[k].astype(F32)
        v = tokf[y].astype(F32)
        inv = inverse_norm(v)
        inner = gh1 * gain_one
        xh1 = v * inv
        igrad[...] = gres[...] + inv * (inner - xh1 * jnp.mean(inner * xh1, -1, keepdims=True))
        igrad_c = here(igrad, igrad_o)

        tail_n = dense_near(tail_x, tail)
        arrive(bx)
        for a in range(16):
            bsum[a] = (bz[xh, a].astype(F32) + bxg[a].astype(F32)).astype(BF)
        bo = [cp.start(bsum.at[p], bout.at[c], q) for p, q in zip(place_index, cpeers)]
        last.append(here(bsum.at[c], bout.at[c]))
        head_n = dense_near(head_x, head)
        outs = dense_y(tail_n, tail) + dense_y(head_n, head)

        lout[...] = (resid[...] + sum_end(1, last_o)).astype(BF)
        last += [igrad_c, here(lout, lout_o)]
        for copy in last:
            copy.wait()
        for copy in cp.started:
            if not any(copy is r for r in sent_already):
                copy.wait_send()
            if not any(copy is r for r in got_already):
                copy.wait_recv()

    pl.run_scoped(
        dense,
        pltpu.VMEM((2, 2, 64, 1536), BF),
        pltpu.VMEM((2, 2, 64, 1536), BF),
        pltpu.VMEM((1, 2, 2, 64, 1536), BF),
        pltpu.VMEM((1, 4, 64, 1536), BF),
        pltpu.VMEM((1536, 1152), BF),
        pltpu.VMEM((4, 128, 1536), BF),
        pltpu.VMEM((512, 640), BF),
        pltpu.VMEM((4, 4, 128, 256), BF),
        pltpu.VMEM((4, 384, 128), F32),
        pltpu.VMEM((512, 384), BF),
        pltpu.VMEM((512, 384), BF),
        pltpu.VMEM((2048, 128), F32),
        pltpu.VMEM((2048, 128), F32),
        pltpu.VMEM((4, 4, 128, 256), BF),
        pltpu.VMEM((512, 640), BF),
        pltpu.VMEM((4, 128, 1536), BF),
        pltpu.VMEM((4, 2, 2, 2, 4, 16, 1152), BF),
        pltpu.VMEM((2, 4, 2, 16, 1152), BF),
        pltpu.VMEM((2, 4, 16, 1152), BF),
        pltpu.VMEM((4, 16, 1152), BF),
        pltpu.VMEM((2, 16, 16, 256), BF),
        pltpu.VMEM((16, 16, 256), BF),
    )


def back(*ins):
    outs = (
        SDS((2, 3, 2, 4, 192, 512), BF),
        SDS((2, 16, 48, 1536), BF),
        SDS((2, 16, 48, 1536), BF),
        SDS((2, 16, 48, 1536), BF),
        SDS((16, 96, 256), BF),
        SDS((16, 96, 256), BF),
        SDS((8, 2, 128, 128), BF),
        SDS((8, 128, 128), BF),
        SDS((8, 2, 128, 128), BF),
        SDS((8, 128, 128), BF),
        SDS((2, 4, 2, 128, 1536), BF),
        SDS((2, 4, 2, 128, 1536), BF),
        SDS((3, 2, 3, 2, 192, 512), BF),
        SDS((2, 3, 2, 192, 512), BF),
        SDS((2, 3, 192, 512), BF),
        SDS((2, 2, 2, 64, 1536), BF),
        SDS((2, 4, 64, 1536), BF),
        SDS((4, 16, 1152), BF),
        SDS((16, 16, 256), BF),
        SDS((128, 1536), BF),
        SDS((128, 1536), F32),
    )
    out = pl.pallas_call(
        back_kernel,
        out_shape=outs,
        in_specs=[ANY] * len(ins),
        out_specs=(ANY,) * 21,
        scratch_shapes=[
            pltpu.SemaphoreType.DMA((128,)),
            pltpu.SemaphoreType.DMA((128,)),
            pltpu.SemaphoreType.DMA((80,)),
            pltpu.VMEM((128, 1536), BF),
            pltpu.VMEM((128, 1536), F32),
            pltpu.VMEM((2, 2, 2, 64, 1536), BF),
            pltpu.VMEM((2, 4, 64, 1536), BF),
            pltpu.VMEM((2, 2, 64, 1536), BF),
            pltpu.VMEM((2, 2, 64, 1536), BF),
            pltpu.VMEM((2, 2, 64, 1536), BF),
            pltpu.VMEM((2, 2, 64, 1536), BF),
            pltpu.VMEM((2, 3, 64, 1536), BF),
            pltpu.VMEM((2, 3, 64, 1536), BF),
            pltpu.VMEM((128, 1536), F32),
            pltpu.VMEM((128, 1536), BF),
            pltpu.VMEM((128, 1536), F32),
            pltpu.VMEM((4, 128, 1536), BF),
            pltpu.VMEM((3, 4, 128, 256), BF),
            pltpu.VMEM((3, 128, 1536), BF),
            pltpu.VMEM((4, 2, 2, 4, 16, 1152), BF),
            pltpu.VMEM((3, 4, 2, 2, 16, 1152), BF),
            pltpu.VMEM((4, 2, 16, 1152), BF),
            pltpu.VMEM((4, 16, 1152), BF),
            pltpu.VMEM((3, 16, 2, 16, 256), BF),
            pltpu.VMEM((16, 16, 256), BF),
            pltpu.VMEM((1536, 256), BF),
            pltpu.VMEM((1536, 256), BF),
            pltpu.VMEM((16, 2, 4, 16, 256), BF),
            pltpu.VMEM((256, 1536), F32),
        ],
        compiler_params=pltpu.CompilerParams(
            collective_id=2, has_side_effects=True, vmem_limit_bytes=62 * 2**20
        ),
        cost_estimate=pl.CostEstimate(flops=36 * 10**9, bytes_accessed=150 * 10**6, transcendentals=5 * 10**6),
    )(*ins)
    return out[19], out[20], out[17], out[18], out[13], out[14]


def unpack_kernel(
    lout, igrad, aout, bout, sb, xb,
    lout_o, igrad_o, gains_o, wq_o, wk_o, wv_o, wo_o, sg_o, su_o, sd_o, eg_o, eu_o, ed_o,
):
    xh = lax.axis_index("fsdp") // 4
    lout_o[...] = lout[...]
    igrad_o[...] = igrad[...]
    for e in range(2):
        for m, ref in enumerate((eg_o, eu_o, ed_o)):
            ref[xh * 2 + e] = sb[e, m, xh].astype(F32)
            ref[2 - xh * 2 + e] = xb[e, m].astype(F32)
    gain_sum = jnp.zeros((16, 128), F32)
    for k in range(4):
        wide, thin = slice(k * 384, (k + 1) * 384), slice(k * 128, (k + 1) * 128)
        block = aout[k].astype(F32)
        wq_o[:, wide] = block[:12, 0:384]
        wk_o[:, thin] = block[:12, 384:512]
        wv_o[:, thin] = block[:12, 512:640]
        gain_sum = gain_sum + block[:, 640:768]
        wo_o[:, wide] = block[:12, 768:1152]
    gains_o[...] = gain_sum
    front_half = lax.broadcasted_iota(jnp.int32, (16, 128), 1) < 64
    for k in range(8):
        at = slice(k * 128, (k + 1) * 128)
        one, two = bout[2 * k].astype(F32), bout[2 * k + 1].astype(F32)
        sg_o[:, at] = jnp.where(front_half, one[:, :128], half_turn(two[:, :128]))[:12]
        su_o[:, at] = jnp.where(front_half, half_turn(one[:, :128]), two[:, :128])[:12]
        sd_o[:, at] = jnp.where(front_half, one[:, 128:], half_turn(two[:, 128:]))[:12]


def unpack(*ins):
    outs = (
        SDS((128, 1536), BF),
        SDS((128, 1536), F32),
        SDS((16, 128), F32),
        SDS((12, 1536), F32),
        SDS((12, 512), F32),
        SDS((12, 512), F32),
        SDS((12, 1536), F32),
        SDS((12, 1024), F32),
        SDS((12, 1024), F32),
        SDS((12, 1024), F32),
        SDS((4, 192, 512), F32),
        SDS((4, 192, 512), F32),
        SDS((4, 192, 512), F32),
    )
    return pl.pallas_call(
        unpack_kernel,
        out_shape=outs,
        in_specs=[VM] * len(ins),
        out_specs=(VM,) * len(outs),
        compiler_params=pltpu.CompilerParams(vmem_limit_bytes=VMEM_LIMIT),
    )(*ins)


def local(
    tokens,
    cotangent,
    routes,
    gates,
    attn_gain,
    ffn_gain,
    w_query,
    w_key,
    w_value,
    w_out,
    shared_gate,
    shared_up,
    shared_down,
    expert_gate,
    expert_up,
    expert_down,
):
    tok = tokens.reshape(128, 1536)
    cot = cotangent.reshape(128, 1536)
    gains = jnp.stack([attn_gain, ffn_gain])
    (cot_f, h2_f, wexp, tok_f, kv_f, gy, pick, gated, gz, _, w, sw, qkv, att, lse, resid) = front(
        tok,
        cot,
        jnp.transpose(routes, (2, 0, 1)),
        jnp.transpose(gates, (2, 0, 1)),
        gains,
        w_query,
        w_key,
        w_value,
        w_out.T,
        shared_gate,
        shared_up,
        shared_down.T,
        expert_gate,
        expert_up,
        jnp.transpose(expert_down, (0, 2, 1)),
    )
    parts = back(
        pick, gated, gy, gz, wexp, h2_f, cot_f, resid, cot, w, sw, tok_f, qkv, kv_f, lse, att
    )
    (layer_out, input_grad, gain_grads, wq, wk, wv, wo, sg, su, sd, eg, eu, ed) = unpack(*parts)
    return (
        layer_out.reshape(1, 128, 1536),
        input_grad.reshape(1, 128, 1536),
        gain_grads[:12, 0],
        gain_grads[:12, 1],
        wq,
        wk,
        wv,
        wo.T,
        sg,
        su,
        sd.T,
        eg,
        eu,
        jnp.transpose(ed, (0, 2, 1)),
    )


def solution(mesh):
    both = ("ctx", "fsdp")
    rows = P("fsdp", "ctx", None)
    weights = (P(both),) * 2 + (P(both, None),) * 3 + (P(None, both),)
    weights = weights + (P(both, None),) * 2 + (P(None, both),)
    weights = weights + (P("ctx", "fsdp", None),) * 2 + (P("ctx", None, "fsdp"),)
    return jax.shard_map(
        local, mesh=mesh, in_specs=(rows,) * 4 + weights, out_specs=(rows,) * 2 + weights, check_vma=False
    )
```

```python
import jax
import jax.numpy as jnp
from jax import lax
from jax.experimental import pallas as pl
from jax.experimental.pallas import tpu as pltpu
from jax.sharding import PartitionSpec as P

BF = jnp.bfloat16
F32 = jnp.float32
EPS = 1e-05
MESH = pl.DeviceIdType.MESH
ANY = pl.BlockSpec(memory_space=pl.ANY)
VM = pl.BlockSpec(memory_space=pltpu.VMEM)
SDS = jax.ShapeDtypeStruct
SCALE = 128 ** (-0.5)
VMEM_LIMIT = 56 * 2**20


def div(x, n):
    return lax.div(x, lax.full_like(x, n))


def rem(x, n):
    return lax.rem(x, lax.full_like(x, n))


def nn(a, b):
    return lax.dot_general(a, b, (((1,), (0,)), ((), ())), preferred_element_type=F32)


def nt(a, b):
    return lax.dot_general(a, b, (((1,), (1,)), ((), ())), preferred_element_type=F32)


def tn(a, b):
    return lax.dot_general(a, b, (((0,), (0,)), ((), ())), preferred_element_type=F32)


def silu_parts(pre_act):
    sig = 1.0 / (1.0 + jnp.exp(-pre_act))
    return pre_act * sig, sig * (1.0 + pre_act * (1.0 - sig))


def coords():
    c = lax.axis_index("ctx")
    f = lax.axis_index("fsdp")
    return c // 4, (c // 2) % 2, c % 2, f // 4, f % 4


def dev(y, xl, co, xh, z):
    return (y * 4 + xl * 2 + co, xh * 4 + z)


def barrier(peers):
    sem = pltpu.get_barrier_semaphore()
    for peer in peers:
        pl.semaphore_signal(sem, inc=1, device_id=peer, device_id_type=MESH)
    pl.semaphore_wait(sem, len(peers))


class Copies:
    def __init__(self, send, recv):
        self.send, self.recv, self.n, self.started = send, recv, 0, []

    def start(self, src, dst, peer):
        copy = pltpu.make_async_remote_copy(
            src, dst, self.send.at[self.n], self.recv.at[self.n], device_id=peer, device_id_type=MESH
        )
        copy.start()
        self.n += 1
        self.started.append(copy)
        return copy

    def finish(self, received=()):
        for copy in self.started:
            copy.wait_send()
            if not any(copy is r for r in received):
                copy.wait_recv()


Y_STEPS = (1, 2, 3)


def one_hot_rows():
    row = lax.broadcasted_iota(jnp.int32, (96, 128), 0)
    col = lax.broadcasted_iota(jnp.int32, (96, 128), 1)
    return jnp.where(div(row, 12) * 16 + rem(row, 12) == col, 1.0, 0.0).astype(BF)


def eye_rows():
    row = lax.broadcasted_iota(jnp.int32, (8, 128), 0)
    col = lax.broadcasted_iota(jnp.int32, (8, 128), 1)
    return jnp.where(row == col, 1.0, 0.0).astype(BF)


def inverse_norm(values):
    return lax.rsqrt(jnp.mean(values * values, -1, keepdims=True) + EPS)


def head_rows(ref, j, first=0):
    rows = slice(j * 128, (j + 1) * 128)
    return jnp.concatenate([ref[rows, first + h * 128 : first + (h + 1) * 128] for h in range(3)], 0)


def allowed(n):
    i = rem(lax.axis_index("ctx"), 4)
    row = rem(lax.broadcasted_iota(jnp.int32, (384, n), 0), 128)
    col = lax.broadcasted_iota(jnp.int32, (384, n), 1)
    return col <= i * 128 + row


def ctx_places(y, xl, co):
    return [
        ((y + dy) % 4, (xl + dx) % 2, (co + dc) % 2)
        for dy in range(4)
        for dx in (0, 1)
        for dc in (0, 1)
        if (dy, dx, dc) != (0, 0, 0)
    ]


def x_place(xh, xl, d):
    x = (xh * 2 + xl + d) % 4
    return x // 2, x % 2


def plane_gather(cp, arrive, src, out, places, sib, split):
    y, xl, co, xh, z = places
    low, high = pl.ds(0, split), pl.ds(split, 128 - split)
    ypeers = [dev((y + d) % 4, xl, co, xh, z) for d in Y_STEPS]
    xpeers = []
    for d in Y_STEPS:
        h, l = x_place(xh, xl, d)
        xpeers.append(dev(y, l, co, h, z))
    mine = (xh, y, xl, co)

    def first_y():
        return [cp.start(src.at[high], out.at[mine + (high,)], p) for p in ypeers]

    def first_x():
        return [cp.start(src.at[low], out.at[mine + (low,)], p) for p in xpeers]

    def piece_y(d):
        return out.at[:, (y + d) % 4, :, co, low]

    def piece_x(d):
        h, l = x_place(xh, xl, d)
        return out.at[h, :, l, co, high]

    def half_y(d, n):
        return out.at[n, (y + d) % 4, :, co, low]

    def half_x(d, n):
        h, l = x_place(xh, xl, d)
        return out.at[h, pl.ds(2 * n, 2), l, co, high]

    def then(firsts, piece, peers):
        for copy in firsts:
            arrive(copy)
        return [
            cp.start(piece(0), piece(0), peers[0]),
            cp.start(piece(0), piece(0), peers[2]),
            cp.start(piece(0), piece(0), sib),
        ]

    def middle(seconds, piece, half, peers):
        arrive(seconds[0])
        one = cp.start(half(3, 0), half(3, 0), peers[0])
        arrive(seconds[1])
        two = cp.start(half(1, 1), half(1, 1), peers[2])
        sibs = [cp.start(piece(d), piece(d), sib) for d in (3, 1)]
        return [one, two] + sibs

    def last(middles, piece):
        for copy in middles[:2]:
            arrive(copy)
        return middles[2:] + [cp.start(piece(2), piece(2), sib)]

    def then_y(firsts):
        return then(firsts, piece_y, ypeers)

    def then_x(firsts):
        return then(firsts, piece_x, xpeers)

    def middle_y(seconds):
        return middle(seconds, piece_y, half_y, ypeers)

    def middle_x(seconds):
        return middle(seconds, piece_x, half_x, xpeers)

    def last_y(middles):
        return last(middles, piece_y)

    def last_x(middles):
        return last(middles, piece_x)

    return (first_y, then_y, middle_y, last_y), (first_x, then_x, middle_x, last_x)


def dispatch_rows(rg, first):
    masks, gates = [], []
    for e in range(2):
        ms, gs = [], []
        for s in range(2):
            hit = jnp.where(rg[s, 0:6] == (first + e).astype(F32), 1.0, 0.0)
            ms.append(jnp.sum(hit, 0, keepdims=True))
            gs.append(jnp.sum(hit * rg[s, 8:14], 0, keepdims=True))
        masks.append(jnp.concatenate(ms, 1))
        gates.append(jnp.concatenate(gs, 1))
    mask = jnp.concatenate(masks + [jnp.zeros((6, 256), F32)], 0)
    before = lax.broadcasted_iota(jnp.int32, (256, 256), 0)
    after = lax.broadcasted_iota(jnp.int32, (256, 256), 1)
    tri = jnp.where((before <= after) & (before // 128 == after // 128), 1.0, 0.0).astype(BF)
    place = nn(mask.astype(BF), tri) - 1.0
    lane = lax.broadcasted_iota(jnp.int32, (1, 256), 1)
    slot = lax.broadcasted_iota(jnp.int32, (48, 256), 0).astype(F32)
    picks, gated = [], []
    for e in range(2):
        at = place[e : e + 1] + jnp.where(lane >= 128, 24.0, 0.0)
        at = jnp.where(masks[e] > 0.0, at, -1.0)
        hit = jnp.where(slot == at, 1.0, 0.0)
        picks.append(hit)
        gated.append(hit * gates[e])
    return jnp.concatenate(picks, 0).astype(BF), jnp.concatenate(gated, 0).astype(BF)


def eye(rows, cols):
    row = lax.broadcasted_iota(jnp.int32, (rows, cols), 0)
    col = lax.broadcasted_iota(jnp.int32, (rows, cols), 1)
    return jnp.where(row == col, 1.0, 0.0).astype(BF)


def half_turn(x):
    return pltpu.roll(x, 64, 1)


def front_kernel(
    tok, cot, routes, gates, gains_in, wq, wk, wv, wo, sg, su, sd, eg, eu, ed,
    cotf, h2f, wexp, tokf_o, kvf_o, gy, pick_o, gated_o, gz_o, rgf,
    w_o, sw_o, qkv_o, att_o, lse_o, resid_o,
    send, recv, loc, w, sw, qkv, att, lse, resid, a_s, b_s, own, rg_s, a2, wf, b1, bf, tokf, kvf, s_s, part, got, h2,
):
    y, xl, co, xh, z = coords()
    i, c, f = xl * 2 + co, y * 4 + xl * 2 + co, xh * 4 + z
    f_far = (1 - xh) * 4 + z
    sib = dev(y, xl, 1 - co, xh, z)
    xpeer = dev(y, 1 - xl, co, xh, z)
    xfar = dev(y, xl, co, 1 - xh, z)
    ypeers = [dev((y + d) % 4, xl, co, xh, z) for d in Y_STEPS]
    zpeers = [dev(y, xl, co, xh, (z + d) % 4) for d in Y_STEPS]
    places = ctx_places(y, xl, co)
    cpeers = [dev(*p, xh, z) for p in places]
    plane = cpeers + [dev(*p, 1 - xh, z) for p in places + [(y, xl, co)]]
    peers = plane + zpeers
    sem = pltpu.get_barrier_semaphore()
    for peer in peers:
        pl.semaphore_signal(sem, inc=1, device_id=peer, device_id_type=MESH)

    e16 = eye(16, 12)
    q16, k16, v16 = (nn(e16, ref[...]).astype(BF) for ref in (wq, wk, wv))
    o16 = nn(e16, wo[...]).astype(BF)
    gain_rows = nn(eye(128, 2), gains_in[...]).astype(BF)
    gain16 = nt(e16, gain_rows).astype(BF)
    for k in range(4):
        wide, thin = slice(k * 384, (k + 1) * 384), slice(k * 128, (k + 1) * 128)
        a_s[k] = jnp.concatenate([q16[:, wide], k16[:, thin], v16[:, thin], gain16, o16[:, wide]], 1)
    pl.semaphore_wait(sem, len(peers))

    cp = Copies(send, recv)
    n_local = [0]

    def here(src, dst):
        copy = pltpu.make_async_copy(src, dst, loc.at[n_local[0]])
        n_local[0] += 1
        copy.start()
        return copy

    got_already = []

    def arrive(copy):
        copy.wait_recv()
        got_already.append(copy)

    me = (y, xl, co, xh, z)
    ya = [cp.start(a_s.at[(y + d) % 4], a2.at[y, xl], p) for d, p in zip(Y_STEPS, ypeers)]
    la = here(a_s.at[y], a2.at[y, xl])
    lt = here(tok, tokf.at[y])
    owns = [here(ref, own.at[:, k]) for k, ref in enumerate((eg, eu, ed))]
    own_cot = here(cot, cotf.at[xh, y, xl, co])
    over_y, over_x = plane_gather(cp, arrive, cot, cotf, me, sib, 80)
    cot_y, cot_then_y, cot_middle_y, cot_last_y = over_y
    cot_x, cot_then_x, cot_middle_x, cot_last_x = over_x
    yt = [cp.start(tok, tokf.at[y], p) for p in ypeers]
    cy = cot_y()
    g16, u16, d16 = nn(e16, sg[...]), nn(e16, su[...]), nn(e16, sd[...])
    front_half = lax.broadcasted_iota(jnp.int32, (16, 128), 1) < 64
    for k in range(8):
        at = slice(k * 128, (k + 1) * 128)
        g, u, d = g16[:, at], u16[:, at], d16[:, at]
        for n in range(2):
            if n:
                g, d = half_turn(g), half_turn(d)
            else:
                u = half_turn(u)
            b_s[2 * k + n, :, 0:128] = jnp.where(front_half, g, u).astype(BF)
            b_s[2 * k + n, :, 128:256] = jnp.where(front_half, d, 0.0).astype(BF)
            if not n:
                u = half_turn(u)
    rg_s[...] = jnp.zeros_like(rg_s)
    for k in range(6):
        rg_s[k : k + 1] = routes[k].astype(F32)
        rg_s[8 + k : 9 + k] = gates[k]
    lb = here(b_s.at[c], b1.at[c])
    lr = here(rg_s, rgf.at[xh, c])
    for copy in owns:
        copy.wait()
    later = [here(own.at[pl.ds(xh * 2, 2)], wexp.at[:, :, f])]
    la.wait()
    for copy in ya:
        arrive(copy)
    xa = cp.start(a2.at[:, xl], a2.at[:, xl], xpeer)
    bs = [cp.start(b_s.at[p[0] * 4 + p[1] * 2 + p[2]], b1.at[c], q) for p, q in zip(places, cpeers)]
    rgs = [cp.start(rg_s, rgf.at[xh, c], q) for q in plane]
    arrive(xa)

    head, tail = pl.ds(0, 768), pl.ds(768, 384)

    def slices(cols):
        return a2.at[:, :, :, cols], wf.at[:, :, co, f, :, cols], wf.at[:, :, co, f_far, :, cols]

    src, mine, far = slices(head)
    hx = cp.start(src, mine, xfar)
    hz = [cp.start(src, mine, p) for p in zpeers]
    lw = here(a2, wf.at[:, :, co, f])
    cx = cot_x()
    src_t, mine_t, far_t = slices(tail)
    tx = cp.start(src_t, mine_t, xfar)
    lw.wait()
    to_sib = [cp.start(mine, mine, sib)]
    arrive(hx)
    hz2 = [cp.start(far, far, p) for p in zpeers]
    to_sib.append(cp.start(far, far, sib))
    tz = [cp.start(src_t, mine_t, p) for p in zpeers]
    for copies, h in ((hz, xh), (hz2, 1 - xh)):
        for d, copy in zip(Y_STEPS, copies):
            arrive(copy)
            piece = wf.at[:, :, co, h * 4 + (z + 4 - d) % 4, :, head]
            to_sib.append(cp.start(piece, piece, sib))
    own_cot.wait()
    cy2 = cot_then_y(cx)
    arrive(tx)
    tz2 = [cp.start(far_t, far_t, p) for p in zpeers]
    tail_sib = [cp.start(mine_t, mine_t, sib), cp.start(far_t, far_t, sib)]
    own_z = [cp.start(own.at[pl.ds(xh * 2, 2)], wexp.at[:, :, f], zpeers[k]) for k in (0, 2)]
    lb.wait()
    for copy in bs:
        arrive(copy)
    bx = cp.start(b1, bf.at[:, f], xfar)
    bz = [cp.start(b1, bf.at[:, f], p) for p in zpeers]
    lb = here(b1, bf.at[:, f])
    for copy in to_sib:
        arrive(copy)
    rows = one_hot_rows()

    def compact(cols):
        for yy in range(4):
            for k in range(4):
                at = (yy * 4 + k) * 96
                block = wf[yy, k // 2, k % 2, :, :, cols].reshape(128, -1)
                w[at : at + 96, cols] = nn(rows, block).astype(BF)

    compact(slice(0, 768))
    gains = nt(eye_rows(), w[:, 640:768])
    gain_one, gain_two = gains[0:1], gains[1:2]

    lt.wait()
    for copy in yt:
        arrive(copy)
    for j in range(4):
        v = tokf[j].astype(F32)
        rows_j = slice(j * 128, (j + 1) * 128)
        h1 = (v * inverse_norm(v) * gain_one).astype(BF)
        qkv_j = nn(h1, w[:, :640]).astype(BF)
        qkv[rows_j] = qkv_j
        kvf[j, i] = qkv_j[:, 384:]
    kx = cp.start(kvf.at[:, i], kvf.at[:, i], xpeer)
    ks = [cp.start(kvf.at[:, i], kvf.at[:, i], sib)]
    saved = [here(tokf, tokf_o), here(qkv, qkv_o)]
    for copies, h in ((tz, xh), (tz2, 1 - xh)):
        for d, copy in zip(Y_STEPS, copies):
            arrive(copy)
            piece = wf.at[:, :, co, h * 4 + (z + 4 - d) % 4, :, tail]
            tail_sib.append(cp.start(piece, piece, sib))
    arrive(kx)
    piece = kvf.at[:, (1 - xl) * 2 + co]
    ks.append(cp.start(piece, piece, sib))
    ex = [cp.start(own.at[pl.ds(2 - xh * 2, 2)], wexp.at[:, :, f], xfar)]
    cx2 = cot_then_x(cy)
    for copy in ks:
        arrive(copy)
    saved.append(here(kvf, kvf_o))

    for j in range(4):
        n = (j + 1) * 512
        q = head_rows(qkv, j)
        for t in range(j + 1):
            s = nt(q, kvf[t].reshape(512, 256)[:, :128]) * SCALE
            if t == j:
                s = jnp.where(allowed(512), s, -1e30)
            s_s[:, t * 512 : (t + 1) * 512] = s
        s = s_s[:, :n]
        m = jnp.max(s, -1, keepdims=True)
        p = jnp.exp(s - m)
        total = jnp.sum(p, -1, keepdims=True)
        o = nn(p.astype(BF), kvf[0 : j + 1].reshape(n, 256)[:, 128:]) / total
        rows_j = slice(j * 128, (j + 1) * 128)
        for h in range(3):
            att[rows_j, h * 128 : (h + 1) * 128] = o[h * 128 : (h + 1) * 128].astype(BF)
        lse[j] = jnp.broadcast_to(m + jnp.log(total), (384, 128))
    for copy in tail_sib:
        arrive(copy)
    compact(slice(768, 1152))
    saved += [here(w, w_o), here(att, att_o), here(lse, lse_o)]
    for j in range(4):
        part[j] = nt(att[j * 128 : (j + 1) * 128], w[:, 768:1152]).astype(BF)
    ps = [
        cp.start(part.at[(y + d) % 4], got.at[k], p) for k, (d, p) in enumerate(zip(Y_STEPS, ypeers))
    ]
    def pass_on(copies, h):
        sent = []
        for e, (copy, d) in enumerate(zip(copies, (3, 1))):
            arrive(copy)
            piece = wexp.at[e, :, h * 4 + (z + d) % 4]
            sent.append(cp.start(piece, piece, zpeers[2 * e]))
        return sent

    cy3 = cot_middle_y(cy2)
    arrive(bx)
    bz += [cp.start(bf.at[:, f_far], bf.at[:, f_far], p) for p in zpeers]
    pass_on(own_z, xh)
    total = tokf[y].astype(F32) + part[y].astype(F32)
    for k, copy in enumerate(ps):
        arrive(copy)
        total = total + got[k].astype(F32)
    resid[...] = total
    saved.append(here(resid, resid_o))
    h2[...] = (total * inverse_norm(total) * gain_two).astype(BF)
    over_y, over_x = plane_gather(cp, arrive, h2, h2f, me, sib, 64)
    h2_y, h2_then_y, h2_middle_y, h2_last_y = over_y
    h2_x, h2_then_x, h2_middle_x, h2_last_x = over_x
    hx = h2_x()
    hy = h2_y()
    own_h2 = here(h2, h2f.at[xh, y, xl, co])

    cx3 = cot_middle_x(cx2)
    for copy in ex:
        arrive(copy)
    far_rows = wexp.at[:, :, f_far]
    far_z = [cp.start(far_rows, far_rows, zpeers[k]) for k in (0, 2)]
    own_h2.wait()
    hy2 = h2_then_y(hx)
    hx2 = h2_then_x(hy)
    cot_sib = [cy2[2], cx2[2]] + cot_last_y(cy3) + cot_last_x(cx3)
    lb.wait()
    for copy in bz:
        arrive(copy)
    for k in range(16):
        sw[k * 96 : (k + 1) * 96] = nn(rows, bf[k].reshape(128, 256)).astype(BF)
    saved.append(here(sw, sw_o))
    lr.wait()
    for copy in rgs + cot_sib:
        arrive(copy)

    first = c * 4 + xh * 2

    def gated_rows(rg_ref, cot_ref, gy_ref, pick_ref, gated_ref, gz_ref):
        pick, gated = dispatch_rows(rg_ref, first)
        g = cot_ref[...].reshape(256, 1536)
        gy_ref[...] = nn(gated, g).astype(BF).reshape(2, 1, 48, 1536)
        gz_ref[0] = nn(g, sw[:, 128:256])
        pick_ref[0], gated_ref[0] = pick, gated

    picks = pl.BlockSpec((1, 96, 256), lambda p: (p, 0, 0))
    whole = pl.BlockSpec((1, 256, 128), lambda p: (p, 0, 0))
    def gated_half(h):
        at = pl.ds(h * 8, 8)
        pltpu.emit_pipeline(
            gated_rows,
            grid=(8,),
            in_specs=[
                pl.BlockSpec((2, 16, 128), lambda p: (p, 0, 0)),
                pl.BlockSpec(
                    (1, 1, 2, 128, 1536), lambda p: (p // 2, p % 2, 0, 0, 0), pipeline_mode=pl.Buffered(4)
                ),
            ],
            out_specs=[pl.BlockSpec((2, 1, 48, 1536), lambda p: (0, p, 0, 0)), picks, picks, whole],
        )(rgf.at[h], cotf.at[h], gy.at[:, at], pick_o.at[at], gated_o.at[at], gz_o.at[at])

    gated_half(0)
    pass_on(far_z, 1 - xh)
    hy3 = h2_middle_y(hy2)
    hx3 = h2_middle_x(hx2)
    gated_half(1)
    h2_last_y(hy3)
    h2_last_x(hx3)
    for copy in later + saved:
        copy.wait()
    cp.finish(got_already)


def front(*ins):
    outs = (
        SDS((2, 4, 2, 2, 128, 1536), BF),
        SDS((2, 4, 2, 2, 128, 1536), BF),
        SDS((2, 3, 8, 192, 512), BF),
        SDS((4, 128, 1536), BF),
        SDS((4, 4, 128, 256), BF),
        SDS((2, 16, 48, 1536), BF),
        SDS((16, 96, 256), BF),
        SDS((16, 96, 256), BF),
        SDS((16, 256, 128), F32),
        SDS((2, 16, 16, 128), F32),
        SDS((1536, 1152), BF),
        SDS((1536, 256), BF),
        SDS((512, 640), BF),
        SDS((512, 384), BF),
        SDS((4, 384, 128), F32),
        SDS((128, 1536), F32),
    )
    return pl.pallas_call(
        front_kernel,
        out_shape=outs,
        in_specs=[ANY] * 2 + [VM] * (len(ins) - 5) + [ANY] * 3,
        out_specs=(ANY,) * 16,
        scratch_shapes=[
            pltpu.SemaphoreType.DMA((160,)),
            pltpu.SemaphoreType.DMA((160,)),
            pltpu.SemaphoreType.DMA((24,)),
            pltpu.VMEM((1536, 1152), BF),
            pltpu.VMEM((1536, 256), BF),
            pltpu.VMEM((512, 640), BF),
            pltpu.VMEM((512, 384), BF),
            pltpu.VMEM((4, 384, 128), F32),
            pltpu.VMEM((128, 1536), F32),
            pltpu.VMEM((4, 16, 1152), BF),
            pltpu.VMEM((16, 16, 256), BF),
            pltpu.VMEM((4, 3, 192, 512), BF),
            pltpu.VMEM((16, 128), F32),
            pltpu.VMEM((4, 2, 16, 1152), BF),
            pltpu.VMEM((4, 2, 2, 8, 16, 1152), BF),
            pltpu.VMEM((16, 16, 256), BF),
            pltpu.VMEM((16, 8, 16, 256), BF),
            pltpu.VMEM((4, 128, 1536), BF),
            pltpu.VMEM((4, 4, 128, 256), BF),
            pltpu.VMEM((384, 2048), F32),
            pltpu.VMEM((4, 128, 1536), BF),
            pltpu.VMEM((3, 128, 1536), BF),
            pltpu.VMEM((128, 1536), BF),
        ],
        compiler_params=pltpu.CompilerParams(
            collective_id=1, has_side_effects=True, vmem_limit_bytes=VMEM_LIMIT
        ),
        cost_estimate=pl.CostEstimate(flops=6 * 10**9, bytes_accessed=60 * 10**6, transcendentals=3 * 10**6),
    )(*ins)


def add_blocks(*refs):
    total = refs[0][...].astype(F32)
    for ref in refs[1:-1]:
        total = total + ref[...].astype(F32)
    refs[-1][...] = total.astype(refs[-1].dtype)


def add_arrays(block, ins, out):
    spec = pl.BlockSpec((1,) + block, lambda m, r: (m, 0, r, 0))
    pltpu.emit_pipeline(add_blocks, grid=(3, 2), in_specs=[spec] * len(ins), out_specs=[spec])(*ins, out)


def back_kernel(
    pick_in, gated_in, gy_in, gz_in, wexp, h2f, cotf, resid_i, cot_i, w_i, sw_i, tokf_i, qkv_i, kvf_i, lse_i, att_i,
    eg, y_b, y_s, g_s, pick_s, gated_s, hid_b, hid_s, gcd_b, gcd_s, gh2p, outp, zb, sb, xb, goy, gox, aout, bout,
    lout_o, igrad_o,
    send, recv, loc, lout, igrad, goty, gotx, midy, midx, moy, mox, gety, getx, resid, cot, gres, gattn, dkvr, gh1g, dath, zg, xg, xgot, bgot, bxg,
    sw, sdw, db, ds,
):
    y, xl, co, xh, z = coords()
    i, c = xl * 2 + co, y * 4 + xl * 2 + co
    sib = dev(y, xl, 1 - co, xh, z)
    xpeer = dev(y, 1 - xl, co, xh, z)
    xfar = dev(y, xl, co, 1 - xh, z)
    ypeers = [dev((y + d) % 4, xl, co, xh, z) for d in Y_STEPS]
    zpeers = [dev(y, xl, co, xh, (z + d) % 4) for d in Y_STEPS]
    places = ctx_places(y, xl, co)
    cpeers = [dev(*p, xh, z) for p in places]
    xpeers = []
    for d in Y_STEPS:
        hh, ll = x_place(xh, xl, d)
        xpeers.append(dev(y, ll, co, hh, z))
    barrier(cpeers + [dev(y, k, co, 1 - xh, z) for k in range(2)] + zpeers)
    cp = Copies(send, recv)
    n_local = [0]

    def here(src, dst):
        copy = pltpu.make_async_copy(src, dst, loc.at[n_local[0]])
        n_local[0] += 1
        copy.start()
        return copy

    got_already, sent_already = [], []

    def arrive(copy):
        copy.wait_recv()
        got_already.append(copy)

    def gone(copies):
        for copy in copies:
            copy.wait_send()
            sent_already.append(copy)

    low, high = pl.ds(0, 64), pl.ds(64, 64)
    ynext, znext = [(y + d) % 4 for d in range(4)], [(z + d) % 4 for d in range(4)]
    xnext = [x_place(xh, xl, d) for d in range(4)]
    oco, oxl, oxh = 1 - co, 1 - xl, 1 - xh
    xh8, oxh8 = xh * 8, 8 - xh * 8
    place_index = [p[0] * 4 + p[1] * 2 + p[2] for p in places]
    kv_peers = [(a * 2 + b, dev(y, a, b, xh, z)) for a, b in ((oxl, co), (oxl, oco), (xl, oco))]
    front_cols, back_cols = pl.ds(0, 128), pl.ds(128, 128)
    mine_cols = pl.ds(pl.multiple_of(co * 128, 128), 128)
    first = [
        here(sw_i.at[:, front_cols], sw.at[:, front_cols]),
        here(sw_i.at[:, back_cols], sdw.at[:, front_cols]),
        here(resid_i, resid),
        here(cot_i, cot),
    ]
    pairs = pl.BlockSpec((1, 1, 2, 128, 1536), lambda p: (div(p, 2), rem(p, 2), 0, 0, 0))
    picks = pl.BlockSpec((1, 96, 256), lambda p: (p, 0, 0))

    def expert_copies(e):
        return [
            pltpu.make_async_remote_copy(
                eg.at[e, :, :, znext[d]],
                zb.at[k, e],
                send.at[e * 3 + k],
                recv.at[e * 3 + k],
                device_id=zpeers[k],
                device_id_type=MESH,
            )
            for k, d in enumerate(Y_STEPS)
        ]

    def expert_push(e):
        for copy in expert_copies(e):
            copy.start()

    def expert_rows(e, gg):
        return pltpu.make_async_remote_copy(
            gg.at[e], g_s.at[e], send.at[6 + e], recv.at[6 + e], device_id=sib, device_id_type=MESH
        )

    def expert_out(e, xy):
        return pltpu.make_async_remote_copy(
            xy.at[e], y_s.at[e], send.at[8 + e], recv.at[8 + e], device_id=sib, device_id_type=MESH
        )

    cp.n = 12
    early = [
        cp.start(sw_i.at[:, front_cols], sw.at[:, back_cols], sib),
        cp.start(sw_i.at[:, back_cols], sdw.at[:, back_cols], sib),
        cp.start(pick_in, pick_s, sib),
        cp.start(gated_in, gated_s, sib),
    ]
    for copy in first[:2]:
        copy.wait()

    ds[...] = jnp.zeros_like(ds)

    def hidden_rows(k):
        src, dst = ((gcd_b, gcd_s), (hid_b, hid_s))[k]
        return pltpu.make_async_remote_copy(
            src.at[:, oco], dst, send.at[10 + k], recv.at[10 + k], device_id=sib, device_id_type=MESH
        )

    def at8(own):
        return pl.ds(xh8 if own else oxh8, 8)

    blocks = pl.BlockSpec((1, 1, 128, 1536), lambda p: (div(p, 2), rem(p, 2), 0, 0))
    thin = pl.BlockSpec((1, 2, 128, 128), lambda p: (p, 0, 0, 0))

    def experts(xy, gg, dw):
        lg = here(gy_in, gg)

        def grads_copy(e):
            return pltpu.make_async_copy(dw, eg.at[e], loc.at[78 + e])

        def work(w, u_s, ga_s, gb_s):
            lw = [here(wexp.at[0], w.at[0])]

            def own_rows(pick_ref, h2_ref, gz_ref, hid_ref, gcd_ref):
                h2 = h2_ref[...].reshape(256, 1536)
                xy[:, xh8 + pl.program_id(0)] = nn(pick_ref[0], h2).astype(BF).reshape(2, 48, 1536)
                pre, gz = nn(h2, sw[:, 0:128]), gz_ref[0]
                act, slope = silu_parts(pre)
                up = half_turn(pre)
                lane = lax.broadcasted_iota(jnp.int32, (256, 128), 1)
                hid = jnp.where(lane < 64, act * up, 0.0).astype(BF)
                gcd = jnp.where(lane < 64, gz * up * slope, half_turn(gz * act)).astype(BF)
                hid_ref[0] = hid.reshape(2, 128, 128)
                gcd_ref[0] = gcd.reshape(2, 128, 128)
                ds[0:128] += tn(gcd, h2)

            def other_rows(pick_ref, h2_ref):
                x = nn(pick_ref[0], h2_ref[...].reshape(256, 1536)).astype(BF)
                xy[:, oxh8 + pl.program_id(0)] = x.reshape(2, 48, 1536)

            deep = pl.BlockSpec(
                (1, 1, 2, 128, 1536), lambda p: (div(p, 2), rem(p, 2), 0, 0, 0), pipeline_mode=pl.Buffered(4)
            )
            pltpu.emit_pipeline(
                own_rows,
                grid=(8,),
                in_specs=[picks, deep, pl.BlockSpec((1, 256, 128), lambda p: (p, 0, 0))],
                out_specs=[thin, thin],
            )(pick_in.at[at8(True)], h2f.at[xh], gz_in.at[at8(True)], hid_b, gcd_b)
            for e in range(2):
                hidden_rows(e).start()
            pltpu.emit_pipeline(other_rows, grid=(8,), in_specs=[picks, deep])(
                pick_in.at[at8(False)], h2f.at[oxh]
            )
            lw.append(here(wexp.at[1], w.at[1]))
            lg.wait()
            for e in range(2):
                lw[e].wait()
                for t in range(2):
                    cols = slice(t * 256, (t + 1) * 256)
                    x, g = xy[e].reshape(768, 1536), gg[e].reshape(768, 1536)
                    a = nn(x, w[e, 0, :, :, cols].reshape(1536, 256))
                    b = nn(x, w[e, 1, :, :, cols].reshape(1536, 256))
                    gu = nn(g, w[e, 2, :, :, cols].reshape(1536, 256))
                    act, slope = silu_parts(a)
                    u_s[:, cols] = (act * b).astype(BF)
                    ga_s[:, cols] = (gu * b * slope).astype(BF)
                    gb_s[:, cols] = (gu * act).astype(BF)
                if e:
                    grads_copy(0).wait()
                    expert_push(0)

                def row_tile(t, carry):
                    at = pl.ds(pl.multiple_of(t * 384, 384), 384)
                    two, h, half = pl.ds(t * 2, 2), div(t, 2), pl.ds(rem(t, 2) * 2, 2)
                    g = gg[e, :, :, at].reshape(768, 384)
                    dw[2, h, half] = tn(g, u_s[...]).astype(BF).reshape(2, 192, 512)
                    back = nt(ga_s[...], w[e, 0, two].reshape(384, 512))
                    back = back + nt(gb_s[...], w[e, 1, two].reshape(384, 512))
                    gg[e, :, :, at] = back.astype(BF).reshape(16, 48, 384)
                    return carry

                def tile(t, carry):
                    at = pl.ds(pl.multiple_of(t * 384, 384), 384)
                    two, h, half = pl.ds(t * 2, 2), div(t, 2), pl.ds(rem(t, 2) * 2, 2)
                    x = xy[e, :, :, at].reshape(768, 384)
                    dw[0, h, half] = tn(x, ga_s[...]).astype(BF).reshape(2, 192, 512)
                    dw[1, h, half] = tn(x, gb_s[...]).astype(BF).reshape(2, 192, 512)
                    out = nt(u_s[...], w[e, 2, two].reshape(384, 512))
                    xy[e, :, :, at] = out.astype(BF).reshape(16, 48, 384)
                    return carry

                lax.fori_loop(0, 4, row_tile, 0)
                expert_rows(e, gg).start()
                lax.fori_loop(0, 4, tile, 0)
                expert_out(e, xy).start()
                grads_copy(e).start()

        pl.run_scoped(
            work,
            pltpu.VMEM((2, 3, 8, 192, 512), BF),
            pltpu.VMEM((768, 512), BF),
            pltpu.VMEM((768, 512), BF),
            pltpu.VMEM((768, 512), BF),
        )
        ly = here(xy, y_b)
        for e in range(2):
            expert_rows(e, gg).wait()
            hidden_rows(e).wait()

        def row_sums(pick_ref, other_ref, rows_ref, hid_ref, more_ref, gh_ref):
            p = pl.program_id(0)
            picks = jnp.concatenate([pick_ref[0, :, mine_cols], other_ref[0, :, mine_cols]], 0)
            rows = jnp.concatenate([gg[:, p].reshape(96, 1536), rows_ref[...].reshape(96, 1536)], 0)
            gh = tn(picks, rows)
            own = div(p, 8) == xh

            @pl.when(own)
            def _():
                hidden = jnp.concatenate([hid_ref[0, 0], more_ref[0]], 1)
                gh_ref[...] = (gh + nt(hidden, sw[...])).astype(BF).reshape(1, 1, 1, 128, 1536)

            @pl.when(jnp.logical_not(own))
            def _():
                gh_ref[...] = gh.astype(BF).reshape(1, 1, 1, 128, 1536)

        def own_pair(p):
            return jnp.minimum(jnp.maximum(p - xh8, 0), 7)

        deep_rows = pl.BlockSpec((2, 1, 48, 1536), lambda p: (0, p, 0, 0), pipeline_mode=pl.Buffered(3))
        for copy in early:
            arrive(copy)
        pltpu.emit_pipeline(
            row_sums,
            grid=(16,),
            in_specs=[
                picks,
                picks,
                deep_rows,
                pl.BlockSpec((1, 1, 128, 128), lambda p: (own_pair(p), 0, 0, 0)),
                pl.BlockSpec((1, 128, 128), lambda p: (own_pair(p), 0, 0)),
            ],
            out_specs=[pl.BlockSpec((1, 1, 1, 128, 1536), lambda p: (div(p, 8), rem(div(p, 2), 4), rem(p, 2), 0, 0))],
        )(pick_in, pick_s, g_s, gcd_b.at[:, pl.ds(co, 1)], gcd_s, gh2p)
        grads_copy(1).wait()
        expert_push(1)
        ly.wait()
        for e in range(2):
            expert_out(e, xy).wait()

    pl.run_scoped(
        experts,
        pltpu.VMEM((2, 16, 48, 1536), BF),
        pltpu.VMEM((2, 16, 48, 1536), BF),
        pltpu.VMEM((3, 2, 4, 192, 512), BF),
    )

    def dense(
        augy, augx, miney, minex, w, tokf, qkv, kvf, lse, att, go, dk, dv, dkvs, gqkv, gh1s, da, zs, s2, s3, bz, bsum
    ):
        def sum_piece(xp, axis, d):
            if axis == "y":
                return xp.at[:, ynext[d], :, low]
            return xp.at[xnext[d][0], :, xnext[d][1], high]

        def sum_half(xp, axis, d, n):
            if axis == "y":
                return xp.at[n, ynext[d], :, low]
            return xp.at[xnext[d][0], pl.ds(2 * n, 2), xnext[d][1], high]

        def landing(to, axis, k, n):
            return to.at[k, n] if axis == "y" else to.at[k, pl.ds(2 * n, 2)]

        def sum_push(xp, mids, to):
            halves, sent, loads = {}, [], {}
            for axis, peers in (("y", ypeers), ("x", xpeers)):
                for n in range(2):
                    halves[axis, n] = cp.start(sum_half(xp, axis, 2, n), mids[axis].at[n], peers[2 * n])
            for axis, peers in (("y", ypeers), ("x", xpeers)):
                for n in range(2):
                    src = sum_half(xp, axis, (1, 3)[n], 1 - n)
                    sent.append(cp.start(src, landing(to[axis], axis, n, 1 - n), peers[2 * n]))
                    loads[axis, n] = here(sum_half(xp, axis, (1, 3)[n], n), aug[axis].at[n])
            return halves, sent, loads

        def sum_middle(axis, mids, to, started):
            halves, sent, loads = started
            peers = ypeers if axis == "y" else xpeers
            for n in range(2):
                loads[axis, n].wait()
                arrive(halves[axis, n])
                for k in range(2):
                    tot = aug[axis][n, k].astype(F32) + mids[axis][n, k].astype(F32)
                    aug[axis][n, k] = tot.astype(BF)
                sent.append(cp.start(aug[axis].at[n], landing(to[axis], axis, n, n), peers[2 * n]))

        aug = {"y": augy, "x": augx}
        mids_g, mids_o = {"y": midy, "x": midx}, {"y": moy, "x": mox}
        to_g, to_o = {"y": goty, "x": gotx}, {"y": goy, "x": gox}

        def sum_own(xp):
            return [here(sum_piece(xp, "y", 0), miney.at[0]), here(sum_piece(xp, "x", 0), minex.at[0])]

        def sum_second():
            for h in range(2):
                for l in range(2):
                    tot = miney[0, h, l].astype(F32)
                    for k in range(2):
                        tot = tot + goty[k, h, l].astype(F32)
                    miney[0, h, l] = tot.astype(BF)
            for a in range(4):
                tot = minex[0, a].astype(F32)
                for k in range(2):
                    tot = tot + gotx[k, a].astype(F32)
                minex[0, a] = tot.astype(BF)

        def sum_last(nth):
            sent = []
            for k, d in enumerate(Y_STEPS):
                hh, ll = xnext[d]
                sent.append(cp.start(miney.at[0, hh, ll], gety.at[nth, k], xpeers[k]))
                sent.append(cp.start(minex.at[0, ynext[d]], getx.at[nth, k], ypeers[k]))
            return sent

        def sum_end(nth, sent):
            for copy in sent:
                arrive(copy)
            top, bottom = miney[0, xh, xl].astype(F32), minex[0, y].astype(F32)
            for k in range(3):
                top = top + gety[nth, k].astype(F32)
                bottom = bottom + getx[nth, k].astype(F32)
            return jnp.concatenate([top, bottom], 0)

        sums_g = sum_push(gh2p, mids_g, to_g)
        own_g = sum_own(gh2p)
        first.append(here(w_i, w))
        second = [here(qkv_i, qkv), here(kvf_i, kvf), here(lse_i, lse), here(att_i, att)]
        third = [here(tokf_i, tokf)]

        def expert_sums(e):
            for copy in expert_copies(e):
                copy.wait()
            ins = [eg.at[e, :, :, z], zb.at[0, e], zb.at[1, e], zb.at[2, e]]
            add_arrays((2, 96, 512), ins, sb.at[e])

        def expert_far(e):
            return cp.start(sb.at[e, :, oxh], xb.at[e], xfar)


        def output_rows(own):
            def body(pick_ref, other_ref, rows_ref, more_ref, *refs):
                picks = jnp.concatenate([pick_ref[0, :, mine_cols], other_ref[0, :, mine_cols]], 0)
                rows = [rows_ref[...].reshape(96, 1536), more_ref[...].reshape(96, 1536)]
                out = tn(picks, jnp.concatenate(rows, 0))
                if own:
                    out = out + nt(jnp.concatenate([refs[0][0, 0], refs[1][0]], 1), sdw[...])
                refs[-1][...] = out.astype(BF).reshape(1, 1, 128, 1536)

            at = at8(own)
            rows = pl.BlockSpec((2, 1, 48, 1536), lambda p: (0, p, 0, 0))
            specs = [picks, picks, rows, rows]
            args = [gated_in.at[at], gated_s.at[at], y_b.at[:, at], y_s.at[:, at]]
            if own:
                specs += [
                    pl.BlockSpec((1, 1, 128, 128), lambda p: (p, 0, 0, 0)),
                    pl.BlockSpec((1, 128, 128), lambda p: (p, 0, 0)),
                ]
                args += [hid_b.at[:, pl.ds(co, 1)], hid_s]
            pltpu.emit_pipeline(body, grid=(8,), in_specs=specs, out_specs=[blocks])(
                *args, outp.at[xh if own else oxh]
            )

        output_rows(True)
        sum_middle("y", mids_g, to_g, sums_g)
        sum_middle("x", mids_g, to_g, sums_g)
        output_rows(False)

        for copy in first[2:]:
            copy.wait()
        gains = nt(eye_rows(), w[:, 640:768])
        gain_one, gain_two = gains[0:1], gains[1:2]
        inv = inverse_norm(resid[...])
        xh2 = resid[...] * inv
        for copy in sums_g[1]:
            arrive(copy)
        for copy in own_g:
            copy.wait()
        sum_second()
        last_g = sum_last(0)
        gh2 = sum_end(0, last_g)
        gain_two_grad = jnp.sum(gh2 * xh2, 0, keepdims=True)
        inner = gh2 * gain_two
        row = inv * (inner - xh2 * jnp.mean(inner * xh2, -1, keepdims=True))
        gres[...] = cot[...].astype(F32) + row
        gattn[y] = gres[...].astype(BF)
        ga = [cp.start(gattn.at[y], gattn.at[y], p) for p in ypeers]

        gone(list(sums_g[0].values()) + sums_g[1] + last_g)
        sums_o = sum_push(outp, mids_o, to_o)
        own_o = sum_own(outp)

        for copy in second:
            copy.wait()
        sum_middle("x", mids_o, to_o, sums_o)
        expert_sums(0)
        def down_rows(cot_ref, hid_ref):
            ds[128:256] += tn(hid_ref[0].reshape(256, 128), cot_ref[...].reshape(256, 1536))

        pltpu.emit_pipeline(down_rows, grid=(8,), in_specs=[pairs, thin])(cotf.at[xh], hid_b)
        rows = one_hot_rows()
        shared_grads = tn(ds[...].astype(BF), eye(256, 256)).astype(BF)
        for k in range(16):
            block = shared_grads[k * 96 : (k + 1) * 96]
            db[k] = tn(rows, block).astype(BF).reshape(2, 4, 16, 256)
        bs = [cp.start(db.at[:, :, znext[d]], bgot.at[k], p) for k, (d, p) in enumerate(zip(Y_STEPS, zpeers))]

        for copy in ga:
            arrive(copy)
        dk[...] = jnp.zeros_like(dk)
        dv[...] = jnp.zeros_like(dv)
        for j in range(4):
            rows_j = slice(j * 128, (j + 1) * 128)
            go[rows_j] = nn(gattn[j], w[:, 768:1152]).astype(BF)
            q, g = head_rows(qkv, j), head_rows(go, j)
            delta = jnp.sum(head_rows(att, j).astype(F32) * g.astype(F32), -1, keepdims=True)
            total = lse[j][:, :1]
            dq = jnp.zeros((384, 128), F32)
            for t in range(j + 1):
                keys = kvf[t].reshape(512, 256)
                s = nt(q, keys[:, :128]) * SCALE
                p = jnp.exp(s - total)
                if t == j:
                    p = jnp.where(allowed(512), p, 0.0)
                gs = (p * (nt(g, keys[:, 128:]) - delta)).astype(BF)
                at = slice(t * 512, (t + 1) * 512)
                dv[at] += tn(p.astype(BF), g)
                dk[at] += tn(gs, q)
                dq = dq + nn(gs, keys[:, :128])
            dq = (dq * SCALE).astype(BF)
            for h in range(3):
                gqkv[rows_j, h * 128 : (h + 1) * 128] = dq[h * 128 : (h + 1) * 128]
        for j in range(4):
            for k in range(4):
                at = slice((j * 4 + k) * 128, (j * 4 + k + 1) * 128)
                dkvs[j, k, :, 0:128] = (dk[at] * SCALE).astype(BF)
                dkvs[j, k, :, 128:256] = dv[at].astype(BF)
        kvs = [
            cp.start(dkvs.at[:, p], dkvr.at[k], q)
            for k, (p, q) in enumerate(kv_peers)
        ]
        ex0 = expert_far(0)
        sum_middle("y", mids_o, to_o, sums_o)
        def expand(block, yy, cols):
            for k in range(4):
                part = tn(rows, block[k * 96 : (k + 1) * 96]).astype(BF)
                da[yy, k // 2, k % 2, :, :, :, cols] = part.reshape(2, 4, 16, -1)

        def dense_core(cols):
            return cp.start(da.at[:, :, oco, :, :, :, cols], dath.at[:, :, :, :, :, cols], sib)

        def dense_z(copy, cols):
            arrive(copy)
            for a in range(4):
                for b in range(2):
                    tot = da[a, b, co, :, :, :, cols].astype(F32) + dath[a, b, :, :, :, cols].astype(F32)
                    da[a, b, co, :, :, :, cols] = tot.astype(BF)
            return [
                cp.start(da.at[:, :, co, :, znext[d], :, cols], zg.at[k, :, :, :, :, cols], p)
                for k, (d, p) in enumerate(zip(Y_STEPS, zpeers))
            ]

        def dense_far(copies, cols):
            for copy in copies:
                arrive(copy)
            for a in range(4):
                for b in range(2):
                    tot = da[a, b, co, :, z, :, cols].astype(F32)
                    for k in range(3):
                        tot = tot + zg[k, a, b, :, :, cols].astype(F32)
                    for h in range(2):
                        zs[h, a, b, :, cols] = tot[h].astype(BF)
            return cp.start(zs.at[oxh, :, :, :, cols], xg.at[:, :, :, cols], xfar)

        def dense_near(copy, cols):
            arrive(copy)
            for a in range(4):
                for b in range(2):
                    tot = zs[xh, a, b, :, cols].astype(F32) + xg[a, b, :, cols].astype(F32)
                    s2[b, a, :, cols] = tot.astype(BF)
            return cp.start(s2.at[oxl, :, :, cols], xgot.at[:, :, cols], xpeer)

        def dense_y(copy, cols):
            arrive(copy)
            for a in range(4):
                s3[a, :, cols] = (s2[xl, a, :, cols].astype(F32) + xgot[a, :, cols].astype(F32)).astype(BF)
            last.append(here(s3.at[y, :, cols], aout.at[y, :, cols]))
            return [
                cp.start(s3.at[ynext[d], :, cols], aout.at[y, :, cols], p) for d, p in zip(Y_STEPS, ypeers)
            ]

        head, tail = pl.ds(0, 768), pl.ds(768, 384)
        last = []
        for yy in range(4):
            tile = slice(yy * 384, (yy + 1) * 384)
            block = tn(gattn[:, :, tile].reshape(512, 384), att[...])
            expand(block.astype(BF), yy, tail)
        tail_c = dense_core(tail)
        expert_sums(1)
        ex1 = expert_far(1)

        tail_z = dense_z(tail_c, tail)
        for copy in third:
            copy.wait()
        for copy in kvs:
            arrive(copy)
        gone(ga)
        gain_one_grad = jnp.zeros((1, 1536), F32)
        for j in range(4):
            rows_j = slice(j * 128, (j + 1) * 128)
            kv = dkvs[j, i].astype(F32)
            for k in range(3):
                kv = kv + dkvr[k, j].astype(F32)
            gqkv[rows_j, 384:640] = kv.astype(BF)
            gh1 = nt(gqkv[rows_j], w[:, :640])
            v = tokf[j].astype(F32)
            scaled = v * inverse_norm(v)
            gain_one_grad = gain_one_grad + jnp.sum(gh1 * scaled, 0, keepdims=True)
            gattn[j] = (scaled * gain_one).astype(BF)
            gh1s[j] = gh1.astype(BF)
        hs = [
            cp.start(gh1s.at[ynext[d]], gh1g.at[k], p) for k, (d, p) in enumerate(zip(Y_STEPS, ypeers))
        ]
        gain_rows = jnp.concatenate([gain_one_grad, gain_two_grad, jnp.zeros((6, 1536), F32)], 0)
        for yy in range(4):
            tile = slice(yy * 384, (yy + 1) * 384)
            block = tn(gattn[:, :, tile].reshape(512, 384), gqkv[...])
            expand(block.astype(BF), yy, pl.ds(0, 640))
            expand(tn(gain_rows[:, tile].astype(BF), eye_rows()).astype(BF), yy, pl.ds(640, 128))
        head_c = dense_core(head)
        head_z = dense_z(head_c, head)

        tail_x = dense_far(tail_z, tail)
        for copy in bs:
            arrive(copy)
        for a in range(16):
            tot = db[a, :, z].astype(F32)
            for k in range(3):
                tot = tot + bgot[k, a].astype(F32)
            bz[0, a], bz[1, a] = tot[0].astype(BF), tot[1].astype(BF)
        bx = cp.start(bz.at[oxh], bxg, xfar)

        for copy in sums_o[1]:
            arrive(copy)
        back_in = [here(goy, goty), here(gox, gotx)]
        for copy in back_in + own_o:
            copy.wait()
        sum_second()
        last_o = sum_last(1)
        head_x = dense_far(head_z, head)
        gh1 = gh1s[y].astype(F32)
        for k, copy in enumerate(hs):
            arrive(copy)
            gh1 = gh1 + gh1g[k].astype(F32)
        v = tokf[y].astype(F32)
        inv = inverse_norm(v)
        inner = gh1 * gain_one
        xh1 = v * inv
        igrad[...] = gres[...] + inv * (inner - xh1 * jnp.mean(inner * xh1, -1, keepdims=True))
        igrad_c = here(igrad, igrad_o)

        tail_n = dense_near(tail_x, tail)
        arrive(bx)
        for a in range(16):
            bsum[a] = (bz[xh, a].astype(F32) + bxg[a].astype(F32)).astype(BF)
        bo = [cp.start(bsum.at[p], bout.at[c], q) for p, q in zip(place_index, cpeers)]
        last.append(here(bsum.at[c], bout.at[c]))
        head_n = dense_near(head_x, head)
        outs = dense_y(tail_n, tail) + dense_y(head_n, head)

        lout[...] = (resid[...] + sum_end(1, last_o)).astype(BF)
        last += [igrad_c, here(lout, lout_o)]
        for copy in last:
            copy.wait()
        for copy in cp.started:
            if not any(copy is r for r in sent_already):
                copy.wait_send()
            if not any(copy is r for r in got_already):
                copy.wait_recv()

    pl.run_scoped(
        dense,
        pltpu.VMEM((2, 2, 64, 1536), BF),
        pltpu.VMEM((2, 2, 64, 1536), BF),
        pltpu.VMEM((1, 2, 2, 64, 1536), BF),
        pltpu.VMEM((1, 4, 64, 1536), BF),
        pltpu.VMEM((1536, 1152), BF),
        pltpu.VMEM((4, 128, 1536), BF),
        pltpu.VMEM((512, 640), BF),
        pltpu.VMEM((4, 4, 128, 256), BF),
        pltpu.VMEM((4, 384, 128), F32),
        pltpu.VMEM((512, 384), BF),
        pltpu.VMEM((512, 384), BF),
        pltpu.VMEM((2048, 128), F32),
        pltpu.VMEM((2048, 128), F32),
        pltpu.VMEM((4, 4, 128, 256), BF),
        pltpu.VMEM((512, 640), BF),
        pltpu.VMEM((4, 128, 1536), BF),
        pltpu.VMEM((4, 2, 2, 2, 4, 16, 1152), BF),
        pltpu.VMEM((2, 4, 2, 16, 1152), BF),
        pltpu.VMEM((2, 4, 16, 1152), BF),
        pltpu.VMEM((4, 16, 1152), BF),
        pltpu.VMEM((2, 16, 16, 256), BF),
        pltpu.VMEM((16, 16, 256), BF),
    )


def back(*ins):
    outs = (
        SDS((2, 3, 2, 4, 192, 512), BF),
        SDS((2, 16, 48, 1536), BF),
        SDS((2, 16, 48, 1536), BF),
        SDS((2, 16, 48, 1536), BF),
        SDS((16, 96, 256), BF),
        SDS((16, 96, 256), BF),
        SDS((8, 2, 128, 128), BF),
        SDS((8, 128, 128), BF),
        SDS((8, 2, 128, 128), BF),
        SDS((8, 128, 128), BF),
        SDS((2, 4, 2, 128, 1536), BF),
        SDS((2, 4, 2, 128, 1536), BF),
        SDS((3, 2, 3, 2, 192, 512), BF),
        SDS((2, 3, 2, 192, 512), BF),
        SDS((2, 3, 192, 512), BF),
        SDS((2, 2, 2, 64, 1536), BF),
        SDS((2, 4, 64, 1536), BF),
        SDS((4, 16, 1152), BF),
        SDS((16, 16, 256), BF),
        SDS((128, 1536), BF),
        SDS((128, 1536), F32),
    )
    out = pl.pallas_call(
        back_kernel,
        out_shape=outs,
        in_specs=[ANY] * len(ins),
        out_specs=(ANY,) * 21,
        scratch_shapes=[
            pltpu.SemaphoreType.DMA((128,)),
            pltpu.SemaphoreType.DMA((128,)),
            pltpu.SemaphoreType.DMA((80,)),
            pltpu.VMEM((128, 1536), BF),
            pltpu.VMEM((128, 1536), F32),
            pltpu.VMEM((2, 2, 2, 64, 1536), BF),
            pltpu.VMEM((2, 4, 64, 1536), BF),
            pltpu.VMEM((2, 2, 64, 1536), BF),
            pltpu.VMEM((2, 2, 64, 1536), BF),
            pltpu.VMEM((2, 2, 64, 1536), BF),
            pltpu.VMEM((2, 2, 64, 1536), BF),
            pltpu.VMEM((2, 3, 64, 1536), BF),
            pltpu.VMEM((2, 3, 64, 1536), BF),
            pltpu.VMEM((128, 1536), F32),
            pltpu.VMEM((128, 1536), BF),
            pltpu.VMEM((128, 1536), F32),
            pltpu.VMEM((4, 128, 1536), BF),
            pltpu.VMEM((3, 4, 128, 256), BF),
            pltpu.VMEM((3, 128, 1536), BF),
            pltpu.VMEM((4, 2, 2, 4, 16, 1152), BF),
            pltpu.VMEM((3, 4, 2, 2, 16, 1152), BF),
            pltpu.VMEM((4, 2, 16, 1152), BF),
            pltpu.VMEM((4, 16, 1152), BF),
            pltpu.VMEM((3, 16, 2, 16, 256), BF),
            pltpu.VMEM((16, 16, 256), BF),
            pltpu.VMEM((1536, 256), BF),
            pltpu.VMEM((1536, 256), BF),
            pltpu.VMEM((16, 2, 4, 16, 256), BF),
            pltpu.VMEM((256, 1536), F32),
        ],
        compiler_params=pltpu.CompilerParams(
            collective_id=2, has_side_effects=True, vmem_limit_bytes=62 * 2**20
        ),
        cost_estimate=pl.CostEstimate(flops=36 * 10**9, bytes_accessed=150 * 10**6, transcendentals=5 * 10**6),
    )(*ins)
    return out[19], out[20], out[17], out[18], out[13], out[14]


def unpack_kernel(
    lout, igrad, aout, bout, sb, xb,
    lout_o, igrad_o, gains_o, wq_o, wk_o, wv_o, wo_o, sg_o, su_o, sd_o, eg_o, eu_o, ed_o,
):
    xh = lax.axis_index("fsdp") // 4
    lout_o[...] = lout[...]
    igrad_o[...] = igrad[...]
    for e in range(2):
        for m, ref in enumerate((eg_o, eu_o, ed_o)):
            ref[xh * 2 + e] = sb[e, m, xh].astype(F32)
            ref[2 - xh * 2 + e] = xb[e, m].astype(F32)
    gain_sum = jnp.zeros((16, 128), F32)
    for k in range(4):
        wide, thin = slice(k * 384, (k + 1) * 384), slice(k * 128, (k + 1) * 128)
        block = aout[k].astype(F32)
        wq_o[:, wide] = block[:12, 0:384]
        wk_o[:, thin] = block[:12, 384:512]
        wv_o[:, thin] = block[:12, 512:640]
        gain_sum = gain_sum + block[:, 640:768]
        wo_o[:, wide] = block[:12, 768:1152]
    gains_o[...] = gain_sum
    front_half = lax.broadcasted_iota(jnp.int32, (16, 128), 1) < 64
    for k in range(8):
        at = slice(k * 128, (k + 1) * 128)
        one, two = bout[2 * k].astype(F32), bout[2 * k + 1].astype(F32)
        sg_o[:, at] = jnp.where(front_half, one[:, :128], half_turn(two[:, :128]))[:12]
        su_o[:, at] = jnp.where(front_half, half_turn(one[:, :128]), two[:, :128])[:12]
        sd_o[:, at] = jnp.where(front_half, one[:, 128:], half_turn(two[:, 128:]))[:12]


def unpack(*ins):
    outs = (
        SDS((128, 1536), BF),
        SDS((128, 1536), F32),
        SDS((16, 128), F32),
        SDS((12, 1536), F32),
        SDS((12, 512), F32),
        SDS((12, 512), F32),
        SDS((12, 1536), F32),
        SDS((12, 1024), F32),
        SDS((12, 1024), F32),
        SDS((12, 1024), F32),
        SDS((4, 192, 512), F32),
        SDS((4, 192, 512), F32),
        SDS((4, 192, 512), F32),
    )
    return pl.pallas_call(
        unpack_kernel,
        out_shape=outs,
        in_specs=[VM] * len(ins),
        out_specs=(VM,) * len(outs),
        compiler_params=pltpu.CompilerParams(vmem_limit_bytes=VMEM_LIMIT),
    )(*ins)


def local(
    tokens,
    cotangent,
    routes,
    gates,
    attn_gain,
    ffn_gain,
    w_query,
    w_key,
    w_value,
    w_out,
    shared_gate,
    shared_up,
    shared_down,
    expert_gate,
    expert_up,
    expert_down,
):
    tok = tokens.reshape(128, 1536)
    cot = cotangent.reshape(128, 1536)
    gains = jnp.stack([attn_gain, ffn_gain])
    (cot_f, h2_f, wexp, tok_f, kv_f, gy, pick, gated, gz, _, w, sw, qkv, att, lse, resid) = front(
        tok,
        cot,
        jnp.transpose(routes, (2, 0, 1)),
        jnp.transpose(gates, (2, 0, 1)),
        gains,
        w_query,
        w_key,
        w_value,
        w_out.T,
        shared_gate,
        shared_up,
        shared_down.T,
        expert_gate,
        expert_up,
        jnp.transpose(expert_down, (0, 2, 1)),
    )
    parts = back(
        pick, gated, gy, gz, wexp, h2_f, cot_f, resid, cot, w, sw, tok_f, qkv, kv_f, lse, att
    )
    (layer_out, input_grad, gain_grads, wq, wk, wv, wo, sg, su, sd, eg, eu, ed) = unpack(*parts)
    return (
        layer_out.reshape(1, 128, 1536),
        input_grad.reshape(1, 128, 1536),
        gain_grads[:12, 0],
        gain_grads[:12, 1],
        wq,
        wk,
        wv,
        wo.T,
        sg,
        su,
        sd.T,
        eg,
        eu,
        jnp.transpose(ed, (0, 2, 1)),
    )


def solution(mesh):
    both = ("ctx", "fsdp")
    rows = P("fsdp", "ctx", None)
    weights = (P(both),) * 2 + (P(both, None),) * 3 + (P(None, both),)
    weights = weights + (P(both, None),) * 2 + (P(None, both),)
    weights = weights + (P("ctx", "fsdp", None),) * 2 + (P("ctx", None, "fsdp"),)
    return jax.shard_map(
        local, mesh=mesh, in_specs=(rows,) * 4 + weights, out_specs=(rows,) * 2 + weights, check_vma=False
    )
```
